32 devices in a mesh: shard: 2 (over x), tensor: 4 (over z), section: 4 (over y, core).
Axes of the slice: x: 2, y: 2, z: 4, core: 2. Of those that a mesh axis runs over, the one named last changes fastest.
Arguments:
- activations: bfloat16 [8, 512, 2304], P(None, 'shard', ('tensor', 'section')), may hold values from -6 to 6
- router_grad: bfloat16 [8, 512], P(None, 'shard'), may hold values from -6 to 6
- token_ids: int32 [512], P('shard'), may hold values from 0 to 8191
- norm_terms: bfloat16 [2, 512, 2304], P(None, 'shard', ('tensor', 'section'))
- old_factors: float32 [8, 2304, 2304], P('shard', 'tensor', 'section'), as said below
- old_router_factor: float32 [8, 8], replicated, as said below
- old_norm_diag: float32 [2, 2304], P(None, ('tensor', 'section')), may hold values from 0.5 to 5
- old_embed_diag: float32 [8192], P('tensor'), may hold values from 0.05 to 0.5
Outputs:
- precond_attn: float32 [4, 2304, 2304], P(None, 'tensor', 'section')
- precond_router: float32 [8, 2304], P(None, 'tensor')
- precond_norms: float32 [2, 2304], P(None, ('tensor', 'section'))
- precond_embed: float32 [8192, 2304], P('tensor', 'section')
The draws below stay inside these ranges and needn't reach their ends.
Inputs may be any that keep to these rules, and one draw needn't show every extreme that they name: `old_factors`: each matrix is symmetric with a positive diagonal. `old_router_factor`: symmetric with a positive diagonal.
All inputs are finite; a program needn't handle non-finite values.
Results may differ from the reference program's by a relative error of at most 0.0083.
Values may be sent and summed in bfloat16 or wider, within the bound.
No kernel may reach another device: no remote copies, remote signals or barrier semaphores. Data moves between devices by JAX's collectives and lax.ppermute only.
A program may use at most 128 MiB of HBM per device.

```python
import math
import jax
import jax.numpy as jnp
import numpy as np
from jax import lax

D = 2304
EXPERTS = 8
VOCAB = 8192
NFAC = 8
TOK_DEV = 256
TOKENS = 512


def symmetric_factors(key, count, width):
    key_diag, key_off = jax.random.split(key)
    index = jnp.arange(width, dtype=jnp.float32)
    ramp = 1.0 + 2.0 * index / max(width - 1, 1)
    diag = jnp.exp(jax.random.uniform(key_diag, (count, width), jnp.float32, math.log(0.5), math.log(2.0))) * ramp
    raw = jnp.clip(jax.random.normal(key_off, (count, width, width), jnp.float32), -3.0, 3.0)
    paired = 0.5 * (raw + jnp.swapaxes(raw, 1, 2))
    root = jnp.sqrt(diag)
    offdiag = paired * (0.4 / math.sqrt(width)) * root[:, :, None] * root[:, None, :]
    identity = jnp.eye(width, dtype=jnp.float32)
    return offdiag * (1.0 - identity) + diag[:, :, None] * identity


def draw_old_factors(key, part):
    return symmetric_factors(jax.random.fold_in(key, 11), NFAC, D)


def draw_old_router_factor(key, part):
    return symmetric_factors(jax.random.fold_in(key, 12), 1, EXPERTS)[0]


def draw_norm_terms(key, part):
    inner = jax.random.fold_in(key, 13)
    blocks = TOKENS // TOK_DEV
    rows = (jnp.arange(TOKENS, dtype=jnp.int32) // TOK_DEV).astype(jnp.float32)
    ramp = 1.0 + 2.0 * rows / max(blocks - 1, 1)
    base = jnp.clip(jax.random.normal(inner, (2, TOKENS, D), jnp.float32), -5.0, 5.0)
    return (0.3 * base * ramp[None, :, None]).astype(jnp.bfloat16)


def touch_ends(values, rng, smallest, top_value):
    longest = values.shape.index(max(values.shape))
    spots = []
    for shift in (0, 1):
        where = [jax.random.randint(jax.random.fold_in(rng, axis), (), 0, length) for axis, length in enumerate(values.shape)]
        where[longest] = (where[longest] + shift) % values.shape[longest]
        spots.append(tuple(where))
    return values.at[spots[0]].set(smallest).at[spots[1]].set(top_value)


def block_levels(rng, shape, shards, low, largest):
    loudness = 1.0
    for dim, blocks in shards:
        draws = jax.random.uniform(jax.random.fold_in(jax.random.fold_in(rng, 6), dim), (blocks,), jnp.float32, low / len(shards), largest / len(shards))
        loudness = loudness * jnp.repeat(jnp.exp(draws), shape[dim] // blocks).reshape((-1,) + (1,) * (len(shape) - 1 - dim))
    return loudness


def rank_table(amount, lean):
    loads = [(1 << 20) // math.isqrt(rank ** lean) + 1 for rank in range(1, amount + 1)]
    scale = 1 + sum(loads) // (1 << 30)
    return np.cumsum(np.array([max(1, weight // scale) for weight in loads]))


def ranked(own_key, dims, number_of, lean):
    grid = rank_table(number_of, lean)
    ticket = jax.random.randint(jax.random.fold_in(own_key, 1), dims, 0, int(grid[number_of - 1]))
    rank = jnp.searchsorted(jnp.asarray(grid, jnp.int32), ticket, side="right")
    return jax.random.permutation(jax.random.fold_in(own_key, 2), number_of)[rank].astype(jnp.int32)


def centred(stream_key, shape, scale, limit, shards=(), kind=jnp.bfloat16):
    entries = scale * jax.random.normal(stream_key, shape, jnp.float32)
    if shards:
        entries = entries * block_levels(stream_key, shape, shards, -0.22, 0.18)
    return jnp.clip(entries, -limit, limit).astype(kind)


def setup_inputs(seed: int = 0) -> dict:
    splits = jax.random.split(jax.random.key(seed), 9)
    activations = centred(splits[0], (NFAC, TOKENS, D), 1.0, 6.0, ((1, 2), (2, 16)))
    router_grad = centred(splits[1], (EXPERTS, TOKENS), 1.0, 6.0, ((1, 2),))
    token_ids = touch_ends(ranked(splits[2], (TOKENS,), VOCAB, 2), jax.random.fold_in(splits[2], 3), 0, VOCAB - 1).astype(jnp.int32)
    norm_terms = draw_norm_terms(jax.random.fold_in(splits[8], 71), 0)
    old_factors = draw_old_factors(jax.random.fold_in(splits[8], 71), 0)
    old_router_factor = draw_old_router_factor(jax.random.fold_in(splits[8], 71), 0)
    old_norm_diag = jnp.clip(jnp.exp(math.log(5.0) - 2.3025851 * jax.random.uniform(splits[6], (2, D), jnp.float32) ** block_levels(splits[6], (2, D), ((1, 16),), -0.2, 0.2)), 0.5, 5.0)
    old_embed_diag = jnp.clip(jnp.exp(math.log(0.5) - 2.3025851 * jax.random.uniform(splits[7], (VOCAB,), jnp.float32) ** block_levels(splits[7], (VOCAB,), ((0, 4),), -0.2, 0.2)), 0.05, 0.5)
    return {"activations": activations, "router_grad": router_grad, "token_ids": token_ids, "norm_terms": norm_terms, "old_factors": old_factors, "old_router_factor": old_router_factor, "old_norm_diag": old_norm_diag, "old_embed_diag": old_embed_diag}


factor_decay = 0.5
damping = 0.01
learning_rate = 0.05


def newton_schulz(matrix):
    width = matrix.shape[0]
    trace = jnp.sum(jnp.diagonal(matrix))
    factor_scale = width / (3.0 * trace)
    identity = jnp.eye(width, dtype=jnp.float32)
    matrix_low = lax.optimization_barrier(matrix.astype(jnp.bfloat16))
    first = 2.0 * factor_scale * identity - factor_scale * factor_scale * matrix_low.astype(jnp.float32)
    first_low = first.astype(jnp.bfloat16)
    image = jnp.dot(matrix_low, first_low, preferred_element_type=jnp.float32).astype(jnp.bfloat16)
    product = jnp.dot(first_low, image, preferred_element_type=jnp.float32)
    return (2.0 * first - product).astype(jnp.bfloat16)


def reference(activations, router_grad, token_ids, norm_terms, old_factors, old_router_factor, old_norm_diag, old_embed_diag):
    identity = jnp.eye(D, dtype=jnp.float32)
    inverses = []
    for index in range(NFAC):
        features = activations[index]
        fresh = jnp.dot(features.T, features, preferred_element_type=jnp.float32) / TOKENS
        matrix = factor_decay * old_factors[index] + (1.0 - factor_decay) * fresh + damping * identity
        inverses.append(newton_schulz(matrix))
    lefts = [jnp.dot(activations[m], inverses[m].T, preferred_element_type=jnp.float32).astype(jnp.bfloat16) for m in (0, 4, 6)]
    rights = [jnp.dot(activations[m], inverses[m], preferred_element_type=jnp.float32).astype(jnp.bfloat16) for m in (1, 2, 3, 5, 7)]
    pairs = ((0, 0), (0, 1), (0, 2), (1, 3))
    precond_attn = jnp.stack([learning_rate * jnp.dot(lefts[p].T, rights[w], preferred_element_type=jnp.float32) for p, w in pairs])
    router_fresh = jnp.dot(router_grad, router_grad.T, preferred_element_type=jnp.float32) / TOKENS
    router_matrix = factor_decay * old_router_factor + (1.0 - factor_decay) * router_fresh + damping * jnp.eye(EXPERTS, dtype=jnp.float32)
    router_inverse = newton_schulz(router_matrix)
    router_right = jnp.dot(router_grad.T, router_inverse, preferred_element_type=jnp.float32).astype(jnp.bfloat16)
    precond_router = learning_rate * jnp.dot(router_right.T, lefts[2], preferred_element_type=jnp.float32)
    norm_values = norm_terms.astype(jnp.float32)
    norm_total = jnp.sum(norm_values, axis=1)
    norm_squares = jnp.sum(norm_values * norm_values, axis=1)
    precond_norms = learning_rate * norm_total / (factor_decay * old_norm_diag + (1.0 - factor_decay) * (norm_squares / TOKENS) + damping)
    vocab_ids = jnp.arange(VOCAB, dtype=jnp.int32)
    onehot = (vocab_ids[:, None] == token_ids[None, :]).astype(jnp.bfloat16)
    embed_sum = jnp.dot(onehot, rights[4], preferred_element_type=jnp.float32)
    counts = jnp.sum(onehot, axis=1, dtype=jnp.float32)
    divisor = factor_decay * old_embed_diag + (1.0 - factor_decay) * (counts / TOKENS) + damping
    precond_embed = learning_rate * embed_sum / divisor[:, None]
    return (precond_attn, precond_router, precond_norms, precond_embed)
```

```python
import math

import jax
import jax.numpy as jnp
from jax import lax
from jax.sharding import PartitionSpec as P

D = 2304
EXPERTS = 8
VOCAB = 8192


factor_decay = 0.5
damping = 0.01
learning_rate = 0.05


def local_inverse(matrix):
    width = matrix.shape[0]
    trace = jnp.sum(jnp.diagonal(matrix))
    factor_scale = width / (3.0 * trace)
    identity = jnp.eye(width, dtype=jnp.float32)
    matrix_low = lax.optimization_barrier(matrix.astype(jnp.bfloat16))
    first = 2.0 * factor_scale * identity - factor_scale * factor_scale * matrix_low.astype(
        jnp.float32
    )
    first_low = first.astype(jnp.bfloat16)
    image = jnp.dot(matrix_low, first_low, preferred_element_type=jnp.float32).astype(jnp.bfloat16)
    product = jnp.dot(first_low, image, preferred_element_type=jnp.float32)
    return (2.0 * first - product).astype(jnp.bfloat16)


def fold_with(columns, piece):
    return jnp.einsum("kij,kjl->kil", piece, columns, preferred_element_type=jnp.float32)


def general_plan(
    activations,
    router_grad,
    token_ids,
    norm_terms,
    old_factors,
    old_router_factor,
    old_norm_diag,
    old_embed_diag,
):
    n_tensor = lax.axis_size("tensor")
    n_section = lax.axis_size("section")
    n_shard = lax.axis_size("shard")
    tensor_rank = lax.axis_index("tensor")
    section_rank = lax.axis_index("section")
    row_block = D // n_tensor
    col_block = D // n_section
    tokens_all = activations.shape[1] * n_shard
    row_start = tensor_rank * row_block
    col_start = section_rank * col_block

    def collect(carry, piece):
        whole = lax.all_gather(piece, ("tensor", "section"), axis=1, tiled=True)
        rows_part = lax.dynamic_slice_in_dim(whole, row_start, row_block, 1)
        cols_part = lax.dynamic_slice_in_dim(whole, col_start, col_block, 1)
        return (carry, (rows_part, cols_part))

    unused_carry, (row_parts, col_parts) = lax.scan(collect, jnp.int32(0), activations)
    partial_value = jnp.einsum(
        "mnr,mnc->mrc", row_parts, col_parts, preferred_element_type=jnp.float32
    )
    fresh = lax.psum_scatter(partial_value, "shard", scatter_dimension=0, tiled=True) / tokens_all
    row_index = lax.broadcasted_iota(jnp.int32, (row_block, col_block), 0) + row_start
    col_index = lax.broadcasted_iota(jnp.int32, (row_block, col_block), 1) + col_start
    eye_block = (row_index == col_index).astype(jnp.float32)
    matrix = factor_decay * old_factors + (1.0 - factor_decay) * fresh + damping * eye_block
    diag_part = jnp.sum(matrix * eye_block, axis=(1, 2))
    trace = lax.psum(diag_part, ("tensor", "section"))
    factor_scale = (D / (3.0 * trace))[:, None, None]
    matrix_low = lax.optimization_barrier(matrix.astype(jnp.bfloat16))
    first = 2.0 * factor_scale * eye_block - factor_scale * factor_scale * matrix_low.astype(
        jnp.float32
    )
    first_low = first.astype(jnp.bfloat16)
    first_cols = lax.all_gather(first_low, "tensor", axis=1, tiled=True)
    image = fold_with(first_cols, lax.all_gather(matrix_low, "section", axis=2, tiled=True))
    image_cols = lax.all_gather(image.astype(jnp.bfloat16), "tensor", axis=1, tiled=True)
    product = fold_with(image_cols, lax.all_gather(first_low, "section", axis=2, tiled=True))
    inverse_low = (2.0 * first - product).astype(jnp.bfloat16)
    inverses = lax.all_gather(inverse_low, "shard", axis=0, tiled=True)
    left_terms = jnp.stack(
        [
            jnp.einsum("nc,rc->nr", col_parts[m], inverses[m], preferred_element_type=jnp.float32)
            for m in (0, 4, 6)
        ]
    )
    left = lax.psum(left_terms, "section").astype(jnp.bfloat16)
    right_terms = jnp.stack(
        [
            jnp.einsum("nr,rc->nc", row_parts[m], inverses[m], preferred_element_type=jnp.float32)
            for m in (1, 2, 3, 5, 7)
        ]
    )
    right = lax.psum(right_terms, "tensor").astype(jnp.bfloat16)
    norm_values = norm_terms.astype(jnp.float32)
    router_part = jnp.einsum(
        "en,fn->ef", router_grad, router_grad, preferred_element_type=jnp.float32
    )
    router_sum, norm_total, norm_squares = lax.psum(
        (router_part, jnp.sum(norm_values, axis=1), jnp.sum(norm_values * norm_values, axis=1)),
        "shard",
    )
    router_matrix = (
        factor_decay * old_router_factor
        + (1.0 - factor_decay) * (router_sum / tokens_all)
        + damping * jnp.eye(EXPERTS, dtype=jnp.float32)
    )
    router_inverse = local_inverse(router_matrix)
    router_right = jnp.einsum(
        "en,ef->nf", router_grad, router_inverse, preferred_element_type=jnp.float32
    ).astype(jnp.bfloat16)
    precond_norms = (
        learning_rate
        * norm_total
        / (
            factor_decay * old_norm_diag
            + (1.0 - factor_decay) * (norm_squares / tokens_all)
            + damping
        )
    )
    ids_all = lax.all_gather(token_ids, "shard", axis=0, tiled=True)
    embed_all = lax.all_gather(right[4], "shard", axis=0, tiled=True)
    paired_left = jnp.stack([left[0], left[0], left[0], left[1]])
    attn_terms = jnp.einsum(
        "wnr,wnc->wrc", paired_left, right[:4], preferred_element_type=jnp.float32
    )
    router_term = jnp.einsum("nf,nr->fr", router_right, left[2], preferred_element_type=jnp.float32)
    attn_sum, router_total = lax.psum((attn_terms, router_term), "shard")
    precond_attn = learning_rate * attn_sum
    precond_router = learning_rate * router_total
    vocab_block = VOCAB // n_tensor
    step_rows = math.gcd(vocab_block, 512)
    vocab_start = tensor_rank * vocab_block

    def embed_block(block_index):
        ids_here = vocab_start + block_index * step_rows + lax.iota(jnp.int32, step_rows)
        onehot = (ids_here[:, None] == ids_all[None, :]).astype(jnp.bfloat16)
        summed = jnp.dot(onehot, embed_all, preferred_element_type=jnp.float32)
        tallies = jnp.sum(onehot, axis=1, dtype=jnp.float32)
        return (summed, tallies)

    block_sums, block_counts = lax.map(
        embed_block, jnp.arange(vocab_block // step_rows, dtype=jnp.int32)
    )
    embed_sum = block_sums.reshape(vocab_block, col_block)
    counts = block_counts.reshape(vocab_block)
    divisor = factor_decay * old_embed_diag + (1.0 - factor_decay) * (counts / tokens_all) + damping
    precond_embed = learning_rate * embed_sum / divisor[:, None]
    return (precond_attn, precond_router, precond_norms, precond_embed)


def split_three(values):
    high = lax.reduce_precision(values, 8, 7)
    rest = values - high
    middle = lax.reduce_precision(rest, 8, 7)
    return jnp.stack([high, middle, rest - middle], axis=-2).astype(jnp.bfloat16)


def swap(value, axis, size, step):
    return lax.ppermute(value, axis, [(i, i ^ step) for i in range(size)])


def layer_plan(
    activations,
    router_grad,
    token_ids,
    norm_terms,
    old_factors,
    old_router_factor,
    old_norm_diag,
    old_embed_diag,
):
    n_tensor = lax.axis_size("tensor")
    n_section = lax.axis_size("section")
    n_shard = lax.axis_size("shard")
    layer = lax.axis_index("tensor")
    section = lax.axis_index("section")
    side = section // 2
    core = section % 2
    owned, row_block, col_block = old_factors.shape
    tokens = activations.shape[1]
    tokens_all = tokens * n_shard
    half = 2 * col_block
    weight = (1.0 - factor_decay) / tokens_all

    moved = lax.all_to_all(activations, ("shard", "tensor"), 0, 0, tiled=True)
    gathered = lax.all_gather(moved, "section", axis=0)
    features = gathered.reshape(n_section, n_shard, n_tensor, tokens, -1)
    features = features.transpose(1, 3, 2, 0, 4).reshape(tokens_all, D)

    row_index = lax.broadcasted_iota(jnp.int32, (row_block, col_block), 0) + layer * row_block
    col_index = lax.broadcasted_iota(jnp.int32, (row_block, col_block), 1) + section * col_block
    old_diag = jnp.sum(jnp.where(row_index == col_index, old_factors, 0.0), axis=1)
    parts = split_three(old_diag)
    message = jnp.concatenate(
        [old_factors.astype(jnp.bfloat16), jnp.pad(parts, ((0, 0), (0, 13), (0, 0)))], axis=1
    )
    blocks = lax.all_to_all(message, "tensor", 0, 0, tiled=True)
    old_traces = lax.psum(jnp.sum(old_diag, axis=1), ("tensor", "section"))
    diag_here = jnp.sum(
        blocks[:, row_block : row_block + 3].astype(jnp.float32), axis=(0, 1)
    )
    own_cols = lax.dynamic_slice_in_dim(features, section * col_block, col_block, 1)
    fresh = jnp.einsum("nr,nc->rc", features, own_cols, preferred_element_type=jnp.float32)
    on_diag = lax.broadcasted_iota(jnp.int32, (D, col_block), 0) == (
        lax.broadcasted_iota(jnp.int32, (D, col_block), 1) + section * col_block
    )
    old_cols = blocks[:, :row_block].reshape(D, col_block).astype(jnp.float32)
    matrix = (
        factor_decay * jnp.where(on_diag, diag_here[None, :], old_cols)
        + weight * fresh
        + jnp.where(on_diag, damping, 0.0)
    )
    matrix_low = matrix.astype(jnp.bfloat16)
    matrix_diag = jnp.sum(jnp.where(on_diag, matrix, 0.0), axis=0)
    other_cols = swap(matrix_low, "section", n_section, 1)
    other_diag = swap(matrix_diag, "section", n_section, 1)
    first_core = core == 0
    cols_low = jnp.concatenate(
        [jnp.where(first_core, matrix_low, other_cols), jnp.where(first_core, other_cols, matrix_low)],
        axis=1,
    )
    low_diag = lax.reduce_precision(
        jnp.concatenate(
            [
                jnp.where(first_core, matrix_diag, other_diag),
                jnp.where(first_core, other_diag, matrix_diag),
            ]
        ),
        8,
        7,
    )

    values = features.astype(jnp.float32)
    trace = (
        factor_decay * lax.dynamic_index_in_dim(old_traces, layer, 0, False)
        + weight * jnp.sum(values * values)
        + damping * D
    )
    scale = D / (3.0 * trace)
    square = scale * scale
    first_diag = lax.reduce_precision(2.0 * scale - square * low_diag, 8, 7)

    def whole_rows(mine):
        theirs = swap(mine, "section", n_section, 2)
        return jnp.concatenate(
            [jnp.where(side == 0, mine, theirs), jnp.where(side == 0, theirs, mine)], axis=1
        )

    def times(rows):
        return jnp.dot(rows, cols_low, preferred_element_type=jnp.float32)

    rows = lax.dynamic_slice_in_dim(features, core * tokens, tokens, 0)
    rows_half = lax.dynamic_slice_in_dim(rows, side * half, half, 1).astype(jnp.float32)
    product = times(rows)
    by_first = 2.0 * scale * rows_half - square * product
    step_one = first_diag * rows_half - square * (product - low_diag * rows_half)
    step_one_low = lax.reduce_precision(step_one, 8, 7)
    step_two = times(whole_rows(step_one_low.astype(jnp.bfloat16))) + low_diag * (
        step_one - step_one_low
    )
    step_two_low = lax.reduce_precision(step_two, 8, 7)
    step_three = first_diag * step_two - square * (
        times(whole_rows(step_two_low.astype(jnp.bfloat16))) - low_diag * step_two_low
    )
    result = (2.0 * by_first - step_three).astype(jnp.bfloat16)

    keep = lax.dynamic_slice_in_dim(result, core * col_block, col_block, 1)
    give = lax.dynamic_slice_in_dim(result, (1 - core) * col_block, col_block, 1)
    got = swap(give, "section", n_section, 1)
    own = jnp.concatenate([jnp.where(first_core, keep, got), jnp.where(first_core, got, keep)], axis=0)
    results = lax.all_gather(own, ("shard", "tensor"), axis=0)

    grad_all = lax.all_gather(router_grad, "shard", axis=1, tiled=True)
    ids_all = lax.all_gather(token_ids, "shard", axis=0, tiled=True)
    norm_values = norm_terms.astype(jnp.float32)
    norm_total, norm_squares = lax.psum(
        (jnp.sum(norm_values, axis=1), jnp.sum(norm_values * norm_values, axis=1)), "shard"
    )
    router_matrix = (
        factor_decay * old_router_factor
        + weight * jnp.einsum("en,fn->ef", grad_all, grad_all, preferred_element_type=jnp.float32)
        + damping * jnp.eye(EXPERTS, dtype=jnp.float32)
    )
    router_inverse = local_inverse(router_matrix)
    router_right = jnp.einsum(
        "en,ef->fn", grad_all, router_inverse, preferred_element_type=jnp.float32
    ).astype(jnp.bfloat16)
    precond_norms = (
        learning_rate
        * norm_total
        / (
            factor_decay * old_norm_diag
            + (1.0 - factor_decay) * (norm_squares / tokens_all)
            + damping
        )
    )

    router_cols = learning_rate * jnp.dot(
        router_right, results[6], preferred_element_type=jnp.float32
    )
    router_high = lax.reduce_precision(router_cols, 8, 7)
    bundle = jnp.concatenate(
        [
            results[0],
            results[4],
            router_high.astype(jnp.bfloat16),
            (router_cols - router_high).astype(jnp.bfloat16),
        ],
        axis=0,
    )

    def place(index, step):
        return index * n_section + (index ^ step)

    both = ("tensor", "section")
    across = lax.ppermute(bundle, both, [(place(i, 0), place(i, 2)) for i in range(n_tensor)])
    bundle = jnp.where(section == layer, bundle, across)
    near = lax.ppermute(
        bundle,
        both,
        [(place(i, 0), place(i, 1)) for i in range(n_tensor)]
        + [(place(i, 2), place(i, 3)) for i in range(n_tensor)],
    )
    bundle = jnp.where((section ^ layer) % 2 == 0, bundle, near)
    left_query = bundle[:tokens_all]
    left_out = bundle[tokens_all : 2 * tokens_all]
    tail = bundle[2 * tokens_all :].astype(jnp.float32)
    precond_router = tail[:EXPERTS] + tail[EXPERTS:]
    lefts = jnp.stack([left_query, left_query, left_query, left_out])
    rights = jnp.stack([results[1], results[2], results[3], results[5]])
    precond_attn = learning_rate * jnp.einsum(
        "wnr,wnc->wrc", lefts, rights, preferred_element_type=jnp.float32
    )

    vocab_block = old_embed_diag.shape[0]
    ids_here = layer * vocab_block + lax.iota(jnp.int32, vocab_block)
    matches = ids_here[:, None] == ids_all[None, :]
    counts = jnp.sum(matches.astype(jnp.float32), axis=1)
    divisor = factor_decay * old_embed_diag + (1.0 - factor_decay) * (counts / tokens_all) + damping
    embed_sum = jnp.dot(
        matches.astype(jnp.bfloat16), results[7], preferred_element_type=jnp.float32
    )
    precond_embed = embed_sum * (learning_rate / divisor)[:, None]
    return (precond_attn, precond_router, precond_norms, precond_embed)


def per_device(*arguments):
    one_each = arguments[4].shape[0] == lax.axis_size("tensor") == lax.axis_size("section")
    if one_each and lax.axis_size("section") == 4 and lax.axis_size("shard") == 2:
        return layer_plan(*arguments)
    return general_plan(*arguments)


def solution(mesh):
    return jax.shard_map(
        per_device,
        mesh=mesh,
        in_specs=(
            P(None, "shard", ("tensor", "section")),
            P(None, "shard"),
            P("shard"),
            P(None, "shard", ("tensor", "section")),
            P("shard", "tensor", "section"),
            P(),
            P(None, ("tensor", "section")),
            P("tensor"),
        ),
        out_specs=(
            P(None, "tensor", "section"),
            P(None, "tensor"),
            P(None, ("tensor", "section")),
            P("tensor", "section"),
        ),
        check_vma=False,
    )
```

```python
import math

import jax
import jax.numpy as jnp
from jax import lax
from jax.experimental import pallas as pl
from jax.experimental.pallas import tpu as pltpu
from jax.sharding import PartitionSpec as P

D = 2304
EXPERTS = 8
VOCAB = 8192


factor_decay = 0.5
damping = 0.01
learning_rate = 0.05


def local_inverse(matrix):
    width = matrix.shape[0]
    trace = jnp.sum(jnp.diagonal(matrix))
    factor_scale = width / (3.0 * trace)
    identity = jnp.eye(width, dtype=jnp.float32)
    matrix_low = lax.optimization_barrier(matrix.astype(jnp.bfloat16))
    first = 2.0 * factor_scale * identity - factor_scale * factor_scale * matrix_low.astype(
        jnp.float32
    )
    first_low = first.astype(jnp.bfloat16)
    image = jnp.dot(matrix_low, first_low, preferred_element_type=jnp.float32).astype(jnp.bfloat16)
    product = jnp.dot(first_low, image, preferred_element_type=jnp.float32)
    return (2.0 * first - product).astype(jnp.bfloat16)


def fold_with(columns, piece):
    return jnp.einsum("kij,kjl->kil", piece, columns, preferred_element_type=jnp.float32)


def general_plan(
    activations,
    router_grad,
    token_ids,
    norm_terms,
    old_factors,
    old_router_factor,
    old_norm_diag,
    old_embed_diag,
):
    n_tensor = lax.axis_size("tensor")
    n_section = lax.axis_size("section")
    n_shard = lax.axis_size("shard")
    tensor_rank = lax.axis_index("tensor")
    section_rank = lax.axis_index("section")
    row_block = D // n_tensor
    col_block = D // n_section
    tokens_all = activations.shape[1] * n_shard
    row_start = tensor_rank * row_block
    col_start = section_rank * col_block

    def collect(carry, piece):
        whole = lax.all_gather(piece, ("tensor", "section"), axis=1, tiled=True)
        rows_part = lax.dynamic_slice_in_dim(whole, row_start, row_block, 1)
        cols_part = lax.dynamic_slice_in_dim(whole, col_start, col_block, 1)
        return (carry, (rows_part, cols_part))

    unused_carry, (row_parts, col_parts) = lax.scan(collect, jnp.int32(0), activations)
    partial_value = jnp.einsum(
        "mnr,mnc->mrc", row_parts, col_parts, preferred_element_type=jnp.float32
    )
    fresh = lax.psum_scatter(partial_value, "shard", scatter_dimension=0, tiled=True) / tokens_all
    row_index = lax.broadcasted_iota(jnp.int32, (row_block, col_block), 0) + row_start
    col_index = lax.broadcasted_iota(jnp.int32, (row_block, col_block), 1) + col_start
    eye_block = (row_index == col_index).astype(jnp.float32)
    matrix = factor_decay * old_factors + (1.0 - factor_decay) * fresh + damping * eye_block
    diag_part = jnp.sum(matrix * eye_block, axis=(1, 2))
    trace = lax.psum(diag_part, ("tensor", "section"))
    factor_scale = (D / (3.0 * trace))[:, None, None]
    matrix_low = lax.optimization_barrier(matrix.astype(jnp.bfloat16))
    first = 2.0 * factor_scale * eye_block - factor_scale * factor_scale * matrix_low.astype(
        jnp.float32
    )
    first_low = first.astype(jnp.bfloat16)
    first_cols = lax.all_gather(first_low, "tensor", axis=1, tiled=True)
    image = fold_with(first_cols, lax.all_gather(matrix_low, "section", axis=2, tiled=True))
    image_cols = lax.all_gather(image.astype(jnp.bfloat16), "tensor", axis=1, tiled=True)
    product = fold_with(image_cols, lax.all_gather(first_low, "section", axis=2, tiled=True))
    inverse_low = (2.0 * first - product).astype(jnp.bfloat16)
    inverses = lax.all_gather(inverse_low, "shard", axis=0, tiled=True)
    left_terms = jnp.stack(
        [
            jnp.einsum("nc,rc->nr", col_parts[m], inverses[m], preferred_element_type=jnp.float32)
            for m in (0, 4, 6)
        ]
    )
    left = lax.psum(left_terms, "section").astype(jnp.bfloat16)
    right_terms = jnp.stack(
        [
            jnp.einsum("nr,rc->nc", row_parts[m], inverses[m], preferred_element_type=jnp.float32)
            for m in (1, 2, 3, 5, 7)
        ]
    )
    right = lax.psum(right_terms, "tensor").astype(jnp.bfloat16)
    norm_values = norm_terms.astype(jnp.float32)
    router_part = jnp.einsum(
        "en,fn->ef", router_grad, router_grad, preferred_element_type=jnp.float32
    )
    router_sum, norm_total, norm_squares = lax.psum(
        (router_part, jnp.sum(norm_values, axis=1), jnp.sum(norm_values * norm_values, axis=1)),
        "shard",
    )
    router_matrix = (
        factor_decay * old_router_factor
        + (1.0 - factor_decay) * (router_sum / tokens_all)
        + damping * jnp.eye(EXPERTS, dtype=jnp.float32)
    )
    router_inverse = local_inverse(router_matrix)
    router_right = jnp.einsum(
        "en,ef->nf", router_grad, router_inverse, preferred_element_type=jnp.float32
    ).astype(jnp.bfloat16)
    precond_norms = (
        learning_rate
        * norm_total
        / (
            factor_decay * old_norm_diag
            + (1.0 - factor_decay) * (norm_squares / tokens_all)
            + damping
        )
    )
    ids_all = lax.all_gather(token_ids, "shard", axis=0, tiled=True)
    embed_all = lax.all_gather(right[4], "shard", axis=0, tiled=True)
    paired_left = jnp.stack([left[0], left[0], left[0], left[1]])
    attn_terms = jnp.einsum(
        "wnr,wnc->wrc", paired_left, right[:4], preferred_element_type=jnp.float32
    )
    router_term = jnp.einsum("nf,nr->fr", router_right, left[2], preferred_element_type=jnp.float32)
    attn_sum, router_total = lax.psum((attn_terms, router_term), "shard")
    precond_attn = learning_rate * attn_sum
    precond_router = learning_rate * router_total
    vocab_block = VOCAB // n_tensor
    step_rows = math.gcd(vocab_block, 512)
    vocab_start = tensor_rank * vocab_block

    def embed_block(block_index):
        ids_here = vocab_start + block_index * step_rows + lax.iota(jnp.int32, step_rows)
        onehot = (ids_here[:, None] == ids_all[None, :]).astype(jnp.bfloat16)
        summed = jnp.dot(onehot, embed_all, preferred_element_type=jnp.float32)
        tallies = jnp.sum(onehot, axis=1, dtype=jnp.float32)
        return (summed, tallies)

    block_sums, block_counts = lax.map(
        embed_block, jnp.arange(vocab_block // step_rows, dtype=jnp.int32)
    )
    embed_sum = block_sums.reshape(vocab_block, col_block)
    counts = block_counts.reshape(vocab_block)
    divisor = factor_decay * old_embed_diag + (1.0 - factor_decay) * (counts / tokens_all) + damping
    precond_embed = learning_rate * embed_sum / divisor[:, None]
    return (precond_attn, precond_router, precond_norms, precond_embed)


def split_three(values):
    high = lax.reduce_precision(values, 8, 7)
    rest = values - high
    middle = lax.reduce_precision(rest, 8, 7)
    return jnp.stack([high, middle, rest - middle], axis=-2).astype(jnp.bfloat16)


def swap(value, axis, size, step):
    return lax.ppermute(value, axis, [(i, i ^ step) for i in range(size)])


def local_diagonals(blocks):
    width = blocks.shape[1]
    pieces = []
    for start in range(0, width, 128):
        size = min(128, width - start)
        tile = blocks[:, start : start + size, start : start + size]
        pieces.append(jnp.sum(tile * jnp.eye(size, dtype=tile.dtype), axis=1))
    return jnp.concatenate(pieces, axis=1)


def attn_kernel(shard_ref, left_own, left_other, own_1, own_2, own_3, other_1, other_2, other_3, out):
    first = shard_ref[0] == 0

    def product(left, right):
        out[0] = learning_rate * lax.dot_general(
            left, right, (((1,), (1,)), ((), ())), preferred_element_type=jnp.float32
        )

    @pl.when(pl.program_id(0) == 0)
    def _():
        left = jnp.where(first, left_own[...], left_other[...])
        product(left, jnp.where(first, own_1[...], other_1[...]))

    @pl.when(pl.program_id(0) == 1)
    def _():
        left = jnp.where(first, left_own[...], left_other[...])
        product(left, jnp.where(first, own_2[...], other_2[...]))

    @pl.when(pl.program_id(0) == 2)
    def _():
        left = jnp.where(first, left_own[...], left_other[...])
        product(left, jnp.where(first, own_3[...], other_3[...]))

    @pl.when(pl.program_id(0) == 3)
    def _():
        left = jnp.where(first, left_other[...], left_own[...])
        product(left, jnp.where(first, other_1[...], own_1[...]))


def attn_products(shard, operands):
    rows, tokens_all = operands[0].shape
    cols = operands[2].shape[0]
    whole = [pl.BlockSpec(value.shape, lambda w: (0, 0)) for value in operands]
    return pl.pallas_call(
        attn_kernel,
        grid=(4,),
        out_shape=jax.ShapeDtypeStruct((4, rows, cols), jnp.float32),
        in_specs=[pl.BlockSpec(memory_space=pltpu.SMEM)] + whole,
        out_specs=pl.BlockSpec((1, rows, cols), lambda w: (w, 0, 0)),
        compiler_params=pltpu.CompilerParams(vmem_limit_bytes=40 * 1024 * 1024),
        cost_estimate=pl.CostEstimate(
            flops=8 * rows * cols * tokens_all,
            bytes_accessed=16 * rows * cols + 16 * rows * tokens_all,
            transcendentals=0,
        ),
    )(shard.reshape(1), *operands)


def layer_plan(
    activations,
    router_grad,
    token_ids,
    norm_terms,
    old_factors,
    old_router_factor,
    old_norm_diag,
    old_embed_diag,
):
    n_tensor = lax.axis_size("tensor")
    n_section = lax.axis_size("section")
    n_shard = lax.axis_size("shard")
    shard = lax.axis_index("shard")
    layer = lax.axis_index("tensor")
    section = lax.axis_index("section")
    core = section % 2
    owned, row_block, col_block = old_factors.shape
    tokens = activations.shape[1]
    features_dev = activations.shape[2]
    tokens_all = tokens * n_shard
    half = 2 * col_block
    weight = (1.0 - factor_decay) / tokens_all
    half_place = (section // 2) ^ (layer // 2)
    core_place = core ^ (layer % 2)
    own_place = section ^ layer

    blocks = [None] * n_tensor
    for step in (3, 2, 1):
        away = lax.dynamic_index_in_dim(old_factors, layer ^ step, 0, False)
        blocks[step] = swap(away.astype(jnp.bfloat16), "tensor", n_tensor, step)
    blocks[0] = lax.dynamic_index_in_dim(old_factors, layer, 0, False).astype(jnp.bfloat16)

    diagonals = local_diagonals(old_factors) * (layer == section).astype(jnp.float32)
    extra = jnp.pad(split_three(diagonals), ((0, 0), (0, 0), (0, 3 * tokens - col_block)))
    extra = jnp.pad(extra.reshape(owned, 9, tokens), ((0, 0), (0, 7), (0, 0)))
    extra = jnp.concatenate(
        [jnp.where(shard == 0, extra, 0), jnp.where(shard == 1, extra, 0)], axis=0
    )
    message = jnp.concatenate([jnp.swapaxes(activations, 1, 2), extra], axis=1)
    moved = lax.all_to_all(message, ("shard", "tensor"), 0, 0, tiled=True)
    gathered = lax.all_gather(moved, "section", axis=0)
    gathered = gathered.reshape(n_section, n_shard, n_tensor, features_dev + 16, tokens)
    by_place = [
        lax.dynamic_index_in_dim(gathered, layer ^ step, 2, False) for step in range(n_tensor)
    ]
    features = jnp.stack([part[:, :, :features_dev] for part in by_place], axis=0)
    features = features.transpose(2, 0, 1, 3, 4).reshape(n_shard, D, tokens)
    codes = jnp.sum(
        gathered[:, :, :, features_dev : features_dev + 9].astype(jnp.float32), axis=(1, 2)
    )
    old_diag = jnp.sum(codes.reshape(n_section, 3, 3 * tokens), axis=1)[:, :col_block]
    old_diag = jnp.concatenate(
        [
            lax.dynamic_index_in_dim(old_diag, layer ^ step, 0, False)
            for step in range(n_tensor)
        ]
    )
    values = features.astype(jnp.float32)
    squares = jnp.sum(values * values, axis=(0, 2))
    matrix_diag = factor_decay * old_diag + weight * squares + damping
    scale = D / (3.0 * jnp.sum(matrix_diag))
    square = scale * scale
    all_low_diag = lax.reduce_precision(matrix_diag, 8, 7)
    low_diag = lax.dynamic_slice_in_dim(all_low_diag, half_place * half, half, 0)
    own_diag = lax.dynamic_slice_in_dim(all_low_diag, own_place * col_block, col_block, 0)
    first_diag = lax.reduce_precision(2.0 * scale - square * low_diag, 8, 7)
    rows = jnp.swapaxes(lax.dynamic_index_in_dim(features, core, 0, False), 0, 1)
    rows_half = lax.dynamic_slice_in_dim(rows, half_place * half, half, 1).astype(jnp.float32)

    own_features = lax.dynamic_slice_in_dim(features, own_place * col_block, col_block, 1)
    eye = lax.broadcasted_iota(jnp.int32, (row_block, col_block), 0) == lax.broadcasted_iota(
        jnp.int32, (row_block, col_block), 1
    )
    low_blocks = []
    for step in range(n_tensor):
        part = features[:, step * row_block : (step + 1) * row_block]
        fresh = jnp.einsum("xrn,xcn->rc", part, own_features, preferred_element_type=jnp.float32)
        block = factor_decay * blocks[step].astype(jnp.float32) + weight * fresh
        low_blocks.append(
            jnp.where(eye & (own_place == step), own_diag[None, :], block).astype(jnp.bfloat16)
        )
    own_cols = jnp.concatenate(low_blocks, axis=0)
    other_cols = swap(own_cols, "section", n_section, 1)

    def whole_rows(mine):
        theirs = swap(mine, "section", n_section, 2)
        low = half_place == 0
        return jnp.concatenate(
            [jnp.where(low, mine, theirs), jnp.where(low, theirs, mine)], axis=1
        )

    def times(left):
        own = jnp.dot(left, own_cols, preferred_element_type=jnp.float32)
        other = jnp.dot(left, other_cols, preferred_element_type=jnp.float32)
        low = core_place == 0
        return jnp.concatenate([jnp.where(low, own, other), jnp.where(low, other, own)], axis=1)

    product = times(rows)
    by_first = 2.0 * scale * rows_half - square * product
    step_one = first_diag * rows_half - square * (product - low_diag * rows_half)
    step_one_low = lax.reduce_precision(step_one, 8, 7)
    step_two = times(whole_rows(step_one_low.astype(jnp.bfloat16))) + low_diag * (
        step_one - step_one_low
    )
    step_two_low = lax.reduce_precision(step_two, 8, 7)
    step_three = first_diag * step_two - square * (
        times(whole_rows(step_two_low.astype(jnp.bfloat16))) - low_diag * step_two_low
    )
    result = jnp.swapaxes((2.0 * by_first - step_three).astype(jnp.bfloat16), 0, 1)

    keep = lax.dynamic_slice_in_dim(result, core_place * col_block, col_block, 0)
    give = lax.dynamic_slice_in_dim(result, (1 - core_place) * col_block, col_block, 0)
    got = swap(give, "section", n_section, 1)
    own = jnp.concatenate(
        [jnp.where(core == 0, keep, got), jnp.where(core == 0, got, keep)], axis=1
    )

    axes = ("shard", "tensor")

    def send(value, moves):
        return lax.ppermute(
            value, axes, [(x * n_tensor + a, x * n_tensor + b) for x, a, b in moves]
        )

    down_1 = send(own, [(0, 3, 2), (0, 2, 1), (0, 1, 0), (1, 3, 2), (1, 1, 0)])
    up_1 = send(own, [(0, 1, 2), (0, 2, 3), (1, 1, 2)])
    down_2 = send(down_1, [(0, 2, 1), (0, 1, 0), (1, 2, 1)])
    up_2 = send(up_1, [(0, 2, 3), (1, 2, 3)])
    down_3 = send(down_2, [(0, 1, 0), (1, 1, 0)])

    def by_layer(*options):
        chosen = options[3]
        for index in (2, 1, 0):
            chosen = jnp.where(layer == index, options[index], chosen)
        return chosen

    own_1 = by_layer(down_1, own, up_1, up_2)
    own_2 = by_layer(down_2, down_1, own, up_1)
    own_3 = by_layer(down_3, down_2, down_1, own)
    other_1 = swap(own_1, "shard", n_shard, 1)
    other_2 = swap(own_2, "shard", n_shard, 1)
    other_3 = swap(own_3, "shard", n_shard, 1)

    everywhere = ("shard", "tensor", "section")

    def place(x, z, s):
        return (x * n_tensor + z) * n_section + s

    planes = range(n_shard)
    layers = range(n_tensor)

    def scatter(value, source):
        moved_here = lax.ppermute(
            value,
            everywhere,
            [(place(x, source, s), place(x, s, s)) for x in planes for s in layers if s != source],
        )
        return jnp.where(layer == source, value, moved_here)

    def across_shards(value):
        return lax.ppermute(
            value, everywhere, [(place(x, t, t), place(1 - x, t, t)) for x in planes for t in layers]
        )

    def hand_round(value):
        across = lax.ppermute(
            value, everywhere, [(place(x, t, t), place(x, t, t ^ 2)) for x in planes for t in layers]
        )
        value = jnp.where(section == layer, value, across)
        near = lax.ppermute(
            value,
            everywhere,
            [(place(x, t, t ^ a), place(x, t, t ^ a ^ 1)) for x in planes for t in layers for a in (0, 2)],
        )
        return jnp.where((section ^ layer) % 2 == 0, value, near)

    left_here = scatter(own, 0)
    left_there = across_shards(left_here)
    left_own = hand_round(left_here)
    left_other = hand_round(left_there)
    precond_attn = attn_products(
        shard, (left_own, left_other, own_1, own_2, own_3, other_1, other_2, other_3)
    )

    grad_all = lax.all_gather(router_grad, "shard", axis=1, tiled=True)
    ids_all = lax.all_gather(token_ids, "shard", axis=0, tiled=True)
    norm_values = norm_terms.astype(jnp.float32)
    norm_total, norm_squares = lax.psum(
        (jnp.sum(norm_values, axis=1), jnp.sum(norm_values * norm_values, axis=1)), "shard"
    )
    router_matrix = (
        factor_decay * old_router_factor
        + weight * jnp.einsum("en,fn->ef", grad_all, grad_all, preferred_element_type=jnp.float32)
        + damping * jnp.eye(EXPERTS, dtype=jnp.float32)
    )
    router_inverse = local_inverse(router_matrix)
    router_right = jnp.einsum(
        "en,ef->fn", grad_all, router_inverse, preferred_element_type=jnp.float32
    ).astype(jnp.bfloat16)
    precond_norms = (
        learning_rate
        * norm_total
        / (
            factor_decay * old_norm_diag
            + (1.0 - factor_decay) * (norm_squares / tokens_all)
            + damping
        )
    )
    router_cols = learning_rate * jnp.einsum(
        "fn,cn->fc", router_right, own, preferred_element_type=jnp.float32
    )
    router_swapped = swap(router_cols, "shard", n_shard, 1)
    router_cols = jnp.where(shard == 1, router_cols, router_swapped)
    precond_router = hand_round(scatter(router_cols, 2))

    vocab_block = old_embed_diag.shape[0]
    ids_here = layer * vocab_block + lax.iota(jnp.int32, vocab_block)
    matches = ids_here[:, None] == ids_all[None, :]
    counts = jnp.sum(matches.astype(jnp.float32), axis=1)
    divisor = factor_decay * old_embed_diag + (1.0 - factor_decay) * (counts / tokens_all) + damping
    embed_grads = jnp.where(shard == 1, own_3, other_3)
    embed_sum = jnp.einsum(
        "vn,cn->vc", matches.astype(jnp.bfloat16), embed_grads, preferred_element_type=jnp.float32
    )
    precond_embed = embed_sum * (learning_rate / divisor)[:, None]
    return (precond_attn, precond_router, precond_norms, precond_embed)


def per_device(*arguments):
    one_each = arguments[4].shape[0] == lax.axis_size("tensor") == lax.axis_size("section")
    if one_each and lax.axis_size("section") == 4 and lax.axis_size("shard") == 2:
        return layer_plan(*arguments)
    return general_plan(*arguments)


def solution(mesh):
    return jax.shard_map(
        per_device,
        mesh=mesh,
        in_specs=(
            P(None, "shard", ("tensor", "section")),
            P(None, "shard"),
            P("shard"),
            P(None, "shard", ("tensor", "section")),
            P("shard", "tensor", "section"),
            P(),
            P(None, ("tensor", "section")),
            P("tensor"),
        ),
        out_specs=(
            P(None, "tensor", "section"),
            P(None, "tensor"),
            P(None, ("tensor", "section")),
            P("tensor", "section"),
        ),
        check_vma=False,
    )
```

```python
import functools
import math

import jax
import jax.numpy as jnp
from jax import lax
from jax.experimental import pallas as pl
from jax.experimental.pallas import tpu as pltpu
from jax.sharding import PartitionSpec as P

D = 2304
EXPERTS = 8
VOCAB = 8192


factor_decay = 0.5
damping = 0.01
learning_rate = 0.05


def local_inverse(matrix):
    width = matrix.shape[0]
    trace = jnp.sum(jnp.diagonal(matrix))
    factor_scale = width / (3.0 * trace)
    identity = jnp.eye(width, dtype=jnp.float32)
    matrix_low = lax.optimization_barrier(matrix.astype(jnp.bfloat16))
    first = 2.0 * factor_scale * identity - factor_scale * factor_scale * matrix_low.astype(
        jnp.float32
    )
    first_low = first.astype(jnp.bfloat16)
    image = jnp.dot(matrix_low, first_low, preferred_element_type=jnp.float32).astype(jnp.bfloat16)
    product = jnp.dot(first_low, image, preferred_element_type=jnp.float32)
    return (2.0 * first - product).astype(jnp.bfloat16)


def fold_with(columns, piece):
    return jnp.einsum("kij,kjl->kil", piece, columns, preferred_element_type=jnp.float32)


def general_plan(
    activations,
    router_grad,
    token_ids,
    norm_terms,
    old_factors,
    old_router_factor,
    old_norm_diag,
    old_embed_diag,
):
    n_tensor = lax.axis_size("tensor")
    n_section = lax.axis_size("section")
    n_shard = lax.axis_size("shard")
    tensor_rank = lax.axis_index("tensor")
    section_rank = lax.axis_index("section")
    row_block = D // n_tensor
    col_block = D // n_section
    tokens_all = activations.shape[1] * n_shard
    row_start = tensor_rank * row_block
    col_start = section_rank * col_block

    def collect(carry, piece):
        whole = lax.all_gather(piece, ("tensor", "section"), axis=1, tiled=True)
        rows_part = lax.dynamic_slice_in_dim(whole, row_start, row_block, 1)
        cols_part = lax.dynamic_slice_in_dim(whole, col_start, col_block, 1)
        return (carry, (rows_part, cols_part))

    unused_carry, (row_parts, col_parts) = lax.scan(collect, jnp.int32(0), activations)
    partial_value = jnp.einsum(
        "mnr,mnc->mrc", row_parts, col_parts, preferred_element_type=jnp.float32
    )
    fresh = lax.psum_scatter(partial_value, "shard", scatter_dimension=0, tiled=True) / tokens_all
    row_index = lax.broadcasted_iota(jnp.int32, (row_block, col_block), 0) + row_start
    col_index = lax.broadcasted_iota(jnp.int32, (row_block, col_block), 1) + col_start
    eye_block = (row_index == col_index).astype(jnp.float32)
    matrix = factor_decay * old_factors + (1.0 - factor_decay) * fresh + damping * eye_block
    diag_part = jnp.sum(matrix * eye_block, axis=(1, 2))
    trace = lax.psum(diag_part, ("tensor", "section"))
    factor_scale = (D / (3.0 * trace))[:, None, None]
    matrix_low = lax.optimization_barrier(matrix.astype(jnp.bfloat16))
    first = 2.0 * factor_scale * eye_block - factor_scale * factor_scale * matrix_low.astype(
        jnp.float32
    )
    first_low = first.astype(jnp.bfloat16)
    first_cols = lax.all_gather(first_low, "tensor", axis=1, tiled=True)
    image = fold_with(first_cols, lax.all_gather(matrix_low, "section", axis=2, tiled=True))
    image_cols = lax.all_gather(image.astype(jnp.bfloat16), "tensor", axis=1, tiled=True)
    product = fold_with(image_cols, lax.all_gather(first_low, "section", axis=2, tiled=True))
    inverse_low = (2.0 * first - product).astype(jnp.bfloat16)
    inverses = lax.all_gather(inverse_low, "shard", axis=0, tiled=True)
    left_terms = jnp.stack(
        [
            jnp.einsum("nc,rc->nr", col_parts[m], inverses[m], preferred_element_type=jnp.float32)
            for m in (0, 4, 6)
        ]
    )
    left = lax.psum(left_terms, "section").astype(jnp.bfloat16)
    right_terms = jnp.stack(
        [
            jnp.einsum("nr,rc->nc", row_parts[m], inverses[m], preferred_element_type=jnp.float32)
            for m in (1, 2, 3, 5, 7)
        ]
    )
    right = lax.psum(right_terms, "tensor").astype(jnp.bfloat16)
    norm_values = norm_terms.astype(jnp.float32)
    router_part = jnp.einsum(
        "en,fn->ef", router_grad, router_grad, preferred_element_type=jnp.float32
    )
    router_sum, norm_total, norm_squares = lax.psum(
        (router_part, jnp.sum(norm_values, axis=1), jnp.sum(norm_values * norm_values, axis=1)),
        "shard",
    )
    router_matrix = (
        factor_decay * old_router_factor
        + (1.0 - factor_decay) * (router_sum / tokens_all)
        + damping * jnp.eye(EXPERTS, dtype=jnp.float32)
    )
    router_inverse = local_inverse(router_matrix)
    router_right = jnp.einsum(
        "en,ef->nf", router_grad, router_inverse, preferred_element_type=jnp.float32
    ).astype(jnp.bfloat16)
    precond_norms = (
        learning_rate
        * norm_total
        / (
            factor_decay * old_norm_diag
            + (1.0 - factor_decay) * (norm_squares / tokens_all)
            + damping
        )
    )
    ids_all = lax.all_gather(token_ids, "shard", axis=0, tiled=True)
    embed_all = lax.all_gather(right[4], "shard", axis=0, tiled=True)
    paired_left = jnp.stack([left[0], left[0], left[0], left[1]])
    attn_terms = jnp.einsum(
        "wnr,wnc->wrc", paired_left, right[:4], preferred_element_type=jnp.float32
    )
    router_term = jnp.einsum("nf,nr->fr", router_right, left[2], preferred_element_type=jnp.float32)
    attn_sum, router_total = lax.psum((attn_terms, router_term), "shard")
    precond_attn = learning_rate * attn_sum
    precond_router = learning_rate * router_total
    vocab_block = VOCAB // n_tensor
    step_rows = math.gcd(vocab_block, 512)
    vocab_start = tensor_rank * vocab_block

    def embed_block(block_index):
        ids_here = vocab_start + block_index * step_rows + lax.iota(jnp.int32, step_rows)
        onehot = (ids_here[:, None] == ids_all[None, :]).astype(jnp.bfloat16)
        summed = jnp.dot(onehot, embed_all, preferred_element_type=jnp.float32)
        tallies = jnp.sum(onehot, axis=1, dtype=jnp.float32)
        return (summed, tallies)

    block_sums, block_counts = lax.map(
        embed_block, jnp.arange(vocab_block // step_rows, dtype=jnp.int32)
    )
    embed_sum = block_sums.reshape(vocab_block, col_block)
    counts = block_counts.reshape(vocab_block)
    divisor = factor_decay * old_embed_diag + (1.0 - factor_decay) * (counts / tokens_all) + damping
    precond_embed = learning_rate * embed_sum / divisor[:, None]
    return (precond_attn, precond_router, precond_norms, precond_embed)


def split_three(values):
    high = lax.reduce_precision(values, 8, 7)
    rest = values - high
    middle = lax.reduce_precision(rest, 8, 7)
    return jnp.stack([high, middle, rest - middle], axis=-2).astype(jnp.bfloat16)


def swap(value, axis, size, step):
    return lax.ppermute(value, axis, [(i, i ^ step) for i in range(size)])


def local_diagonals(blocks):
    width = blocks.shape[1]
    pieces = []
    for start in range(0, width, 128):
        size = min(128, width - start)
        tile = blocks[:, start : start + size, start : start + size]
        pieces.append(jnp.sum(tile * jnp.eye(size, dtype=tile.dtype), axis=1))
    return jnp.concatenate(pieces, axis=1)


def rounded(values):
    return values.astype(jnp.bfloat16).astype(jnp.float32)


def params():
    return pltpu.CompilerParams(vmem_limit_bytes=40 * 1024 * 1024)


def factor_kernel(place_ref, part, own, old, diag, out, *, step, weight):
    fresh = jnp.zeros(out.shape, jnp.float32)
    for index in range(part.shape[0]):
        fresh += lax.dot_general(
            part[index], own[index], (((1,), (1,)), ((), ())), preferred_element_type=jnp.float32
        )
    block = factor_decay * old[...].astype(jnp.float32) + weight * fresh
    on_diag = lax.broadcasted_iota(jnp.int32, out.shape, 0) == lax.broadcasted_iota(
        jnp.int32, out.shape, 1
    )
    block = jnp.where(on_diag & (place_ref[0] == step), diag[0], block)
    out[...] = block.astype(jnp.bfloat16)


def factor_block(place, features, old, diag, step, weight):
    groups, _, tokens = features.shape
    rows, cols = old.shape
    return pl.pallas_call(
        functools.partial(factor_kernel, step=step, weight=weight),
        grid_spec=pltpu.PrefetchScalarGridSpec(
            num_scalar_prefetch=1,
            grid=(1,),
            in_specs=[
                pl.BlockSpec((groups, rows, tokens), lambda i, place: (0, step, 0)),
                pl.BlockSpec((groups, cols, tokens), lambda i, place: (0, place[0], 0)),
                pl.BlockSpec((rows, cols), lambda i, place: (0, 0)),
                pl.BlockSpec((1, 1, cols), lambda i, place: (place[0], 0, 0)),
            ],
            out_specs=pl.BlockSpec((rows, cols), lambda i, place: (0, 0)),
        ),
        out_shape=jax.ShapeDtypeStruct((rows, cols), jnp.bfloat16),
        compiler_params=params(),
        cost_estimate=pl.CostEstimate(
            flops=2 * groups * rows * cols * tokens,
            bytes_accessed=4 * rows * cols + 4 * groups * rows * tokens,
            transcendentals=0,
        ),
    )(place, features, features, old, diag)


def fetch_blocks(blocks, held, sems):
    copies = [
        pltpu.make_async_copy(blocks[index], held.at[index], sems.at[index])
        for index in range(len(blocks))
    ]
    for copy in copies:
        copy.start()
    return copies


def block_products(pieces, count, copies, held):
    own = other = None
    for step in range(count):
        piece = pieces(step)
        copies[step].wait()
        term = jnp.dot(piece, held[step], preferred_element_type=jnp.float32)
        own = term if own is None else own + term
        copies[count + step].wait()
        term = jnp.dot(piece, held[count + step], preferred_element_type=jnp.float32)
        other = term if other is None else other + term
    return own, other


def first_kernel(place_ref, scale_ref, rows, diag, *refs):
    blocks, (by_first, step_one, message), (held, sems) = refs[:8], refs[8:11], refs[11:]
    copies = fetch_blocks(blocks, held, sems)
    products = block_products(lambda step: rows[step], 4, copies, held)
    scale = scale_ref[0]
    square = scale * scale
    lows = []
    for index in range(2):
        values = rows[place_ref[0] ^ index].astype(jnp.float32)
        low_diag = diag[place_ref[0] ^ index]
        first_diag = rounded(2.0 * scale - square * low_diag)
        by_first[index] = 2.0 * scale * values - square * products[index]
        one = first_diag * values - square * (products[index] - low_diag * values)
        step_one[index] = one
        lows.append(one.astype(jnp.bfloat16))
    message[...] = jnp.concatenate(lows, axis=1)


def put_pieces(pieces, mine, theirs):
    width = pieces.shape[2]
    for index in range(2):
        pieces[index] = mine[:, index * width : (index + 1) * width]
        pieces[2 + index] = theirs[:, index * width : (index + 1) * width]


def second_kernel(place_ref, mine, theirs, step_one, diag, *refs):
    blocks, (step_two, message), (held, sems, pieces) = refs[:8], refs[8:10], refs[10:]
    copies = fetch_blocks(blocks, held, sems)
    put_pieces(pieces, mine, theirs)
    products = block_products(lambda step: pieces[place_ref[0] ^ step], 4, copies, held)
    lows = []
    for index in range(2):
        low_diag = diag[place_ref[0] ^ index]
        one = step_one[index]
        two = products[index] + low_diag * (one - rounded(one))
        step_two[index] = two
        lows.append(two.astype(jnp.bfloat16))
    message[...] = jnp.concatenate(lows, axis=1)


def third_kernel(place_ref, scale_ref, mine, theirs, step_two, by_first, diag, *refs):
    blocks, (keep, give), (held, sems, pieces) = refs[:8], refs[8:10], refs[10:]
    copies = fetch_blocks(blocks, held, sems)
    put_pieces(pieces, mine, theirs)
    products = block_products(lambda step: pieces[place_ref[0] ^ step], 4, copies, held)
    scale = scale_ref[0]
    square = scale * scale
    for index, out in ((0, keep), (1, give)):
        low_diag = diag[place_ref[0] ^ index]
        first_diag = rounded(2.0 * scale - square * low_diag)
        two = step_two[index]
        three = first_diag * two - square * (products[index] - low_diag * rounded(two))
        out[...] = (2.0 * by_first[index] - three).T.astype(jnp.bfloat16)


def chain_call(kernel, scalars, arrays, blocks, out_shape, pieces):
    tokens = out_shape[0].shape[-1] if pieces is None else pieces[1]
    width = blocks[0].shape[1]
    vmem = pl.BlockSpec(memory_space=pltpu.VMEM)
    scratch = [
        pltpu.VMEM((len(blocks),) + blocks[0].shape, jnp.bfloat16),
        pltpu.SemaphoreType.DMA((len(blocks),)),
    ]
    if pieces is not None:
        scratch.append(pltpu.VMEM(pieces, jnp.bfloat16))
    return pl.pallas_call(
        kernel,
        in_specs=[pl.BlockSpec(memory_space=pltpu.SMEM)] * len(scalars)
        + [vmem] * len(arrays)
        + [pl.BlockSpec(memory_space=pl.ANY)] * len(blocks),
        out_specs=[vmem] * len(out_shape),
        out_shape=out_shape,
        scratch_shapes=scratch,
        compiler_params=params(),
        cost_estimate=pl.CostEstimate(
            flops=2 * len(blocks) * tokens * width * width,
            bytes_accessed=2 * len(blocks) * width * width,
            transcendentals=0,
        ),
    )(*scalars, *arrays, *blocks)


def attn_kernel(shard_ref, left_own, left_other, own_1, own_2, own_3, other_1, other_2, other_3, out):
    first = shard_ref[0] == 0

    def product(left, right):
        out[0] = learning_rate * lax.dot_general(
            left, right, (((1,), (1,)), ((), ())), preferred_element_type=jnp.float32
        )

    @pl.when(pl.program_id(0) == 0)
    def _():
        left = jnp.where(first, left_own[...], left_other[...])
        product(left, jnp.where(first, own_1[...], other_1[...]))

    @pl.when(pl.program_id(0) == 1)
    def _():
        left = jnp.where(first, left_own[...], left_other[...])
        product(left, jnp.where(first, own_2[...], other_2[...]))

    @pl.when(pl.program_id(0) == 2)
    def _():
        left = jnp.where(first, left_own[...], left_other[...])
        product(left, jnp.where(first, own_3[...], other_3[...]))

    @pl.when(pl.program_id(0) == 3)
    def _():
        left = jnp.where(first, left_other[...], left_own[...])
        product(left, jnp.where(first, other_1[...], own_1[...]))


def attn_products(shard, operands):
    rows, tokens_all = operands[0].shape
    cols = operands[2].shape[0]
    whole = [pl.BlockSpec(value.shape, lambda w: (0, 0)) for value in operands]
    return pl.pallas_call(
        attn_kernel,
        grid=(4,),
        out_shape=jax.ShapeDtypeStruct((4, rows, cols), jnp.float32),
        in_specs=[pl.BlockSpec(memory_space=pltpu.SMEM)] + whole,
        out_specs=pl.BlockSpec((1, rows, cols), lambda w: (w, 0, 0)),
        compiler_params=params(),
        cost_estimate=pl.CostEstimate(
            flops=8 * rows * cols * tokens_all,
            bytes_accessed=16 * rows * cols + 16 * rows * tokens_all,
            transcendentals=0,
        ),
    )(shard.reshape(1), *operands)


def layer_plan(
    activations,
    router_grad,
    token_ids,
    norm_terms,
    old_factors,
    old_router_factor,
    old_norm_diag,
    old_embed_diag,
):
    n_tensor = lax.axis_size("tensor")
    n_section = lax.axis_size("section")
    n_shard = lax.axis_size("shard")
    shard = lax.axis_index("shard")
    layer = lax.axis_index("tensor")
    section = lax.axis_index("section")
    core = section % 2
    owned, row_block, col_block = old_factors.shape
    tokens = activations.shape[1]
    features_dev = activations.shape[2]
    tokens_all = tokens * n_shard
    weight = (1.0 - factor_decay) / tokens_all
    own_place = section ^ layer
    place = own_place.reshape(1)

    def by_index(array, index, axis=0):
        return lax.dynamic_index_in_dim(array, index, axis, False)

    diagonals = local_diagonals(old_factors) * (layer == section).astype(jnp.float32)
    extra = jnp.pad(split_three(diagonals), ((0, 0), (0, 0), (0, 3 * tokens - col_block)))
    extra = jnp.pad(extra.reshape(owned, 9, tokens), ((0, 0), (0, 7), (0, 0)))
    by_feature = jnp.swapaxes(activations, 1, 2)
    axes = ("shard", "tensor")
    token_parts = {}
    for away in range(n_shard):
        for step in range(n_tensor):
            factor = (shard ^ away) * n_tensor + (layer ^ step)
            message = by_index(by_feature, factor)
            if away == 0:
                message = jnp.concatenate([message, by_index(extra, layer ^ step)], axis=0)
            if away or step:
                moves = [
                    (x * n_tensor + z, (x ^ away) * n_tensor + (z ^ step))
                    for x in range(n_shard)
                    for z in range(n_tensor)
                ]
                message = lax.ppermute(message, axes, moves)
            token_parts[away, step] = message
    collected = jnp.stack(
        [
            jnp.concatenate(
                [
                    token_parts[0, step][:features_dev],
                    token_parts[1, step],
                    token_parts[0, step][features_dev:],
                ],
                axis=0,
            )
            for step in range(n_tensor)
        ]
    )
    gathered = lax.all_gather(collected, "section", axis=0)

    blocks = [by_index(old_factors, layer).astype(jnp.bfloat16)]
    for step in (1, 2, 3):
        away = by_index(old_factors, layer ^ step)
        blocks.append(swap(away.astype(jnp.bfloat16), "tensor", n_tensor, step))

    def both_shards(value, axis):
        other = swap(value, "shard", n_shard, 1)
        return jnp.where(
            shard == 0,
            jnp.concatenate([value, other], axis=axis),
            jnp.concatenate([other, value], axis=axis),
        )

    grad_all = both_shards(router_grad, 1)
    ids_all = both_shards(token_ids, 0)
    norm_values = norm_terms.astype(jnp.float32)
    norm_sums = jnp.stack([jnp.sum(norm_values, axis=1), jnp.sum(norm_values * norm_values, axis=1)])
    norm_sums = norm_sums + swap(norm_sums, "shard", n_shard, 1)
    gathered, grad_all, ids_all, norm_sums = lax.optimization_barrier(
        (gathered, grad_all, ids_all, norm_sums)
    )

    features = gathered[:, :, : 2 * features_dev].reshape(
        n_section, n_tensor, n_shard, features_dev, tokens
    )
    features = features.transpose(2, 1, 0, 3, 4).reshape(n_shard, D, tokens)
    codes = jnp.sum(
        gathered[:, :, 2 * features_dev : 2 * features_dev + 9].astype(jnp.float32), axis=1
    )
    old_diag = jnp.sum(codes.reshape(n_section, 3, 3 * tokens), axis=1)[:, :col_block]
    old_diag = jnp.stack([by_index(old_diag, layer ^ step) for step in range(n_tensor)])
    values = features.astype(jnp.float32)
    squares = jnp.sum(values * values, axis=(0, 2)).reshape(n_tensor, col_block)
    matrix_diag = factor_decay * old_diag + weight * squares + damping
    scale = (D / (3.0 * jnp.sum(matrix_diag))).reshape(1)
    low_diag = lax.reduce_precision(matrix_diag, 8, 7)[:, None, :]
    rows = by_index(features, core).reshape(n_tensor, row_block, tokens)
    rows = jnp.swapaxes(rows, 1, 2)

    own_cols = [
        factor_block(place, features, blocks[step], low_diag, step, weight)
        for step in range(n_tensor)
    ]
    other_cols = [swap(block, "section", n_section, 1) for block in own_cols]
    cols = own_cols + other_cols

    def shaped(dtype, *shape):
        return jax.ShapeDtypeStruct(shape, dtype)

    wide = shaped(jnp.float32, 2, tokens, col_block)
    sent = shaped(jnp.bfloat16, tokens, 2 * col_block)
    part = shaped(jnp.bfloat16, col_block, tokens)
    pieces = (n_tensor, tokens, col_block)
    by_first, step_one, message = chain_call(
        first_kernel, (place, scale), (rows, low_diag), cols, (wide, wide, sent), None
    )
    theirs = swap(message, "section", n_section, 2)
    step_two, message = chain_call(
        second_kernel, (place,), (message, theirs, step_one, low_diag), cols, (wide, sent), pieces
    )
    theirs = swap(message, "section", n_section, 2)
    keep, give = chain_call(
        third_kernel,
        (place, scale),
        (message, theirs, step_two, by_first, low_diag),
        cols,
        (part, part),
        pieces,
    )
    got = swap(give, "section", n_section, 1)
    own = jnp.where(
        core == shard, jnp.concatenate([keep, got], axis=1), jnp.concatenate([got, keep], axis=1)
    )

    def send(value, moves):
        return lax.ppermute(
            value, axes, [(x * n_tensor + a, x * n_tensor + b) for x, a, b in moves]
        )

    def across(value, layers):
        return lax.ppermute(
            value,
            axes,
            [(x * n_tensor + z, (1 - x) * n_tensor + z) for x, z in layers],
        )

    everywhere = ("shard", "tensor", "section")

    def spot(x, z, s):
        return (x * n_tensor + z) * n_section + s

    planes = range(n_shard)
    layers = range(n_tensor)

    def scatter(value, source):
        moved_here = lax.ppermute(
            value,
            everywhere,
            [(spot(x, source, s), spot(x, s, s)) for x in planes for s in layers if s != source],
        )
        return jnp.where(layer == source, value, moved_here)

    def to_side(value):
        got = lax.ppermute(
            value, everywhere, [(spot(x, t, t), spot(x, t, t ^ 2)) for x in planes for t in layers]
        )
        return jnp.where(section == layer, value, got)

    def to_core(value):
        got = lax.ppermute(
            value,
            everywhere,
            [(spot(x, t, t ^ a), spot(x, t, t ^ a ^ 1)) for x in planes for t in layers for a in (0, 2)],
        )
        return jnp.where((section ^ layer) % 2 == 0, value, got)

    down_1 = send(own, [(0, 3, 2), (0, 2, 1), (0, 1, 0), (1, 3, 2), (1, 1, 0)])
    up_1 = send(own, [(0, 1, 2), (0, 2, 3), (1, 1, 2)])
    over_0 = across(own, [(0, 1), (0, 2), (0, 3), (1, 1), (1, 3)])
    left_here = scatter(own, 0)
    down_1, up_1, over_0 = lax.optimization_barrier((down_1, up_1, over_0))

    down_2 = send(down_1, [(0, 2, 1), (0, 1, 0), (1, 2, 1)])
    up_2 = send(up_1, [(0, 2, 3), (1, 2, 3)])
    over_1 = across(
        jnp.where(layer == 3, up_1, down_1),
        [(0, 0), (0, 1), (0, 2), (0, 3), (1, 0), (1, 2)],
    )
    down_2, up_2, over_1, left_here = lax.optimization_barrier((down_2, up_2, over_1, left_here))

    down_3 = send(down_2, [(0, 1, 0), (1, 1, 0)])
    over_2 = across(
        jnp.where(layer < 2, down_2, jnp.where(layer == 2, up_1, up_2)),
        [(0, 0), (0, 1), (0, 2), (0, 3), (1, 1), (1, 2), (1, 3)],
    )
    left_there = lax.ppermute(
        left_here, everywhere, [(spot(x, t, t), spot(1 - x, t, t)) for x in planes for t in layers]
    )
    left_here = to_side(left_here)
    down_3, over_2, left_there, left_here = lax.optimization_barrier(
        (down_3, over_2, left_there, left_here)
    )

    over_3 = across(down_3, [(0, 0), (1, 0)])
    left_there = to_core(to_side(left_there))
    left_here = to_core(left_here)

    def by_layer(*options):
        chosen = options[3]
        for index in (2, 1, 0):
            chosen = jnp.where(layer == index, options[index], chosen)
        return chosen

    own_1 = by_layer(down_1, own, up_1, up_2)
    own_2 = by_layer(down_2, down_1, own, up_1)
    own_3 = by_layer(down_3, down_2, down_1, own)
    other_1 = by_layer(over_1, over_0, over_2, over_2)
    other_2 = by_layer(over_2, over_1, over_0, over_1)
    other_3 = by_layer(over_3, over_2, over_1, over_0)
    precond_attn = attn_products(
        shard, (left_here, left_there, own_1, own_2, own_3, other_1, other_2, other_3)
    )

    router_matrix = (
        factor_decay * old_router_factor
        + weight * jnp.einsum("en,fn->ef", grad_all, grad_all, preferred_element_type=jnp.float32)
        + damping * jnp.eye(EXPERTS, dtype=jnp.float32)
    )
    router_inverse = local_inverse(router_matrix)
    router_right = jnp.einsum(
        "en,ef->fn", grad_all, router_inverse, preferred_element_type=jnp.float32
    ).astype(jnp.bfloat16)
    precond_norms = (
        learning_rate
        * norm_sums[0]
        / (
            factor_decay * old_norm_diag
            + (1.0 - factor_decay) * (norm_sums[1] / tokens_all)
            + damping
        )
    )
    router_cols = learning_rate * jnp.einsum(
        "fn,cn->fc", router_right, own, preferred_element_type=jnp.float32
    )
    router_cols = jnp.where(shard == 1, router_cols, across(router_cols, [(1, 2)]))
    precond_router = to_core(to_side(scatter(router_cols, 2)))

    vocab_block = old_embed_diag.shape[0]
    ids_here = layer * vocab_block + lax.iota(jnp.int32, vocab_block)
    matches = ids_here[:, None] == ids_all[None, :]
    counts = jnp.sum(matches.astype(jnp.float32), axis=1)
    divisor = factor_decay * old_embed_diag + (1.0 - factor_decay) * (counts / tokens_all) + damping
    embed_grads = jnp.where(shard == 1, own_3, other_3)
    embed_sum = jnp.einsum(
        "vn,cn->vc", matches.astype(jnp.bfloat16), embed_grads, preferred_element_type=jnp.float32
    )
    precond_embed = embed_sum * (learning_rate / divisor)[:, None]
    return (precond_attn, precond_router, precond_norms, precond_embed)


def per_device(*arguments):
    one_each = arguments[4].shape[0] == lax.axis_size("tensor") == lax.axis_size("section")
    if one_each and lax.axis_size("section") == 4 and lax.axis_size("shard") == 2:
        return layer_plan(*arguments)
    return general_plan(*arguments)


def solution(mesh):
    return jax.shard_map(
        per_device,
        mesh=mesh,
        in_specs=(
            P(None, "shard", ("tensor", "section")),
            P(None, "shard"),
            P("shard"),
            P(None, "shard", ("tensor", "section")),
            P("shard", "tensor", "section"),
            P(),
            P(None, ("tensor", "section")),
            P("tensor"),
        ),
        out_specs=(
            P(None, "tensor", "section"),
            P(None, "tensor"),
            P(None, ("tensor", "section")),
            P("tensor", "section"),
        ),
        check_vma=False,
    )
```

```python
import functools
import math

import jax
import jax.numpy as jnp
from jax import lax
from jax.experimental import pallas as pl
from jax.experimental.pallas import tpu as pltpu
from jax.sharding import PartitionSpec as P

D = 2304
EXPERTS = 8
VOCAB = 8192


factor_decay = 0.5
damping = 0.01
learning_rate = 0.05


def local_inverse(matrix):
    width = matrix.shape[0]
    trace = jnp.sum(jnp.diagonal(matrix))
    factor_scale = width / (3.0 * trace)
    identity = jnp.eye(width, dtype=jnp.float32)
    matrix_low = lax.optimization_barrier(matrix.astype(jnp.bfloat16))
    first = 2.0 * factor_scale * identity - factor_scale * factor_scale * matrix_low.astype(
        jnp.float32
    )
    first_low = first.astype(jnp.bfloat16)
    image = jnp.dot(matrix_low, first_low, preferred_element_type=jnp.float32).astype(jnp.bfloat16)
    product = jnp.dot(first_low, image, preferred_element_type=jnp.float32)
    return (2.0 * first - product).astype(jnp.bfloat16)


def fold_with(columns, piece):
    return jnp.einsum("kij,kjl->kil", piece, columns, preferred_element_type=jnp.float32)


def general_plan(
    activations,
    router_grad,
    token_ids,
    norm_terms,
    old_factors,
    old_router_factor,
    old_norm_diag,
    old_embed_diag,
):
    n_tensor = lax.axis_size("tensor")
    n_section = lax.axis_size("section")
    n_shard = lax.axis_size("shard")
    tensor_rank = lax.axis_index("tensor")
    section_rank = lax.axis_index("section")
    row_block = D // n_tensor
    col_block = D // n_section
    tokens_all = activations.shape[1] * n_shard
    row_start = tensor_rank * row_block
    col_start = section_rank * col_block

    def collect(carry, piece):
        whole = lax.all_gather(piece, ("tensor", "section"), axis=1, tiled=True)
        rows_part = lax.dynamic_slice_in_dim(whole, row_start, row_block, 1)
        cols_part = lax.dynamic_slice_in_dim(whole, col_start, col_block, 1)
        return (carry, (rows_part, cols_part))

    unused_carry, (row_parts, col_parts) = lax.scan(collect, jnp.int32(0), activations)
    partial_value = jnp.einsum(
        "mnr,mnc->mrc", row_parts, col_parts, preferred_element_type=jnp.float32
    )
    fresh = lax.psum_scatter(partial_value, "shard", scatter_dimension=0, tiled=True) / tokens_all
    row_index = lax.broadcasted_iota(jnp.int32, (row_block, col_block), 0) + row_start
    col_index = lax.broadcasted_iota(jnp.int32, (row_block, col_block), 1) + col_start
    eye_block = (row_index == col_index).astype(jnp.float32)
    matrix = factor_decay * old_factors + (1.0 - factor_decay) * fresh + damping * eye_block
    diag_part = jnp.sum(matrix * eye_block, axis=(1, 2))
    trace = lax.psum(diag_part, ("tensor", "section"))
    factor_scale = (D / (3.0 * trace))[:, None, None]
    matrix_low = lax.optimization_barrier(matrix.astype(jnp.bfloat16))
    first = 2.0 * factor_scale * eye_block - factor_scale * factor_scale * matrix_low.astype(
        jnp.float32
    )
    first_low = first.astype(jnp.bfloat16)
    first_cols = lax.all_gather(first_low, "tensor", axis=1, tiled=True)
    image = fold_with(first_cols, lax.all_gather(matrix_low, "section", axis=2, tiled=True))
    image_cols = lax.all_gather(image.astype(jnp.bfloat16), "tensor", axis=1, tiled=True)
    product = fold_with(image_cols, lax.all_gather(first_low, "section", axis=2, tiled=True))
    inverse_low = (2.0 * first - product).astype(jnp.bfloat16)
    inverses = lax.all_gather(inverse_low, "shard", axis=0, tiled=True)
    left_terms = jnp.stack(
        [
            jnp.einsum("nc,rc->nr", col_parts[m], inverses[m], preferred_element_type=jnp.float32)
            for m in (0, 4, 6)
        ]
    )
    left = lax.psum(left_terms, "section").astype(jnp.bfloat16)
    right_terms = jnp.stack(
        [
            jnp.einsum("nr,rc->nc", row_parts[m], inverses[m], preferred_element_type=jnp.float32)
            for m in (1, 2, 3, 5, 7)
        ]
    )
    right = lax.psum(right_terms, "tensor").astype(jnp.bfloat16)
    norm_values = norm_terms.astype(jnp.float32)
    router_part = jnp.einsum(
        "en,fn->ef", router_grad, router_grad, preferred_element_type=jnp.float32
    )
    router_sum, norm_total, norm_squares = lax.psum(
        (router_part, jnp.sum(norm_values, axis=1), jnp.sum(norm_values * norm_values, axis=1)),
        "shard",
    )
    router_matrix = (
        factor_decay * old_router_factor
        + (1.0 - factor_decay) * (router_sum / tokens_all)
        + damping * jnp.eye(EXPERTS, dtype=jnp.float32)
    )
    router_inverse = local_inverse(router_matrix)
    router_right = jnp.einsum(
        "en,ef->nf", router_grad, router_inverse, preferred_element_type=jnp.float32
    ).astype(jnp.bfloat16)
    precond_norms = (
        learning_rate
        * norm_total
        / (
            factor_decay * old_norm_diag
            + (1.0 - factor_decay) * (norm_squares / tokens_all)
            + damping
        )
    )
    ids_all = lax.all_gather(token_ids, "shard", axis=0, tiled=True)
    embed_all = lax.all_gather(right[4], "shard", axis=0, tiled=True)
    paired_left = jnp.stack([left[0], left[0], left[0], left[1]])
    attn_terms = jnp.einsum(
        "wnr,wnc->wrc", paired_left, right[:4], preferred_element_type=jnp.float32
    )
    router_term = jnp.einsum("nf,nr->fr", router_right, left[2], preferred_element_type=jnp.float32)
    attn_sum, router_total = lax.psum((attn_terms, router_term), "shard")
    precond_attn = learning_rate * attn_sum
    precond_router = learning_rate * router_total
    vocab_block = VOCAB // n_tensor
    step_rows = math.gcd(vocab_block, 512)
    vocab_start = tensor_rank * vocab_block

    def embed_block(block_index):
        ids_here = vocab_start + block_index * step_rows + lax.iota(jnp.int32, step_rows)
        onehot = (ids_here[:, None] == ids_all[None, :]).astype(jnp.bfloat16)
        summed = jnp.dot(onehot, embed_all, preferred_element_type=jnp.float32)
        tallies = jnp.sum(onehot, axis=1, dtype=jnp.float32)
        return (summed, tallies)

    block_sums, block_counts = lax.map(
        embed_block, jnp.arange(vocab_block // step_rows, dtype=jnp.int32)
    )
    embed_sum = block_sums.reshape(vocab_block, col_block)
    counts = block_counts.reshape(vocab_block)
    divisor = factor_decay * old_embed_diag + (1.0 - factor_decay) * (counts / tokens_all) + damping
    precond_embed = learning_rate * embed_sum / divisor[:, None]
    return (precond_attn, precond_router, precond_norms, precond_embed)


def split_three(values):
    high = lax.reduce_precision(values, 8, 7)
    rest = values - high
    middle = lax.reduce_precision(rest, 8, 7)
    return jnp.stack([high, middle, rest - middle], axis=-2).astype(jnp.bfloat16)


def swap(value, axis, size, step):
    return lax.ppermute(value, axis, [(i, i ^ step) for i in range(size)])


def local_diagonals(blocks):
    width = blocks.shape[1]
    pieces = []
    for start in range(0, width, 128):
        size = min(128, width - start)
        tile = blocks[:, start : start + size, start : start + size]
        pieces.append(jnp.sum(tile * jnp.eye(size, dtype=tile.dtype), axis=1))
    return jnp.concatenate(pieces, axis=1)


def rounded(values):
    return values.astype(jnp.bfloat16).astype(jnp.float32)


def params():
    return pltpu.CompilerParams(vmem_limit_bytes=40 * 1024 * 1024)


def factor_kernel(place_ref, part, own, old, diag, out, *, step, weight):
    fresh = jnp.zeros(out.shape, jnp.float32)
    for index in range(part.shape[0]):
        fresh += lax.dot_general(
            part[index], own[index], (((1,), (1,)), ((), ())), preferred_element_type=jnp.float32
        )
    block = factor_decay * old[...].astype(jnp.float32) + weight * fresh
    on_diag = lax.broadcasted_iota(jnp.int32, out.shape, 0) == lax.broadcasted_iota(
        jnp.int32, out.shape, 1
    )
    block = jnp.where(on_diag & (place_ref[0] == step), diag[0], block)
    out[...] = block.astype(jnp.bfloat16)


def factor_block(place, features, old, diag, step, weight):
    groups, _, tokens = features.shape
    rows, cols = old.shape
    return pl.pallas_call(
        functools.partial(factor_kernel, step=step, weight=weight),
        grid_spec=pltpu.PrefetchScalarGridSpec(
            num_scalar_prefetch=1,
            grid=(1,),
            in_specs=[
                pl.BlockSpec((groups, rows, tokens), lambda i, place: (0, step, 0)),
                pl.BlockSpec((groups, cols, tokens), lambda i, place: (0, place[0], 0)),
                pl.BlockSpec((rows, cols), lambda i, place: (0, 0)),
                pl.BlockSpec((1, 1, cols), lambda i, place: (place[0], 0, 0)),
            ],
            out_specs=pl.BlockSpec((rows, cols), lambda i, place: (0, 0)),
        ),
        out_shape=jax.ShapeDtypeStruct((rows, cols), jnp.bfloat16),
        compiler_params=params(),
        cost_estimate=pl.CostEstimate(
            flops=2 * groups * rows * cols * tokens,
            bytes_accessed=4 * rows * cols + 4 * groups * rows * tokens,
            transcendentals=0,
        ),
    )(place, features, features, old, diag)


def fetch_blocks(place_ref, blocks, held, sems):
    count = len(blocks) // 2
    depth = blocks[0].shape[0]
    copies = []
    for index in range(2 * count):
        slot = pl.multiple_of((place_ref[0] ^ (index % count)) * depth, depth)
        copies.append(
            pltpu.make_async_copy(
                blocks[index], held.at[index // count, pl.ds(slot, depth)], sems.at[index]
            )
        )
    for copy in copies:
        copy.start()
    return copies


def block_products(rows, copies, held):
    count = len(copies) // 2
    products = []
    for index in range(2):
        for copy in copies[index * count : (index + 1) * count]:
            copy.wait()
        products.append(jnp.dot(rows, held[index], preferred_element_type=jnp.float32))
    return products


def first_parts(place_ref, scale, rows, diag, product, index):
    width = product.shape[1]
    square = scale * scale
    values = rows[:, index * width : (index + 1) * width].astype(jnp.float32)
    low_diag = diag[place_ref[0] ^ index]
    first_diag = rounded(2.0 * scale - square * low_diag)
    by_first = 2.0 * scale * values - square * product
    step_one = first_diag * values - square * (product - low_diag * values)
    return by_first, step_one, low_diag, first_diag


def first_kernel(place_ref, scale_ref, rows, diag, *refs):
    blocks, (kept, message), (held, sems) = refs[:8], refs[8:10], refs[10:]
    copies = fetch_blocks(place_ref, blocks, held, sems)
    products = block_products(rows[...], copies, held)
    lows = []
    for index in range(2):
        kept[index] = products[index]
        parts = first_parts(place_ref, scale_ref[0], rows, diag, products[index], index)
        lows.append(parts[1].astype(jnp.bfloat16))
    message[...] = jnp.concatenate(lows, axis=1)


def second_kernel(place_ref, scale_ref, mine, theirs, rows, diag, before, *refs):
    blocks, (kept, message), (held, sems) = refs[:8], refs[8:10], refs[10:]
    copies = fetch_blocks(place_ref, blocks, held, sems)
    both = jnp.concatenate([mine[...], theirs[...]], axis=1)
    products = block_products(both, copies, held)
    square = scale_ref[0] * scale_ref[0]
    lows = []
    for index in range(2):
        by_first, one, low_diag, first_diag = first_parts(
            place_ref, scale_ref[0], rows, diag, before[index], index
        )
        two = products[index] + low_diag * (one - rounded(one))
        low = two.astype(jnp.bfloat16)
        kept[index] = (
            2.0 * by_first - first_diag * two - square * low_diag * low.astype(jnp.float32)
        )
        lows.append(low)
    message[...] = jnp.concatenate(lows, axis=1)


def third_kernel(place_ref, scale_ref, mine, theirs, before, *refs):
    blocks, (keep, give), (held, sems) = refs[:8], refs[8:10], refs[10:]
    copies = fetch_blocks(place_ref, blocks, held, sems)
    both = jnp.concatenate([mine[...], theirs[...]], axis=1)
    products = block_products(both, copies, held)
    square = scale_ref[0] * scale_ref[0]
    for index, out in ((0, keep), (1, give)):
        out[...] = (before[index] + square * products[index]).T.astype(jnp.bfloat16)


def chain_call(kernel, scalars, arrays, blocks, out_shape):
    depth, width = blocks[0].shape
    count = len(blocks) // 2
    tokens = arrays[0].shape[0]
    vmem = pl.BlockSpec(memory_space=pltpu.VMEM)
    return pl.pallas_call(
        kernel,
        in_specs=[pl.BlockSpec(memory_space=pltpu.SMEM)] * len(scalars)
        + [vmem] * len(arrays)
        + [pl.BlockSpec(memory_space=pl.ANY)] * len(blocks),
        out_specs=[vmem] * len(out_shape),
        out_shape=out_shape,
        scratch_shapes=[
            pltpu.VMEM((2, count * depth, width), jnp.bfloat16),
            pltpu.SemaphoreType.DMA((len(blocks),)),
        ],
        compiler_params=params(),
        cost_estimate=pl.CostEstimate(
            flops=2 * len(blocks) * tokens * depth * width,
            bytes_accessed=2 * len(blocks) * depth * width,
            transcendentals=0,
        ),
    )(*scalars, *arrays, *blocks)


def attn_kernel(shard_ref, left_own, left_other, own_1, own_2, own_3, other_1, other_2, other_3, out):
    first = shard_ref[0] == 0

    def product(left, right):
        out[0] = learning_rate * lax.dot_general(
            left, right, (((1,), (1,)), ((), ())), preferred_element_type=jnp.float32
        )

    @pl.when(pl.program_id(0) == 0)
    def _():
        left = jnp.where(first, left_own[...], left_other[...])
        product(left, jnp.where(first, own_1[...], other_1[...]))

    @pl.when(pl.program_id(0) == 1)
    def _():
        left = jnp.where(first, left_own[...], left_other[...])
        product(left, jnp.where(first, own_2[...], other_2[...]))

    @pl.when(pl.program_id(0) == 2)
    def _():
        left = jnp.where(first, left_own[...], left_other[...])
        product(left, jnp.where(first, own_3[...], other_3[...]))

    @pl.when(pl.program_id(0) == 3)
    def _():
        left = jnp.where(first, left_other[...], left_own[...])
        product(left, jnp.where(first, other_1[...], own_1[...]))


def attn_products(shard, operands):
    rows, tokens_all = operands[0].shape
    cols = operands[2].shape[0]
    whole = [pl.BlockSpec(value.shape, lambda w: (0, 0)) for value in operands]
    return pl.pallas_call(
        attn_kernel,
        grid=(4,),
        out_shape=jax.ShapeDtypeStruct((4, rows, cols), jnp.float32),
        in_specs=[pl.BlockSpec(memory_space=pltpu.SMEM)] + whole,
        out_specs=pl.BlockSpec((1, rows, cols), lambda w: (w, 0, 0)),
        compiler_params=params(),
        cost_estimate=pl.CostEstimate(
            flops=8 * rows * cols * tokens_all,
            bytes_accessed=16 * rows * cols + 16 * rows * tokens_all,
            transcendentals=0,
        ),
    )(shard.reshape(1), *operands)


def layer_plan(
    activations,
    router_grad,
    token_ids,
    norm_terms,
    old_factors,
    old_router_factor,
    old_norm_diag,
    old_embed_diag,
):
    n_tensor = lax.axis_size("tensor")
    n_section = lax.axis_size("section")
    n_shard = lax.axis_size("shard")
    shard = lax.axis_index("shard")
    layer = lax.axis_index("tensor")
    section = lax.axis_index("section")
    core = section % 2
    owned, row_block, col_block = old_factors.shape
    tokens = activations.shape[1]
    features_dev = activations.shape[2]
    tokens_all = tokens * n_shard
    weight = (1.0 - factor_decay) / tokens_all
    own_place = section ^ layer
    place = own_place.reshape(1)

    def by_index(array, index, axis=0):
        return lax.dynamic_index_in_dim(array, index, axis, False)

    diagonals = local_diagonals(old_factors) * (layer == section).astype(jnp.float32)
    extra = jnp.pad(split_three(diagonals), ((0, 0), (0, 0), (0, 3 * tokens - col_block)))
    extra = jnp.pad(extra.reshape(owned, 9, tokens), ((0, 0), (0, 7), (0, 0)))
    by_feature = jnp.swapaxes(activations, 1, 2)
    axes = ("shard", "tensor")
    token_parts = {}
    for away in range(n_shard):
        for step in range(n_tensor):
            factor = (shard ^ away) * n_tensor + (layer ^ step)
            message = by_index(by_feature, factor)
            if away == 0:
                message = jnp.concatenate([message, by_index(extra, layer ^ step)], axis=0)
            if away or step:
                moves = [
                    (x * n_tensor + z, (x ^ away) * n_tensor + (z ^ step))
                    for x in range(n_shard)
                    for z in range(n_tensor)
                ]
                message = lax.ppermute(message, axes, moves)
            token_parts[away, step] = message
    def old_block(step, start, size):
        away = by_index(old_factors, layer ^ step)[start : start + size].astype(jnp.bfloat16)
        return swap(away, "tensor", n_tensor, step) if step else away

    part_rows = row_block // 2
    early = old_block(2, 0, part_rows)
    late = old_block(2, part_rows, part_rows)
    collected = jnp.stack(
        [
            jnp.concatenate(
                [
                    token_parts[0, step][:features_dev],
                    token_parts[1, step],
                    token_parts[0, step][features_dev:],
                ],
                axis=0,
            )
            for step in range(n_tensor)
        ]
    )
    collected, early = lax.optimization_barrier((collected, early))
    gathered = lax.all_gather(collected, "section", axis=0)
    blocks = [
        old_block(0, 0, row_block),
        old_block(1, 0, row_block),
        jnp.concatenate([early, late], axis=0),
        old_block(3, 0, row_block),
    ]

    def both_shards(value, axis):
        other = swap(value, "shard", n_shard, 1)
        return jnp.where(
            shard == 0,
            jnp.concatenate([value, other], axis=axis),
            jnp.concatenate([other, value], axis=axis),
        )

    grad_all = both_shards(router_grad, 1)
    ids_all = both_shards(token_ids, 0)
    norm_values = norm_terms.astype(jnp.float32)
    norm_sums = jnp.stack([jnp.sum(norm_values, axis=1), jnp.sum(norm_values * norm_values, axis=1)])
    norm_sums = norm_sums + swap(norm_sums, "shard", n_shard, 1)
    gathered, grad_all, ids_all, norm_sums = lax.optimization_barrier(
        (gathered, grad_all, ids_all, norm_sums)
    )

    features = gathered[:, :, : 2 * features_dev].reshape(
        n_section, n_tensor, n_shard, features_dev, tokens
    )
    features = features.transpose(2, 1, 0, 3, 4).reshape(n_shard, D, tokens)
    codes = jnp.sum(
        gathered[:, :, 2 * features_dev : 2 * features_dev + 9].astype(jnp.float32), axis=1
    )
    old_diag = jnp.sum(codes.reshape(n_section, 3, 3 * tokens), axis=1)[:, :col_block]
    old_diag = jnp.stack([by_index(old_diag, layer ^ step) for step in range(n_tensor)])
    values = features.astype(jnp.float32)
    squares = jnp.sum(values * values, axis=(0, 2)).reshape(n_tensor, col_block)
    matrix_diag = factor_decay * old_diag + weight * squares + damping
    scale = (D / (3.0 * jnp.sum(matrix_diag))).reshape(1)
    low_diag = lax.reduce_precision(matrix_diag, 8, 7)[:, None, :]
    rows = by_index(features, core).reshape(n_tensor, row_block, tokens)
    rows = jnp.concatenate(
        [jnp.swapaxes(by_index(rows, own_place ^ index), 0, 1) for index in range(n_tensor)], axis=1
    )
    features, rows = lax.optimization_barrier((features, rows))

    own_cols = [
        factor_block(place, features, blocks[step], low_diag, step, weight)
        for step in range(n_tensor)
    ]
    other_cols = [swap(block, "section", n_section, 1) for block in own_cols]
    cols = own_cols + other_cols

    wide = jax.ShapeDtypeStruct((2, tokens, col_block), jnp.float32)
    sent = jax.ShapeDtypeStruct((tokens, 2 * col_block), jnp.bfloat16)
    part = jax.ShapeDtypeStruct((col_block, tokens), jnp.bfloat16)
    scalars = (place, scale)
    kept, message = chain_call(first_kernel, scalars, (rows, low_diag), cols, (wide, sent))
    theirs = swap(message, "section", n_section, 2)
    kept, message = chain_call(
        second_kernel, scalars, (message, theirs, rows, low_diag, kept), cols, (wide, sent)
    )
    theirs = swap(message, "section", n_section, 2)
    keep, give = chain_call(third_kernel, scalars, (message, theirs, kept), cols, (part, part))
    got = swap(give, "section", n_section, 1)
    own = jnp.where(
        core == shard, jnp.concatenate([keep, got], axis=1), jnp.concatenate([got, keep], axis=1)
    )

    def useful(x, z):
        return z != 0 and (x, z) != (1, 2)

    def send(value, step, held):
        moves = [
            (x * n_tensor + z, x * n_tensor + (z ^ step))
            for x in range(n_shard)
            for z in range(n_tensor)
            if useful(x, z ^ held)
        ]
        return lax.ppermute(value, axes, moves)

    def across(value, held):
        moves = [
            (x * n_tensor + z, (1 - x) * n_tensor + z)
            for x in range(n_shard)
            for z in range(n_tensor)
            if useful(x, z ^ held)
        ]
        return lax.ppermute(value, axes, moves)

    everywhere = ("shard", "tensor", "section")

    def spot(x, z, s):
        return (x * n_tensor + z) * n_section + s

    planes = range(n_shard)
    layers = range(n_tensor)

    def scatter(value, source):
        moved_here = lax.ppermute(
            value,
            everywhere,
            [(spot(x, source, s), spot(x, s, s)) for x in planes for s in layers if s != source],
        )
        return jnp.where(layer == source, value, moved_here)

    near_2 = send(own, 2, 0)
    near_1 = send(own, 1, 0)
    over_0 = across(own, 0)
    left_here = scatter(own, 0)
    near_1, over_0 = lax.optimization_barrier((near_1, over_0))
    left_here, near_2 = lax.optimization_barrier((left_here, near_2))
    over_1 = across(near_1, 1)
    near_3 = send(near_2, 1, 2)
    over_2 = across(near_2, 2)
    over_3 = across(near_3, 3)
    left_there = lax.ppermute(
        left_here, everywhere, [(spot(x, t, t), spot(1 - x, t, t)) for x in planes for t in layers]
    )

    router_matrix = (
        factor_decay * old_router_factor
        + weight * jnp.einsum("en,fn->ef", grad_all, grad_all, preferred_element_type=jnp.float32)
        + damping * jnp.eye(EXPERTS, dtype=jnp.float32)
    )
    router_inverse = local_inverse(router_matrix)
    router_right = jnp.einsum(
        "en,ef->fn", grad_all, router_inverse, preferred_element_type=jnp.float32
    ).astype(jnp.bfloat16)
    router_cols = learning_rate * jnp.einsum(
        "fn,cn->fc", router_right, own, preferred_element_type=jnp.float32
    )
    router_there = lax.ppermute(router_cols, axes, [(n_tensor + 2, 2)])
    router_cols = scatter(jnp.where(shard == 1, router_cols, router_there), 2)
    router_high = lax.reduce_precision(router_cols, 8, 7)
    codes = jnp.concatenate([router_high, router_cols - router_high], axis=0).astype(jnp.bfloat16)
    codes = jnp.pad(codes, ((0, 0), (0, 2 * tokens_all - col_block))).reshape(-1, tokens_all)
    bundle = jnp.concatenate([left_here, left_there, codes], axis=0)
    bundle, over_1, near_3 = lax.optimization_barrier((bundle, over_1, near_3))
    to_side = [(spot(x, t, t), spot(x, t, t ^ 2)) for x in planes for t in layers]
    bundle = jnp.where(section == layer, bundle, lax.ppermute(bundle, everywhere, to_side))
    bundle, over_2 = lax.optimization_barrier((bundle, over_2))
    to_core = [
        (spot(x, t, t ^ a), spot(x, t, t ^ a ^ 1)) for x in planes for t in layers for a in (0, 2)
    ]
    bundle = jnp.where(
        (section ^ layer) % 2 == 0, bundle, lax.ppermute(bundle, everywhere, to_core)
    )
    left_here = bundle[:col_block]
    left_there = bundle[col_block : 2 * col_block]
    codes = bundle[2 * col_block :].reshape(2 * EXPERTS, -1)[:, :col_block].astype(jnp.float32)
    precond_router = codes[:EXPERTS] + codes[EXPERTS:]

    def by_layer(options, factor):
        chosen = options[factor ^ 3]
        for index in (2, 1, 0):
            chosen = jnp.where(layer == index, options[factor ^ index], chosen)
        return chosen

    mine = (own, near_1, near_2, near_3)
    others = (over_0, over_1, over_2, over_3)
    own_1, own_2, own_3 = (by_layer(mine, factor) for factor in (1, 2, 3))
    other_1, other_2, other_3 = (by_layer(others, factor) for factor in (1, 2, 3))
    precond_attn = attn_products(
        shard, (left_here, left_there, own_1, own_2, own_3, other_1, other_2, other_3)
    )

    precond_norms = (
        learning_rate
        * norm_sums[0]
        / (
            factor_decay * old_norm_diag
            + (1.0 - factor_decay) * (norm_sums[1] / tokens_all)
            + damping
        )
    )
    vocab_block = old_embed_diag.shape[0]
    ids_here = layer * vocab_block + lax.iota(jnp.int32, vocab_block)
    matches = ids_here[:, None] == ids_all[None, :]
    counts = jnp.sum(matches.astype(jnp.float32), axis=1)
    divisor = factor_decay * old_embed_diag + (1.0 - factor_decay) * (counts / tokens_all) + damping
    embed_grads = jnp.where(shard == 1, own_3, other_3)
    embed_sum = jnp.einsum(
        "vn,cn->vc", matches.astype(jnp.bfloat16), embed_grads, preferred_element_type=jnp.float32
    )
    precond_embed = embed_sum * (learning_rate / divisor)[:, None]
    return (precond_attn, precond_router, precond_norms, precond_embed)


def per_device(*arguments):
    one_each = arguments[4].shape[0] == lax.axis_size("tensor") == lax.axis_size("section")
    if one_each and lax.axis_size("section") == 4 and lax.axis_size("shard") == 2:
        return layer_plan(*arguments)
    return general_plan(*arguments)


def solution(mesh):
    return jax.shard_map(
        per_device,
        mesh=mesh,
        in_specs=(
            P(None, "shard", ("tensor", "section")),
            P(None, "shard"),
            P("shard"),
            P(None, "shard", ("tensor", "section")),
            P("shard", "tensor", "section"),
            P(),
            P(None, ("tensor", "section")),
            P("tensor"),
        ),
        out_specs=(
            P(None, "tensor", "section"),
            P(None, "tensor"),
            P(None, ("tensor", "section")),
            P("tensor", "section"),
        ),
        check_vma=False,
    )
```

```python
import functools
import math

import jax
import jax.numpy as jnp
from jax import lax
from jax.experimental import pallas as pl
from jax.experimental.pallas import tpu as pltpu
from jax.sharding import PartitionSpec as P

D = 2304
EXPERTS = 8
VOCAB = 8192


factor_decay = 0.5
damping = 0.01
learning_rate = 0.05


def local_inverse(matrix):
    width = matrix.shape[0]
    trace = jnp.sum(jnp.diagonal(matrix))
    factor_scale = width / (3.0 * trace)
    identity = jnp.eye(width, dtype=jnp.float32)
    matrix_low = lax.optimization_barrier(matrix.astype(jnp.bfloat16))
    first = 2.0 * factor_scale * identity - factor_scale * factor_scale * matrix_low.astype(
        jnp.float32
    )
    first_low = first.astype(jnp.bfloat16)
    image = jnp.dot(matrix_low, first_low, preferred_element_type=jnp.float32).astype(jnp.bfloat16)
    product = jnp.dot(first_low, image, preferred_element_type=jnp.float32)
    return (2.0 * first - product).astype(jnp.bfloat16)


def fold_with(columns, piece):
    return jnp.einsum("kij,kjl->kil", piece, columns, preferred_element_type=jnp.float32)


def general_plan(
    activations,
    router_grad,
    token_ids,
    norm_terms,
    old_factors,
    old_router_factor,
    old_norm_diag,
    old_embed_diag,
):
    n_tensor = lax.axis_size("tensor")
    n_section = lax.axis_size("section")
    n_shard = lax.axis_size("shard")
    tensor_rank = lax.axis_index("tensor")
    section_rank = lax.axis_index("section")
    row_block = D // n_tensor
    col_block = D // n_section
    tokens_all = activations.shape[1] * n_shard
    row_start = tensor_rank * row_block
    col_start = section_rank * col_block

    def collect(carry, piece):
        whole = lax.all_gather(piece, ("tensor", "section"), axis=1, tiled=True)
        rows_part = lax.dynamic_slice_in_dim(whole, row_start, row_block, 1)
        cols_part = lax.dynamic_slice_in_dim(whole, col_start, col_block, 1)
        return (carry, (rows_part, cols_part))

    unused_carry, (row_parts, col_parts) = lax.scan(collect, jnp.int32(0), activations)
    partial_value = jnp.einsum(
        "mnr,mnc->mrc", row_parts, col_parts, preferred_element_type=jnp.float32
    )
    fresh = lax.psum_scatter(partial_value, "shard", scatter_dimension=0, tiled=True) / tokens_all
    row_index = lax.broadcasted_iota(jnp.int32, (row_block, col_block), 0) + row_start
    col_index = lax.broadcasted_iota(jnp.int32, (row_block, col_block), 1) + col_start
    eye_block = (row_index == col_index).astype(jnp.float32)
    matrix = factor_decay * old_factors + (1.0 - factor_decay) * fresh + damping * eye_block
    diag_part = jnp.sum(matrix * eye_block, axis=(1, 2))
    trace = lax.psum(diag_part, ("tensor", "section"))
    factor_scale = (D / (3.0 * trace))[:, None, None]
    matrix_low = lax.optimization_barrier(matrix.astype(jnp.bfloat16))
    first = 2.0 * factor_scale * eye_block - factor_scale * factor_scale * matrix_low.astype(
        jnp.float32
    )
    first_low = first.astype(jnp.bfloat16)
    first_cols = lax.all_gather(first_low, "tensor", axis=1, tiled=True)
    image = fold_with(first_cols, lax.all_gather(matrix_low, "section", axis=2, tiled=True))
    image_cols = lax.all_gather(image.astype(jnp.bfloat16), "tensor", axis=1, tiled=True)
    product = fold_with(image_cols, lax.all_gather(first_low, "section", axis=2, tiled=True))
    inverse_low = (2.0 * first - product).astype(jnp.bfloat16)
    inverses = lax.all_gather(inverse_low, "shard", axis=0, tiled=True)
    left_terms = jnp.stack(
        [
            jnp.einsum("nc,rc->nr", col_parts[m], inverses[m], preferred_element_type=jnp.float32)
            for m in (0, 4, 6)
        ]
    )
    left = lax.psum(left_terms, "section").astype(jnp.bfloat16)
    right_terms = jnp.stack(
        [
            jnp.einsum("nr,rc->nc", row_parts[m], inverses[m], preferred_element_type=jnp.float32)
            for m in (1, 2, 3, 5, 7)
        ]
    )
    right = lax.psum(right_terms, "tensor").astype(jnp.bfloat16)
    norm_values = norm_terms.astype(jnp.float32)
    router_part = jnp.einsum(
        "en,fn->ef", router_grad, router_grad, preferred_element_type=jnp.float32
    )
    router_sum, norm_total, norm_squares = lax.psum(
        (router_part, jnp.sum(norm_values, axis=1), jnp.sum(norm_values * norm_values, axis=1)),
        "shard",
    )
    router_matrix = (
        factor_decay * old_router_factor
        + (1.0 - factor_decay) * (router_sum / tokens_all)
        + damping * jnp.eye(EXPERTS, dtype=jnp.float32)
    )
    router_inverse = local_inverse(router_matrix)
    router_right = jnp.einsum(
        "en,ef->nf", router_grad, router_inverse, preferred_element_type=jnp.float32
    ).astype(jnp.bfloat16)
    precond_norms = (
        learning_rate
        * norm_total
        / (
            factor_decay * old_norm_diag
            + (1.0 - factor_decay) * (norm_squares / tokens_all)
            + damping
        )
    )
    ids_all = lax.all_gather(token_ids, "shard", axis=0, tiled=True)
    embed_all = lax.all_gather(right[4], "shard", axis=0, tiled=True)
    paired_left = jnp.stack([left[0], left[0], left[0], left[1]])
    attn_terms = jnp.einsum(
        "wnr,wnc->wrc", paired_left, right[:4], preferred_element_type=jnp.float32
    )
    router_term = jnp.einsum("nf,nr->fr", router_right, left[2], preferred_element_type=jnp.float32)
    attn_sum, router_total = lax.psum((attn_terms, router_term), "shard")
    precond_attn = learning_rate * attn_sum
    precond_router = learning_rate * router_total
    vocab_block = VOCAB // n_tensor
    step_rows = math.gcd(vocab_block, 512)
    vocab_start = tensor_rank * vocab_block

    def embed_block(block_index):
        ids_here = vocab_start + block_index * step_rows + lax.iota(jnp.int32, step_rows)
        onehot = (ids_here[:, None] == ids_all[None, :]).astype(jnp.bfloat16)
        summed = jnp.dot(onehot, embed_all, preferred_element_type=jnp.float32)
        tallies = jnp.sum(onehot, axis=1, dtype=jnp.float32)
        return (summed, tallies)

    block_sums, block_counts = lax.map(
        embed_block, jnp.arange(vocab_block // step_rows, dtype=jnp.int32)
    )
    embed_sum = block_sums.reshape(vocab_block, col_block)
    counts = block_counts.reshape(vocab_block)
    divisor = factor_decay * old_embed_diag + (1.0 - factor_decay) * (counts / tokens_all) + damping
    precond_embed = learning_rate * embed_sum / divisor[:, None]
    return (precond_attn, precond_router, precond_norms, precond_embed)


def split_three(values):
    high = lax.reduce_precision(values, 8, 7)
    rest = values - high
    middle = lax.reduce_precision(rest, 8, 7)
    return jnp.stack([high, middle, rest - middle], axis=-2).astype(jnp.bfloat16)


def swap(value, axis, size, step):
    return lax.ppermute(value, axis, [(i, i ^ step) for i in range(size)])


def local_diagonals(blocks):
    width = blocks.shape[1]
    pieces = []
    for start in range(0, width, 128):
        size = min(128, width - start)
        tile = blocks[:, start : start + size, start : start + size]
        pieces.append(jnp.sum(tile * jnp.eye(size, dtype=tile.dtype), axis=1))
    return jnp.concatenate(pieces, axis=1)


def rounded(values):
    return values.astype(jnp.bfloat16).astype(jnp.float32)


def params():
    return pltpu.CompilerParams(vmem_limit_bytes=40 * 1024 * 1024)


def factor_kernel(place_ref, part, own, old, diag, out, *, step, weight):
    fresh = jnp.zeros(out.shape, jnp.float32)
    for index in range(part.shape[0]):
        fresh += lax.dot_general(
            part[index], own[index], (((1,), (1,)), ((), ())), preferred_element_type=jnp.float32
        )
    block = factor_decay * old[...].astype(jnp.float32) + weight * fresh
    on_diag = lax.broadcasted_iota(jnp.int32, out.shape, 0) == lax.broadcasted_iota(
        jnp.int32, out.shape, 1
    )
    block = jnp.where(on_diag & (place_ref[0] == step), diag[0], block)
    out[...] = block.astype(jnp.bfloat16)


def factor_block(place, features, old, diag, step, weight):
    groups, _, tokens = features.shape
    rows, cols = old.shape
    return pl.pallas_call(
        functools.partial(factor_kernel, step=step, weight=weight),
        grid_spec=pltpu.PrefetchScalarGridSpec(
            num_scalar_prefetch=1,
            grid=(1,),
            in_specs=[
                pl.BlockSpec((groups, rows, tokens), lambda i, place: (0, step, 0)),
                pl.BlockSpec((groups, cols, tokens), lambda i, place: (0, place[0], 0)),
                pl.BlockSpec((rows, cols), lambda i, place: (0, 0)),
                pl.BlockSpec((1, 1, cols), lambda i, place: (place[0], 0, 0)),
            ],
            out_specs=pl.BlockSpec((rows, cols), lambda i, place: (0, 0)),
        ),
        out_shape=jax.ShapeDtypeStruct((rows, cols), jnp.bfloat16),
        compiler_params=params(),
        cost_estimate=pl.CostEstimate(
            flops=2 * groups * rows * cols * tokens,
            bytes_accessed=4 * rows * cols + 4 * groups * rows * tokens,
            transcendentals=0,
        ),
    )(place, features, features, old, diag)


def fetch_blocks(place_ref, blocks, held, sems):
    count = len(blocks) // 2
    depth = blocks[0].shape[0]
    copies = []
    for index in range(2 * count):
        slot = pl.multiple_of((place_ref[0] ^ (index % count)) * depth, depth)
        copies.append(
            pltpu.make_async_copy(
                blocks[index], held.at[index // count, pl.ds(slot, depth)], sems.at[index]
            )
        )
    for copy in copies:
        copy.start()
    return copies


def block_products(rows, copies, held):
    count = len(copies) // 2
    products = []
    for index in range(2):
        for copy in copies[index * count : (index + 1) * count]:
            copy.wait()
        products.append(jnp.dot(rows, held[index], preferred_element_type=jnp.float32))
    return products


def first_parts(place_ref, scale, rows, diag, product, index):
    width = product.shape[1]
    square = scale * scale
    values = rows[:, index * width : (index + 1) * width].astype(jnp.float32)
    low_diag = diag[place_ref[0] ^ index]
    first_diag = rounded(2.0 * scale - square * low_diag)
    by_first = 2.0 * scale * values - square * product
    step_one = first_diag * values - square * (product - low_diag * values)
    return by_first, step_one, low_diag, first_diag


def first_kernel(place_ref, scale_ref, rows, diag, *refs):
    blocks, (kept, message), (held, sems) = refs[:8], refs[8:10], refs[10:]
    copies = fetch_blocks(place_ref, blocks, held, sems)
    products = block_products(rows[...], copies, held)
    lows = []
    for index in range(2):
        kept[index] = products[index]
        parts = first_parts(place_ref, scale_ref[0], rows, diag, products[index], index)
        lows.append(parts[1].astype(jnp.bfloat16))
    message[...] = jnp.concatenate(lows, axis=1)


def second_kernel(place_ref, scale_ref, mine, theirs, rows, diag, before, *refs):
    blocks, (kept, message), (held, sems) = refs[:8], refs[8:10], refs[10:]
    copies = fetch_blocks(place_ref, blocks, held, sems)
    both = jnp.concatenate([mine[...], theirs[...]], axis=1)
    products = block_products(both, copies, held)
    square = scale_ref[0] * scale_ref[0]
    lows = []
    for index in range(2):
        by_first, one, low_diag, first_diag = first_parts(
            place_ref, scale_ref[0], rows, diag, before[index], index
        )
        two = products[index] + low_diag * (one - rounded(one))
        low = two.astype(jnp.bfloat16)
        kept[index] = (
            2.0 * by_first - first_diag * two - square * low_diag * low.astype(jnp.float32)
        )
        lows.append(low)
    message[...] = jnp.concatenate(lows, axis=1)


def third_kernel(place_ref, scale_ref, mine, theirs, before, *refs):
    blocks, (keep, give), (held, sems) = refs[:8], refs[8:10], refs[10:]
    copies = fetch_blocks(place_ref, blocks, held, sems)
    both = jnp.concatenate([mine[...], theirs[...]], axis=1)
    products = block_products(both, copies, held)
    square = scale_ref[0] * scale_ref[0]
    for index, out in ((0, keep), (1, give)):
        out[...] = (before[index] + square * products[index]).T.astype(jnp.bfloat16)


def chain_call(kernel, scalars, arrays, blocks, out_shape):
    depth, width = blocks[0].shape
    count = len(blocks) // 2
    tokens = arrays[0].shape[0]
    vmem = pl.BlockSpec(memory_space=pltpu.VMEM)
    return pl.pallas_call(
        kernel,
        in_specs=[pl.BlockSpec(memory_space=pltpu.SMEM)] * len(scalars)
        + [vmem] * len(arrays)
        + [pl.BlockSpec(memory_space=pl.ANY)] * len(blocks),
        out_specs=[vmem] * len(out_shape),
        out_shape=out_shape,
        scratch_shapes=[
            pltpu.VMEM((2, count * depth, width), jnp.bfloat16),
            pltpu.SemaphoreType.DMA((len(blocks),)),
        ],
        compiler_params=params(),
        cost_estimate=pl.CostEstimate(
            flops=2 * len(blocks) * tokens * depth * width,
            bytes_accessed=2 * len(blocks) * depth * width,
            transcendentals=0,
        ),
    )(*scalars, *arrays, *blocks)


def output_kernel(
    where_ref, left_mine, left_other, ids, scale, *refs, attn_steps, vocab_block
):
    mine, others, spread = refs[:4], refs[4:8], refs[8:12]
    attn, embed, held, sems = refs[12:]
    shard, layer, step = where_ref[0], where_ref[1], pl.program_id(0)
    first = shard == 0

    def fetch(slot, from_mine, index):
        for place in range(4):
            for group, wanted in ((mine, from_mine), (others, jnp.logical_not(from_mine))):

                @pl.when(wanted & (index == place))
                def _():
                    pltpu.make_async_copy(group[place], held.at[slot], sems.at[slot]).start()

    @pl.when(step == 0)
    def _():
        fetch(0, first, layer)
        for place in range(4):

            @pl.when(layer == place)
            def _():
                pltpu.make_async_copy(spread[place], held.at[1], sems.at[1]).start()

        fetch(2, first, 3 - layer)
        fetch(3, jnp.logical_not(first), layer)
        fetch(4, jnp.logical_not(first), 3 - layer)

    def arrived(slot):
        pltpu.make_async_copy(mine[0], held.at[slot], sems.at[slot]).wait()
        return held[slot]

    def product(left, right):
        return lax.dot_general(
            left, right, (((1,), (1,)), ((), ())), preferred_element_type=jnp.float32
        )

    for slot in range(attn_steps):

        @pl.when(step == slot)
        def _():
            same = first if slot < 3 else jnp.logical_not(first)
            left = jnp.where(same, left_mine[...], left_other[...])
            attn[0] = learning_rate * product(left, arrived(slot))

    @pl.when(step == attn_steps)
    def _():
        arrived(4)

    @pl.when(step >= attn_steps)
    def _():
        rows = embed.shape[0]
        start = layer * vocab_block + (step - attn_steps) * rows
        here = lax.broadcasted_iota(jnp.int32, (rows, ids.shape[1]), 0) + start
        matches = (here == ids[...]).astype(jnp.float32).astype(jnp.bfloat16)
        embed[...] = product(matches, held[4]) * scale[...]


def output_products(where, bundle, ids, scale, mine, others, spread):
    cols, tokens_all = mine[0].shape
    vocab_block = scale.shape[0]
    parts = 4
    rows = vocab_block // parts

    def embed_place(step):
        return (jnp.maximum(step - 4, 0), 0)

    return pl.pallas_call(
        functools.partial(output_kernel, attn_steps=4, vocab_block=vocab_block),
        grid=(4 + parts,),
        out_shape=(
            jax.ShapeDtypeStruct((4, cols, cols), jnp.float32),
            jax.ShapeDtypeStruct((vocab_block, cols), jnp.float32),
        ),
        in_specs=[
            pl.BlockSpec(memory_space=pltpu.SMEM),
            pl.BlockSpec((cols, tokens_all), lambda step: (0, 0)),
            pl.BlockSpec((cols, tokens_all), lambda step: (1, 0)),
            pl.BlockSpec((1, tokens_all), lambda step: (0, 0)),
            pl.BlockSpec((rows, 1), embed_place),
        ]
        + [pl.BlockSpec(memory_space=pl.ANY)] * 12,
        out_specs=(
            pl.BlockSpec((1, cols, cols), lambda step: (jnp.minimum(step, 3), 0, 0)),
            pl.BlockSpec((rows, cols), embed_place),
        ),
        scratch_shapes=[
            pltpu.VMEM((5, cols, tokens_all), jnp.bfloat16),
            pltpu.SemaphoreType.DMA((5,)),
        ],
        compiler_params=params(),
        cost_estimate=pl.CostEstimate(
            flops=2 * cols * tokens_all * (4 * cols + vocab_block),
            bytes_accessed=4 * cols * (4 * cols + vocab_block) + 14 * cols * tokens_all,
            transcendentals=0,
        ),
    )(where, bundle, bundle, ids, scale, *mine, *others, *spread)


def layer_plan(
    activations,
    router_grad,
    token_ids,
    norm_terms,
    old_factors,
    old_router_factor,
    old_norm_diag,
    old_embed_diag,
):
    n_tensor = lax.axis_size("tensor")
    n_section = lax.axis_size("section")
    n_shard = lax.axis_size("shard")
    shard = lax.axis_index("shard")
    layer = lax.axis_index("tensor")
    section = lax.axis_index("section")
    core = section % 2
    owned, row_block, col_block = old_factors.shape
    tokens = activations.shape[1]
    features_dev = activations.shape[2]
    tokens_all = tokens * n_shard
    weight = (1.0 - factor_decay) / tokens_all
    own_place = section ^ layer
    place = own_place.reshape(1)
    axes = ("shard", "tensor")

    def by_index(array, index, axis=0):
        return lax.dynamic_index_in_dim(array, index, axis, False)

    def held_by(layer_index):
        return jnp.where(layer_index == 3, 3, lax.rem(layer_index + 1, 3))

    def old_block(step):
        away = by_index(old_factors, held_by(layer ^ step)).astype(jnp.bfloat16)
        return swap(away, "tensor", n_tensor, step) if step else away

    early = old_block(2)

    by_feature = jnp.swapaxes(activations, 1, 2)
    kept_tokens = lax.dynamic_slice_in_dim(by_feature, shard * owned, owned, 0)
    sent_tokens = lax.dynamic_slice_in_dim(by_feature, (1 - shard) * owned, owned, 0)
    other_tokens = swap(sent_tokens, "shard", n_shard, 1)
    diagonals = local_diagonals(old_factors) * (layer == section).astype(jnp.float32)
    extra = jnp.pad(split_three(diagonals), ((0, 0), (0, 0), (0, 3 * tokens - col_block)))
    extra = jnp.pad(extra.reshape(owned, 9, tokens), ((0, 0), (0, 7), (0, 0)))
    collected = []
    for step in range(n_tensor):
        factor = held_by(layer ^ step)
        message = jnp.concatenate(
            [by_index(kept_tokens, factor), by_index(other_tokens, factor), by_index(extra, factor)],
            axis=0,
        )
        collected.append(swap(message, "tensor", n_tensor, step) if step else message)
    collected, early = lax.optimization_barrier((jnp.stack(collected), early))
    gathered = lax.all_gather(collected, "section", axis=0)
    blocks = [old_block(0), old_block(1), early, old_block(3)]

    def both_shards(value, axis):
        other = swap(value, "shard", n_shard, 1)
        return jnp.where(
            shard == 0,
            jnp.concatenate([value, other], axis=axis),
            jnp.concatenate([other, value], axis=axis),
        )

    grad_all = both_shards(router_grad, 1)
    ids_all = both_shards(token_ids, 0)
    norm_values = norm_terms.astype(jnp.float32)
    norm_sums = jnp.stack([jnp.sum(norm_values, axis=1), jnp.sum(norm_values * norm_values, axis=1)])
    norm_sums = norm_sums + swap(norm_sums, "shard", n_shard, 1)
    gathered, grad_all, ids_all, norm_sums = lax.optimization_barrier(
        (gathered, grad_all, ids_all, norm_sums)
    )

    features = gathered[:, :, : 2 * features_dev].reshape(
        n_section, n_tensor, n_shard, features_dev, tokens
    )
    features = features.transpose(2, 1, 0, 3, 4).reshape(n_shard, D, tokens)
    codes = jnp.sum(
        gathered[:, :, 2 * features_dev : 2 * features_dev + 9].astype(jnp.float32), axis=1
    )
    old_diag = jnp.sum(codes.reshape(n_section, 3, 3 * tokens), axis=1)[:, :col_block]
    old_diag = jnp.stack([by_index(old_diag, layer ^ step) for step in range(n_tensor)])
    values = features.astype(jnp.float32)
    squares = jnp.sum(values * values, axis=(0, 2)).reshape(n_tensor, col_block)
    matrix_diag = factor_decay * old_diag + weight * squares + damping
    scale = (D / (3.0 * jnp.sum(matrix_diag))).reshape(1)
    low_diag = lax.reduce_precision(matrix_diag, 8, 7)[:, None, :]
    rows = by_index(features, core).reshape(n_tensor, row_block, tokens)
    rows = jnp.concatenate(
        [jnp.swapaxes(by_index(rows, own_place ^ index), 0, 1) for index in range(n_tensor)], axis=1
    )
    features, rows = lax.optimization_barrier((features, rows))

    own_cols = [
        factor_block(place, features, blocks[step], low_diag, step, weight)
        for step in range(n_tensor)
    ]
    other_cols = [swap(block, "section", n_section, 1) for block in own_cols]
    cols = own_cols + other_cols

    wide = jax.ShapeDtypeStruct((2, tokens, col_block), jnp.float32)
    sent = jax.ShapeDtypeStruct((tokens, 2 * col_block), jnp.bfloat16)
    part = jax.ShapeDtypeStruct((col_block, tokens), jnp.bfloat16)
    scalars = (place, scale)
    kept, message = chain_call(first_kernel, scalars, (rows, low_diag), cols, (wide, sent))
    theirs = swap(message, "section", n_section, 2)
    kept, message = chain_call(
        second_kernel, scalars, (message, theirs, rows, low_diag, kept), cols, (wide, sent)
    )
    theirs = swap(message, "section", n_section, 2)
    keep, give = chain_call(third_kernel, scalars, (message, theirs, kept), cols, (part, part))
    got = swap(give, "section", n_section, 1)
    own = jnp.where(
        core == shard, jnp.concatenate([keep, got], axis=1), jnp.concatenate([got, keep], axis=1)
    )

    def send(value, pairs):
        moves = [(x * n_tensor + a, x * n_tensor + b) for x in planes for a, b in pairs]
        return lax.ppermute(value, axes, moves)

    def across(value, at):
        moves = [(x * n_tensor + z, (1 - x) * n_tensor + z) for x, z in at]
        return lax.ppermute(value, axes, moves)

    everywhere = ("shard", "tensor", "section")
    planes = range(n_shard)
    layers = range(n_tensor)

    def spot(x, z, s):
        return (x * n_tensor + z) * n_section + s

    def scatter(value, source):
        moved_here = lax.ppermute(
            value,
            everywhere,
            [(spot(x, source, s), spot(x, s, s)) for x in planes for s in layers if s != source],
        )
        return jnp.where(layer == source, value, moved_here)

    hop_1 = send(own, [(0, 1), (3, 2)])
    over_0 = across(own, [(0, 0), (1, 0), (0, 1), (0, 3), (1, 3)])
    left_here = scatter(own, 2)
    hop_1, over_0, left_here = lax.optimization_barrier((hop_1, over_0, left_here))
    hop_2 = send(hop_1, [(1, 2), (2, 1)])
    over_1 = across(hop_1, [(x, z) for x in planes for z in (1, 2)])
    middle = jnp.where(shard == 0, own, over_0)
    spread_0 = send(middle, [(1, 0)])
    left_there = lax.ppermute(
        left_here, everywhere, [(spot(x, t, t), spot(1 - x, t, t)) for x in planes for t in layers]
    )

    router_matrix = (
        factor_decay * old_router_factor
        + weight * jnp.einsum("en,fn->ef", grad_all, grad_all, preferred_element_type=jnp.float32)
        + damping * jnp.eye(EXPERTS, dtype=jnp.float32)
    )
    router_inverse = local_inverse(router_matrix)
    router_right = jnp.einsum(
        "en,ef->fn", grad_all, router_inverse, preferred_element_type=jnp.float32
    ).astype(jnp.bfloat16)
    router_cols = learning_rate * jnp.einsum(
        "fn,cn->fc", router_right, own, preferred_element_type=jnp.float32
    )
    router_there = across(router_cols, [(1, 1)])
    router_cols = scatter(jnp.where(shard == 1, router_cols, router_there), 1)
    router_high = lax.reduce_precision(router_cols, 8, 7)
    codes = jnp.concatenate([router_high, router_cols - router_high], axis=0).astype(jnp.bfloat16)
    codes_tail = jnp.pad(codes[:, tokens_all:], ((0, 0), (0, 2 * tokens_all - col_block)))
    bundle = jnp.concatenate([left_here, left_there, codes[:, :tokens_all], codes_tail], axis=0)

    bundle, hop_2, over_1, spread_0, middle = lax.optimization_barrier(
        (bundle, hop_2, over_1, spread_0, middle)
    )
    hop_3 = send(hop_2, [(1, 0), (2, 3)])
    over_2 = across(hop_2, [(x, z) for x in planes for z in (1, 2)])
    spread_2 = send(middle, [(1, 2)])
    to_side = [(spot(x, t, t), spot(x, t, t ^ 2)) for x in planes for t in layers]
    bundle = jnp.where(section == layer, bundle, lax.ppermute(bundle, everywhere, to_side))
    bundle, hop_3, over_2, spread_2 = lax.optimization_barrier((bundle, hop_3, over_2, spread_2))
    over_3 = across(hop_3, [(x, z) for x in planes for z in (0, 3)])
    spread_3 = send(spread_2, [(2, 3)])
    to_core = [
        (spot(x, t, t ^ a), spot(x, t, t ^ a ^ 1)) for x in planes for t in layers for a in (0, 2)
    ]
    bundle = jnp.where(
        (section ^ layer) % 2 == 0, bundle, lax.ppermute(bundle, everywhere, to_core)
    )
    codes = bundle[2 * col_block :]
    codes = jnp.concatenate(
        [codes[: 2 * EXPERTS], codes[2 * EXPERTS :, : col_block - tokens_all]], axis=1
    ).astype(jnp.float32)
    precond_router = codes[:EXPERTS] + codes[EXPERTS:]

    vocab_block = old_embed_diag.shape[0]
    ids_here = layer * vocab_block + lax.iota(jnp.int32, vocab_block)
    counts = jnp.sum((ids_here[:, None] == ids_all[None, :]).astype(jnp.float32), axis=1)
    divisor = factor_decay * old_embed_diag + (1.0 - factor_decay) * (counts / tokens_all) + damping
    precond_attn, precond_embed = output_products(
        jnp.stack([shard, layer]),
        bundle,
        ids_all[None, :],
        (learning_rate / divisor)[:, None],
        (own, hop_1, hop_2, hop_3),
        (over_0, over_1, over_2, over_3),
        (spread_0, middle, spread_2, spread_3),
    )

    precond_norms = (
        learning_rate
        * norm_sums[0]
        / (
            factor_decay * old_norm_diag
            + (1.0 - factor_decay) * (norm_sums[1] / tokens_all)
            + damping
        )
    )
    return (precond_attn, precond_router, precond_norms, precond_embed)


def per_device(*arguments):
    one_each = arguments[4].shape[0] == lax.axis_size("tensor") == lax.axis_size("section")
    if one_each and lax.axis_size("section") == 4 and lax.axis_size("shard") == 2:
        return layer_plan(*arguments)
    return general_plan(*arguments)


def solution(mesh):
    return jax.shard_map(
        per_device,
        mesh=mesh,
        in_specs=(
            P(None, "shard", ("tensor", "section")),
            P(None, "shard"),
            P("shard"),
            P(None, "shard", ("tensor", "section")),
            P("shard", "tensor", "section"),
            P(),
            P(None, ("tensor", "section")),
            P("tensor"),
        ),
        out_specs=(
            P(None, "tensor", "section"),
            P(None, "tensor"),
            P(None, ("tensor", "section")),
            P("tensor", "section"),
        ),
        check_vma=False,
    )
```

```python
import functools
import math

import jax
import jax.numpy as jnp
from jax import lax
from jax.experimental import pallas as pl
from jax.experimental.pallas import tpu as pltpu
from jax.sharding import PartitionSpec as P

D = 2304
EXPERTS = 8
VOCAB = 8192


factor_decay = 0.5
damping = 0.01
learning_rate = 0.05


def local_inverse(matrix):
    width = matrix.shape[0]
    trace = jnp.sum(jnp.diagonal(matrix))
    factor_scale = width / (3.0 * trace)
    identity = jnp.eye(width, dtype=jnp.float32)
    matrix_low = lax.optimization_barrier(matrix.astype(jnp.bfloat16))
    first = 2.0 * factor_scale * identity - factor_scale * factor_scale * matrix_low.astype(
        jnp.float32
    )
    first_low = first.astype(jnp.bfloat16)
    image = jnp.dot(matrix_low, first_low, preferred_element_type=jnp.float32).astype(jnp.bfloat16)
    product = jnp.dot(first_low, image, preferred_element_type=jnp.float32)
    return (2.0 * first - product).astype(jnp.bfloat16)


def fold_with(columns, piece):
    return jnp.einsum("kij,kjl->kil", piece, columns, preferred_element_type=jnp.float32)


def general_plan(
    activations,
    router_grad,
    token_ids,
    norm_terms,
    old_factors,
    old_router_factor,
    old_norm_diag,
    old_embed_diag,
):
    n_tensor = lax.axis_size("tensor")
    n_section = lax.axis_size("section")
    n_shard = lax.axis_size("shard")
    tensor_rank = lax.axis_index("tensor")
    section_rank = lax.axis_index("section")
    row_block = D // n_tensor
    col_block = D // n_section
    tokens_all = activations.shape[1] * n_shard
    row_start = tensor_rank * row_block
    col_start = section_rank * col_block

    def collect(carry, piece):
        whole = lax.all_gather(piece, ("tensor", "section"), axis=1, tiled=True)
        rows_part = lax.dynamic_slice_in_dim(whole, row_start, row_block, 1)
        cols_part = lax.dynamic_slice_in_dim(whole, col_start, col_block, 1)
        return (carry, (rows_part, cols_part))

    unused_carry, (row_parts, col_parts) = lax.scan(collect, jnp.int32(0), activations)
    partial_value = jnp.einsum(
        "mnr,mnc->mrc", row_parts, col_parts, preferred_element_type=jnp.float32
    )
    fresh = lax.psum_scatter(partial_value, "shard", scatter_dimension=0, tiled=True) / tokens_all
    row_index = lax.broadcasted_iota(jnp.int32, (row_block, col_block), 0) + row_start
    col_index = lax.broadcasted_iota(jnp.int32, (row_block, col_block), 1) + col_start
    eye_block = (row_index == col_index).astype(jnp.float32)
    matrix = factor_decay * old_factors + (1.0 - factor_decay) * fresh + damping * eye_block
    diag_part = jnp.sum(matrix * eye_block, axis=(1, 2))
    trace = lax.psum(diag_part, ("tensor", "section"))
    factor_scale = (D / (3.0 * trace))[:, None, None]
    matrix_low = lax.optimization_barrier(matrix.astype(jnp.bfloat16))
    first = 2.0 * factor_scale * eye_block - factor_scale * factor_scale * matrix_low.astype(
        jnp.float32
    )
    first_low = first.astype(jnp.bfloat16)
    first_cols = lax.all_gather(first_low, "tensor", axis=1, tiled=True)
    image = fold_with(first_cols, lax.all_gather(matrix_low, "section", axis=2, tiled=True))
    image_cols = lax.all_gather(image.astype(jnp.bfloat16), "tensor", axis=1, tiled=True)
    product = fold_with(image_cols, lax.all_gather(first_low, "section", axis=2, tiled=True))
    inverse_low = (2.0 * first - product).astype(jnp.bfloat16)
    inverses = lax.all_gather(inverse_low, "shard", axis=0, tiled=True)
    left_terms = jnp.stack(
        [
            jnp.einsum("nc,rc->nr", col_parts[m], inverses[m], preferred_element_type=jnp.float32)
            for m in (0, 4, 6)
        ]
    )
    left = lax.psum(left_terms, "section").astype(jnp.bfloat16)
    right_terms = jnp.stack(
        [
            jnp.einsum("nr,rc->nc", row_parts[m], inverses[m], preferred_element_type=jnp.float32)
            for m in (1, 2, 3, 5, 7)
        ]
    )
    right = lax.psum(right_terms, "tensor").astype(jnp.bfloat16)
    norm_values = norm_terms.astype(jnp.float32)
    router_part = jnp.einsum(
        "en,fn->ef", router_grad, router_grad, preferred_element_type=jnp.float32
    )
    router_sum, norm_total, norm_squares = lax.psum(
        (router_part, jnp.sum(norm_values, axis=1), jnp.sum(norm_values * norm_values, axis=1)),
        "shard",
    )
    router_matrix = (
        factor_decay * old_router_factor
        + (1.0 - factor_decay) * (router_sum / tokens_all)
        + damping * jnp.eye(EXPERTS, dtype=jnp.float32)
    )
    router_inverse = local_inverse(router_matrix)
    router_right = jnp.einsum(
        "en,ef->nf", router_grad, router_inverse, preferred_element_type=jnp.float32
    ).astype(jnp.bfloat16)
    precond_norms = (
        learning_rate
        * norm_total
        / (
            factor_decay * old_norm_diag
            + (1.0 - factor_decay) * (norm_squares / tokens_all)
            + damping
        )
    )
    ids_all = lax.all_gather(token_ids, "shard", axis=0, tiled=True)
    embed_all = lax.all_gather(right[4], "shard", axis=0, tiled=True)
    paired_left = jnp.stack([left[0], left[0], left[0], left[1]])
    attn_terms = jnp.einsum(
        "wnr,wnc->wrc", paired_left, right[:4], preferred_element_type=jnp.float32
    )
    router_term = jnp.einsum("nf,nr->fr", router_right, left[2], preferred_element_type=jnp.float32)
    attn_sum, router_total = lax.psum((attn_terms, router_term), "shard")
    precond_attn = learning_rate * attn_sum
    precond_router = learning_rate * router_total
    vocab_block = VOCAB // n_tensor
    step_rows = math.gcd(vocab_block, 512)
    vocab_start = tensor_rank * vocab_block

    def embed_block(block_index):
        ids_here = vocab_start + block_index * step_rows + lax.iota(jnp.int32, step_rows)
        onehot = (ids_here[:, None] == ids_all[None, :]).astype(jnp.bfloat16)
        summed = jnp.dot(onehot, embed_all, preferred_element_type=jnp.float32)
        tallies = jnp.sum(onehot, axis=1, dtype=jnp.float32)
        return (summed, tallies)

    block_sums, block_counts = lax.map(
        embed_block, jnp.arange(vocab_block // step_rows, dtype=jnp.int32)
    )
    embed_sum = block_sums.reshape(vocab_block, col_block)
    counts = block_counts.reshape(vocab_block)
    divisor = factor_decay * old_embed_diag + (1.0 - factor_decay) * (counts / tokens_all) + damping
    precond_embed = learning_rate * embed_sum / divisor[:, None]
    return (precond_attn, precond_router, precond_norms, precond_embed)


def split_three(values):
    high = lax.reduce_precision(values, 8, 7)
    rest = values - high
    middle = lax.reduce_precision(rest, 8, 7)
    return jnp.stack([high, middle, rest - middle], axis=-2).astype(jnp.bfloat16)


def swap(value, axis, size, step):
    return lax.ppermute(value, axis, [(i, i ^ step) for i in range(size)])


def local_diagonals(blocks):
    width = blocks.shape[1]
    pieces = []
    for start in range(0, width, 128):
        size = min(128, width - start)
        tile = blocks[:, start : start + size, start : start + size]
        pieces.append(jnp.sum(tile * jnp.eye(size, dtype=tile.dtype), axis=1))
    return jnp.concatenate(pieces, axis=1)


def rounded(values):
    return values.astype(jnp.bfloat16).astype(jnp.float32)


def params():
    return pltpu.CompilerParams(vmem_limit_bytes=40 * 1024 * 1024)


def layout_kernel(place_ref, gathered, features, rows, low_diag, trace, old, *, weight):
    own_place, layer, core = place_ref[0], place_ref[1], place_ref[2]
    sections, steps, _, tokens = gathered.shape
    groups, depth, _ = features.shape
    part = depth // (sections * steps)
    width = depth // steps
    for section in range(sections):
        codes = jnp.zeros((16, tokens), jnp.float32)
        for step in range(steps):
            start = (step * sections + section) * part
            for group in range(groups):
                features[group, start : start + part] = gathered[
                    section, step, group * part : (group + 1) * part
                ]
            codes += gathered[section, step, groups * part :].astype(jnp.float32)
        codes = codes[0:3] + codes[3:6] + codes[6:9]
        pieces = [codes[0:1], codes[1:2], codes[2:3, : width - 2 * tokens]]
        old[section ^ layer] = jnp.concatenate(pieces, axis=1)
    ones = jnp.ones((8, tokens), jnp.bfloat16)
    total = jnp.float32(0.0)
    for step in range(steps):
        squares = jnp.zeros((8, width), jnp.float32)
        for group in range(groups):
            values = features[group, step * width : (step + 1) * width].astype(jnp.float32)
            values = values * values
            high = values.astype(jnp.bfloat16)
            low = (values - high.astype(jnp.float32)).astype(jnp.bfloat16)
            for piece in (high, low):
                squares += lax.dot_general(
                    ones, piece, (((1,), (1,)), ((), ())), preferred_element_type=jnp.float32
                )
        diag = factor_decay * old[step] + weight * squares[0:1] + damping
        total += jnp.sum(diag)
        low_diag[step] = rounded(diag)
        start = pl.multiple_of((own_place ^ step) * width, width)
        mine = features[core, pl.ds(start, width)]
        rows[:, step * width : (step + 1) * width] = mine.T
    trace[0] = total


def lay_out(places, gathered, weight):
    sections, steps, height, tokens = gathered.shape
    part = (height - 16) // 2
    depth = sections * steps * part
    width = depth // steps
    vmem = pl.BlockSpec(memory_space=pltpu.VMEM)
    smem = pl.BlockSpec(memory_space=pltpu.SMEM)
    return pl.pallas_call(
        functools.partial(layout_kernel, weight=weight),
        in_specs=[smem, vmem],
        out_specs=[vmem, vmem, vmem, smem],
        out_shape=[
            jax.ShapeDtypeStruct((2, depth, tokens), jnp.bfloat16),
            jax.ShapeDtypeStruct((tokens, depth), jnp.bfloat16),
            jax.ShapeDtypeStruct((steps, 1, width), jnp.float32),
            jax.ShapeDtypeStruct((1,), jnp.float32),
        ],
        scratch_shapes=[pltpu.VMEM((steps, 1, width), jnp.float32)],
        compiler_params=params(),
        cost_estimate=pl.CostEstimate(
            flops=64 * depth * tokens, bytes_accessed=14 * depth * tokens, transcendentals=0
        ),
    )(places, gathered)


def factor_kernel(place_ref, part, own, old, diag, out, *, step, weight):
    fresh = jnp.zeros(out.shape, jnp.float32)
    for index in range(part.shape[0]):
        fresh += lax.dot_general(
            part[index], own[index], (((1,), (1,)), ((), ())), preferred_element_type=jnp.float32
        )
    block = factor_decay * old[...].astype(jnp.float32) + weight * fresh
    on_diag = lax.broadcasted_iota(jnp.int32, out.shape, 0) == lax.broadcasted_iota(
        jnp.int32, out.shape, 1
    )
    block = jnp.where(on_diag & (place_ref[0] == step), diag[0], block)
    out[...] = block.astype(jnp.bfloat16)


def factor_block(place, features, old, diag, step, weight):
    groups, _, tokens = features.shape
    rows, cols = old.shape
    return pl.pallas_call(
        functools.partial(factor_kernel, step=step, weight=weight),
        grid_spec=pltpu.PrefetchScalarGridSpec(
            num_scalar_prefetch=1,
            grid=(1,),
            in_specs=[
                pl.BlockSpec((groups, rows, tokens), lambda i, place: (0, step, 0)),
                pl.BlockSpec((groups, cols, tokens), lambda i, place: (0, place[0], 0)),
                pl.BlockSpec((rows, cols), lambda i, place: (0, 0)),
                pl.BlockSpec((1, 1, cols), lambda i, place: (place[0], 0, 0)),
            ],
            out_specs=pl.BlockSpec((rows, cols), lambda i, place: (0, 0)),
        ),
        out_shape=jax.ShapeDtypeStruct((rows, cols), jnp.bfloat16),
        compiler_params=params(),
        cost_estimate=pl.CostEstimate(
            flops=2 * groups * rows * cols * tokens,
            bytes_accessed=4 * rows * cols + 4 * groups * rows * tokens,
            transcendentals=0,
        ),
    )(place, features, features, old, diag)


def fetch_blocks(place_ref, blocks, held, sems):
    count = len(blocks) // 2
    depth = blocks[0].shape[0]
    copies = []
    for index in range(2 * count):
        slot = pl.multiple_of((place_ref[0] ^ (index % count)) * depth, depth)
        copies.append(
            pltpu.make_async_copy(
                blocks[index], held.at[index // count, pl.ds(slot, depth)], sems.at[index]
            )
        )
    for copy in copies:
        copy.start()
    return copies


def block_products(rows, copies, held):
    count = len(copies) // 2
    products = []
    for index in range(2):
        for copy in copies[index * count : (index + 1) * count]:
            copy.wait()
        products.append(jnp.dot(rows, held[index], preferred_element_type=jnp.float32))
    return products


def first_parts(place_ref, scale, rows, diag, product, index):
    width = product.shape[1]
    square = scale * scale
    values = rows[:, index * width : (index + 1) * width].astype(jnp.float32)
    low_diag = diag[place_ref[0] ^ index]
    first_diag = rounded(2.0 * scale - square * low_diag)
    by_first = 2.0 * scale * values - square * product
    step_one = first_diag * values - square * (product - low_diag * values)
    return by_first, step_one, low_diag, first_diag


def first_kernel(place_ref, scale_ref, rows, diag, *refs):
    blocks, (kept, message), (held, sems) = refs[:8], refs[8:10], refs[10:]
    copies = fetch_blocks(place_ref, blocks, held, sems)
    products = block_products(rows[...], copies, held)
    lows = []
    for index in range(2):
        kept[index] = products[index]
        parts = first_parts(place_ref, scale_ref[0], rows, diag, products[index], index)
        lows.append(parts[1].astype(jnp.bfloat16))
    message[...] = jnp.concatenate(lows, axis=1)


def second_kernel(place_ref, scale_ref, mine, theirs, rows, diag, before, *refs):
    blocks, (kept, message), (held, sems) = refs[:8], refs[8:10], refs[10:]
    copies = fetch_blocks(place_ref, blocks, held, sems)
    both = jnp.concatenate([mine[...], theirs[...]], axis=1)
    products = block_products(both, copies, held)
    square = scale_ref[0] * scale_ref[0]
    lows = []
    for index in range(2):
        by_first, one, low_diag, first_diag = first_parts(
            place_ref, scale_ref[0], rows, diag, before[index], index
        )
        two = products[index] + low_diag * (one - rounded(one))
        low = two.astype(jnp.bfloat16)
        kept[index] = (
            2.0 * by_first - first_diag * two - square * low_diag * low.astype(jnp.float32)
        )
        lows.append(low)
    message[...] = jnp.concatenate(lows, axis=1)


def third_kernel(place_ref, scale_ref, mine, theirs, before, *refs):
    blocks, (keep, give), (held, sems) = refs[:8], refs[8:10], refs[10:]
    copies = fetch_blocks(place_ref, blocks, held, sems)
    both = jnp.concatenate([mine[...], theirs[...]], axis=1)
    products = block_products(both, copies, held)
    square = scale_ref[0] * scale_ref[0]
    for index, out in ((0, keep), (1, give)):
        out[...] = (before[index] + square * products[index]).T.astype(jnp.bfloat16)


def chain_call(kernel, scalars, arrays, blocks, out_shape):
    depth, width = blocks[0].shape
    count = len(blocks) // 2
    tokens = arrays[0].shape[0]
    vmem = pl.BlockSpec(memory_space=pltpu.VMEM)
    return pl.pallas_call(
        kernel,
        in_specs=[pl.BlockSpec(memory_space=pltpu.SMEM)] * len(scalars)
        + [vmem] * len(arrays)
        + [pl.BlockSpec(memory_space=pltpu.HBM)] * len(blocks),
        out_specs=[vmem] * len(out_shape),
        out_shape=out_shape,
        scratch_shapes=[
            pltpu.VMEM((2, count * depth, width), jnp.bfloat16),
            pltpu.SemaphoreType.DMA((len(blocks),)),
        ],
        compiler_params=params(),
        cost_estimate=pl.CostEstimate(
            flops=2 * len(blocks) * tokens * depth * width,
            bytes_accessed=2 * len(blocks) * depth * width,
            transcendentals=0,
        ),
    )(*scalars, *arrays, *blocks)


def output_kernel(where_ref, left_mine, left_other, ids, scale, *refs, vocab_block):
    mine, others = refs[:4], refs[4:8]
    attn, embed, held, sems = refs[8:]
    shard, layer, step = where_ref[0], where_ref[1], pl.program_id(0)
    first = shard == 0

    @pl.when(step == 0)
    def _():
        for slot, source in enumerate((0, 1, 3, 0, 3)):
            from_mine = first if slot < 3 else jnp.logical_not(first)
            for place in range(4):
                for group, wanted in ((mine, from_mine), (others, jnp.logical_not(from_mine))):

                    @pl.when(wanted & ((layer ^ source) == place))
                    def _():
                        pltpu.make_async_copy(group[place], held.at[slot], sems.at[slot]).start()

    def arrived(slot):
        pltpu.make_async_copy(mine[0], held.at[slot], sems.at[slot]).wait()
        return held[slot]

    for slot in range(4):

        @pl.when(step == slot)
        def _():
            same = first if slot < 3 else jnp.logical_not(first)
            left = jnp.where(same, left_mine[...], left_other[...])
            attn[0] = learning_rate * lax.dot_general(
                left, arrived(slot), (((1,), (1,)), ((), ())), preferred_element_type=jnp.float32
            )

    @pl.when(step == 4)
    def _():
        arrived(4)

    @pl.when(step >= 4)
    def _():
        cols = embed.shape[1]
        start = layer * vocab_block + (step - 4) * cols
        here = lax.broadcasted_iota(jnp.int32, (ids.shape[0], cols), 1) + start
        matches = (here == ids[...]).astype(jnp.float32).astype(jnp.bfloat16)
        embed[...] = jnp.dot(held[4], matches, preferred_element_type=jnp.float32) * scale[...]


def output_products(where, bundle, ids, scale, mine, others):
    cols, tokens_all = mine[0].shape
    vocab_block = scale.shape[1]
    parts = 4
    part = vocab_block // parts

    def embed_place(step):
        return (0, jnp.maximum(step - 4, 0))

    return pl.pallas_call(
        functools.partial(output_kernel, vocab_block=vocab_block),
        grid=(4 + parts,),
        out_shape=(
            jax.ShapeDtypeStruct((4, cols, cols), jnp.float32),
            jax.ShapeDtypeStruct((cols, vocab_block), jnp.float32),
        ),
        in_specs=[
            pl.BlockSpec(memory_space=pltpu.SMEM),
            pl.BlockSpec((cols, tokens_all), lambda step: (0, 0)),
            pl.BlockSpec((cols, tokens_all), lambda step: (1, 0)),
            pl.BlockSpec((tokens_all, 1), lambda step: (0, 0)),
            pl.BlockSpec((1, part), embed_place),
        ]
        + [pl.BlockSpec(memory_space=pltpu.HBM)] * 8,
        out_specs=(
            pl.BlockSpec((1, cols, cols), lambda step: (jnp.minimum(step, 3), 0, 0)),
            pl.BlockSpec((cols, part), embed_place),
        ),
        scratch_shapes=[
            pltpu.VMEM((5, cols, tokens_all), jnp.bfloat16),
            pltpu.SemaphoreType.DMA((5,)),
        ],
        compiler_params=params(),
        cost_estimate=pl.CostEstimate(
            flops=2 * cols * tokens_all * (4 * cols + vocab_block),
            bytes_accessed=4 * cols * (4 * cols + vocab_block) + 14 * cols * tokens_all,
            transcendentals=0,
        ),
    )(where, bundle, bundle, ids, scale, *mine, *others)


def layer_plan(
    activations,
    router_grad,
    token_ids,
    norm_terms,
    old_factors,
    old_router_factor,
    old_norm_diag,
    old_embed_diag,
):
    n_tensor = lax.axis_size("tensor")
    n_section = lax.axis_size("section")
    n_shard = lax.axis_size("shard")
    shard = lax.axis_index("shard")
    layer = lax.axis_index("tensor")
    section = lax.axis_index("section")
    core = section % 2
    owned, row_block, col_block = old_factors.shape
    tokens = activations.shape[1]
    features_dev = activations.shape[2]
    tokens_all = tokens * n_shard
    weight = (1.0 - factor_decay) / tokens_all
    own_place = section ^ layer
    place = own_place.reshape(1)
    axes = ("shard", "tensor")

    def by_index(array, index, axis=0):
        return lax.dynamic_index_in_dim(array, index, axis, False)

    def held_by(layer_index):
        return jnp.where(layer_index == 3, 3, lax.rem(layer_index + 1, 3))

    def old_block(factors, step, start, size):
        away = by_index(factors, held_by(layer ^ step))[start : start + size]
        away = away.astype(jnp.bfloat16)
        return swap(away, "tensor", n_tensor, step) if step else away

    part_rows = row_block // 2
    early = old_block(old_factors, 2, 0, part_rows)
    later_factors = lax.optimization_barrier(old_factors)

    by_feature = jnp.swapaxes(activations, 1, 2)
    kept_tokens = lax.dynamic_slice_in_dim(by_feature, shard * owned, owned, 0)
    sent_tokens = lax.dynamic_slice_in_dim(by_feature, (1 - shard) * owned, owned, 0)
    other_tokens = swap(sent_tokens, "shard", n_shard, 1)
    diagonals = local_diagonals(old_factors) * (layer == section).astype(jnp.float32)
    extra = jnp.pad(split_three(diagonals), ((0, 0), (0, 0), (0, 3 * tokens - col_block)))
    extra = jnp.pad(extra.reshape(owned, 9, tokens), ((0, 0), (0, 7), (0, 0)))
    collected = []
    for step in range(n_tensor):
        factor = held_by(layer ^ step)
        message = jnp.concatenate(
            [by_index(kept_tokens, factor), by_index(other_tokens, factor), by_index(extra, factor)],
            axis=0,
        )
        collected.append(swap(message, "tensor", n_tensor, step) if step else message)
    collected, early = lax.optimization_barrier((jnp.stack(collected), early))
    gathered = lax.all_gather(collected, "section", axis=0)
    late = old_block(later_factors, 2, part_rows, part_rows)
    blocks = [
        old_block(later_factors, 0, 0, row_block),
        old_block(later_factors, 1, 0, row_block),
        jnp.concatenate([early, late], axis=0),
        old_block(later_factors, 3, 0, row_block),
    ]

    def both_shards(value, axis):
        other = swap(value, "shard", n_shard, 1)
        return jnp.where(
            shard == 0,
            jnp.concatenate([value, other], axis=axis),
            jnp.concatenate([other, value], axis=axis),
        )

    grad_all = both_shards(router_grad, 1)
    ids_all = both_shards(token_ids, 0)
    norm_values = norm_terms.astype(jnp.float32)
    norm_sums = jnp.stack([jnp.sum(norm_values, axis=1), jnp.sum(norm_values * norm_values, axis=1)])
    norm_sums = norm_sums + swap(norm_sums, "shard", n_shard, 1)
    vocab_block = old_embed_diag.shape[0]
    ids_here = layer * vocab_block + lax.iota(jnp.int32, vocab_block)
    counts = jnp.sum((ids_all[:, None] == ids_here[None, :]).astype(jnp.float32), axis=0)
    divisor = factor_decay * old_embed_diag + (1.0 - factor_decay) * (counts / tokens_all) + damping
    embed_scale = (learning_rate / divisor)[None, :]
    embed_ids = ids_all[:, None]
    gathered, grad_all, embed_ids, embed_scale, norm_sums = lax.optimization_barrier(
        (gathered, grad_all, embed_ids, embed_scale, norm_sums)
    )

    features, rows, low_diag, trace = lay_out(
        jnp.stack([own_place, layer, core]), gathered, weight
    )
    scale = D / (3.0 * trace)

    own_cols = [
        factor_block(place, features, blocks[step], low_diag, step, weight)
        for step in range(n_tensor)
    ]
    other_cols = [swap(block, "section", n_section, 1) for block in own_cols]
    cols = own_cols + other_cols

    wide = jax.ShapeDtypeStruct((2, tokens, col_block), jnp.float32)
    sent = jax.ShapeDtypeStruct((tokens, 2 * col_block), jnp.bfloat16)
    part = jax.ShapeDtypeStruct((col_block, tokens), jnp.bfloat16)
    scalars = (place, scale)
    kept, message = chain_call(first_kernel, scalars, (rows, low_diag), cols, (wide, sent))
    theirs = swap(message, "section", n_section, 2)
    kept, message = chain_call(
        second_kernel, scalars, (message, theirs, rows, low_diag, kept), cols, (wide, sent)
    )
    theirs = swap(message, "section", n_section, 2)
    keep, give = chain_call(third_kernel, scalars, (message, theirs, kept), cols, (part, part))
    got = swap(give, "section", n_section, 1)
    own = jnp.where(
        core == shard, jnp.concatenate([keep, got], axis=1), jnp.concatenate([got, keep], axis=1)
    )

    planes = range(n_shard)
    layers = range(n_tensor)

    def useful(x, z):
        return z != 2 and (x, z) != (1, 1)

    def send(value, step, held):
        moves = [
            (x * n_tensor + z, x * n_tensor + (z ^ step))
            for x in planes
            for z in layers
            if useful(x, z ^ held)
        ]
        return lax.ppermute(value, axes, moves)

    def across(value, held):
        moves = [
            (x * n_tensor + z, (1 - x) * n_tensor + z)
            for x in planes
            for z in layers
            if useful(x, z ^ held)
        ]
        return lax.ppermute(value, axes, moves)

    everywhere = ("shard", "tensor", "section")

    def spot(x, z, s):
        return (x * n_tensor + z) * n_section + s

    def scatter(value, source):
        moved_here = lax.ppermute(
            value,
            everywhere,
            [(spot(x, source, s), spot(x, s, s)) for x in planes for s in layers if s != source],
        )
        return jnp.where(layer == source, value, moved_here)

    router_matrix = (
        factor_decay * old_router_factor
        + weight * jnp.einsum("en,fn->ef", grad_all, grad_all, preferred_element_type=jnp.float32)
        + damping * jnp.eye(EXPERTS, dtype=jnp.float32)
    )
    router_inverse = local_inverse(router_matrix)
    router_right = jnp.einsum(
        "en,ef->fn", grad_all, router_inverse, preferred_element_type=jnp.float32
    ).astype(jnp.bfloat16)

    near_1 = send(own, 1, 0)
    near_2 = send(own, 2, 0)
    over_0 = across(own, 0)
    left_here = scatter(own, 2)
    router_cols = learning_rate * jnp.einsum(
        "fn,cn->fc", router_right, own, preferred_element_type=jnp.float32
    )
    router_cols = scatter(router_cols, 1)
    router_high = lax.reduce_precision(router_cols, 8, 7)
    codes = jnp.concatenate([router_high, router_cols - router_high], axis=0).astype(jnp.bfloat16)
    codes_tail = jnp.pad(codes[:, tokens_all:], ((0, 0), (0, 2 * tokens_all - col_block)))
    codes = jnp.concatenate([codes[:, :tokens_all], codes_tail], axis=0)
    near_1, over_0 = lax.optimization_barrier((near_1, over_0))
    over_1 = across(near_1, 1)
    left_here, near_2, codes = lax.optimization_barrier((left_here, near_2, codes))
    left_there = lax.ppermute(
        jnp.concatenate([left_here, codes], axis=0),
        everywhere,
        [(spot(x, t, t), spot(1 - x, t, t)) for x in planes for t in layers],
    )
    near_3 = send(near_2, 1, 2)
    over_2 = across(near_2, 2)
    codes = jnp.where(shard == 1, codes, left_there[col_block:])
    bundle = jnp.concatenate([left_here, left_there[:col_block], codes], axis=0)
    bundle, over_1 = lax.optimization_barrier((bundle, over_1))
    to_side = [(spot(x, t, t), spot(x, t, t ^ 2)) for x in planes for t in layers]
    bundle = jnp.where(section == layer, bundle, lax.ppermute(bundle, everywhere, to_side))
    bundle, near_3, over_2 = lax.optimization_barrier((bundle, near_3, over_2))
    over_3 = across(near_3, 3)
    to_core = [
        (spot(x, t, t ^ a), spot(x, t, t ^ a ^ 1)) for x in planes for t in layers for a in (0, 2)
    ]
    bundle = jnp.where(
        (section ^ layer) % 2 == 0, bundle, lax.ppermute(bundle, everywhere, to_core)
    )
    codes = bundle[2 * col_block :]
    codes = jnp.concatenate(
        [codes[: 2 * EXPERTS], codes[2 * EXPERTS :, : col_block - tokens_all]], axis=1
    ).astype(jnp.float32)
    precond_router = codes[:EXPERTS] + codes[EXPERTS:]

    precond_attn, embed_columns = output_products(
        jnp.stack([shard, layer]),
        bundle,
        embed_ids,
        embed_scale,
        (own, near_1, near_2, near_3),
        (over_0, over_1, over_2, over_3),
    )
    precond_embed = embed_columns.T

    precond_norms = (
        learning_rate
        * norm_sums[0]
        / (
            factor_decay * old_norm_diag
            + (1.0 - factor_decay) * (norm_sums[1] / tokens_all)
            + damping
        )
    )
    return (precond_attn, precond_router, precond_norms, precond_embed)


def per_device(*arguments):
    one_each = arguments[4].shape[0] == lax.axis_size("tensor") == lax.axis_size("section")
    if one_each and lax.axis_size("section") == 4 and lax.axis_size("shard") == 2:
        return layer_plan(*arguments)
    return general_plan(*arguments)


def solution(mesh):
    return jax.shard_map(
        per_device,
        mesh=mesh,
        in_specs=(
            P(None, "shard", ("tensor", "section")),
            P(None, "shard"),
            P("shard"),
            P(None, "shard", ("tensor", "section")),
            P("shard", "tensor", "section"),
            P(),
            P(None, ("tensor", "section")),
            P("tensor"),
        ),
        out_specs=(
            P(None, "tensor", "section"),
            P(None, "tensor"),
            P(None, ("tensor", "section")),
            P("tensor", "section"),
        ),
        check_vma=False,
    )
```

```python
import functools
import math

import jax
import jax.numpy as jnp
from jax import lax
from jax.experimental import pallas as pl
from jax.experimental.pallas import tpu as pltpu
from jax.sharding import PartitionSpec as P

D = 2304
EXPERTS = 8
VOCAB = 8192


factor_decay = 0.5
damping = 0.01
learning_rate = 0.05


def local_inverse(matrix):
    width = matrix.shape[0]
    trace = jnp.sum(jnp.diagonal(matrix))
    factor_scale = width / (3.0 * trace)
    identity = jnp.eye(width, dtype=jnp.float32)
    matrix_low = lax.optimization_barrier(matrix.astype(jnp.bfloat16))
    first = 2.0 * factor_scale * identity - factor_scale * factor_scale * matrix_low.astype(
        jnp.float32
    )
    first_low = first.astype(jnp.bfloat16)
    image = jnp.dot(matrix_low, first_low, preferred_element_type=jnp.float32).astype(jnp.bfloat16)
    product = jnp.dot(first_low, image, preferred_element_type=jnp.float32)
    return (2.0 * first - product).astype(jnp.bfloat16)


def fold_with(columns, piece):
    return jnp.einsum("kij,kjl->kil", piece, columns, preferred_element_type=jnp.float32)


def general_plan(
    activations,
    router_grad,
    token_ids,
    norm_terms,
    old_factors,
    old_router_factor,
    old_norm_diag,
    old_embed_diag,
):
    n_tensor = lax.axis_size("tensor")
    n_section = lax.axis_size("section")
    n_shard = lax.axis_size("shard")
    tensor_rank = lax.axis_index("tensor")
    section_rank = lax.axis_index("section")
    row_block = D // n_tensor
    col_block = D // n_section
    tokens_all = activations.shape[1] * n_shard
    row_start = tensor_rank * row_block
    col_start = section_rank * col_block

    def collect(carry, piece):
        whole = lax.all_gather(piece, ("tensor", "section"), axis=1, tiled=True)
        rows_part = lax.dynamic_slice_in_dim(whole, row_start, row_block, 1)
        cols_part = lax.dynamic_slice_in_dim(whole, col_start, col_block, 1)
        return (carry, (rows_part, cols_part))

    unused_carry, (row_parts, col_parts) = lax.scan(collect, jnp.int32(0), activations)
    partial_value = jnp.einsum(
        "mnr,mnc->mrc", row_parts, col_parts, preferred_element_type=jnp.float32
    )
    fresh = lax.psum_scatter(partial_value, "shard", scatter_dimension=0, tiled=True) / tokens_all
    row_index = lax.broadcasted_iota(jnp.int32, (row_block, col_block), 0) + row_start
    col_index = lax.broadcasted_iota(jnp.int32, (row_block, col_block), 1) + col_start
    eye_block = (row_index == col_index).astype(jnp.float32)
    matrix = factor_decay * old_factors + (1.0 - factor_decay) * fresh + damping * eye_block
    diag_part = jnp.sum(matrix * eye_block, axis=(1, 2))
    trace = lax.psum(diag_part, ("tensor", "section"))
    factor_scale = (D / (3.0 * trace))[:, None, None]
    matrix_low = lax.optimization_barrier(matrix.astype(jnp.bfloat16))
    first = 2.0 * factor_scale * eye_block - factor_scale * factor_scale * matrix_low.astype(
        jnp.float32
    )
    first_low = first.astype(jnp.bfloat16)
    first_cols = lax.all_gather(first_low, "tensor", axis=1, tiled=True)
    image = fold_with(first_cols, lax.all_gather(matrix_low, "section", axis=2, tiled=True))
    image_cols = lax.all_gather(image.astype(jnp.bfloat16), "tensor", axis=1, tiled=True)
    product = fold_with(image_cols, lax.all_gather(first_low, "section", axis=2, tiled=True))
    inverse_low = (2.0 * first - product).astype(jnp.bfloat16)
    inverses = lax.all_gather(inverse_low, "shard", axis=0, tiled=True)
    left_terms = jnp.stack(
        [
            jnp.einsum("nc,rc->nr", col_parts[m], inverses[m], preferred_element_type=jnp.float32)
            for m in (0, 4, 6)
        ]
    )
    left = lax.psum(left_terms, "section").astype(jnp.bfloat16)
    right_terms = jnp.stack(
        [
            jnp.einsum("nr,rc->nc", row_parts[m], inverses[m], preferred_element_type=jnp.float32)
            for m in (1, 2, 3, 5, 7)
        ]
    )
    right = lax.psum(right_terms, "tensor").astype(jnp.bfloat16)
    norm_values = norm_terms.astype(jnp.float32)
    router_part = jnp.einsum(
        "en,fn->ef", router_grad, router_grad, preferred_element_type=jnp.float32
    )
    router_sum, norm_total, norm_squares = lax.psum(
        (router_part, jnp.sum(norm_values, axis=1), jnp.sum(norm_values * norm_values, axis=1)),
        "shard",
    )
    router_matrix = (
        factor_decay * old_router_factor
        + (1.0 - factor_decay) * (router_sum / tokens_all)
        + damping * jnp.eye(EXPERTS, dtype=jnp.float32)
    )
    router_inverse = local_inverse(router_matrix)
    router_right = jnp.einsum(
        "en,ef->nf", router_grad, router_inverse, preferred_element_type=jnp.float32
    ).astype(jnp.bfloat16)
    precond_norms = (
        learning_rate
        * norm_total
        / (
            factor_decay * old_norm_diag
            + (1.0 - factor_decay) * (norm_squares / tokens_all)
            + damping
        )
    )
    ids_all = lax.all_gather(token_ids, "shard", axis=0, tiled=True)
    embed_all = lax.all_gather(right[4], "shard", axis=0, tiled=True)
    paired_left = jnp.stack([left[0], left[0], left[0], left[1]])
    attn_terms = jnp.einsum(
        "wnr,wnc->wrc", paired_left, right[:4], preferred_element_type=jnp.float32
    )
    router_term = jnp.einsum("nf,nr->fr", router_right, left[2], preferred_element_type=jnp.float32)
    attn_sum, router_total = lax.psum((attn_terms, router_term), "shard")
    precond_attn = learning_rate * attn_sum
    precond_router = learning_rate * router_total
    vocab_block = VOCAB // n_tensor
    step_rows = math.gcd(vocab_block, 512)
    vocab_start = tensor_rank * vocab_block

    def embed_block(block_index):
        ids_here = vocab_start + block_index * step_rows + lax.iota(jnp.int32, step_rows)
        onehot = (ids_here[:, None] == ids_all[None, :]).astype(jnp.bfloat16)
        summed = jnp.dot(onehot, embed_all, preferred_element_type=jnp.float32)
        tallies = jnp.sum(onehot, axis=1, dtype=jnp.float32)
        return (summed, tallies)

    block_sums, block_counts = lax.map(
        embed_block, jnp.arange(vocab_block // step_rows, dtype=jnp.int32)
    )
    embed_sum = block_sums.reshape(vocab_block, col_block)
    counts = block_counts.reshape(vocab_block)
    divisor = factor_decay * old_embed_diag + (1.0 - factor_decay) * (counts / tokens_all) + damping
    precond_embed = learning_rate * embed_sum / divisor[:, None]
    return (precond_attn, precond_router, precond_norms, precond_embed)


def split_three(values):
    high = lax.reduce_precision(values, 8, 7)
    rest = values - high
    middle = lax.reduce_precision(rest, 8, 7)
    return jnp.stack([high, middle, rest - middle], axis=-2).astype(jnp.bfloat16)


def swap(value, axis, size, step):
    return lax.ppermute(value, axis, [(i, i ^ step) for i in range(size)])


def local_diagonals(blocks):
    width = blocks.shape[1]
    pieces = []
    for start in range(0, width, 128):
        size = min(128, width - start)
        tile = blocks[:, start : start + size, start : start + size]
        pieces.append(jnp.sum(tile * jnp.eye(size, dtype=tile.dtype), axis=1))
    return jnp.concatenate(pieces, axis=1)


def rounded(values):
    return values.astype(jnp.bfloat16).astype(jnp.float32)


def params():
    return pltpu.CompilerParams(vmem_limit_bytes=40 * 1024 * 1024)


def layout_kernel(place_ref, gathered, features, rows, low_diag, trace, old, *, weight):
    own_place, layer, core = place_ref[0], place_ref[1], place_ref[2]
    sections, steps, _, tokens = gathered.shape
    groups, depth, _ = features.shape
    part = depth // (sections * steps)
    width = depth // steps
    for section in range(sections):
        codes = jnp.zeros((16, tokens), jnp.float32)
        for step in range(steps):
            start = (step * sections + section) * part
            for group in range(groups):
                features[group, start : start + part] = gathered[
                    section, step, group * part : (group + 1) * part
                ]
            codes += gathered[section, step, groups * part :].astype(jnp.float32)
        codes = codes[0:3] + codes[3:6] + codes[6:9]
        pieces = [codes[0:1], codes[1:2], codes[2:3, : width - 2 * tokens]]
        old[section ^ layer] = jnp.concatenate(pieces, axis=1)
    ones = jnp.ones((8, tokens), jnp.bfloat16)
    total = jnp.float32(0.0)
    for step in range(steps):
        squares = jnp.zeros((8, width), jnp.float32)
        for group in range(groups):
            values = features[group, step * width : (step + 1) * width].astype(jnp.float32)
            values = values * values
            high = values.astype(jnp.bfloat16)
            low = (values - high.astype(jnp.float32)).astype(jnp.bfloat16)
            for piece in (high, low):
                squares += lax.dot_general(
                    ones, piece, (((1,), (1,)), ((), ())), preferred_element_type=jnp.float32
                )
        diag = factor_decay * old[step] + weight * squares[0:1] + damping
        total += jnp.sum(diag)
        low_diag[step] = rounded(diag)
        start = pl.multiple_of((own_place ^ step) * width, width)
        mine = features[core, pl.ds(start, width)]
        rows[:, step * width : (step + 1) * width] = mine.T
    trace[0] = total


def lay_out(places, gathered, weight):
    sections, steps, height, tokens = gathered.shape
    part = (height - 16) // 2
    depth = sections * steps * part
    width = depth // steps
    vmem = pl.BlockSpec(memory_space=pltpu.VMEM)
    smem = pl.BlockSpec(memory_space=pltpu.SMEM)
    return pl.pallas_call(
        functools.partial(layout_kernel, weight=weight),
        in_specs=[smem, vmem],
        out_specs=[vmem, vmem, vmem, smem],
        out_shape=[
            jax.ShapeDtypeStruct((2, depth, tokens), jnp.bfloat16),
            jax.ShapeDtypeStruct((tokens, depth), jnp.bfloat16),
            jax.ShapeDtypeStruct((steps, 1, width), jnp.float32),
            jax.ShapeDtypeStruct((1,), jnp.float32),
        ],
        scratch_shapes=[pltpu.VMEM((steps, 1, width), jnp.float32)],
        compiler_params=params(),
        cost_estimate=pl.CostEstimate(
            flops=64 * depth * tokens, bytes_accessed=14 * depth * tokens, transcendentals=0
        ),
    )(places, gathered)


def factor_kernel(place_ref, part, own, old, diag, out, *, step, weight):
    fresh = jnp.zeros(out.shape, jnp.float32)
    for index in range(part.shape[0]):
        fresh += lax.dot_general(
            part[index], own[index], (((1,), (1,)), ((), ())), preferred_element_type=jnp.float32
        )
    block = factor_decay * old[...].astype(jnp.float32) + weight * fresh
    on_diag = lax.broadcasted_iota(jnp.int32, out.shape, 0) == lax.broadcasted_iota(
        jnp.int32, out.shape, 1
    )
    block = jnp.where(on_diag & (place_ref[0] == step), diag[0], block)
    out[...] = block.astype(jnp.bfloat16)


def factor_block(place, features, old, diag, step, weight):
    groups, _, tokens = features.shape
    rows, cols = old.shape
    return pl.pallas_call(
        functools.partial(factor_kernel, step=step, weight=weight),
        grid_spec=pltpu.PrefetchScalarGridSpec(
            num_scalar_prefetch=1,
            grid=(1,),
            in_specs=[
                pl.BlockSpec((groups, rows, tokens), lambda i, place: (0, step, 0)),
                pl.BlockSpec((groups, cols, tokens), lambda i, place: (0, place[0], 0)),
                pl.BlockSpec((rows, cols), lambda i, place: (0, 0)),
                pl.BlockSpec((1, 1, cols), lambda i, place: (place[0], 0, 0)),
            ],
            out_specs=pl.BlockSpec((rows, cols), lambda i, place: (0, 0)),
        ),
        out_shape=jax.ShapeDtypeStruct((rows, cols), jnp.bfloat16),
        compiler_params=params(),
        cost_estimate=pl.CostEstimate(
            flops=2 * groups * rows * cols * tokens,
            bytes_accessed=4 * rows * cols + 4 * groups * rows * tokens,
            transcendentals=0,
        ),
    )(place, features, features, old, diag)


def fetch_blocks(place_ref, blocks, held, sems):
    count = len(blocks) // 2
    depth = blocks[0].shape[0]
    copies = []
    for index in range(2 * count):
        slot = pl.multiple_of((place_ref[0] ^ (index % count)) * depth, depth)
        copies.append(
            pltpu.make_async_copy(
                blocks[index], held.at[index // count, pl.ds(slot, depth)], sems.at[index]
            )
        )
    for copy in copies:
        copy.start()
    return copies


def block_products(rows, copies, held):
    count = len(copies) // 2
    products = []
    for index in range(2):
        for copy in copies[index * count : (index + 1) * count]:
            copy.wait()
        products.append(jnp.dot(rows, held[index], preferred_element_type=jnp.float32))
    return products


def first_parts(place_ref, scale, rows, diag, product, index):
    width = product.shape[1]
    square = scale * scale
    values = rows[:, index * width : (index + 1) * width].astype(jnp.float32)
    low_diag = diag[place_ref[0] ^ index]
    first_diag = rounded(2.0 * scale - square * low_diag)
    by_first = 2.0 * scale * values - square * product
    step_one = first_diag * values - square * (product - low_diag * values)
    return by_first, step_one, low_diag, first_diag


def first_kernel(place_ref, scale_ref, rows, diag, *refs):
    blocks, (kept, message), (held, sems) = refs[:8], refs[8:10], refs[10:]
    copies = fetch_blocks(place_ref, blocks, held, sems)
    products = block_products(rows[...], copies, held)
    lows = []
    for index in range(2):
        kept[index] = products[index]
        parts = first_parts(place_ref, scale_ref[0], rows, diag, products[index], index)
        lows.append(parts[1].astype(jnp.bfloat16))
    message[...] = jnp.concatenate(lows, axis=1)


def second_kernel(place_ref, scale_ref, mine, theirs, rows, diag, before, *refs):
    blocks, (kept, message), (held, sems) = refs[:8], refs[8:10], refs[10:]
    copies = fetch_blocks(place_ref, blocks, held, sems)
    both = jnp.concatenate([mine[...], theirs[...]], axis=1)
    products = block_products(both, copies, held)
    square = scale_ref[0] * scale_ref[0]
    lows = []
    for index in range(2):
        by_first, one, low_diag, first_diag = first_parts(
            place_ref, scale_ref[0], rows, diag, before[index], index
        )
        two = products[index] + low_diag * (one - rounded(one))
        low = two.astype(jnp.bfloat16)
        kept[index] = (
            2.0 * by_first - first_diag * two - square * low_diag * low.astype(jnp.float32)
        )
        lows.append(low)
    message[...] = jnp.concatenate(lows, axis=1)


def third_kernel(place_ref, scale_ref, mine, theirs, before, *refs):
    blocks, (keep, give), (held, sems) = refs[:8], refs[8:10], refs[10:]
    copies = fetch_blocks(place_ref, blocks, held, sems)
    both = jnp.concatenate([mine[...], theirs[...]], axis=1)
    products = block_products(both, copies, held)
    square = scale_ref[0] * scale_ref[0]
    for index, out in ((0, keep), (1, give)):
        out[...] = (before[index] + square * products[index]).T.astype(jnp.bfloat16)


def chain_call(kernel, scalars, arrays, blocks, out_shape):
    depth, width = blocks[0].shape
    count = len(blocks) // 2
    tokens = arrays[0].shape[0]
    vmem = pl.BlockSpec(memory_space=pltpu.VMEM)
    return pl.pallas_call(
        kernel,
        in_specs=[pl.BlockSpec(memory_space=pltpu.SMEM)] * len(scalars)
        + [vmem] * len(arrays)
        + [pl.BlockSpec(memory_space=pl.ANY)] * len(blocks),
        out_specs=[vmem] * len(out_shape),
        out_shape=out_shape,
        scratch_shapes=[
            pltpu.VMEM((2, count * depth, width), jnp.bfloat16),
            pltpu.SemaphoreType.DMA((len(blocks),)),
        ],
        compiler_params=params(),
        cost_estimate=pl.CostEstimate(
            flops=2 * len(blocks) * tokens * depth * width,
            bytes_accessed=2 * len(blocks) * depth * width,
            transcendentals=0,
        ),
    )(*scalars, *arrays, *blocks)


def output_kernel(where_ref, left, matches, scale, *refs):
    mine, others = refs[:4], refs[4:8]
    attn, embed, held, sems = refs[8:]
    shard, layer, step = where_ref[0], where_ref[1], pl.program_id(0)
    first = shard == 0

    @pl.when(step == 0)
    def _():
        for slot, source in enumerate((0, 1, 3, 0, 3)):
            from_mine = first if slot < 3 else jnp.logical_not(first)
            for place in range(4):
                for group, wanted in ((mine, from_mine), (others, jnp.logical_not(from_mine))):

                    @pl.when(wanted & ((layer ^ source) == place))
                    def _():
                        pltpu.make_async_copy(group[place], held.at[slot], sems.at[slot]).start()

    def arrived(slot):
        pltpu.make_async_copy(mine[0], held.at[slot], sems.at[slot]).wait()

    for slot in range(4):

        @pl.when(step == slot)
        def _():
            arrived(slot)
            attn[0] = learning_rate * lax.dot_general(
                left[...], held[slot], (((1,), (1,)), ((), ())), preferred_element_type=jnp.float32
            )

    @pl.when(step == 4)
    def _():
        arrived(4)

    @pl.when(step >= 4)
    def _():
        product = jnp.dot(held[4], matches[...], preferred_element_type=jnp.float32)
        embed[...] = product * scale[...]


def output_products(where, bundle, matches, scale, mine, others):
    cols, tokens_all = mine[0].shape
    vocab_block = scale.shape[1]
    parts = 4
    part = vocab_block // parts

    def embed_place(step, where):
        return (0, jnp.maximum(step - 4, 0))

    def left_place(step, where):
        return (jnp.where(step < 3, where[0], 1 - where[0]), 0)

    return pl.pallas_call(
        output_kernel,
        grid_spec=pltpu.PrefetchScalarGridSpec(
            num_scalar_prefetch=1,
            grid=(4 + parts,),
            in_specs=[
                pl.BlockSpec((cols, tokens_all), left_place),
                pl.BlockSpec((tokens_all, part), embed_place),
                pl.BlockSpec((1, part), embed_place),
            ]
            + [pl.BlockSpec(memory_space=pl.ANY)] * 8,
            out_specs=(
                pl.BlockSpec((1, cols, cols), lambda step, where: (jnp.minimum(step, 3), 0, 0)),
                pl.BlockSpec((cols, part), embed_place),
            ),
            scratch_shapes=[
                pltpu.VMEM((5, cols, tokens_all), jnp.bfloat16),
                pltpu.SemaphoreType.DMA((5,)),
            ],
        ),
        out_shape=(
            jax.ShapeDtypeStruct((4, cols, cols), jnp.float32),
            jax.ShapeDtypeStruct((cols, vocab_block), jnp.float32),
        ),
        compiler_params=params(),
        cost_estimate=pl.CostEstimate(
            flops=2 * cols * tokens_all * (4 * cols + vocab_block),
            bytes_accessed=4 * cols * (4 * cols + vocab_block) + 14 * cols * tokens_all,
            transcendentals=0,
        ),
    )(where, bundle, matches, scale, *mine, *others)


def layer_plan(
    activations,
    router_grad,
    token_ids,
    norm_terms,
    old_factors,
    old_router_factor,
    old_norm_diag,
    old_embed_diag,
):
    n_tensor = lax.axis_size("tensor")
    n_section = lax.axis_size("section")
    n_shard = lax.axis_size("shard")
    shard = lax.axis_index("shard")
    layer = lax.axis_index("tensor")
    section = lax.axis_index("section")
    core = section % 2
    owned, row_block, col_block = old_factors.shape
    tokens = activations.shape[1]
    features_dev = activations.shape[2]
    tokens_all = tokens * n_shard
    weight = (1.0 - factor_decay) / tokens_all
    own_place = section ^ layer
    place = own_place.reshape(1)
    axes = ("shard", "tensor")

    def by_index(array, index, axis=0):
        return lax.dynamic_index_in_dim(array, index, axis, False)

    def held_by(layer_index):
        return jnp.where(layer_index == 3, 3, lax.rem(layer_index + 1, 3))

    by_feature = jnp.swapaxes(activations, 1, 2)
    diagonals = local_diagonals(old_factors) * (layer == section).astype(jnp.float32)
    extra = jnp.pad(split_three(diagonals), ((0, 0), (0, 0), (0, 3 * tokens - col_block)))
    extra = jnp.pad(extra.reshape(owned, 9, tokens), ((0, 0), (0, 7), (0, 0)))
    collected = []
    for step in range(n_tensor):
        factor = held_by(layer ^ step)
        message = jnp.concatenate(
            [
                by_index(by_feature, shard * owned + factor),
                by_index(by_feature, (1 - shard) * owned + factor),
                by_index(extra, factor),
            ],
            axis=0,
        )
        collected.append(swap(message, "tensor", n_tensor, step) if step else message)
    collected = jnp.stack(collected)
    other_tokens = swap(
        collected[:, features_dev : 2 * features_dev], "shard", n_shard, 1
    )

    part_rows = row_block // 2

    def old_block(factors, step, start, size):
        away = by_index(factors, held_by(layer ^ step))[start : start + size]
        return away.astype(jnp.bfloat16)

    early = swap(old_block(old_factors, 2, 0, part_rows), "tensor", n_tensor, 2)
    later_factors = lax.optimization_barrier(old_factors)
    late = old_block(later_factors, 2, part_rows, part_rows)
    blocks = [old_block(later_factors, step, 0, row_block) for step in (0, 1, 3)]
    other_tokens, collected, early, late, blocks = lax.optimization_barrier(
        (other_tokens, collected, early, late, blocks)
    )
    collected = jnp.concatenate(
        [collected[:, :features_dev], other_tokens, collected[:, 2 * features_dev :]], axis=1
    )
    gathered = lax.all_gather(collected, "section", axis=0)
    late = swap(late, "tensor", n_tensor, 2)
    blocks = [
        blocks[0],
        swap(blocks[1], "tensor", n_tensor, 1),
        jnp.concatenate([early, late], axis=0),
        swap(blocks[2], "tensor", n_tensor, 3),
    ]

    def both_shards(value, axis):
        other = swap(value, "shard", n_shard, 1)
        return jnp.where(
            shard == 0,
            jnp.concatenate([value, other], axis=axis),
            jnp.concatenate([other, value], axis=axis),
        )

    grad_all = both_shards(router_grad, 1)
    ids_all = both_shards(token_ids, 0)
    norm_values = norm_terms.astype(jnp.float32)
    norm_sums = jnp.stack([jnp.sum(norm_values, axis=1), jnp.sum(norm_values * norm_values, axis=1)])
    norm_sums = norm_sums + swap(norm_sums, "shard", n_shard, 1)
    vocab_block = old_embed_diag.shape[0]
    ids_here = layer * vocab_block + lax.iota(jnp.int32, vocab_block)
    matches = (ids_all[:, None] == ids_here[None, :]).astype(jnp.bfloat16)
    counts = jnp.sum(matches, axis=0, dtype=jnp.float32)
    divisor = factor_decay * old_embed_diag + (1.0 - factor_decay) * (counts / tokens_all) + damping
    embed_scale = (learning_rate / divisor)[None, :]
    gathered, grad_all, matches, embed_scale, norm_sums = lax.optimization_barrier(
        (gathered, grad_all, matches, embed_scale, norm_sums)
    )

    features, rows, low_diag, trace = lay_out(
        jnp.stack([own_place, layer, core]), gathered, weight
    )
    scale = D / (3.0 * trace)

    own_cols = [
        factor_block(place, features, blocks[step], low_diag, step, weight)
        for step in range(n_tensor)
    ]
    other_cols = [swap(block, "section", n_section, 1) for block in own_cols]
    cols = own_cols + other_cols

    wide = jax.ShapeDtypeStruct((2, tokens, col_block), jnp.float32)
    sent = jax.ShapeDtypeStruct((tokens, 2 * col_block), jnp.bfloat16)
    part = jax.ShapeDtypeStruct((col_block, tokens), jnp.bfloat16)
    scalars = (place, scale)
    kept, message = chain_call(first_kernel, scalars, (rows, low_diag), cols, (wide, sent))
    theirs = swap(message, "section", n_section, 2)
    kept, message = chain_call(
        second_kernel, scalars, (message, theirs, rows, low_diag, kept), cols, (wide, sent)
    )
    theirs = swap(message, "section", n_section, 2)
    keep, give = chain_call(third_kernel, scalars, (message, theirs, kept), cols, (part, part))
    got = swap(give, "section", n_section, 1)
    own = jnp.where(
        core == shard, jnp.concatenate([keep, got], axis=1), jnp.concatenate([got, keep], axis=1)
    )

    planes = range(n_shard)
    layers = range(n_tensor)

    def useful(x, z):
        return z != 2 and (x, z) != (1, 1)

    def send(value, step, held):
        moves = [
            (x * n_tensor + z, x * n_tensor + (z ^ step))
            for x in planes
            for z in layers
            if useful(x, z ^ held)
        ]
        return lax.ppermute(value, axes, moves)

    def across(value, held):
        moves = [
            (x * n_tensor + z, (1 - x) * n_tensor + z)
            for x in planes
            for z in layers
            if useful(x, z ^ held)
        ]
        return lax.ppermute(value, axes, moves)

    everywhere = ("shard", "tensor", "section")

    def spot(x, z, s):
        return (x * n_tensor + z) * n_section + s

    def scatter(value, source):
        moved_here = lax.ppermute(
            value,
            everywhere,
            [(spot(x, source, s), spot(x, s, s)) for x in planes for s in layers if s != source],
        )
        return jnp.where(layer == source, value, moved_here)

    router_matrix = (
        factor_decay * old_router_factor
        + weight * jnp.einsum("en,fn->ef", grad_all, grad_all, preferred_element_type=jnp.float32)
        + damping * jnp.eye(EXPERTS, dtype=jnp.float32)
    )
    router_inverse = local_inverse(router_matrix)
    router_right = jnp.einsum(
        "en,ef->fn", grad_all, router_inverse, preferred_element_type=jnp.float32
    ).astype(jnp.bfloat16)

    near_1 = send(own, 1, 0)
    near_2 = send(own, 2, 0)
    over_0 = across(own, 0)
    left_here = scatter(own, 2)
    router_cols = learning_rate * jnp.einsum(
        "fn,cn->fc", router_right, own, preferred_element_type=jnp.float32
    )
    router_cols = scatter(router_cols, 1)
    router_high = lax.reduce_precision(router_cols, 8, 7)
    codes = jnp.concatenate([router_high, router_cols - router_high], axis=0).astype(jnp.bfloat16)
    codes_tail = jnp.pad(codes[:, tokens_all:], ((0, 0), (0, 2 * tokens_all - col_block)))
    codes = jnp.concatenate([codes[:, :tokens_all], codes_tail], axis=0)
    near_1, over_0 = lax.optimization_barrier((near_1, over_0))
    over_1 = across(near_1, 1)
    left_here, near_2, codes, over_1 = lax.optimization_barrier(
        (left_here, near_2, codes, over_1)
    )
    left_there = lax.ppermute(
        jnp.concatenate([left_here, codes], axis=0),
        everywhere,
        [(spot(x, t, t), spot(1 - x, t, t)) for x in planes for t in layers],
    )
    near_3 = send(near_2, 1, 2)
    over_2 = across(near_2, 2)
    codes = jnp.where(shard == 1, codes, left_there[col_block:])
    bundle = jnp.concatenate([left_here, left_there[:col_block], codes], axis=0)
    bundle, near_3 = lax.optimization_barrier((bundle, near_3))
    to_side = [(spot(x, t, t), spot(x, t, t ^ 2)) for x in planes for t in layers]
    bundle = jnp.where(section == layer, bundle, lax.ppermute(bundle, everywhere, to_side))
    over_3 = across(near_3, 3)
    bundle, over_2, over_3 = lax.optimization_barrier((bundle, over_2, over_3))
    to_core = [
        (spot(x, t, t ^ a), spot(x, t, t ^ a ^ 1)) for x in planes for t in layers for a in (0, 2)
    ]
    bundle = jnp.where(
        (section ^ layer) % 2 == 0, bundle, lax.ppermute(bundle, everywhere, to_core)
    )
    codes = bundle[2 * col_block :]
    codes = jnp.concatenate(
        [codes[: 2 * EXPERTS], codes[2 * EXPERTS :, : col_block - tokens_all]], axis=1
    ).astype(jnp.float32)
    precond_router = codes[:EXPERTS] + codes[EXPERTS:]

    precond_attn, embed_columns = output_products(
        jnp.stack([shard, layer]),
        bundle,
        matches,
        embed_scale,
        (own, near_1, near_2, near_3),
        (over_0, over_1, over_2, over_3),
    )
    precond_embed = embed_columns.T

    precond_norms = (
        learning_rate
        * norm_sums[0]
        / (
            factor_decay * old_norm_diag
            + (1.0 - factor_decay) * (norm_sums[1] / tokens_all)
            + damping
        )
    )
    return (precond_attn, precond_router, precond_norms, precond_embed)


def per_device(*arguments):
    one_each = arguments[4].shape[0] == lax.axis_size("tensor") == lax.axis_size("section")
    if one_each and lax.axis_size("section") == 4 and lax.axis_size("shard") == 2:
        return layer_plan(*arguments)
    return general_plan(*arguments)


def solution(mesh):
    return jax.shard_map(
        per_device,
        mesh=mesh,
        in_specs=(
            P(None, "shard", ("tensor", "section")),
            P(None, "shard"),
            P("shard"),
            P(None, "shard", ("tensor", "section")),
            P("shard", "tensor", "section"),
            P(),
            P(None, ("tensor", "section")),
            P("tensor"),
        ),
        out_specs=(
            P(None, "tensor", "section"),
            P(None, "tensor"),
            P(None, ("tensor", "section")),
            P("tensor", "section"),
        ),
        check_vma=False,
    )
```

```python
import functools
import math

import jax
import jax.numpy as jnp
from jax import lax
from jax.experimental import pallas as pl
from jax.experimental.pallas import tpu as pltpu
from jax.sharding import PartitionSpec as P

D = 2304
EXPERTS = 8
VOCAB = 8192


factor_decay = 0.5
damping = 0.01
learning_rate = 0.05


def local_inverse(matrix):
    width = matrix.shape[0]
    trace = jnp.sum(jnp.diagonal(matrix))
    factor_scale = width / (3.0 * trace)
    identity = jnp.eye(width, dtype=jnp.float32)
    matrix_low = lax.optimization_barrier(matrix.astype(jnp.bfloat16))
    first = 2.0 * factor_scale * identity - factor_scale * factor_scale * matrix_low.astype(
        jnp.float32
    )
    first_low = first.astype(jnp.bfloat16)
    image = jnp.dot(matrix_low, first_low, preferred_element_type=jnp.float32).astype(jnp.bfloat16)
    product = jnp.dot(first_low, image, preferred_element_type=jnp.float32)
    return (2.0 * first - product).astype(jnp.bfloat16)


def fold_with(columns, piece):
    return jnp.einsum("kij,kjl->kil", piece, columns, preferred_element_type=jnp.float32)


def general_plan(
    activations,
    router_grad,
    token_ids,
    norm_terms,
    old_factors,
    old_router_factor,
    old_norm_diag,
    old_embed_diag,
):
    n_tensor = lax.axis_size("tensor")
    n_section = lax.axis_size("section")
    n_shard = lax.axis_size("shard")
    tensor_rank = lax.axis_index("tensor")
    section_rank = lax.axis_index("section")
    row_block = D // n_tensor
    col_block = D // n_section
    tokens_all = activations.shape[1] * n_shard
    row_start = tensor_rank * row_block
    col_start = section_rank * col_block

    def collect(carry, piece):
        whole = lax.all_gather(piece, ("tensor", "section"), axis=1, tiled=True)
        rows_part = lax.dynamic_slice_in_dim(whole, row_start, row_block, 1)
        cols_part = lax.dynamic_slice_in_dim(whole, col_start, col_block, 1)
        return (carry, (rows_part, cols_part))

    unused_carry, (row_parts, col_parts) = lax.scan(collect, jnp.int32(0), activations)
    partial_value = jnp.einsum(
        "mnr,mnc->mrc", row_parts, col_parts, preferred_element_type=jnp.float32
    )
    fresh = lax.psum_scatter(partial_value, "shard", scatter_dimension=0, tiled=True) / tokens_all
    row_index = lax.broadcasted_iota(jnp.int32, (row_block, col_block), 0) + row_start
    col_index = lax.broadcasted_iota(jnp.int32, (row_block, col_block), 1) + col_start
    eye_block = (row_index == col_index).astype(jnp.float32)
    matrix = factor_decay * old_factors + (1.0 - factor_decay) * fresh + damping * eye_block
    diag_part = jnp.sum(matrix * eye_block, axis=(1, 2))
    trace = lax.psum(diag_part, ("tensor", "section"))
    factor_scale = (D / (3.0 * trace))[:, None, None]
    matrix_low = lax.optimization_barrier(matrix.astype(jnp.bfloat16))
    first = 2.0 * factor_scale * eye_block - factor_scale * factor_scale * matrix_low.astype(
        jnp.float32
    )
    first_low = first.astype(jnp.bfloat16)
    first_cols = lax.all_gather(first_low, "tensor", axis=1, tiled=True)
    image = fold_with(first_cols, lax.all_gather(matrix_low, "section", axis=2, tiled=True))
    image_cols = lax.all_gather(image.astype(jnp.bfloat16), "tensor", axis=1, tiled=True)
    product = fold_with(image_cols, lax.all_gather(first_low, "section", axis=2, tiled=True))
    inverse_low = (2.0 * first - product).astype(jnp.bfloat16)
    inverses = lax.all_gather(inverse_low, "shard", axis=0, tiled=True)
    left_terms = jnp.stack(
        [
            jnp.einsum("nc,rc->nr", col_parts[m], inverses[m], preferred_element_type=jnp.float32)
            for m in (0, 4, 6)
        ]
    )
    left = lax.psum(left_terms, "section").astype(jnp.bfloat16)
    right_terms = jnp.stack(
        [
            jnp.einsum("nr,rc->nc", row_parts[m], inverses[m], preferred_element_type=jnp.float32)
            for m in (1, 2, 3, 5, 7)
        ]
    )
    right = lax.psum(right_terms, "tensor").astype(jnp.bfloat16)
    norm_values = norm_terms.astype(jnp.float32)
    router_part = jnp.einsum(
        "en,fn->ef", router_grad, router_grad, preferred_element_type=jnp.float32
    )
    router_sum, norm_total, norm_squares = lax.psum(
        (router_part, jnp.sum(norm_values, axis=1), jnp.sum(norm_values * norm_values, axis=1)),
        "shard",
    )
    router_matrix = (
        factor_decay * old_router_factor
        + (1.0 - factor_decay) * (router_sum / tokens_all)
        + damping * jnp.eye(EXPERTS, dtype=jnp.float32)
    )
    router_inverse = local_inverse(router_matrix)
    router_right = jnp.einsum(
        "en,ef->nf", router_grad, router_inverse, preferred_element_type=jnp.float32
    ).astype(jnp.bfloat16)
    precond_norms = (
        learning_rate
        * norm_total
        / (
            factor_decay * old_norm_diag
            + (1.0 - factor_decay) * (norm_squares / tokens_all)
            + damping
        )
    )
    ids_all = lax.all_gather(token_ids, "shard", axis=0, tiled=True)
    embed_all = lax.all_gather(right[4], "shard", axis=0, tiled=True)
    paired_left = jnp.stack([left[0], left[0], left[0], left[1]])
    attn_terms = jnp.einsum(
        "wnr,wnc->wrc", paired_left, right[:4], preferred_element_type=jnp.float32
    )
    router_term = jnp.einsum("nf,nr->fr", router_right, left[2], preferred_element_type=jnp.float32)
    attn_sum, router_total = lax.psum((attn_terms, router_term), "shard")
    precond_attn = learning_rate * attn_sum
    precond_router = learning_rate * router_total
    vocab_block = VOCAB // n_tensor
    step_rows = math.gcd(vocab_block, 512)
    vocab_start = tensor_rank * vocab_block

    def embed_block(block_index):
        ids_here = vocab_start + block_index * step_rows + lax.iota(jnp.int32, step_rows)
        onehot = (ids_here[:, None] == ids_all[None, :]).astype(jnp.bfloat16)
        summed = jnp.dot(onehot, embed_all, preferred_element_type=jnp.float32)
        tallies = jnp.sum(onehot, axis=1, dtype=jnp.float32)
        return (summed, tallies)

    block_sums, block_counts = lax.map(
        embed_block, jnp.arange(vocab_block // step_rows, dtype=jnp.int32)
    )
    embed_sum = block_sums.reshape(vocab_block, col_block)
    counts = block_counts.reshape(vocab_block)
    divisor = factor_decay * old_embed_diag + (1.0 - factor_decay) * (counts / tokens_all) + damping
    precond_embed = learning_rate * embed_sum / divisor[:, None]
    return (precond_attn, precond_router, precond_norms, precond_embed)


def split_three(values):
    high = lax.reduce_precision(values, 8, 7)
    rest = values - high
    middle = lax.reduce_precision(rest, 8, 7)
    return jnp.stack([high, middle, rest - middle], axis=-2).astype(jnp.bfloat16)


def swap(value, axis, size, step):
    return lax.ppermute(value, axis, [(i, i ^ step) for i in range(size)])


def local_diagonals(blocks):
    width = blocks.shape[1]
    pieces = []
    for start in range(0, width, 128):
        size = min(128, width - start)
        tile = blocks[:, start : start + size, start : start + size]
        pieces.append(jnp.sum(tile * jnp.eye(size, dtype=tile.dtype), axis=1))
    return jnp.concatenate(pieces, axis=1)


def rounded(values):
    return values.astype(jnp.bfloat16).astype(jnp.float32)


def params():
    return pltpu.CompilerParams(vmem_limit_bytes=40 * 1024 * 1024)


def layout_kernel(place_ref, gathered, features, rows, low_diag, trace, old, *, weight):
    own_place, layer, core = place_ref[0], place_ref[1], place_ref[2]
    sections, steps, _, tokens = gathered.shape
    groups, depth, _ = features.shape
    part = depth // (sections * steps)
    width = depth // steps
    for section in range(sections):
        codes = jnp.zeros((16, tokens), jnp.float32)
        for step in range(steps):
            start = (step * sections + section) * part
            for group in range(groups):
                features[group, start : start + part] = gathered[
                    section, step, group * part : (group + 1) * part
                ]
            codes += gathered[section, step, groups * part :].astype(jnp.float32)
        codes = codes[0:3] + codes[3:6] + codes[6:9]
        pieces = [codes[0:1], codes[1:2], codes[2:3, : width - 2 * tokens]]
        old[section ^ layer] = jnp.concatenate(pieces, axis=1)
    ones = jnp.ones((8, tokens), jnp.bfloat16)
    total = jnp.float32(0.0)
    for step in range(steps):
        squares = jnp.zeros((8, width), jnp.float32)
        for group in range(groups):
            values = features[group, step * width : (step + 1) * width].astype(jnp.float32)
            values = values * values
            high = values.astype(jnp.bfloat16)
            low = (values - high.astype(jnp.float32)).astype(jnp.bfloat16)
            for piece in (high, low):
                squares += lax.dot_general(
                    ones, piece, (((1,), (1,)), ((), ())), preferred_element_type=jnp.float32
                )
        diag = factor_decay * old[step] + weight * squares[0:1] + damping
        total += jnp.sum(diag)
        low_diag[step] = rounded(diag)
        start = pl.multiple_of((own_place ^ step) * width, width)
        mine = features[core, pl.ds(start, width)]
        rows[:, step * width : (step + 1) * width] = mine.T
    trace[0] = total


def lay_out(places, gathered, weight):
    sections, steps, height, tokens = gathered.shape
    part = (height - 16) // 2
    depth = sections * steps * part
    width = depth // steps
    vmem = pl.BlockSpec(memory_space=pltpu.VMEM)
    smem = pl.BlockSpec(memory_space=pltpu.SMEM)
    return pl.pallas_call(
        functools.partial(layout_kernel, weight=weight),
        in_specs=[smem, vmem],
        out_specs=[vmem, vmem, vmem, smem],
        out_shape=[
            jax.ShapeDtypeStruct((2, depth, tokens), jnp.bfloat16),
            jax.ShapeDtypeStruct((tokens, depth), jnp.bfloat16),
            jax.ShapeDtypeStruct((steps, 1, width), jnp.float32),
            jax.ShapeDtypeStruct((1,), jnp.float32),
        ],
        scratch_shapes=[pltpu.VMEM((steps, 1, width), jnp.float32)],
        compiler_params=params(),
        cost_estimate=pl.CostEstimate(
            flops=64 * depth * tokens, bytes_accessed=14 * depth * tokens, transcendentals=0
        ),
    )(places, gathered)


def factor_kernel(place_ref, part, own, old, diag, out, *, step, weight):
    fresh = jnp.zeros(out.shape, jnp.float32)
    for index in range(part.shape[0]):
        fresh += lax.dot_general(
            part[index], own[index], (((1,), (1,)), ((), ())), preferred_element_type=jnp.float32
        )
    block = factor_decay * old[...].astype(jnp.float32) + weight * fresh
    on_diag = lax.broadcasted_iota(jnp.int32, out.shape, 0) == lax.broadcasted_iota(
        jnp.int32, out.shape, 1
    )
    block = jnp.where(on_diag & (place_ref[0] == step), diag[0], block)
    out[...] = block.astype(jnp.bfloat16)


def factor_block(place, features, old, diag, step, weight):
    groups, _, tokens = features.shape
    rows, cols = old.shape
    return pl.pallas_call(
        functools.partial(factor_kernel, step=step, weight=weight),
        grid_spec=pltpu.PrefetchScalarGridSpec(
            num_scalar_prefetch=1,
            grid=(1,),
            in_specs=[
                pl.BlockSpec((groups, rows, tokens), lambda i, place: (0, step, 0)),
                pl.BlockSpec((groups, cols, tokens), lambda i, place: (0, place[0], 0)),
                pl.BlockSpec((rows, cols), lambda i, place: (0, 0)),
                pl.BlockSpec((1, 1, cols), lambda i, place: (place[0], 0, 0)),
            ],
            out_specs=pl.BlockSpec((rows, cols), lambda i, place: (0, 0)),
        ),
        out_shape=jax.ShapeDtypeStruct((rows, cols), jnp.bfloat16),
        compiler_params=params(),
        cost_estimate=pl.CostEstimate(
            flops=2 * groups * rows * cols * tokens,
            bytes_accessed=4 * rows * cols + 4 * groups * rows * tokens,
            transcendentals=0,
        ),
    )(place, features, features, old, diag)


def fetch_blocks(place_ref, blocks, held, sems):
    count = len(blocks) // 2
    depth = blocks[0].shape[0]
    copies = []
    for index in range(2 * count):
        slot = pl.multiple_of((place_ref[0] ^ (index % count)) * depth, depth)
        copies.append(
            pltpu.make_async_copy(
                blocks[index], held.at[index // count, pl.ds(slot, depth)], sems.at[index]
            )
        )
    for copy in copies:
        copy.start()
    return copies


def block_products(rows, copies, held):
    count = len(copies) // 2
    products = []
    for index in range(2):
        for copy in copies[index * count : (index + 1) * count]:
            copy.wait()
        products.append(jnp.dot(rows, held[index], preferred_element_type=jnp.float32))
    return products


def first_parts(place_ref, scale, rows, diag, product, index):
    width = product.shape[1]
    square = scale * scale
    values = rows[:, index * width : (index + 1) * width].astype(jnp.float32)
    low_diag = diag[place_ref[0] ^ index]
    first_diag = rounded(2.0 * scale - square * low_diag)
    by_first = 2.0 * scale * values - square * product
    step_one = first_diag * values - square * (product - low_diag * values)
    return by_first, step_one, low_diag, first_diag


def first_kernel(place_ref, scale_ref, rows, diag, *refs):
    blocks, (kept, message), (held, sems) = refs[:8], refs[8:10], refs[10:]
    copies = fetch_blocks(place_ref, blocks, held, sems)
    products = block_products(rows[...], copies, held)
    lows = []
    for index in range(2):
        kept[index] = products[index]
        parts = first_parts(place_ref, scale_ref[0], rows, diag, products[index], index)
        lows.append(parts[1].astype(jnp.bfloat16))
    message[...] = jnp.concatenate(lows, axis=1)


def second_kernel(place_ref, scale_ref, mine, theirs, rows, diag, before, *refs):
    blocks, (kept, message), (held, sems) = refs[:8], refs[8:10], refs[10:]
    copies = fetch_blocks(place_ref, blocks, held, sems)
    both = jnp.concatenate([mine[...], theirs[...]], axis=1)
    products = block_products(both, copies, held)
    square = scale_ref[0] * scale_ref[0]
    lows = []
    for index in range(2):
        by_first, one, low_diag, first_diag = first_parts(
            place_ref, scale_ref[0], rows, diag, before[index], index
        )
        two = products[index] + low_diag * (one - rounded(one))
        low = two.astype(jnp.bfloat16)
        kept[index] = (
            2.0 * by_first - first_diag * two - square * low_diag * low.astype(jnp.float32)
        )
        lows.append(low)
    message[...] = jnp.concatenate(lows, axis=1)


def third_kernel(place_ref, scale_ref, mine, theirs, before, *refs):
    blocks, (keep, give), (held, sems) = refs[:8], refs[8:10], refs[10:]
    copies = fetch_blocks(place_ref, blocks, held, sems)
    both = jnp.concatenate([mine[...], theirs[...]], axis=1)
    products = block_products(both, copies, held)
    square = scale_ref[0] * scale_ref[0]
    for index, out in ((0, keep), (1, give)):
        out[...] = (before[index] + square * products[index]).T.astype(jnp.bfloat16)


def chain_call(kernel, scalars, arrays, blocks, out_shape):
    depth, width = blocks[0].shape
    count = len(blocks) // 2
    tokens = arrays[0].shape[0]
    vmem = pl.BlockSpec(memory_space=pltpu.VMEM)
    return pl.pallas_call(
        kernel,
        in_specs=[pl.BlockSpec(memory_space=pltpu.SMEM)] * len(scalars)
        + [vmem] * len(arrays)
        + [pl.BlockSpec(memory_space=pl.ANY)] * len(blocks),
        out_specs=[vmem] * len(out_shape),
        out_shape=out_shape,
        scratch_shapes=[
            pltpu.VMEM((2, count * depth, width), jnp.bfloat16),
            pltpu.SemaphoreType.DMA((len(blocks),)),
        ],
        compiler_params=params(),
        cost_estimate=pl.CostEstimate(
            flops=2 * len(blocks) * tokens * depth * width,
            bytes_accessed=2 * len(blocks) * depth * width,
            transcendentals=0,
        ),
    )(*scalars, *arrays, *blocks)


def output_kernel(where_ref, scale, matches, *refs):
    lefts, mine, others = (refs[:4], refs[4:8]), refs[8:12], refs[12:16]
    attn, embed = refs[16:18]
    left_held, held, found, attn_made, embed_made, sems, out_sems = refs[18:]
    shard, layer, turn = where_ref[0], where_ref[1], where_ref[2]
    first = shard == 0
    rows, tokens_all = held.shape[1:]

    found_copy = pltpu.make_async_copy(matches, found, sems.at[7])
    for slot in range(2):
        for group in range(2):
            for place in range(4):

                @pl.when((turn == place) & (((shard ^ slot) == group)))
                def _():
                    source = lefts[group][place].at[pl.ds(0, rows)]
                    pltpu.make_async_copy(source, left_held.at[slot], sems.at[5 + slot]).start()

        if slot == 0:
            for index, source in enumerate((0, 1, 3, 0, 3)):
                from_mine = first if index < 3 else jnp.logical_not(first)
                for place in range(4):
                    for group, wanted in ((mine, from_mine), (others, jnp.logical_not(from_mine))):

                        @pl.when(wanted & ((layer ^ source) == place))
                        def _():
                            pltpu.make_async_copy(
                                group[place], held.at[index], sems.at[index]
                            ).start()

            found_copy.start()

    def arrived(slot):
        target = held.at[slot] if slot < 5 else left_held.at[slot - 5]
        pltpu.make_async_copy(mine[0], target, sems.at[slot]).wait()

    results = []
    arrived(5)
    for slot in range(4):
        if slot == 3:
            arrived(6)
        arrived(slot)
        attn_made[slot] = learning_rate * lax.dot_general(
            left_held[slot // 3],
            held[slot],
            (((1,), (1,)), ((), ())),
            preferred_element_type=jnp.float32,
        )
        results.append(
            pltpu.make_async_copy(attn_made.at[slot], attn.at[slot], out_sems.at[slot])
        )
        results[-1].start()
    arrived(4)
    found_copy.wait()
    part = found.shape[1] // 4
    for index in range(4):
        cols = pl.ds(index * part, part)
        product = jnp.dot(held[4], found[:, cols], preferred_element_type=jnp.float32)
        embed_made[:, cols] = product * scale[:, cols]
        results.append(
            pltpu.make_async_copy(
                embed_made.at[:, cols], embed.at[:, cols], out_sems.at[4 + index]
            )
        )
        results[-1].start()
    for result in results:
        result.wait()


def output_products(where, scale, matches, lefts, mine, others):
    cols, tokens_all = mine[0].shape
    vocab_block = scale.shape[1]
    anywhere = pl.BlockSpec(memory_space=pl.ANY)
    return pl.pallas_call(
        output_kernel,
        in_specs=[
            pl.BlockSpec(memory_space=pltpu.SMEM),
            pl.BlockSpec(memory_space=pltpu.VMEM),
        ]
        + [anywhere] * 17,
        out_specs=(anywhere, anywhere),
        out_shape=(
            jax.ShapeDtypeStruct((4, cols, cols), jnp.float32),
            jax.ShapeDtypeStruct((cols, vocab_block), jnp.float32),
        ),
        scratch_shapes=[
            pltpu.VMEM((2, cols, tokens_all), jnp.bfloat16),
            pltpu.VMEM((5, cols, tokens_all), jnp.bfloat16),
            pltpu.VMEM((tokens_all, vocab_block), jnp.bfloat16),
            pltpu.VMEM((4, cols, cols), jnp.float32),
            pltpu.VMEM((cols, vocab_block), jnp.float32),
            pltpu.SemaphoreType.DMA((8,)),
            pltpu.SemaphoreType.DMA((8,)),
        ],
        compiler_params=params(),
        cost_estimate=pl.CostEstimate(
            flops=2 * cols * tokens_all * (4 * cols + vocab_block),
            bytes_accessed=4 * cols * (4 * cols + vocab_block) + 14 * cols * tokens_all,
            transcendentals=0,
        ),
    )(where, scale, matches, *lefts[0], *lefts[1], *mine, *others)


def layer_plan(
    activations,
    router_grad,
    token_ids,
    norm_terms,
    old_factors,
    old_router_factor,
    old_norm_diag,
    old_embed_diag,
):
    n_tensor = lax.axis_size("tensor")
    n_section = lax.axis_size("section")
    n_shard = lax.axis_size("shard")
    shard = lax.axis_index("shard")
    layer = lax.axis_index("tensor")
    section = lax.axis_index("section")
    core = section % 2
    owned, row_block, col_block = old_factors.shape
    tokens = activations.shape[1]
    features_dev = activations.shape[2]
    tokens_all = tokens * n_shard
    weight = (1.0 - factor_decay) / tokens_all
    own_place = section ^ layer
    place = own_place.reshape(1)
    axes = ("shard", "tensor")

    def by_index(array, index, axis=0):
        return lax.dynamic_index_in_dim(array, index, axis, False)

    def held_by(layer_index):
        return jnp.where(layer_index == 3, 3, lax.rem(layer_index + 1, 3))

    by_feature = jnp.swapaxes(activations, 1, 2)
    diagonals = local_diagonals(old_factors) * (layer == section).astype(jnp.float32)
    extra = jnp.pad(split_three(diagonals), ((0, 0), (0, 0), (0, 3 * tokens - col_block)))
    extra = jnp.pad(extra.reshape(owned, 9, tokens), ((0, 0), (0, 7), (0, 0)))
    collected = []
    for step in range(n_tensor):
        factor = held_by(layer ^ step)
        message = jnp.concatenate(
            [
                by_index(by_feature, shard * owned + factor),
                by_index(by_feature, (1 - shard) * owned + factor),
                by_index(extra, factor),
            ],
            axis=0,
        )
        collected.append(swap(message, "tensor", n_tensor, step) if step else message)
    collected = jnp.stack(collected)
    other_tokens = swap(
        collected[:, features_dev : 2 * features_dev], "shard", n_shard, 1
    )

    def both_shards(value, axis):
        other = swap(value, "shard", n_shard, 1)
        return jnp.where(
            shard == 0,
            jnp.concatenate([value, other], axis=axis),
            jnp.concatenate([other, value], axis=axis),
        )

    grad_all = both_shards(router_grad, 1)
    ids_all = both_shards(token_ids, 0)
    norm_values = norm_terms.astype(jnp.float32)
    norm_sums = jnp.stack([jnp.sum(norm_values, axis=1), jnp.sum(norm_values * norm_values, axis=1)])
    norm_sums = norm_sums + swap(norm_sums, "shard", n_shard, 1)
    vocab_block = old_embed_diag.shape[0]
    ids_here = layer * vocab_block + lax.iota(jnp.int32, vocab_block)
    matches = (ids_all[:, None] == ids_here[None, :]).astype(jnp.bfloat16)
    counts = jnp.sum(matches, axis=0, dtype=jnp.float32)
    divisor = factor_decay * old_embed_diag + (1.0 - factor_decay) * (counts / tokens_all) + damping
    embed_scale = (learning_rate / divisor)[None, :]
    router_matrix = (
        factor_decay * old_router_factor
        + weight * jnp.einsum("en,fn->ef", grad_all, grad_all, preferred_element_type=jnp.float32)
        + damping * jnp.eye(EXPERTS, dtype=jnp.float32)
    )
    router_inverse = local_inverse(router_matrix)
    router_right = jnp.einsum(
        "en,ef->fn", grad_all, router_inverse, preferred_element_type=jnp.float32
    ).astype(jnp.bfloat16)

    part_rows = row_block // 2

    def old_block(factors, step, start, size):
        away = by_index(factors, held_by(layer ^ step))[start : start + size]
        return away.astype(jnp.bfloat16)

    early = swap(old_block(old_factors, 2, 0, part_rows), "tensor", n_tensor, 2)
    later_factors = lax.optimization_barrier(old_factors)
    late = old_block(later_factors, 2, part_rows, part_rows)
    blocks = [old_block(later_factors, step, 0, row_block) for step in (0, 1, 3)]
    other_tokens, collected, early, late, blocks, small = lax.optimization_barrier(
        (other_tokens, collected, early, late, blocks, (router_right, matches, embed_scale, norm_sums))
    )
    router_right, matches, embed_scale, norm_sums = small
    collected = jnp.concatenate(
        [collected[:, :features_dev], other_tokens, collected[:, 2 * features_dev :]], axis=1
    )
    gathered = lax.all_gather(collected, "section", axis=0)
    late = swap(late, "tensor", n_tensor, 2)
    blocks = [
        blocks[0],
        swap(blocks[1], "tensor", n_tensor, 1),
        None,
        swap(blocks[2], "tensor", n_tensor, 3),
    ]

    features, rows, low_diag, trace = lay_out(
        jnp.stack([own_place, layer, core]), gathered, weight
    )
    scale = D / (3.0 * trace)
    early, features = lax.optimization_barrier((early, features))
    blocks[2] = jnp.concatenate([early, late], axis=0)

    own_cols = [
        factor_block(place, features, blocks[step], low_diag, step, weight)
        for step in range(n_tensor)
    ]
    other_cols = [swap(block, "section", n_section, 1) for block in own_cols]
    cols = own_cols + other_cols

    wide = jax.ShapeDtypeStruct((2, tokens, col_block), jnp.float32)
    sent = jax.ShapeDtypeStruct((tokens, 2 * col_block), jnp.bfloat16)
    part = jax.ShapeDtypeStruct((col_block, tokens), jnp.bfloat16)
    scalars = (place, scale)
    kept, message = chain_call(first_kernel, scalars, (rows, low_diag), cols, (wide, sent))
    theirs = swap(message, "section", n_section, 2)
    kept, message = chain_call(
        second_kernel, scalars, (message, theirs, rows, low_diag, kept), cols, (wide, sent)
    )
    theirs = swap(message, "section", n_section, 2)
    keep, give = chain_call(third_kernel, scalars, (message, theirs, kept), cols, (part, part))
    got = swap(give, "section", n_section, 1)
    own = jnp.where(
        core == shard, jnp.concatenate([keep, got], axis=1), jnp.concatenate([got, keep], axis=1)
    )

    planes = range(n_shard)
    layers = range(n_tensor)

    def useful(x, z):
        return z != 2 and (x, z) != (1, 1)

    def send(value, step, held):
        moves = [
            (x * n_tensor + z, x * n_tensor + (z ^ step))
            for x in planes
            for z in layers
            if useful(x, z ^ held)
        ]
        return lax.ppermute(value, axes, moves)

    def across(value, held):
        moves = [
            (x * n_tensor + z, (1 - x) * n_tensor + z)
            for x in planes
            for z in layers
            if useful(x, z ^ held)
        ]
        return lax.ppermute(value, axes, moves)

    everywhere = ("shard", "tensor", "section")

    def spot(x, z, s):
        return (x * n_tensor + z) * n_section + s

    def scatter(value, source):
        moved_here = lax.ppermute(
            value,
            everywhere,
            [(spot(x, source, s), spot(x, s, s)) for x in planes for s in layers if s != source],
        )
        return jnp.where(layer == source, value, moved_here)

    def hand_round(value, *ahead):
        sides = lax.ppermute(
            value, everywhere, [(spot(x, t, t), spot(x, t, t ^ 2)) for x in planes for t in layers]
        )
        sides, *ahead = lax.optimization_barrier((sides, *ahead))
        near = lax.ppermute(
            value, everywhere, [(spot(x, t, t), spot(x, t, t ^ 1)) for x in planes for t in layers]
        )
        far = lax.ppermute(
            sides,
            everywhere,
            [(spot(x, t, t ^ 2), spot(x, t, t ^ 3)) for x in planes for t in layers],
        )
        return (value, near, sides, far), *ahead

    near_1 = send(own, 1, 0)
    near_2 = send(own, 2, 0)
    over_0 = across(own, 0)
    left_here = scatter(own, 2)
    near_1, over_0, own = lax.optimization_barrier((near_1, over_0, own))
    over_1 = across(near_1, 1)
    router_cols = learning_rate * jnp.einsum(
        "fn,cn->fc", router_right, own, preferred_element_type=jnp.float32
    )
    router_cols = scatter(router_cols, 1)
    router_high = lax.reduce_precision(router_cols, 8, 7)
    codes = jnp.concatenate([router_high, router_cols - router_high], axis=0).astype(jnp.bfloat16)
    codes_tail = jnp.pad(codes[:, tokens_all:], ((0, 0), (0, 2 * tokens_all - col_block)))
    left_here = jnp.concatenate([left_here, codes[:, :tokens_all], codes_tail], axis=0)
    left_here, near_2, over_1 = lax.optimization_barrier((left_here, near_2, over_1))
    near_3 = send(near_2, 1, 2)
    over_2 = across(near_2, 2)
    left_there = lax.ppermute(
        left_here, everywhere, [(spot(x, t, t), spot(1 - x, t, t)) for x in planes for t in layers]
    )
    (lefts_here,) = hand_round(left_here)
    left_there, near_3, over_2 = lax.optimization_barrier((left_there, near_3, over_2))
    over_3 = across(near_3, 3)
    lefts_there, over_3 = hand_round(left_there, over_3)
    turn = section ^ layer

    def codes_of(group):
        parts = [part[col_block:] for part in group]
        chosen = parts[3]
        for index in (2, 1, 0):
            chosen = jnp.where(turn == index, parts[index], chosen)
        return chosen

    codes = jnp.where(shard == 1, codes_of(lefts_here), codes_of(lefts_there))
    codes = jnp.concatenate(
        [codes[: 2 * EXPERTS], codes[2 * EXPERTS :, : col_block - tokens_all]], axis=1
    ).astype(jnp.float32)
    precond_router = codes[:EXPERTS] + codes[EXPERTS:]

    precond_attn, embed_columns = output_products(
        jnp.stack([shard, layer, turn]),
        embed_scale,
        matches,
        (lefts_here, lefts_there),
        (own, near_1, near_2, near_3),
        (over_0, over_1, over_2, over_3),
    )
    precond_embed = embed_columns.T

    precond_norms = (
        learning_rate
        * norm_sums[0]
        / (
            factor_decay * old_norm_diag
            + (1.0 - factor_decay) * (norm_sums[1] / tokens_all)
            + damping
        )
    )
    return (precond_attn, precond_router, precond_norms, precond_embed)


def per_device(*arguments):
    one_each = arguments[4].shape[0] == lax.axis_size("tensor") == lax.axis_size("section")
    if one_each and lax.axis_size("section") == 4 and lax.axis_size("shard") == 2:
        return layer_plan(*arguments)
    return general_plan(*arguments)


def solution(mesh):
    return jax.shard_map(
        per_device,
        mesh=mesh,
        in_specs=(
            P(None, "shard", ("tensor", "section")),
            P(None, "shard"),
            P("shard"),
            P(None, "shard", ("tensor", "section")),
            P("shard", "tensor", "section"),
            P(),
            P(None, ("tensor", "section")),
            P("tensor"),
        ),
        out_specs=(
            P(None, "tensor", "section"),
            P(None, "tensor"),
            P(None, ("tensor", "section")),
            P("tensor", "section"),
        ),
        check_vma=False,
    )
```

```python
import functools
import math

import jax
import jax.numpy as jnp
from jax import lax
from jax.experimental import pallas as pl
from jax.experimental.pallas import tpu as pltpu
from jax.sharding import PartitionSpec as P

D = 2304
EXPERTS = 8
VOCAB = 8192


factor_decay = 0.5
damping = 0.01
learning_rate = 0.05


def local_inverse(matrix):
    width = matrix.shape[0]
    trace = jnp.sum(jnp.diagonal(matrix))
    factor_scale = width / (3.0 * trace)
    identity = jnp.eye(width, dtype=jnp.float32)
    matrix_low = lax.optimization_barrier(matrix.astype(jnp.bfloat16))
    first = 2.0 * factor_scale * identity - factor_scale * factor_scale * matrix_low.astype(
        jnp.float32
    )
    first_low = first.astype(jnp.bfloat16)
    image = jnp.dot(matrix_low, first_low, preferred_element_type=jnp.float32).astype(jnp.bfloat16)
    product = jnp.dot(first_low, image, preferred_element_type=jnp.float32)
    return (2.0 * first - product).astype(jnp.bfloat16)


def fold_with(columns, piece):
    return jnp.einsum("kij,kjl->kil", piece, columns, preferred_element_type=jnp.float32)


def general_plan(
    activations,
    router_grad,
    token_ids,
    norm_terms,
    old_factors,
    old_router_factor,
    old_norm_diag,
    old_embed_diag,
):
    n_tensor = lax.axis_size("tensor")
    n_section = lax.axis_size("section")
    n_shard = lax.axis_size("shard")
    tensor_rank = lax.axis_index("tensor")
    section_rank = lax.axis_index("section")
    row_block = D // n_tensor
    col_block = D // n_section
    tokens_all = activations.shape[1] * n_shard
    row_start = tensor_rank * row_block
    col_start = section_rank * col_block

    def collect(carry, piece):
        whole = lax.all_gather(piece, ("tensor", "section"), axis=1, tiled=True)
        rows_part = lax.dynamic_slice_in_dim(whole, row_start, row_block, 1)
        cols_part = lax.dynamic_slice_in_dim(whole, col_start, col_block, 1)
        return (carry, (rows_part, cols_part))

    unused_carry, (row_parts, col_parts) = lax.scan(collect, jnp.int32(0), activations)
    partial_value = jnp.einsum(
        "mnr,mnc->mrc", row_parts, col_parts, preferred_element_type=jnp.float32
    )
    fresh = lax.psum_scatter(partial_value, "shard", scatter_dimension=0, tiled=True) / tokens_all
    row_index = lax.broadcasted_iota(jnp.int32, (row_block, col_block), 0) + row_start
    col_index = lax.broadcasted_iota(jnp.int32, (row_block, col_block), 1) + col_start
    eye_block = (row_index == col_index).astype(jnp.float32)
    matrix = factor_decay * old_factors + (1.0 - factor_decay) * fresh + damping * eye_block
    diag_part = jnp.sum(matrix * eye_block, axis=(1, 2))
    trace = lax.psum(diag_part, ("tensor", "section"))
    factor_scale = (D / (3.0 * trace))[:, None, None]
    matrix_low = lax.optimization_barrier(matrix.astype(jnp.bfloat16))
    first = 2.0 * factor_scale * eye_block - factor_scale * factor_scale * matrix_low.astype(
        jnp.float32
    )
    first_low = first.astype(jnp.bfloat16)
    first_cols = lax.all_gather(first_low, "tensor", axis=1, tiled=True)
    image = fold_with(first_cols, lax.all_gather(matrix_low, "section", axis=2, tiled=True))
    image_cols = lax.all_gather(image.astype(jnp.bfloat16), "tensor", axis=1, tiled=True)
    product = fold_with(image_cols, lax.all_gather(first_low, "section", axis=2, tiled=True))
    inverse_low = (2.0 * first - product).astype(jnp.bfloat16)
    inverses = lax.all_gather(inverse_low, "shard", axis=0, tiled=True)
    left_terms = jnp.stack(
        [
            jnp.einsum("nc,rc->nr", col_parts[m], inverses[m], preferred_element_type=jnp.float32)
            for m in (0, 4, 6)
        ]
    )
    left = lax.psum(left_terms, "section").astype(jnp.bfloat16)
    right_terms = jnp.stack(
        [
            jnp.einsum("nr,rc->nc", row_parts[m], inverses[m], preferred_element_type=jnp.float32)
            for m in (1, 2, 3, 5, 7)
        ]
    )
    right = lax.psum(right_terms, "tensor").astype(jnp.bfloat16)
    norm_values = norm_terms.astype(jnp.float32)
    router_part = jnp.einsum(
        "en,fn->ef", router_grad, router_grad, preferred_element_type=jnp.float32
    )
    router_sum, norm_total, norm_squares = lax.psum(
        (router_part, jnp.sum(norm_values, axis=1), jnp.sum(norm_values * norm_values, axis=1)),
        "shard",
    )
    router_matrix = (
        factor_decay * old_router_factor
        + (1.0 - factor_decay) * (router_sum / tokens_all)
        + damping * jnp.eye(EXPERTS, dtype=jnp.float32)
    )
    router_inverse = local_inverse(router_matrix)
    router_right = jnp.einsum(
        "en,ef->nf", router_grad, router_inverse, preferred_element_type=jnp.float32
    ).astype(jnp.bfloat16)
    precond_norms = (
        learning_rate
        * norm_total
        / (
            factor_decay * old_norm_diag
            + (1.0 - factor_decay) * (norm_squares / tokens_all)
            + damping
        )
    )
    ids_all = lax.all_gather(token_ids, "shard", axis=0, tiled=True)
    embed_all = lax.all_gather(right[4], "shard", axis=0, tiled=True)
    paired_left = jnp.stack([left[0], left[0], left[0], left[1]])
    attn_terms = jnp.einsum(
        "wnr,wnc->wrc", paired_left, right[:4], preferred_element_type=jnp.float32
    )
    router_term = jnp.einsum("nf,nr->fr", router_right, left[2], preferred_element_type=jnp.float32)
    attn_sum, router_total = lax.psum((attn_terms, router_term), "shard")
    precond_attn = learning_rate * attn_sum
    precond_router = learning_rate * router_total
    vocab_block = VOCAB // n_tensor
    step_rows = math.gcd(vocab_block, 512)
    vocab_start = tensor_rank * vocab_block

    def embed_block(block_index):
        ids_here = vocab_start + block_index * step_rows + lax.iota(jnp.int32, step_rows)
        onehot = (ids_here[:, None] == ids_all[None, :]).astype(jnp.bfloat16)
        summed = jnp.dot(onehot, embed_all, preferred_element_type=jnp.float32)
        tallies = jnp.sum(onehot, axis=1, dtype=jnp.float32)
        return (summed, tallies)

    block_sums, block_counts = lax.map(
        embed_block, jnp.arange(vocab_block // step_rows, dtype=jnp.int32)
    )
    embed_sum = block_sums.reshape(vocab_block, col_block)
    counts = block_counts.reshape(vocab_block)
    divisor = factor_decay * old_embed_diag + (1.0 - factor_decay) * (counts / tokens_all) + damping
    precond_embed = learning_rate * embed_sum / divisor[:, None]
    return (precond_attn, precond_router, precond_norms, precond_embed)


def split_three(values):
    high = lax.reduce_precision(values, 8, 7)
    rest = values - high
    middle = lax.reduce_precision(rest, 8, 7)
    return jnp.stack([high, middle, rest - middle], axis=-2).astype(jnp.bfloat16)


def swap(value, axis, size, step):
    return lax.ppermute(value, axis, [(i, i ^ step) for i in range(size)])


def local_diagonals(blocks):
    width = blocks.shape[1]
    pieces = []
    for start in range(0, width, 128):
        size = min(128, width - start)
        tile = blocks[:, start : start + size, start : start + size]
        pieces.append(jnp.sum(tile * jnp.eye(size, dtype=tile.dtype), axis=1))
    return jnp.concatenate(pieces, axis=1)


def rounded(values):
    return values.astype(jnp.bfloat16).astype(jnp.float32)


def params():
    return pltpu.CompilerParams(vmem_limit_bytes=40 * 1024 * 1024)


def layout_kernel(place_ref, gathered, features, rows, low_diag, trace, old, *, weight):
    own_place, layer, core = place_ref[0], place_ref[1], place_ref[2]
    sections, steps, _, tokens = gathered.shape
    groups, depth, _ = features.shape
    part = depth // (sections * steps)
    width = depth // steps
    for section in range(sections):
        codes = jnp.zeros((16, tokens), jnp.float32)
        for step in range(steps):
            start = (step * sections + section) * part
            for group in range(groups):
                features[group, start : start + part] = gathered[
                    section, step, group * part : (group + 1) * part
                ]
            codes += gathered[section, step, groups * part :].astype(jnp.float32)
        codes = codes[0:3] + codes[3:6] + codes[6:9]
        pieces = [codes[0:1], codes[1:2], codes[2:3, : width - 2 * tokens]]
        old[section ^ layer] = jnp.concatenate(pieces, axis=1)
    ones = jnp.ones((8, tokens), jnp.bfloat16)
    total = jnp.float32(0.0)
    for step in range(steps):
        squares = jnp.zeros((8, width), jnp.float32)
        for group in range(groups):
            values = features[group, step * width : (step + 1) * width].astype(jnp.float32)
            values = values * values
            high = values.astype(jnp.bfloat16)
            low = (values - high.astype(jnp.float32)).astype(jnp.bfloat16)
            for piece in (high, low):
                squares += lax.dot_general(
                    ones, piece, (((1,), (1,)), ((), ())), preferred_element_type=jnp.float32
                )
        diag = factor_decay * old[step] + weight * squares[0:1] + damping
        total += jnp.sum(diag)
        low_diag[step] = rounded(diag)
        start = pl.multiple_of((own_place ^ step) * width, width)
        mine = features[core, pl.ds(start, width)]
        rows[:, step * width : (step + 1) * width] = mine.T
    trace[0] = total


def lay_out(places, gathered, weight):
    sections, steps, height, tokens = gathered.shape
    part = (height - 16) // 2
    depth = sections * steps * part
    width = depth // steps
    vmem = pl.BlockSpec(memory_space=pltpu.VMEM)
    smem = pl.BlockSpec(memory_space=pltpu.SMEM)
    return pl.pallas_call(
        functools.partial(layout_kernel, weight=weight),
        in_specs=[smem, vmem],
        out_specs=[vmem, vmem, vmem, smem],
        out_shape=[
            jax.ShapeDtypeStruct((2, depth, tokens), jnp.bfloat16),
            jax.ShapeDtypeStruct((tokens, depth), jnp.bfloat16),
            jax.ShapeDtypeStruct((steps, 1, width), jnp.float32),
            jax.ShapeDtypeStruct((1,), jnp.float32),
        ],
        scratch_shapes=[pltpu.VMEM((steps, 1, width), jnp.float32)],
        compiler_params=params(),
        cost_estimate=pl.CostEstimate(
            flops=64 * depth * tokens, bytes_accessed=14 * depth * tokens, transcendentals=0
        ),
    )(places, gathered)


def factor_kernel(place_ref, part, own, old, diag, out, *, step, weight):
    fresh = jnp.zeros(out.shape, jnp.float32)
    for index in range(part.shape[0]):
        fresh += lax.dot_general(
            part[index], own[index], (((1,), (1,)), ((), ())), preferred_element_type=jnp.float32
        )
    block = factor_decay * old[...].astype(jnp.float32) + weight * fresh
    on_diag = lax.broadcasted_iota(jnp.int32, out.shape, 0) == lax.broadcasted_iota(
        jnp.int32, out.shape, 1
    )
    block = jnp.where(on_diag & (place_ref[0] == step), diag[0], block)
    out[...] = block.astype(jnp.bfloat16)


def factor_block(place, features, old, diag, step, weight):
    groups, _, tokens = features.shape
    rows, cols = old.shape
    return pl.pallas_call(
        functools.partial(factor_kernel, step=step, weight=weight),
        grid_spec=pltpu.PrefetchScalarGridSpec(
            num_scalar_prefetch=1,
            grid=(1,),
            in_specs=[
                pl.BlockSpec((groups, rows, tokens), lambda i, place: (0, step, 0)),
                pl.BlockSpec((groups, cols, tokens), lambda i, place: (0, place[0], 0)),
                pl.BlockSpec((rows, cols), lambda i, place: (0, 0)),
                pl.BlockSpec((1, 1, cols), lambda i, place: (place[0], 0, 0)),
            ],
            out_specs=pl.BlockSpec((rows, cols), lambda i, place: (0, 0)),
        ),
        out_shape=jax.ShapeDtypeStruct((rows, cols), jnp.bfloat16),
        compiler_params=params(),
        cost_estimate=pl.CostEstimate(
            flops=2 * groups * rows * cols * tokens,
            bytes_accessed=4 * rows * cols + 4 * groups * rows * tokens,
            transcendentals=0,
        ),
    )(place, features, features, old, diag)


def fetch_blocks(place_ref, blocks, held, sems):
    count = len(blocks) // 2
    depth = blocks[0].shape[0]
    copies = []
    for index in range(2 * count):
        slot = pl.multiple_of((place_ref[0] ^ (index % count)) * depth, depth)
        copies.append(
            pltpu.make_async_copy(
                blocks[index], held.at[index // count, pl.ds(slot, depth)], sems.at[index]
            )
        )
    for copy in copies:
        copy.start()
    return copies


def block_products(rows, copies, held):
    count = len(copies) // 2
    products = []
    for index in range(2):
        for copy in copies[index * count : (index + 1) * count]:
            copy.wait()
        products.append(jnp.dot(rows, held[index], preferred_element_type=jnp.float32))
    return products


def first_parts(place_ref, scale, rows, diag, product, index):
    width = product.shape[1]
    square = scale * scale
    values = rows[:, index * width : (index + 1) * width].astype(jnp.float32)
    low_diag = diag[place_ref[0] ^ index]
    first_diag = rounded(2.0 * scale - square * low_diag)
    by_first = 2.0 * scale * values - square * product
    step_one = first_diag * values - square * (product - low_diag * values)
    return by_first, step_one, low_diag, first_diag


def first_kernel(place_ref, scale_ref, rows, diag, *refs):
    blocks, (kept, message), (held, sems) = refs[:8], refs[8:10], refs[10:]
    copies = fetch_blocks(place_ref, blocks, held, sems)
    products = block_products(rows[...], copies, held)
    lows = []
    for index in range(2):
        kept[index] = products[index]
        parts = first_parts(place_ref, scale_ref[0], rows, diag, products[index], index)
        lows.append(parts[1].astype(jnp.bfloat16))
    message[...] = jnp.concatenate(lows, axis=1)


def second_kernel(place_ref, scale_ref, mine, theirs, rows, diag, before, *refs):
    blocks, (kept, message), (held, sems) = refs[:8], refs[8:10], refs[10:]
    copies = fetch_blocks(place_ref, blocks, held, sems)
    both = jnp.concatenate([mine[...], theirs[...]], axis=1)
    products = block_products(both, copies, held)
    square = scale_ref[0] * scale_ref[0]
    lows = []
    for index in range(2):
        by_first, one, low_diag, first_diag = first_parts(
            place_ref, scale_ref[0], rows, diag, before[index], index
        )
        two = products[index] + low_diag * (one - rounded(one))
        low = two.astype(jnp.bfloat16)
        kept[index] = (
            2.0 * by_first - first_diag * two - square * low_diag * low.astype(jnp.float32)
        )
        lows.append(low)
    message[...] = jnp.concatenate(lows, axis=1)


def third_kernel(place_ref, scale_ref, mine, theirs, before, *refs):
    blocks, (keep, give), (held, sems) = refs[:8], refs[8:10], refs[10:]
    copies = fetch_blocks(place_ref, blocks, held, sems)
    both = jnp.concatenate([mine[...], theirs[...]], axis=1)
    products = block_products(both, copies, held)
    square = scale_ref[0] * scale_ref[0]
    for index, out in ((0, keep), (1, give)):
        out[...] = (before[index] + square * products[index]).T.astype(jnp.bfloat16)


def chain_call(kernel, scalars, arrays, blocks, out_shape):
    depth, width = blocks[0].shape
    count = len(blocks) // 2
    tokens = arrays[0].shape[0]
    vmem = pl.BlockSpec(memory_space=pltpu.VMEM)
    return pl.pallas_call(
        kernel,
        in_specs=[pl.BlockSpec(memory_space=pltpu.SMEM)] * len(scalars)
        + [vmem] * len(arrays)
        + [pl.BlockSpec(memory_space=pl.ANY)] * len(blocks),
        out_specs=[vmem] * len(out_shape),
        out_shape=out_shape,
        scratch_shapes=[
            pltpu.VMEM((2, count * depth, width), jnp.bfloat16),
            pltpu.SemaphoreType.DMA((len(blocks),)),
        ],
        compiler_params=params(),
        cost_estimate=pl.CostEstimate(
            flops=2 * len(blocks) * tokens * depth * width,
            bytes_accessed=2 * len(blocks) * depth * width,
            transcendentals=0,
        ),
    )(*scalars, *arrays, *blocks)


def left_kernel(take_ref, own, moved, codes, out):
    rows, width = own.shape
    experts, cols = codes.shape
    out[:rows] = jnp.where(take_ref[0] == 1, own[...], moved[...])
    high = codes[...].astype(jnp.bfloat16)
    low = (codes[...] - high.astype(jnp.float32)).astype(jnp.bfloat16)
    both = jnp.concatenate([high, low], axis=0)
    out[rows : rows + 2 * experts] = both[:, :width]
    rest = jnp.zeros((2 * experts, 2 * width - cols), jnp.bfloat16)
    out[rows + 2 * experts :] = jnp.concatenate([both[:, width:], rest], axis=1)


def left_message(take, own, moved, codes):
    rows, width = own.shape
    vmem = pl.BlockSpec(memory_space=pltpu.VMEM)
    return pl.pallas_call(
        left_kernel,
        in_specs=[pl.BlockSpec(memory_space=pltpu.SMEM), vmem, vmem, vmem],
        out_specs=vmem,
        out_shape=jax.ShapeDtypeStruct((rows + 4 * codes.shape[0], width), own.dtype),
        compiler_params=params(),
        cost_estimate=pl.CostEstimate(
            flops=60 * rows * rows * rows * 4, bytes_accessed=8 * rows * width, transcendentals=0
        ),
    )(take.astype(jnp.int32).reshape(1), own, moved, codes)


def output_kernel(where_ref, scale, matches, *refs, parts):
    lefts, refs = (refs[:4], refs[4:8]), refs[8:]
    mine, others, refs = refs[:parts], refs[parts : 2 * parts], refs[2 * parts :]
    attn, embed, left_held, held, found, attn_made, embed_made, sems, out_sems = refs
    shard, turn = where_ref[0], where_ref[1]
    rows = held.shape[1]

    def fetch_left(slot):
        for group in range(2):
            for place in range(4):

                @pl.when((turn == place) & ((shard ^ slot) == group))
                def _():
                    source = lefts[group][place].at[pl.ds(0, rows)]
                    pltpu.make_async_copy(source, left_held.at[slot], sems.at[5 + slot]).start()

    def pieces(slot, group, layer):
        copies, start = [], 0
        for part in group:
            size = part.shape[1]
            target = held.at[slot, pl.ds(start, size)]
            copies.append(pltpu.make_async_copy(part.at[layer], target, sems.at[slot]))
            start += size
        return copies

    layers = (0, 1, 2, 0, 2)
    found_copy = pltpu.make_async_copy(matches, found, sems.at[7])
    fetch_left(0)
    for slot, layer in enumerate(layers):
        for owner, group in enumerate((mine, others)):

            @pl.when((shard ^ owner) == (0 if slot < 3 else 1))
            def _():
                for copy in pieces(slot, group, layer):
                    copy.start()

    fetch_left(1)
    found_copy.start()

    def arrived(slot):
        pltpu.make_async_copy(held.at[slot], held.at[slot], sems.at[slot]).wait()
        return held[slot]

    def left_arrived(slot):
        target = left_held.at[slot]
        pltpu.make_async_copy(target, target, sems.at[5 + slot]).wait()

    results = []
    left_arrived(0)
    for slot in range(4):
        if slot == 3:
            left_arrived(1)
        attn_made[slot] = learning_rate * lax.dot_general(
            left_held[slot // 3],
            arrived(slot),
            (((1,), (1,)), ((), ())),
            preferred_element_type=jnp.float32,
        )
        results.append(
            pltpu.make_async_copy(attn_made.at[slot], attn.at[slot], out_sems.at[slot])
        )
        results[-1].start()
    right = arrived(4)
    found_copy.wait()
    part = found.shape[1] // 4
    for index in range(4):
        cols = pl.ds(index * part, part)
        product = jnp.dot(right, found[:, cols], preferred_element_type=jnp.float32)
        embed_made[:, cols] = product * scale[:, cols]
        results.append(
            pltpu.make_async_copy(
                embed_made.at[:, cols], embed.at[:, cols], out_sems.at[4 + index]
            )
        )
        results[-1].start()
    for result in results:
        result.wait()


def output_products(where, scale, matches, lefts, mine, others):
    parts = len(mine)
    cols, tokens_all = sum(part.shape[1] for part in mine), mine[0].shape[2]
    vocab_block = scale.shape[1]
    anywhere = pl.BlockSpec(memory_space=pl.ANY)
    return pl.pallas_call(
        functools.partial(output_kernel, parts=parts),
        in_specs=[
            pl.BlockSpec(memory_space=pltpu.SMEM),
            pl.BlockSpec(memory_space=pltpu.VMEM),
        ]
        + [anywhere] * (9 + 2 * parts),
        out_specs=(anywhere, anywhere),
        out_shape=(
            jax.ShapeDtypeStruct((4, cols, cols), jnp.float32),
            jax.ShapeDtypeStruct((cols, vocab_block), jnp.float32),
        ),
        scratch_shapes=[
            pltpu.VMEM((2, cols, tokens_all), jnp.bfloat16),
            pltpu.VMEM((5, cols, tokens_all), jnp.bfloat16),
            pltpu.VMEM((tokens_all, vocab_block), jnp.bfloat16),
            pltpu.VMEM((4, cols, cols), jnp.float32),
            pltpu.VMEM((cols, vocab_block), jnp.float32),
            pltpu.SemaphoreType.DMA((8,)),
            pltpu.SemaphoreType.DMA((8,)),
        ],
        compiler_params=pltpu.CompilerParams(vmem_limit_bytes=60 * 1024 * 1024),
        cost_estimate=pl.CostEstimate(
            flops=2 * cols * tokens_all * (4 * cols + vocab_block),
            bytes_accessed=4 * cols * (4 * cols + vocab_block) + 14 * cols * tokens_all,
            transcendentals=0,
        ),
    )(where, scale, matches, *lefts[0], *lefts[1], *mine, *others)


def layer_plan(
    activations,
    router_grad,
    token_ids,
    norm_terms,
    old_factors,
    old_router_factor,
    old_norm_diag,
    old_embed_diag,
):
    n_tensor = lax.axis_size("tensor")
    n_section = lax.axis_size("section")
    n_shard = lax.axis_size("shard")
    shard = lax.axis_index("shard")
    layer = lax.axis_index("tensor")
    section = lax.axis_index("section")
    core = section % 2
    owned, row_block, col_block = old_factors.shape
    tokens = activations.shape[1]
    features_dev = activations.shape[2]
    tokens_all = tokens * n_shard
    weight = (1.0 - factor_decay) / tokens_all
    own_place = section ^ layer
    place = own_place.reshape(1)
    axes = ("shard", "tensor")

    def by_index(array, index, axis=0):
        return lax.dynamic_index_in_dim(array, index, axis, False)

    def held_by(layer_index):
        return lax.rem(layer_index + 1, owned)

    by_feature = jnp.swapaxes(activations, 1, 2)
    diagonals = local_diagonals(old_factors) * (layer == section).astype(jnp.float32)
    extra = jnp.pad(split_three(diagonals), ((0, 0), (0, 0), (0, 3 * tokens - col_block)))
    extra = jnp.pad(extra.reshape(owned, 9, tokens), ((0, 0), (0, 7), (0, 0)))
    collected = []
    for step in range(n_tensor):
        factor = held_by(layer ^ step)
        message = jnp.concatenate(
            [
                by_index(by_feature, shard * owned + factor),
                by_index(by_feature, (1 - shard) * owned + factor),
                by_index(extra, factor),
            ],
            axis=0,
        )
        collected.append(swap(message, "tensor", n_tensor, step) if step else message)
    collected = jnp.stack(collected)
    other_tokens = swap(
        collected[:, features_dev : 2 * features_dev], "shard", n_shard, 1
    )

    def both_shards(value, axis):
        other = swap(value, "shard", n_shard, 1)
        return jnp.where(
            shard == 0,
            jnp.concatenate([value, other], axis=axis),
            jnp.concatenate([other, value], axis=axis),
        )

    grad_all = both_shards(router_grad, 1)
    ids_all = both_shards(token_ids, 0)
    norm_values = norm_terms.astype(jnp.float32)
    norm_sums = jnp.stack([jnp.sum(norm_values, axis=1), jnp.sum(norm_values * norm_values, axis=1)])
    norm_sums = norm_sums + swap(norm_sums, "shard", n_shard, 1)
    vocab_block = old_embed_diag.shape[0]
    ids_here = layer * vocab_block + lax.iota(jnp.int32, vocab_block)
    matches = (ids_all[:, None] == ids_here[None, :]).astype(jnp.bfloat16)
    counts = jnp.sum(matches, axis=0, dtype=jnp.float32)
    divisor = factor_decay * old_embed_diag + (1.0 - factor_decay) * (counts / tokens_all) + damping
    embed_scale = (learning_rate / divisor)[None, :]
    router_matrix = (
        factor_decay * old_router_factor
        + weight * jnp.einsum("en,fn->ef", grad_all, grad_all, preferred_element_type=jnp.float32)
        + damping * jnp.eye(EXPERTS, dtype=jnp.float32)
    )
    router_inverse = local_inverse(router_matrix)
    router_right = jnp.einsum(
        "en,ef->fn", grad_all, router_inverse, preferred_element_type=jnp.float32
    ).astype(jnp.bfloat16)

    def old_block(factors, step):
        return by_index(factors, held_by(layer ^ step)).astype(jnp.bfloat16)

    early = swap(old_block(old_factors, 2), "tensor", n_tensor, 2)
    later_factors = lax.optimization_barrier(old_factors)
    blocks = [old_block(later_factors, step) for step in (0, 1, 3)]
    other_tokens, collected, early, blocks, small = lax.optimization_barrier(
        (other_tokens, collected, early, blocks, (router_right, matches, embed_scale, norm_sums))
    )
    router_right, matches, embed_scale, norm_sums = small
    collected = jnp.concatenate(
        [collected[:, :features_dev], other_tokens, collected[:, 2 * features_dev :]], axis=1
    )
    gathered = lax.all_gather(collected, "section", axis=0)
    blocks = [
        blocks[0],
        swap(blocks[1], "tensor", n_tensor, 1),
        early,
        swap(blocks[2], "tensor", n_tensor, 3),
    ]

    features, rows, low_diag, trace = lay_out(
        jnp.stack([own_place, layer, core]), gathered, weight
    )
    scale = D / (3.0 * trace)
    own_cols = [
        factor_block(place, features, blocks[step], low_diag, step, weight)
        for step in range(n_tensor)
    ]
    other_cols = [swap(block, "section", n_section, 1) for block in own_cols]
    cols = own_cols + other_cols

    wide = jax.ShapeDtypeStruct((2, tokens, col_block), jnp.float32)
    sent = jax.ShapeDtypeStruct((tokens, 2 * col_block), jnp.bfloat16)
    part = jax.ShapeDtypeStruct((col_block, tokens), jnp.bfloat16)
    scalars = (place, scale)
    kept, message = chain_call(first_kernel, scalars, (rows, low_diag), cols, (wide, sent))
    theirs = swap(message, "section", n_section, 2)
    kept, message = chain_call(
        second_kernel, scalars, (message, theirs, rows, low_diag, kept), cols, (wide, sent)
    )
    theirs = swap(message, "section", n_section, 2)
    keep, give = chain_call(third_kernel, scalars, (message, theirs, kept), cols, (part, part))
    got = swap(give, "section", n_section, 1)
    own = jnp.where(
        core == shard, jnp.concatenate([keep, got], axis=1), jnp.concatenate([got, keep], axis=1)
    )

    planes = range(n_shard)
    layers = range(n_tensor)
    everywhere = ("shard", "tensor", "section")

    def spot(x, z, s):
        return (x * n_tensor + z) * n_section + s

    def scatter(value, source):
        return lax.ppermute(
            value,
            everywhere,
            [(spot(x, source, s), spot(x, s, s)) for x in planes for s in layers if s != source],
        )

    def hand_round(value):
        sides = lax.ppermute(
            value, everywhere, [(spot(x, t, t), spot(x, t, t ^ 2)) for x in planes for t in layers]
        )
        near = lax.ppermute(
            value, everywhere, [(spot(x, t, t), spot(x, t, t ^ 1)) for x in planes for t in layers]
        )
        far = lax.ppermute(
            sides,
            everywhere,
            [(spot(x, t, t ^ 2), spot(x, t, t ^ 3)) for x in planes for t in layers],
        )
        return (value, near, sides, far)

    cut = col_block // 3 * 2
    mine = [
        lax.all_gather(own[start:stop], "tensor", axis=0)
        for start, stop in ((0, cut), (cut, col_block))
    ]
    router_cols = learning_rate * jnp.einsum(
        "fn,cn->fc", router_right, own, preferred_element_type=jnp.float32
    )
    router_cols = jnp.where(layer == 1, router_cols, scatter(router_cols, 1))
    left_layer = n_tensor - 1
    left_here = left_message(layer == left_layer, own, scatter(own, left_layer), router_cols)
    left_there = lax.ppermute(
        left_here, everywhere, [(spot(x, t, t), spot(1 - x, t, t)) for x in planes for t in layers]
    )
    lefts_here = hand_round(left_here)

    def hand_over(piece):
        return swap(piece[: n_tensor - 1], "shard", n_shard, 1)

    left_there, mine[0] = lax.optimization_barrier((left_there, mine[0]))
    lefts_there = hand_round(left_there)
    others = [hand_over(mine[0])]
    mine[1], others[0] = lax.optimization_barrier((mine[1], others[0]))
    others.append(hand_over(mine[1]))
    turn = section ^ layer

    def codes_of(group):
        found = [part[col_block:] for part in group]
        chosen = found[3]
        for index in (2, 1, 0):
            chosen = jnp.where(turn == index, found[index], chosen)
        return chosen

    codes = jnp.where(shard == 1, codes_of(lefts_here), codes_of(lefts_there))
    codes = jnp.concatenate(
        [codes[: 2 * EXPERTS], codes[2 * EXPERTS :, : col_block - tokens_all]], axis=1
    ).astype(jnp.float32)
    precond_router = codes[:EXPERTS] + codes[EXPERTS:]

    precond_attn, embed_columns = output_products(
        jnp.stack([shard, turn]), embed_scale, matches, (lefts_here, lefts_there), mine, others
    )
    precond_embed = embed_columns.T

    precond_norms = (
        learning_rate
        * norm_sums[0]
        / (
            factor_decay * old_norm_diag
            + (1.0 - factor_decay) * (norm_sums[1] / tokens_all)
            + damping
        )
    )
    return (precond_attn, precond_router, precond_norms, precond_embed)


def per_device(*arguments):
    one_each = arguments[4].shape[0] == lax.axis_size("tensor") == lax.axis_size("section")
    if one_each and lax.axis_size("section") == 4 and lax.axis_size("shard") == 2:
        return layer_plan(*arguments)
    return general_plan(*arguments)


def solution(mesh):
    return jax.shard_map(
        per_device,
        mesh=mesh,
        in_specs=(
            P(None, "shard", ("tensor", "section")),
            P(None, "shard"),
            P("shard"),
            P(None, "shard", ("tensor", "section")),
            P("shard", "tensor", "section"),
            P(),
            P(None, ("tensor", "section")),
            P("tensor"),
        ),
        out_specs=(
            P(None, "tensor", "section"),
            P(None, "tensor"),
            P(None, ("tensor", "section")),
            P("tensor", "section"),
        ),
        check_vma=False,
    )
```

```python
import functools
import math

import jax
import jax.numpy as jnp
from jax import lax
from jax.experimental import pallas as pl
from jax.experimental.pallas import tpu as pltpu
from jax.sharding import PartitionSpec as P

D = 2304
EXPERTS = 8
VOCAB = 8192


factor_decay = 0.5
damping = 0.01
learning_rate = 0.05


def local_inverse(matrix):
    width = matrix.shape[0]
    trace = jnp.sum(jnp.diagonal(matrix))
    factor_scale = width / (3.0 * trace)
    identity = jnp.eye(width, dtype=jnp.float32)
    matrix_low = lax.optimization_barrier(matrix.astype(jnp.bfloat16))
    first = 2.0 * factor_scale * identity - factor_scale * factor_scale * matrix_low.astype(
        jnp.float32
    )
    first_low = first.astype(jnp.bfloat16)
    image = jnp.dot(matrix_low, first_low, preferred_element_type=jnp.float32).astype(jnp.bfloat16)
    product = jnp.dot(first_low, image, preferred_element_type=jnp.float32)
    return (2.0 * first - product).astype(jnp.bfloat16)


def fold_with(columns, piece):
    return jnp.einsum("kij,kjl->kil", piece, columns, preferred_element_type=jnp.float32)


def general_plan(
    activations,
    router_grad,
    token_ids,
    norm_terms,
    old_factors,
    old_router_factor,
    old_norm_diag,
    old_embed_diag,
):
    n_tensor = lax.axis_size("tensor")
    n_section = lax.axis_size("section")
    n_shard = lax.axis_size("shard")
    tensor_rank = lax.axis_index("tensor")
    section_rank = lax.axis_index("section")
    row_block = D // n_tensor
    col_block = D // n_section
    tokens_all = activations.shape[1] * n_shard
    row_start = tensor_rank * row_block
    col_start = section_rank * col_block

    def collect(carry, piece):
        whole = lax.all_gather(piece, ("tensor", "section"), axis=1, tiled=True)
        rows_part = lax.dynamic_slice_in_dim(whole, row_start, row_block, 1)
        cols_part = lax.dynamic_slice_in_dim(whole, col_start, col_block, 1)
        return (carry, (rows_part, cols_part))

    unused_carry, (row_parts, col_parts) = lax.scan(collect, jnp.int32(0), activations)
    partial_value = jnp.einsum(
        "mnr,mnc->mrc", row_parts, col_parts, preferred_element_type=jnp.float32
    )
    fresh = lax.psum_scatter(partial_value, "shard", scatter_dimension=0, tiled=True) / tokens_all
    row_index = lax.broadcasted_iota(jnp.int32, (row_block, col_block), 0) + row_start
    col_index = lax.broadcasted_iota(jnp.int32, (row_block, col_block), 1) + col_start
    eye_block = (row_index == col_index).astype(jnp.float32)
    matrix = factor_decay * old_factors + (1.0 - factor_decay) * fresh + damping * eye_block
    diag_part = jnp.sum(matrix * eye_block, axis=(1, 2))
    trace = lax.psum(diag_part, ("tensor", "section"))
    factor_scale = (D / (3.0 * trace))[:, None, None]
    matrix_low = lax.optimization_barrier(matrix.astype(jnp.bfloat16))
    first = 2.0 * factor_scale * eye_block - factor_scale * factor_scale * matrix_low.astype(
        jnp.float32
    )
    first_low = first.astype(jnp.bfloat16)
    first_cols = lax.all_gather(first_low, "tensor", axis=1, tiled=True)
    image = fold_with(first_cols, lax.all_gather(matrix_low, "section", axis=2, tiled=True))
    image_cols = lax.all_gather(image.astype(jnp.bfloat16), "tensor", axis=1, tiled=True)
    product = fold_with(image_cols, lax.all_gather(first_low, "section", axis=2, tiled=True))
    inverse_low = (2.0 * first - product).astype(jnp.bfloat16)
    inverses = lax.all_gather(inverse_low, "shard", axis=0, tiled=True)
    left_terms = jnp.stack(
        [
            jnp.einsum("nc,rc->nr", col_parts[m], inverses[m], preferred_element_type=jnp.float32)
            for m in (0, 4, 6)
        ]
    )
    left = lax.psum(left_terms, "section").astype(jnp.bfloat16)
    right_terms = jnp.stack(
        [
            jnp.einsum("nr,rc->nc", row_parts[m], inverses[m], preferred_element_type=jnp.float32)
            for m in (1, 2, 3, 5, 7)
        ]
    )
    right = lax.psum(right_terms, "tensor").astype(jnp.bfloat16)
    norm_values = norm_terms.astype(jnp.float32)
    router_part = jnp.einsum(
        "en,fn->ef", router_grad, router_grad, preferred_element_type=jnp.float32
    )
    router_sum, norm_total, norm_squares = lax.psum(
        (router_part, jnp.sum(norm_values, axis=1), jnp.sum(norm_values * norm_values, axis=1)),
        "shard",
    )
    router_matrix = (
        factor_decay * old_router_factor
        + (1.0 - factor_decay) * (router_sum / tokens_all)
        + damping * jnp.eye(EXPERTS, dtype=jnp.float32)
    )
    router_inverse = local_inverse(router_matrix)
    router_right = jnp.einsum(
        "en,ef->nf", router_grad, router_inverse, preferred_element_type=jnp.float32
    ).astype(jnp.bfloat16)
    precond_norms = (
        learning_rate
        * norm_total
        / (
            factor_decay * old_norm_diag
            + (1.0 - factor_decay) * (norm_squares / tokens_all)
            + damping
        )
    )
    ids_all = lax.all_gather(token_ids, "shard", axis=0, tiled=True)
    embed_all = lax.all_gather(right[4], "shard", axis=0, tiled=True)
    paired_left = jnp.stack([left[0], left[0], left[0], left[1]])
    attn_terms = jnp.einsum(
        "wnr,wnc->wrc", paired_left, right[:4], preferred_element_type=jnp.float32
    )
    router_term = jnp.einsum("nf,nr->fr", router_right, left[2], preferred_element_type=jnp.float32)
    attn_sum, router_total = lax.psum((attn_terms, router_term), "shard")
    precond_attn = learning_rate * attn_sum
    precond_router = learning_rate * router_total
    vocab_block = VOCAB // n_tensor
    step_rows = math.gcd(vocab_block, 512)
    vocab_start = tensor_rank * vocab_block

    def embed_block(block_index):
        ids_here = vocab_start + block_index * step_rows + lax.iota(jnp.int32, step_rows)
        onehot = (ids_here[:, None] == ids_all[None, :]).astype(jnp.bfloat16)
        summed = jnp.dot(onehot, embed_all, preferred_element_type=jnp.float32)
        tallies = jnp.sum(onehot, axis=1, dtype=jnp.float32)
        return (summed, tallies)

    block_sums, block_counts = lax.map(
        embed_block, jnp.arange(vocab_block // step_rows, dtype=jnp.int32)
    )
    embed_sum = block_sums.reshape(vocab_block, col_block)
    counts = block_counts.reshape(vocab_block)
    divisor = factor_decay * old_embed_diag + (1.0 - factor_decay) * (counts / tokens_all) + damping
    precond_embed = learning_rate * embed_sum / divisor[:, None]
    return (precond_attn, precond_router, precond_norms, precond_embed)


def split_three(values):
    high = lax.reduce_precision(values, 8, 7)
    rest = values - high
    middle = lax.reduce_precision(rest, 8, 7)
    return jnp.stack([high, middle, rest - middle], axis=-2).astype(jnp.bfloat16)


def swap(value, axis, size, step):
    return lax.ppermute(value, axis, [(i, i ^ step) for i in range(size)])


def local_diagonals(blocks):
    width = blocks.shape[1]
    pieces = []
    for start in range(0, width, 128):
        size = min(128, width - start)
        tile = blocks[:, start : start + size, start : start + size]
        pieces.append(jnp.sum(tile * jnp.eye(size, dtype=tile.dtype), axis=1))
    return jnp.concatenate(pieces, axis=1)


def rounded(values):
    return values.astype(jnp.bfloat16).astype(jnp.float32)


def params():
    return pltpu.CompilerParams(vmem_limit_bytes=40 * 1024 * 1024)


def layout_kernel(place_ref, gathered, features, rows, low_diag, trace, old, *, weight):
    own_place, layer, core = place_ref[0], place_ref[1], place_ref[2]
    sections, steps, _, tokens = gathered.shape
    groups, depth, _ = features.shape
    part = depth // (sections * steps)
    width = depth // steps
    for section in range(sections):
        codes = jnp.zeros((16, tokens), jnp.float32)
        for step in range(steps):
            start = (step * sections + section) * part
            for group in range(groups):
                features[group, start : start + part] = gathered[
                    section, step, group * part : (group + 1) * part
                ]
            codes += gathered[section, step, groups * part :].astype(jnp.float32)
        codes = codes[0:3] + codes[3:6] + codes[6:9]
        pieces = [codes[0:1], codes[1:2], codes[2:3, : width - 2 * tokens]]
        old[section ^ layer] = jnp.concatenate(pieces, axis=1)
    ones = jnp.ones((8, tokens), jnp.bfloat16)
    total = jnp.float32(0.0)
    for step in range(steps):
        squares = jnp.zeros((8, width), jnp.float32)
        for group in range(groups):
            values = features[group, step * width : (step + 1) * width].astype(jnp.float32)
            values = values * values
            high = values.astype(jnp.bfloat16)
            low = (values - high.astype(jnp.float32)).astype(jnp.bfloat16)
            for piece in (high, low):
                squares += lax.dot_general(
                    ones, piece, (((1,), (1,)), ((), ())), preferred_element_type=jnp.float32
                )
        diag = factor_decay * old[step] + weight * squares[0:1] + damping
        total += jnp.sum(diag)
        low_diag[step] = rounded(diag)
        start = pl.multiple_of((own_place ^ step) * width, width)
        mine = features[core, pl.ds(start, width)]
        rows[:, step * width : (step + 1) * width] = mine.T
    trace[0] = total


def lay_out(places, gathered, weight):
    sections, steps, height, tokens = gathered.shape
    part = (height - 16) // 2
    depth = sections * steps * part
    width = depth // steps
    vmem = pl.BlockSpec(memory_space=pltpu.VMEM)
    smem = pl.BlockSpec(memory_space=pltpu.SMEM)
    return pl.pallas_call(
        functools.partial(layout_kernel, weight=weight),
        in_specs=[smem, vmem],
        out_specs=[vmem, vmem, vmem, smem],
        out_shape=[
            jax.ShapeDtypeStruct((2, depth, tokens), jnp.bfloat16),
            jax.ShapeDtypeStruct((tokens, depth), jnp.bfloat16),
            jax.ShapeDtypeStruct((steps, 1, width), jnp.float32),
            jax.ShapeDtypeStruct((1,), jnp.float32),
        ],
        scratch_shapes=[pltpu.VMEM((steps, 1, width), jnp.float32)],
        compiler_params=params(),
        cost_estimate=pl.CostEstimate(
            flops=64 * depth * tokens, bytes_accessed=14 * depth * tokens, transcendentals=0
        ),
    )(places, gathered)


def factor_kernel(place_ref, part, own, old, diag, out, *, step, weight):
    fresh = jnp.zeros(out.shape, jnp.float32)
    for index in range(part.shape[0]):
        fresh += lax.dot_general(
            part[index], own[index], (((1,), (1,)), ((), ())), preferred_element_type=jnp.float32
        )
    block = factor_decay * old[...].astype(jnp.float32) + weight * fresh
    on_diag = lax.broadcasted_iota(jnp.int32, out.shape, 0) == lax.broadcasted_iota(
        jnp.int32, out.shape, 1
    )
    block = jnp.where(on_diag & (place_ref[0] == step), diag[0], block)
    out[...] = block.astype(jnp.bfloat16)


def factor_block(place, features, old, diag, step, weight):
    groups, _, tokens = features.shape
    rows, cols = old.shape
    return pl.pallas_call(
        functools.partial(factor_kernel, step=step, weight=weight),
        grid_spec=pltpu.PrefetchScalarGridSpec(
            num_scalar_prefetch=1,
            grid=(1,),
            in_specs=[
                pl.BlockSpec((groups, rows, tokens), lambda i, place: (0, step, 0)),
                pl.BlockSpec((groups, cols, tokens), lambda i, place: (0, place[0], 0)),
                pl.BlockSpec((rows, cols), lambda i, place: (0, 0)),
                pl.BlockSpec((1, 1, cols), lambda i, place: (place[0], 0, 0)),
            ],
            out_specs=pl.BlockSpec((rows, cols), lambda i, place: (0, 0)),
        ),
        out_shape=jax.ShapeDtypeStruct((rows, cols), jnp.bfloat16),
        compiler_params=params(),
        cost_estimate=pl.CostEstimate(
            flops=2 * groups * rows * cols * tokens,
            bytes_accessed=4 * rows * cols + 4 * groups * rows * tokens,
            transcendentals=0,
        ),
    )(place, features, features, old, diag)


def fetch_blocks(place_ref, blocks, held, sems):
    count = len(blocks) // 2
    depth = blocks[0].shape[0]
    copies = []
    for index in range(2 * count):
        slot = pl.multiple_of((place_ref[0] ^ (index % count)) * depth, depth)
        copies.append(
            pltpu.make_async_copy(
                blocks[index], held.at[index // count, pl.ds(slot, depth)], sems.at[index]
            )
        )
    for copy in copies:
        copy.start()
    return copies


def block_products(rows, copies, held):
    count = len(copies) // 2
    products = []
    for index in range(2):
        for copy in copies[index * count : (index + 1) * count]:
            copy.wait()
        products.append(jnp.dot(rows, held[index], preferred_element_type=jnp.float32))
    return products


def first_parts(place_ref, scale, rows, diag, product, index):
    width = product.shape[1]
    square = scale * scale
    values = rows[:, index * width : (index + 1) * width].astype(jnp.float32)
    low_diag = diag[place_ref[0] ^ index]
    first_diag = rounded(2.0 * scale - square * low_diag)
    by_first = 2.0 * scale * values - square * product
    step_one = first_diag * values - square * (product - low_diag * values)
    return by_first, step_one, low_diag, first_diag


def first_kernel(place_ref, scale_ref, rows, diag, *refs):
    blocks, (kept, message), (held, sems) = refs[:8], refs[8:10], refs[10:]
    copies = fetch_blocks(place_ref, blocks, held, sems)
    products = block_products(rows[...], copies, held)
    lows = []
    for index in range(2):
        kept[index] = products[index]
        parts = first_parts(place_ref, scale_ref[0], rows, diag, products[index], index)
        lows.append(parts[1].astype(jnp.bfloat16))
    message[...] = jnp.concatenate(lows, axis=1)


def second_kernel(place_ref, scale_ref, mine, theirs, rows, diag, before, *refs):
    blocks, (kept, message), (held, sems) = refs[:8], refs[8:10], refs[10:]
    copies = fetch_blocks(place_ref, blocks, held, sems)
    both = jnp.concatenate([mine[...], theirs[...]], axis=1)
    products = block_products(both, copies, held)
    square = scale_ref[0] * scale_ref[0]
    lows = []
    for index in range(2):
        by_first, one, low_diag, first_diag = first_parts(
            place_ref, scale_ref[0], rows, diag, before[index], index
        )
        two = products[index] + low_diag * (one - rounded(one))
        low = two.astype(jnp.bfloat16)
        kept[index] = (
            2.0 * by_first - first_diag * two - square * low_diag * low.astype(jnp.float32)
        )
        lows.append(low)
    message[...] = jnp.concatenate(lows, axis=1)


def third_kernel(place_ref, scale_ref, mine, theirs, before, *refs):
    blocks, (keep, give), (held, sems) = refs[:8], refs[8:10], refs[10:]
    copies = fetch_blocks(place_ref, blocks, held, sems)
    both = jnp.concatenate([mine[...], theirs[...]], axis=1)
    products = block_products(both, copies, held)
    square = scale_ref[0] * scale_ref[0]
    for index, out in ((0, keep), (1, give)):
        out[...] = (before[index] + square * products[index]).T.astype(jnp.bfloat16)


def chain_call(kernel, scalars, arrays, blocks, out_shape):
    depth, width = blocks[0].shape
    count = len(blocks) // 2
    tokens = arrays[0].shape[0]
    vmem = pl.BlockSpec(memory_space=pltpu.VMEM)
    return pl.pallas_call(
        kernel,
        in_specs=[pl.BlockSpec(memory_space=pltpu.SMEM)] * len(scalars)
        + [vmem] * len(arrays)
        + [pl.BlockSpec(memory_space=pl.ANY)] * len(blocks),
        out_specs=[vmem] * len(out_shape),
        out_shape=out_shape,
        scratch_shapes=[
            pltpu.VMEM((2, count * depth, width), jnp.bfloat16),
            pltpu.SemaphoreType.DMA((len(blocks),)),
        ],
        compiler_params=params(),
        cost_estimate=pl.CostEstimate(
            flops=2 * len(blocks) * tokens * depth * width,
            bytes_accessed=2 * len(blocks) * depth * width,
            transcendentals=0,
        ),
    )(*scalars, *arrays, *blocks)


def left_kernel(take_ref, own, moved, codes, out):
    rows, width = own.shape
    experts, cols = codes.shape
    out[:rows] = jnp.where(take_ref[0] == 1, own[...], moved[...])
    high = codes[...].astype(jnp.bfloat16)
    low = (codes[...] - high.astype(jnp.float32)).astype(jnp.bfloat16)
    both = jnp.concatenate([high, low], axis=0)
    out[rows : rows + 2 * experts] = both[:, :width]
    rest = jnp.zeros((2 * experts, 2 * width - cols), jnp.bfloat16)
    out[rows + 2 * experts :] = jnp.concatenate([both[:, width:], rest], axis=1)


def left_message(take, own, moved, codes):
    rows, width = own.shape
    vmem = pl.BlockSpec(memory_space=pltpu.VMEM)
    return pl.pallas_call(
        left_kernel,
        in_specs=[pl.BlockSpec(memory_space=pltpu.SMEM), vmem, vmem, vmem],
        out_specs=vmem,
        out_shape=jax.ShapeDtypeStruct((rows + 4 * codes.shape[0], width), own.dtype),
        compiler_params=params(),
        cost_estimate=pl.CostEstimate(
            flops=rows * width, bytes_accessed=8 * rows * width, transcendentals=0
        ),
    )(take.astype(jnp.int32).reshape(1), own, moved, codes)


def output_kernel(where_ref, scale, matches, *refs, parts):
    lefts, refs = (refs[:4], refs[4:8]), refs[8:]
    mine, others, refs = refs[:parts], refs[parts : 2 * parts], refs[2 * parts :]
    attn, embed, left_held, held, found, attn_made, embed_made, sems, out_sems = refs
    shard, turn = where_ref[0], where_ref[1]
    rows = held.shape[1]

    def fetch_left(slot):
        for group in range(2):
            for place in range(4):

                @pl.when((turn == place) & ((shard ^ slot) == group))
                def _():
                    source = lefts[group][place].at[pl.ds(0, rows)]
                    pltpu.make_async_copy(source, left_held.at[slot], sems.at[5 + slot]).start()

    def pieces(slot, group, layer):
        copies, start = [], 0
        for part in group:
            size = part.shape[1]
            target = held.at[slot, pl.ds(start, size)]
            copies.append(pltpu.make_async_copy(part.at[layer], target, sems.at[slot]))
            start += size
        return copies

    layers = (0, 1, 2, 0, 2)
    found_copy = pltpu.make_async_copy(matches, found, sems.at[7])
    fetch_left(0)
    for slot, layer in enumerate(layers):
        for owner, group in enumerate((mine, others)):

            @pl.when((shard ^ owner) == (0 if slot < 3 else 1))
            def _():
                for copy in pieces(slot, group, layer):
                    copy.start()

    fetch_left(1)
    found_copy.start()

    def arrived(slot):
        pltpu.make_async_copy(held.at[slot], held.at[slot], sems.at[slot]).wait()
        return held[slot]

    def left_arrived(slot):
        target = left_held.at[slot]
        pltpu.make_async_copy(target, target, sems.at[5 + slot]).wait()

    results = []
    left_arrived(0)
    for slot in range(4):
        if slot == 3:
            left_arrived(1)
        attn_made[slot] = learning_rate * lax.dot_general(
            left_held[slot // 3],
            arrived(slot),
            (((1,), (1,)), ((), ())),
            preferred_element_type=jnp.float32,
        )
        results.append(
            pltpu.make_async_copy(attn_made.at[slot], attn.at[slot], out_sems.at[slot])
        )
        results[-1].start()
    right = arrived(4)
    found_copy.wait()
    part = found.shape[1] // 4
    for index in range(4):
        cols = pl.ds(index * part, part)
        product = jnp.dot(right, found[:, cols], preferred_element_type=jnp.float32)
        embed_made[:, cols] = product * scale[:, cols]
        results.append(
            pltpu.make_async_copy(
                embed_made.at[:, cols], embed.at[:, cols], out_sems.at[4 + index]
            )
        )
        results[-1].start()
    for result in results:
        result.wait()


def output_products(where, scale, matches, lefts, mine, others):
    parts = len(mine)
    cols, tokens_all = sum(part.shape[1] for part in mine), mine[0].shape[2]
    vocab_block = scale.shape[1]
    anywhere = pl.BlockSpec(memory_space=pl.ANY)
    return pl.pallas_call(
        functools.partial(output_kernel, parts=parts),
        in_specs=[
            pl.BlockSpec(memory_space=pltpu.SMEM),
            pl.BlockSpec(memory_space=pltpu.VMEM),
        ]
        + [anywhere] * (9 + 2 * parts),
        out_specs=(anywhere, anywhere),
        out_shape=(
            jax.ShapeDtypeStruct((4, cols, cols), jnp.float32),
            jax.ShapeDtypeStruct((cols, vocab_block), jnp.float32),
        ),
        scratch_shapes=[
            pltpu.VMEM((2, cols, tokens_all), jnp.bfloat16),
            pltpu.VMEM((5, cols, tokens_all), jnp.bfloat16),
            pltpu.VMEM((tokens_all, vocab_block), jnp.bfloat16),
            pltpu.VMEM((4, cols, cols), jnp.float32),
            pltpu.VMEM((cols, vocab_block), jnp.float32),
            pltpu.SemaphoreType.DMA((8,)),
            pltpu.SemaphoreType.DMA((8,)),
        ],
        compiler_params=pltpu.CompilerParams(vmem_limit_bytes=60 * 1024 * 1024),
        cost_estimate=pl.CostEstimate(
            flops=2 * cols * tokens_all * (4 * cols + vocab_block),
            bytes_accessed=4 * cols * (4 * cols + vocab_block) + 14 * cols * tokens_all,
            transcendentals=0,
        ),
    )(where, scale, matches, *lefts[0], *lefts[1], *mine, *others)


def layer_plan(
    activations,
    router_grad,
    token_ids,
    norm_terms,
    old_factors,
    old_router_factor,
    old_norm_diag,
    old_embed_diag,
):
    n_tensor = lax.axis_size("tensor")
    n_section = lax.axis_size("section")
    n_shard = lax.axis_size("shard")
    shard = lax.axis_index("shard")
    layer = lax.axis_index("tensor")
    section = lax.axis_index("section")
    core = section % 2
    owned, row_block, col_block = old_factors.shape
    tokens = activations.shape[1]
    features_dev = activations.shape[2]
    tokens_all = tokens * n_shard
    weight = (1.0 - factor_decay) / tokens_all
    own_place = section ^ layer
    place = own_place.reshape(1)
    axes = ("shard", "tensor")

    def by_index(array, index, axis=0):
        return lax.dynamic_index_in_dim(array, index, axis, False)

    def held_by(layer_index):
        return lax.rem(layer_index + 1, owned)

    by_feature = jnp.swapaxes(activations, 1, 2)
    diagonals = local_diagonals(old_factors) * (layer == section).astype(jnp.float32)
    extra = jnp.pad(split_three(diagonals), ((0, 0), (0, 0), (0, 3 * tokens - col_block)))
    extra = jnp.pad(extra.reshape(owned, 9, tokens), ((0, 0), (0, 7), (0, 0)))
    collected = []
    for step in range(n_tensor):
        factor = held_by(layer ^ step)
        message = jnp.concatenate(
            [
                by_index(by_feature, shard * owned + factor),
                by_index(by_feature, (1 - shard) * owned + factor),
                by_index(extra, factor),
            ],
            axis=0,
        )
        collected.append(swap(message, "tensor", n_tensor, step) if step else message)
    collected = jnp.stack(collected)
    other_tokens = swap(
        collected[:, features_dev : 2 * features_dev], "shard", n_shard, 1
    )

    def both_shards(value, axis):
        other = swap(value, "shard", n_shard, 1)
        return jnp.where(
            shard == 0,
            jnp.concatenate([value, other], axis=axis),
            jnp.concatenate([other, value], axis=axis),
        )

    grad_all = both_shards(router_grad, 1)
    ids_all = both_shards(token_ids, 0)
    norm_values = norm_terms.astype(jnp.float32)
    norm_sums = jnp.stack([jnp.sum(norm_values, axis=1), jnp.sum(norm_values * norm_values, axis=1)])
    norm_sums = norm_sums + swap(norm_sums, "shard", n_shard, 1)
    vocab_block = old_embed_diag.shape[0]
    ids_here = layer * vocab_block + lax.iota(jnp.int32, vocab_block)
    matches = (ids_all[:, None] == ids_here[None, :]).astype(jnp.bfloat16)
    counts = jnp.sum(matches, axis=0, dtype=jnp.float32)
    divisor = factor_decay * old_embed_diag + (1.0 - factor_decay) * (counts / tokens_all) + damping
    embed_scale = (learning_rate / divisor)[None, :]
    router_matrix = (
        factor_decay * old_router_factor
        + weight * jnp.einsum("en,fn->ef", grad_all, grad_all, preferred_element_type=jnp.float32)
        + damping * jnp.eye(EXPERTS, dtype=jnp.float32)
    )
    router_inverse = local_inverse(router_matrix)
    router_right = jnp.einsum(
        "en,ef->fn", grad_all, router_inverse, preferred_element_type=jnp.float32
    ).astype(jnp.bfloat16)

    def old_block(factors, step):
        return by_index(factors, held_by(layer ^ step)).astype(jnp.bfloat16)

    early = swap(old_block(old_factors, 2), "tensor", n_tensor, 2)
    later_factors = lax.optimization_barrier(old_factors)
    blocks = [old_block(later_factors, step) for step in (0, 1, 3)]
    other_tokens, collected, early, blocks, small = lax.optimization_barrier(
        (other_tokens, collected, early, blocks, (router_right, matches, embed_scale, norm_sums))
    )
    router_right, matches, embed_scale, norm_sums = small
    collected = jnp.concatenate(
        [collected[:, :features_dev], other_tokens, collected[:, 2 * features_dev :]], axis=1
    )
    gathered = lax.all_gather(collected, "section", axis=0)
    blocks = [
        blocks[0],
        swap(blocks[1], "tensor", n_tensor, 1),
        early,
        swap(blocks[2], "tensor", n_tensor, 3),
    ]

    features, rows, low_diag, trace = lay_out(
        jnp.stack([own_place, layer, core]), gathered, weight
    )
    scale = D / (3.0 * trace)
    own_cols = [
        factor_block(place, features, blocks[step], low_diag, step, weight)
        for step in range(n_tensor)
    ]
    other_cols = [swap(block, "section", n_section, 1) for block in own_cols]
    cols = own_cols + other_cols

    wide = jax.ShapeDtypeStruct((2, tokens, col_block), jnp.float32)
    sent = jax.ShapeDtypeStruct((tokens, 2 * col_block), jnp.bfloat16)
    part = jax.ShapeDtypeStruct((col_block, tokens), jnp.bfloat16)
    scalars = (place, scale)
    kept, message = chain_call(first_kernel, scalars, (rows, low_diag), cols, (wide, sent))
    theirs = swap(message, "section", n_section, 2)
    kept, message = chain_call(
        second_kernel, scalars, (message, theirs, rows, low_diag, kept), cols, (wide, sent)
    )
    theirs = swap(message, "section", n_section, 2)
    keep, give = chain_call(third_kernel, scalars, (message, theirs, kept), cols, (part, part))
    got = swap(give, "section", n_section, 1)
    own = jnp.where(
        core == shard, jnp.concatenate([keep, got], axis=1), jnp.concatenate([got, keep], axis=1)
    )

    planes = range(n_shard)
    layers = range(n_tensor)
    everywhere = ("shard", "tensor", "section")

    def spot(x, z, s):
        return (x * n_tensor + z) * n_section + s

    def scatter(value, source):
        return lax.ppermute(
            value,
            everywhere,
            [(spot(x, source, s), spot(x, s, s)) for x in planes for s in layers if s != source],
        )

    def hand_round(value):
        sides = lax.ppermute(
            value, everywhere, [(spot(x, t, t), spot(x, t, t ^ 2)) for x in planes for t in layers]
        )
        near = lax.ppermute(
            value, everywhere, [(spot(x, t, t), spot(x, t, t ^ 1)) for x in planes for t in layers]
        )
        far = lax.ppermute(
            sides,
            everywhere,
            [(spot(x, t, t ^ 2), spot(x, t, t ^ 3)) for x in planes for t in layers],
        )
        return (value, near, sides, far)

    parts = 3
    size = col_block // parts
    mine = [
        lax.all_gather(own[part * size : (part + 1) * size], "tensor", axis=0)
        for part in range(parts)
    ]
    router_cols = learning_rate * jnp.einsum(
        "fn,cn->fc", router_right, own, preferred_element_type=jnp.float32
    )
    router_cols = jnp.where(layer == 1, router_cols, scatter(router_cols, 1))
    left_layer = n_tensor - 1
    left_here = left_message(layer == left_layer, own, scatter(own, left_layer), router_cols)
    left_here, mine[0] = lax.optimization_barrier((left_here, mine[0]))
    left_there = lax.ppermute(
        left_here, everywhere, [(spot(x, t, t), spot(1 - x, t, t)) for x in planes for t in layers]
    )
    lefts_here = hand_round(left_here)
    left_there, mine[1] = lax.optimization_barrier((left_there, mine[1]))
    lefts_there = hand_round(left_there)
    others = [swap(piece[: n_tensor - 1], "shard", n_shard, 1) for piece in mine]
    turn = section ^ layer

    def codes_of(group):
        found = [part[col_block:] for part in group]
        chosen = found[3]
        for index in (2, 1, 0):
            chosen = jnp.where(turn == index, found[index], chosen)
        return chosen

    codes = jnp.where(shard == 1, codes_of(lefts_here), codes_of(lefts_there))
    codes = jnp.concatenate(
        [codes[: 2 * EXPERTS], codes[2 * EXPERTS :, : col_block - tokens_all]], axis=1
    ).astype(jnp.float32)
    precond_router = codes[:EXPERTS] + codes[EXPERTS:]

    precond_attn, embed_columns = output_products(
        jnp.stack([shard, turn]), embed_scale, matches, (lefts_here, lefts_there), mine, others
    )
    precond_embed = embed_columns.T

    precond_norms = (
        learning_rate
        * norm_sums[0]
        / (
            factor_decay * old_norm_diag
            + (1.0 - factor_decay) * (norm_sums[1] / tokens_all)
            + damping
        )
    )
    return (precond_attn, precond_router, precond_norms, precond_embed)


def per_device(*arguments):
    one_each = arguments[4].shape[0] == lax.axis_size("tensor") == lax.axis_size("section")
    if one_each and lax.axis_size("section") == 4 and lax.axis_size("shard") == 2:
        return layer_plan(*arguments)
    return general_plan(*arguments)


def solution(mesh):
    return jax.shard_map(
        per_device,
        mesh=mesh,
        in_specs=(
            P(None, "shard", ("tensor", "section")),
            P(None, "shard"),
            P("shard"),
            P(None, "shard", ("tensor", "section")),
            P("shard", "tensor", "section"),
            P(),
            P(None, ("tensor", "section")),
            P("tensor"),
        ),
        out_specs=(
            P(None, "tensor", "section"),
            P(None, "tensor"),
            P(None, ("tensor", "section")),
            P("tensor", "section"),
        ),
        check_vma=False,
    )
```

```python
import functools
import math

import jax
import jax.numpy as jnp
from jax import lax
from jax.experimental import pallas as pl
from jax.experimental.pallas import tpu as pltpu
from jax.sharding import PartitionSpec as P

D = 2304
EXPERTS = 8
VOCAB = 8192


factor_decay = 0.5
damping = 0.01
learning_rate = 0.05


def local_inverse(matrix):
    width = matrix.shape[0]
    trace = jnp.sum(jnp.diagonal(matrix))
    factor_scale = width / (3.0 * trace)
    identity = jnp.eye(width, dtype=jnp.float32)
    matrix_low = lax.optimization_barrier(matrix.astype(jnp.bfloat16))
    first = 2.0 * factor_scale * identity - factor_scale * factor_scale * matrix_low.astype(
        jnp.float32
    )
    first_low = first.astype(jnp.bfloat16)
    image = jnp.dot(matrix_low, first_low, preferred_element_type=jnp.float32).astype(jnp.bfloat16)
    product = jnp.dot(first_low, image, preferred_element_type=jnp.float32)
    return (2.0 * first - product).astype(jnp.bfloat16)


def fold_with(columns, piece):
    return jnp.einsum("kij,kjl->kil", piece, columns, preferred_element_type=jnp.float32)


def general_plan(
    activations,
    router_grad,
    token_ids,
    norm_terms,
    old_factors,
    old_router_factor,
    old_norm_diag,
    old_embed_diag,
):
    n_tensor = lax.axis_size("tensor")
    n_section = lax.axis_size("section")
    n_shard = lax.axis_size("shard")
    tensor_rank = lax.axis_index("tensor")
    section_rank = lax.axis_index("section")
    row_block = D // n_tensor
    col_block = D // n_section
    tokens_all = activations.shape[1] * n_shard
    row_start = tensor_rank * row_block
    col_start = section_rank * col_block

    def collect(carry, piece):
        whole = lax.all_gather(piece, ("tensor", "section"), axis=1, tiled=True)
        rows_part = lax.dynamic_slice_in_dim(whole, row_start, row_block, 1)
        cols_part = lax.dynamic_slice_in_dim(whole, col_start, col_block, 1)
        return (carry, (rows_part, cols_part))

    unused_carry, (row_parts, col_parts) = lax.scan(collect, jnp.int32(0), activations)
    partial_value = jnp.einsum(
        "mnr,mnc->mrc", row_parts, col_parts, preferred_element_type=jnp.float32
    )
    fresh = lax.psum_scatter(partial_value, "shard", scatter_dimension=0, tiled=True) / tokens_all
    row_index = lax.broadcasted_iota(jnp.int32, (row_block, col_block), 0) + row_start
    col_index = lax.broadcasted_iota(jnp.int32, (row_block, col_block), 1) + col_start
    eye_block = (row_index == col_index).astype(jnp.float32)
    matrix = factor_decay * old_factors + (1.0 - factor_decay) * fresh + damping * eye_block
    diag_part = jnp.sum(matrix * eye_block, axis=(1, 2))
    trace = lax.psum(diag_part, ("tensor", "section"))
    factor_scale = (D / (3.0 * trace))[:, None, None]
    matrix_low = lax.optimization_barrier(matrix.astype(jnp.bfloat16))
    first = 2.0 * factor_scale * eye_block - factor_scale * factor_scale * matrix_low.astype(
        jnp.float32
    )
    first_low = first.astype(jnp.bfloat16)
    first_cols = lax.all_gather(first_low, "tensor", axis=1, tiled=True)
    image = fold_with(first_cols, lax.all_gather(matrix_low, "section", axis=2, tiled=True))
    image_cols = lax.all_gather(image.astype(jnp.bfloat16), "tensor", axis=1, tiled=True)
    product = fold_with(image_cols, lax.all_gather(first_low, "section", axis=2, tiled=True))
    inverse_low = (2.0 * first - product).astype(jnp.bfloat16)
    inverses = lax.all_gather(inverse_low, "shard", axis=0, tiled=True)
    left_terms = jnp.stack(
        [
            jnp.einsum("nc,rc->nr", col_parts[m], inverses[m], preferred_element_type=jnp.float32)
            for m in (0, 4, 6)
        ]
    )
    left = lax.psum(left_terms, "section").astype(jnp.bfloat16)
    right_terms = jnp.stack(
        [
            jnp.einsum("nr,rc->nc", row_parts[m], inverses[m], preferred_element_type=jnp.float32)
            for m in (1, 2, 3, 5, 7)
        ]
    )
    right = lax.psum(right_terms, "tensor").astype(jnp.bfloat16)
    norm_values = norm_terms.astype(jnp.float32)
    router_part = jnp.einsum(
        "en,fn->ef", router_grad, router_grad, preferred_element_type=jnp.float32
    )
    router_sum, norm_total, norm_squares = lax.psum(
        (router_part, jnp.sum(norm_values, axis=1), jnp.sum(norm_values * norm_values, axis=1)),
        "shard",
    )
    router_matrix = (
        factor_decay * old_router_factor
        + (1.0 - factor_decay) * (router_sum / tokens_all)
        + damping * jnp.eye(EXPERTS, dtype=jnp.float32)
    )
    router_inverse = local_inverse(router_matrix)
    router_right = jnp.einsum(
        "en,ef->nf", router_grad, router_inverse, preferred_element_type=jnp.float32
    ).astype(jnp.bfloat16)
    precond_norms = (
        learning_rate
        * norm_total
        / (
            factor_decay * old_norm_diag
            + (1.0 - factor_decay) * (norm_squares / tokens_all)
            + damping
        )
    )
    ids_all = lax.all_gather(token_ids, "shard", axis=0, tiled=True)
    embed_all = lax.all_gather(right[4], "shard", axis=0, tiled=True)
    paired_left = jnp.stack([left[0], left[0], left[0], left[1]])
    attn_terms = jnp.einsum(
        "wnr,wnc->wrc", paired_left, right[:4], preferred_element_type=jnp.float32
    )
    router_term = jnp.einsum("nf,nr->fr", router_right, left[2], preferred_element_type=jnp.float32)
    attn_sum, router_total = lax.psum((attn_terms, router_term), "shard")
    precond_attn = learning_rate * attn_sum
    precond_router = learning_rate * router_total
    vocab_block = VOCAB // n_tensor
    step_rows = math.gcd(vocab_block, 512)
    vocab_start = tensor_rank * vocab_block

    def embed_block(block_index):
        ids_here = vocab_start + block_index * step_rows + lax.iota(jnp.int32, step_rows)
        onehot = (ids_here[:, None] == ids_all[None, :]).astype(jnp.bfloat16)
        summed = jnp.dot(onehot, embed_all, preferred_element_type=jnp.float32)
        tallies = jnp.sum(onehot, axis=1, dtype=jnp.float32)
        return (summed, tallies)

    block_sums, block_counts = lax.map(
        embed_block, jnp.arange(vocab_block // step_rows, dtype=jnp.int32)
    )
    embed_sum = block_sums.reshape(vocab_block, col_block)
    counts = block_counts.reshape(vocab_block)
    divisor = factor_decay * old_embed_diag + (1.0 - factor_decay) * (counts / tokens_all) + damping
    precond_embed = learning_rate * embed_sum / divisor[:, None]
    return (precond_attn, precond_router, precond_norms, precond_embed)


def split_three(values):
    high = lax.reduce_precision(values, 8, 7)
    rest = values - high
    middle = lax.reduce_precision(rest, 8, 7)
    return jnp.stack([high, middle, rest - middle], axis=-2).astype(jnp.bfloat16)


def swap(value, axis, size, step):
    return lax.ppermute(value, axis, [(i, i ^ step) for i in range(size)])


def local_diagonals(blocks):
    width = blocks.shape[1]
    pieces = []
    for start in range(0, width, 128):
        size = min(128, width - start)
        tile = blocks[:, start : start + size, start : start + size]
        pieces.append(jnp.sum(tile * jnp.eye(size, dtype=tile.dtype), axis=1))
    return jnp.concatenate(pieces, axis=1)


def rounded(values):
    return values.astype(jnp.bfloat16).astype(jnp.float32)


def params():
    return pltpu.CompilerParams(vmem_limit_bytes=40 * 1024 * 1024)


def layout_kernel(place_ref, *refs, weight):
    gathered, (features, rows, low_diag, trace, old) = refs[:4], refs[4:]
    own_place, layer, core, here = (place_ref[index] for index in range(4))
    steps, _, tokens = gathered[0].shape
    sections = len(gathered)
    groups, depth, _ = features.shape
    part = depth // (sections * steps)
    width = depth // steps
    for away in range(sections):
        section = here ^ away
        codes = jnp.zeros((16, tokens), jnp.float32)
        for step in range(steps):
            start = pl.multiple_of((step * sections + section) * part, 16)
            for group in range(groups):
                features[group, pl.ds(start, part)] = gathered[away][
                    step, group * part : (group + 1) * part
                ]
            codes += gathered[away][step, groups * part :].astype(jnp.float32)
        codes = codes[0:3] + codes[3:6] + codes[6:9]
        pieces = [codes[0:1], codes[1:2], codes[2:3, : width - 2 * tokens]]
        old[section ^ layer] = jnp.concatenate(pieces, axis=1)
    ones = jnp.ones((8, tokens), jnp.bfloat16)
    total = jnp.float32(0.0)
    for step in range(steps):
        squares = jnp.zeros((8, width), jnp.float32)
        for group in range(groups):
            values = features[group, step * width : (step + 1) * width].astype(jnp.float32)
            values = values * values
            high = values.astype(jnp.bfloat16)
            low = (values - high.astype(jnp.float32)).astype(jnp.bfloat16)
            for piece in (high, low):
                squares += lax.dot_general(
                    ones, piece, (((1,), (1,)), ((), ())), preferred_element_type=jnp.float32
                )
        diag = factor_decay * old[step] + weight * squares[0:1] + damping
        total += jnp.sum(diag)
        low_diag[step] = rounded(diag)
        start = pl.multiple_of((own_place ^ step) * width, width)
        mine = features[core, pl.ds(start, width)]
        rows[:, step * width : (step + 1) * width] = mine.T
    trace[0] = total


def lay_out(places, gathered, weight):
    steps, height, tokens = gathered[0].shape
    sections = len(gathered)
    part = (height - 16) // 2
    depth = sections * steps * part
    width = depth // steps
    vmem = pl.BlockSpec(memory_space=pltpu.VMEM)
    smem = pl.BlockSpec(memory_space=pltpu.SMEM)
    return pl.pallas_call(
        functools.partial(layout_kernel, weight=weight),
        in_specs=[smem] + [vmem] * sections,
        out_specs=[vmem, vmem, vmem, smem],
        out_shape=[
            jax.ShapeDtypeStruct((2, depth, tokens), jnp.bfloat16),
            jax.ShapeDtypeStruct((tokens, depth), jnp.bfloat16),
            jax.ShapeDtypeStruct((steps, 1, width), jnp.float32),
            jax.ShapeDtypeStruct((1,), jnp.float32),
        ],
        scratch_shapes=[pltpu.VMEM((steps, 1, width), jnp.float32)],
        compiler_params=params(),
        cost_estimate=pl.CostEstimate(
            flops=64 * depth * tokens, bytes_accessed=14 * depth * tokens, transcendentals=0
        ),
    )(places, *gathered)


def factor_kernel(place_ref, part, own, old, diag, out, *, step, weight):
    fresh = jnp.zeros(out.shape, jnp.float32)
    for index in range(part.shape[0]):
        fresh += lax.dot_general(
            part[index], own[index], (((1,), (1,)), ((), ())), preferred_element_type=jnp.float32
        )
    block = factor_decay * old[...].astype(jnp.float32) + weight * fresh
    on_diag = lax.broadcasted_iota(jnp.int32, out.shape, 0) == lax.broadcasted_iota(
        jnp.int32, out.shape, 1
    )
    block = jnp.where(on_diag & (place_ref[0] == step), diag[0], block)
    out[...] = block.astype(jnp.bfloat16)


def factor_block(place, features, old, diag, step, weight):
    groups, _, tokens = features.shape
    rows, cols = old.shape
    return pl.pallas_call(
        functools.partial(factor_kernel, step=step, weight=weight),
        grid_spec=pltpu.PrefetchScalarGridSpec(
            num_scalar_prefetch=1,
            grid=(1,),
            in_specs=[
                pl.BlockSpec((groups, rows, tokens), lambda i, place: (0, step, 0)),
                pl.BlockSpec((groups, cols, tokens), lambda i, place: (0, place[0], 0)),
                pl.BlockSpec((rows, cols), lambda i, place: (0, 0)),
                pl.BlockSpec((1, 1, cols), lambda i, place: (place[0], 0, 0)),
            ],
            out_specs=pl.BlockSpec((rows, cols), lambda i, place: (0, 0)),
        ),
        out_shape=jax.ShapeDtypeStruct((rows, cols), jnp.bfloat16),
        compiler_params=params(),
        cost_estimate=pl.CostEstimate(
            flops=2 * groups * rows * cols * tokens,
            bytes_accessed=4 * rows * cols + 4 * groups * rows * tokens,
            transcendentals=0,
        ),
    )(place, features, features, old, diag)


def fetch_blocks(place_ref, blocks, held, sems):
    count = len(blocks) // 2
    depth = blocks[0].shape[0]
    copies = []
    for index in range(2 * count):
        slot = pl.multiple_of((place_ref[0] ^ (index % count)) * depth, depth)
        copies.append(
            pltpu.make_async_copy(
                blocks[index], held.at[index // count, pl.ds(slot, depth)], sems.at[index]
            )
        )
    for copy in copies:
        copy.start()
    return copies


def block_products(mine, theirs, held):
    rows = jnp.concatenate([mine[...], theirs[...]], axis=1)
    return [jnp.dot(rows, held[index], preferred_element_type=jnp.float32) for index in range(2)]


def first_parts(place_ref, scale, rows, diag, product, index):
    width = product.shape[1]
    square = scale * scale
    values = rows[:, index * width : (index + 1) * width].astype(jnp.float32)
    low_diag = diag[place_ref[0] ^ index]
    first_diag = rounded(2.0 * scale - square * low_diag)
    by_first = 2.0 * scale * values - square * product
    step_one = first_diag * values - square * (product - low_diag * values)
    return by_first, step_one, low_diag, first_diag


def first_kernel(place_ref, scale_ref, rows, diag, *refs):
    blocks, (kept, message, held, sems) = refs[:8], refs[8:]
    copies = fetch_blocks(place_ref, blocks, held, sems)
    products = []
    for index in range(2):
        for copy in copies[index * 4 : (index + 1) * 4]:
            copy.wait()
        products.append(jnp.dot(rows[...], held[index], preferred_element_type=jnp.float32))
    lows = []
    for index in range(2):
        kept[index] = products[index]
        parts = first_parts(place_ref, scale_ref[0], rows, diag, products[index], index)
        lows.append(parts[1].astype(jnp.bfloat16))
    message[...] = jnp.concatenate(lows, axis=1)


def second_kernel(
    place_ref, scale_ref, mine, theirs, rows, diag, before, held, kept, message
):
    products = block_products(mine, theirs, held)
    square = scale_ref[0] * scale_ref[0]
    lows = []
    for index in range(2):
        by_first, one, low_diag, first_diag = first_parts(
            place_ref, scale_ref[0], rows, diag, before[index], index
        )
        two = products[index] + low_diag * (one - rounded(one))
        low = two.astype(jnp.bfloat16)
        kept[index] = (
            2.0 * by_first - first_diag * two - square * low_diag * low.astype(jnp.float32)
        )
        lows.append(low)
    message[...] = jnp.concatenate(lows, axis=1)


def third_kernel(place_ref, scale_ref, mine, theirs, before, held, keep, give):
    products = block_products(mine, theirs, held)
    square = scale_ref[0] * scale_ref[0]
    for index, out in ((0, keep), (1, give)):
        out[...] = (before[index] + square * products[index]).T.astype(jnp.bfloat16)


def chain_call(kernel, scalars, arrays, blocks, out_shape):
    tokens = arrays[0].shape[0]
    vmem = pl.BlockSpec(memory_space=pltpu.VMEM)
    scratch = [pltpu.SemaphoreType.DMA((len(blocks),))] if blocks else []
    return pl.pallas_call(
        kernel,
        in_specs=[pl.BlockSpec(memory_space=pltpu.SMEM)] * len(scalars)
        + [vmem] * len(arrays)
        + [pl.BlockSpec(memory_space=pl.ANY)] * len(blocks),
        out_specs=[vmem] * len(out_shape),
        out_shape=out_shape,
        scratch_shapes=scratch,
        compiler_params=params(),
        cost_estimate=pl.CostEstimate(
            flops=2 * tokens * D * D, bytes_accessed=2 * D * D, transcendentals=0
        ),
    )(*scalars, *arrays, *blocks)


def output_kernel(where_ref, scale, matches, *refs):
    lefts, mine, others = (refs[:4], refs[4:8]), refs[8:12], refs[12:16]
    attn, embed = refs[16:18]
    left_held, held, found, attn_made, embed_made, sems, out_sems = refs[18:]
    shard, layer, turn = where_ref[0], where_ref[1], where_ref[2]
    first = shard == 0
    rows, tokens_all = held.shape[1:]

    found_copy = pltpu.make_async_copy(matches, found, sems.at[7])
    for slot in range(2):
        for group in range(2):
            for place in range(4):

                @pl.when((turn == place) & (((shard ^ slot) == group)))
                def _():
                    source = lefts[group][place].at[pl.ds(0, rows)]
                    pltpu.make_async_copy(source, left_held.at[slot], sems.at[5 + slot]).start()

        if slot == 0:
            for index, source in enumerate((0, 1, 3, 0, 3)):
                from_mine = first if index < 3 else jnp.logical_not(first)
                for place in range(4):
                    for group, wanted in ((mine, from_mine), (others, jnp.logical_not(from_mine))):

                        @pl.when(wanted & ((layer ^ source) == place))
                        def _():
                            pltpu.make_async_copy(
                                group[place], held.at[index], sems.at[index]
                            ).start()

            found_copy.start()

    def arrived(slot):
        target = held.at[slot] if slot < 5 else left_held.at[slot - 5]
        pltpu.make_async_copy(mine[0], target, sems.at[slot]).wait()

    results = []
    arrived(5)
    for slot in range(4):
        if slot == 3:
            arrived(6)
        arrived(slot)
        attn_made[slot] = learning_rate * lax.dot_general(
            left_held[slot // 3],
            held[slot],
            (((1,), (1,)), ((), ())),
            preferred_element_type=jnp.float32,
        )
        results.append(
            pltpu.make_async_copy(attn_made.at[slot], attn.at[slot], out_sems.at[slot])
        )
        results[-1].start()
    arrived(4)
    found_copy.wait()
    part = found.shape[1] // 4
    for index in range(4):
        cols = pl.ds(index * part, part)
        product = jnp.dot(held[4], found[:, cols], preferred_element_type=jnp.float32)
        embed_made[:, cols] = product * scale[:, cols]
        results.append(
            pltpu.make_async_copy(
                embed_made.at[:, cols], embed.at[:, cols], out_sems.at[4 + index]
            )
        )
        results[-1].start()
    for result in results:
        result.wait()


def output_products(where, scale, matches, lefts, mine, others):
    cols, tokens_all = mine[0].shape
    vocab_block = scale.shape[1]
    anywhere = pl.BlockSpec(memory_space=pl.ANY)
    return pl.pallas_call(
        output_kernel,
        in_specs=[
            pl.BlockSpec(memory_space=pltpu.SMEM),
            pl.BlockSpec(memory_space=pltpu.VMEM),
        ]
        + [anywhere] * 17,
        out_specs=(anywhere, anywhere),
        out_shape=(
            jax.ShapeDtypeStruct((4, cols, cols), jnp.float32),
            jax.ShapeDtypeStruct((cols, vocab_block), jnp.float32),
        ),
        scratch_shapes=[
            pltpu.VMEM((2, cols, tokens_all), jnp.bfloat16),
            pltpu.VMEM((5, cols, tokens_all), jnp.bfloat16),
            pltpu.VMEM((tokens_all, vocab_block), jnp.bfloat16),
            pltpu.VMEM((4, cols, cols), jnp.float32),
            pltpu.VMEM((cols, vocab_block), jnp.float32),
            pltpu.SemaphoreType.DMA((8,)),
            pltpu.SemaphoreType.DMA((8,)),
        ],
        compiler_params=pltpu.CompilerParams(vmem_limit_bytes=60 * 1024 * 1024),
        cost_estimate=pl.CostEstimate(
            flops=2 * cols * tokens_all * (4 * cols + vocab_block),
            bytes_accessed=4 * cols * (4 * cols + vocab_block) + 14 * cols * tokens_all,
            transcendentals=0,
        ),
    )(where, scale, matches, *lefts[0], *lefts[1], *mine, *others)


def layer_plan(
    activations,
    router_grad,
    token_ids,
    norm_terms,
    old_factors,
    old_router_factor,
    old_norm_diag,
    old_embed_diag,
):
    n_tensor = lax.axis_size("tensor")
    n_section = lax.axis_size("section")
    n_shard = lax.axis_size("shard")
    shard = lax.axis_index("shard")
    layer = lax.axis_index("tensor")
    section = lax.axis_index("section")
    core = section % 2
    owned, row_block, col_block = old_factors.shape
    tokens = activations.shape[1]
    features_dev = activations.shape[2]
    tokens_all = tokens * n_shard
    weight = (1.0 - factor_decay) / tokens_all
    own_place = section ^ layer
    place = own_place.reshape(1)
    axes = ("shard", "tensor")

    def by_index(array, index, axis=0):
        return lax.dynamic_index_in_dim(array, index, axis, False)

    def held_by(layer_index):
        return jnp.where(layer_index == 3, 3, lax.rem(layer_index + 1, 3))

    by_feature = jnp.swapaxes(activations, 1, 2)
    diagonals = local_diagonals(old_factors) * (layer == section).astype(jnp.float32)
    extra = jnp.pad(split_three(diagonals), ((0, 0), (0, 0), (0, 3 * tokens - col_block)))
    extra = jnp.pad(extra.reshape(owned, 9, tokens), ((0, 0), (0, 7), (0, 0)))
    collected = []
    for step in range(n_tensor):
        factor = held_by(layer ^ step)
        message = jnp.concatenate(
            [
                by_index(by_feature, shard * owned + factor),
                by_index(by_feature, (1 - shard) * owned + factor),
                by_index(extra, factor),
            ],
            axis=0,
        )
        collected.append(swap(message, "tensor", n_tensor, step) if step else message)
    collected = jnp.stack(collected)
    other_tokens = swap(
        collected[:, features_dev : 2 * features_dev], "shard", n_shard, 1
    )

    def both_shards(value, axis):
        other = swap(value, "shard", n_shard, 1)
        return jnp.where(
            shard == 0,
            jnp.concatenate([value, other], axis=axis),
            jnp.concatenate([other, value], axis=axis),
        )

    grad_all = both_shards(router_grad, 1)
    ids_all = both_shards(token_ids, 0)
    norm_values = norm_terms.astype(jnp.float32)
    norm_sums = jnp.stack([jnp.sum(norm_values, axis=1), jnp.sum(norm_values * norm_values, axis=1)])
    norm_sums = norm_sums + swap(norm_sums, "shard", n_shard, 1)
    vocab_block = old_embed_diag.shape[0]
    ids_here = layer * vocab_block + lax.iota(jnp.int32, vocab_block)
    matches = (ids_all[:, None] == ids_here[None, :]).astype(jnp.bfloat16)
    counts = jnp.sum(matches, axis=0, dtype=jnp.float32)
    divisor = factor_decay * old_embed_diag + (1.0 - factor_decay) * (counts / tokens_all) + damping
    embed_scale = (learning_rate / divisor)[None, :]
    router_matrix = (
        factor_decay * old_router_factor
        + weight * jnp.einsum("en,fn->ef", grad_all, grad_all, preferred_element_type=jnp.float32)
        + damping * jnp.eye(EXPERTS, dtype=jnp.float32)
    )
    router_inverse = local_inverse(router_matrix)
    router_right = jnp.einsum(
        "en,ef->fn", grad_all, router_inverse, preferred_element_type=jnp.float32
    ).astype(jnp.bfloat16)

    part_rows = row_block // 2

    def old_block(factors, step):
        return by_index(factors, held_by(layer ^ step)).astype(jnp.bfloat16)

    early = swap(old_block(old_factors, 2), "tensor", n_tensor, 2)
    later_factors = lax.optimization_barrier(old_factors)
    far_block = old_block(later_factors, 3)
    early_far = swap(far_block[:part_rows], "tensor", n_tensor, 3)
    blocks = [old_block(later_factors, 0), old_block(later_factors, 1), far_block[part_rows:]]
    other_tokens, collected, early, early_far, blocks, small = lax.optimization_barrier(
        (
            other_tokens,
            collected,
            early,
            early_far,
            blocks,
            (router_right, matches, embed_scale, norm_sums),
        )
    )
    router_right, matches, embed_scale, norm_sums = small
    collected = jnp.concatenate(
        [collected[:, :features_dev], other_tokens, collected[:, 2 * features_dev :]], axis=1
    )
    by_side = swap(collected, "section", n_section, 2)
    by_core = swap(collected, "section", n_section, 1)
    late_far = swap(blocks[2], "tensor", n_tensor, 3)
    blocks = [blocks[0], swap(blocks[1], "tensor", n_tensor, 1), early]
    by_side, late_far, blocks[1] = lax.optimization_barrier((by_side, late_far, blocks[1]))
    by_both = swap(by_side, "section", n_section, 1)

    features, rows, low_diag, trace = lay_out(
        jnp.stack([own_place, layer, core, section]),
        (collected, by_core, by_side, by_both),
        weight,
    )
    scale = D / (3.0 * trace)
    early_far, features = lax.optimization_barrier((early_far, features))
    blocks.append(jnp.concatenate([early_far, late_far], axis=0))

    own_cols = [
        factor_block(place, features, blocks[step], low_diag, step, weight)
        for step in range(n_tensor)
    ]
    other_cols = [swap(block, "section", n_section, 1) for block in own_cols]
    cols = own_cols + other_cols

    wide = jax.ShapeDtypeStruct((2, tokens, col_block), jnp.float32)
    sent = jax.ShapeDtypeStruct((tokens, 2 * col_block), jnp.bfloat16)
    part = jax.ShapeDtypeStruct((col_block, tokens), jnp.bfloat16)
    scalars = (place, scale)
    columns = jax.ShapeDtypeStruct((2, D, col_block), jnp.bfloat16)
    kept, message, held = chain_call(
        first_kernel, scalars, (rows, low_diag), cols, (wide, sent, columns)
    )
    theirs = swap(message, "section", n_section, 2)
    kept, message = chain_call(
        second_kernel, scalars, (message, theirs, rows, low_diag, kept, held), (), (wide, sent)
    )
    theirs = swap(message, "section", n_section, 2)
    keep, give = chain_call(
        third_kernel, scalars, (message, theirs, kept, held), (), (part, part)
    )
    got = swap(give, "section", n_section, 1)
    own = jnp.where(
        core == shard, jnp.concatenate([keep, got], axis=1), jnp.concatenate([got, keep], axis=1)
    )

    planes = range(n_shard)
    layers = range(n_tensor)

    def useful(x, z):
        return z != 2 and (x, z) != (1, 1)

    def send(value, step, held):
        moves = [
            (x * n_tensor + z, x * n_tensor + (z ^ step))
            for x in planes
            for z in layers
            if useful(x, z ^ held)
        ]
        return lax.ppermute(value, axes, moves)

    def across(value, held):
        moves = [
            (x * n_tensor + z, (1 - x) * n_tensor + z)
            for x in planes
            for z in layers
            if useful(x, z ^ held)
        ]
        return lax.ppermute(value, axes, moves)

    everywhere = ("shard", "tensor", "section")

    def spot(x, z, s):
        return (x * n_tensor + z) * n_section + s

    def scatter(value, source):
        moved_here = lax.ppermute(
            value,
            everywhere,
            [(spot(x, source, s), spot(x, s, s)) for x in planes for s in layers if s != source],
        )
        return jnp.where(layer == source, value, moved_here)

    def hand_round(value, *ahead):
        sides = lax.ppermute(
            value, everywhere, [(spot(x, t, t), spot(x, t, t ^ 2)) for x in planes for t in layers]
        )
        sides, *ahead = lax.optimization_barrier((sides, *ahead))
        near = lax.ppermute(
            value, everywhere, [(spot(x, t, t), spot(x, t, t ^ 1)) for x in planes for t in layers]
        )
        far = lax.ppermute(
            sides,
            everywhere,
            [(spot(x, t, t ^ 2), spot(x, t, t ^ 3)) for x in planes for t in layers],
        )
        return (value, near, sides, far), *ahead

    near_1 = send(own, 1, 0)
    near_2 = send(own, 2, 0)
    over_0 = across(own, 0)
    left_here = scatter(own, 2)
    near_1, own = lax.optimization_barrier((near_1, own))
    over_1 = across(near_1, 1)
    router_cols = learning_rate * jnp.einsum(
        "fn,cn->fc", router_right, own, preferred_element_type=jnp.float32
    )
    router_cols = scatter(router_cols, 1)
    router_high = lax.reduce_precision(router_cols, 8, 7)
    codes = jnp.concatenate([router_high, router_cols - router_high], axis=0).astype(jnp.bfloat16)
    codes_tail = jnp.pad(codes[:, tokens_all:], ((0, 0), (0, 2 * tokens_all - col_block)))
    left_here = jnp.concatenate([left_here, codes[:, :tokens_all], codes_tail], axis=0)
    left_here, near_2, over_0, over_1 = lax.optimization_barrier(
        (left_here, near_2, over_0, over_1)
    )
    near_3 = send(near_2, 1, 2)
    over_2 = across(near_2, 2)
    left_there = lax.ppermute(
        left_here, everywhere, [(spot(x, t, t), spot(1 - x, t, t)) for x in planes for t in layers]
    )
    (lefts_here,) = hand_round(left_here)
    left_there, near_3, over_2 = lax.optimization_barrier((left_there, near_3, over_2))
    over_3 = across(near_3, 3)
    lefts_there, over_3 = hand_round(left_there, over_3)
    turn = section ^ layer

    def codes_of(group):
        parts = [part[col_block:] for part in group]
        chosen = parts[3]
        for index in (2, 1, 0):
            chosen = jnp.where(turn == index, parts[index], chosen)
        return chosen

    codes = jnp.where(shard == 1, codes_of(lefts_here), codes_of(lefts_there))
    codes = jnp.concatenate(
        [codes[: 2 * EXPERTS], codes[2 * EXPERTS :, : col_block - tokens_all]], axis=1
    ).astype(jnp.float32)
    precond_router = codes[:EXPERTS] + codes[EXPERTS:]

    precond_attn, embed_columns = output_products(
        jnp.stack([shard, layer, turn]),
        embed_scale,
        matches,
        (lefts_here, lefts_there),
        (own, near_1, near_2, near_3),
        (over_0, over_1, over_2, over_3),
    )
    precond_embed = embed_columns.T

    precond_norms = (
        learning_rate
        * norm_sums[0]
        / (
            factor_decay * old_norm_diag
            + (1.0 - factor_decay) * (norm_sums[1] / tokens_all)
            + damping
        )
    )
    return (precond_attn, precond_router, precond_norms, precond_embed)


def per_device(*arguments):
    one_each = arguments[4].shape[0] == lax.axis_size("tensor") == lax.axis_size("section")
    if one_each and lax.axis_size("section") == 4 and lax.axis_size("shard") == 2:
        return layer_plan(*arguments)
    return general_plan(*arguments)


def solution(mesh):
    return jax.shard_map(
        per_device,
        mesh=mesh,
        in_specs=(
            P(None, "shard", ("tensor", "section")),
            P(None, "shard"),
            P("shard"),
            P(None, "shard", ("tensor", "section")),
            P("shard", "tensor", "section"),
            P(),
            P(None, ("tensor", "section")),
            P("tensor"),
        ),
        out_specs=(
            P(None, "tensor", "section"),
            P(None, "tensor"),
            P(None, ("tensor", "section")),
            P("tensor", "section"),
        ),
        check_vma=False,
    )
```

```python
import functools
import math

import jax
import jax.numpy as jnp
from jax import lax
from jax.experimental import pallas as pl
from jax.experimental.pallas import tpu as pltpu
from jax.sharding import PartitionSpec as P

D = 2304
EXPERTS = 8
VOCAB = 8192


factor_decay = 0.5
damping = 0.01
learning_rate = 0.05


def local_inverse(matrix):
    width = matrix.shape[0]
    trace = jnp.sum(jnp.diagonal(matrix))
    factor_scale = width / (3.0 * trace)
    identity = jnp.eye(width, dtype=jnp.float32)
    matrix_low = lax.optimization_barrier(matrix.astype(jnp.bfloat16))
    first = 2.0 * factor_scale * identity - factor_scale * factor_scale * matrix_low.astype(
        jnp.float32
    )
    first_low = first.astype(jnp.bfloat16)
    image = jnp.dot(matrix_low, first_low, preferred_element_type=jnp.float32).astype(jnp.bfloat16)
    product = jnp.dot(first_low, image, preferred_element_type=jnp.float32)
    return (2.0 * first - product).astype(jnp.bfloat16)


def fold_with(columns, piece):
    return jnp.einsum("kij,kjl->kil", piece, columns, preferred_element_type=jnp.float32)


def general_plan(
    activations,
    router_grad,
    token_ids,
    norm_terms,
    old_factors,
    old_router_factor,
    old_norm_diag,
    old_embed_diag,
):
    n_tensor = lax.axis_size("tensor")
    n_section = lax.axis_size("section")
    n_shard = lax.axis_size("shard")
    tensor_rank = lax.axis_index("tensor")
    section_rank = lax.axis_index("section")
    row_block = D // n_tensor
    col_block = D // n_section
    tokens_all = activations.shape[1] * n_shard
    row_start = tensor_rank * row_block
    col_start = section_rank * col_block

    def collect(carry, piece):
        whole = lax.all_gather(piece, ("tensor", "section"), axis=1, tiled=True)
        rows_part = lax.dynamic_slice_in_dim(whole, row_start, row_block, 1)
        cols_part = lax.dynamic_slice_in_dim(whole, col_start, col_block, 1)
        return (carry, (rows_part, cols_part))

    unused_carry, (row_parts, col_parts) = lax.scan(collect, jnp.int32(0), activations)
    partial_value = jnp.einsum(
        "mnr,mnc->mrc", row_parts, col_parts, preferred_element_type=jnp.float32
    )
    fresh = lax.psum_scatter(partial_value, "shard", scatter_dimension=0, tiled=True) / tokens_all
    row_index = lax.broadcasted_iota(jnp.int32, (row_block, col_block), 0) + row_start
    col_index = lax.broadcasted_iota(jnp.int32, (row_block, col_block), 1) + col_start
    eye_block = (row_index == col_index).astype(jnp.float32)
    matrix = factor_decay * old_factors + (1.0 - factor_decay) * fresh + damping * eye_block
    diag_part = jnp.sum(matrix * eye_block, axis=(1, 2))
    trace = lax.psum(diag_part, ("tensor", "section"))
    factor_scale = (D / (3.0 * trace))[:, None, None]
    matrix_low = lax.optimization_barrier(matrix.astype(jnp.bfloat16))
    first = 2.0 * factor_scale * eye_block - factor_scale * factor_scale * matrix_low.astype(
        jnp.float32
    )
    first_low = first.astype(jnp.bfloat16)
    first_cols = lax.all_gather(first_low, "tensor", axis=1, tiled=True)
    image = fold_with(first_cols, lax.all_gather(matrix_low, "section", axis=2, tiled=True))
    image_cols = lax.all_gather(image.astype(jnp.bfloat16), "tensor", axis=1, tiled=True)
    product = fold_with(image_cols, lax.all_gather(first_low, "section", axis=2, tiled=True))
    inverse_low = (2.0 * first - product).astype(jnp.bfloat16)
    inverses = lax.all_gather(inverse_low, "shard", axis=0, tiled=True)
    left_terms = jnp.stack(
        [
            jnp.einsum("nc,rc->nr", col_parts[m], inverses[m], preferred_element_type=jnp.float32)
            for m in (0, 4, 6)
        ]
    )
    left = lax.psum(left_terms, "section").astype(jnp.bfloat16)
    right_terms = jnp.stack(
        [
            jnp.einsum("nr,rc->nc", row_parts[m], inverses[m], preferred_element_type=jnp.float32)
            for m in (1, 2, 3, 5, 7)
        ]
    )
    right = lax.psum(right_terms, "tensor").astype(jnp.bfloat16)
    norm_values = norm_terms.astype(jnp.float32)
    router_part = jnp.einsum(
        "en,fn->ef", router_grad, router_grad, preferred_element_type=jnp.float32
    )
    router_sum, norm_total, norm_squares = lax.psum(
        (router_part, jnp.sum(norm_values, axis=1), jnp.sum(norm_values * norm_values, axis=1)),
        "shard",
    )
    router_matrix = (
        factor_decay * old_router_factor
        + (1.0 - factor_decay) * (router_sum / tokens_all)
        + damping * jnp.eye(EXPERTS, dtype=jnp.float32)
    )
    router_inverse = local_inverse(router_matrix)
    router_right = jnp.einsum(
        "en,ef->nf", router_grad, router_inverse, preferred_element_type=jnp.float32
    ).astype(jnp.bfloat16)
    precond_norms = (
        learning_rate
        * norm_total
        / (
            factor_decay * old_norm_diag
            + (1.0 - factor_decay) * (norm_squares / tokens_all)
            + damping
        )
    )
    ids_all = lax.all_gather(token_ids, "shard", axis=0, tiled=True)
    embed_all = lax.all_gather(right[4], "shard", axis=0, tiled=True)
    paired_left = jnp.stack([left[0], left[0], left[0], left[1]])
    attn_terms = jnp.einsum(
        "wnr,wnc->wrc", paired_left, right[:4], preferred_element_type=jnp.float32
    )
    router_term = jnp.einsum("nf,nr->fr", router_right, left[2], preferred_element_type=jnp.float32)
    attn_sum, router_total = lax.psum((attn_terms, router_term), "shard")
    precond_attn = learning_rate * attn_sum
    precond_router = learning_rate * router_total
    vocab_block = VOCAB // n_tensor
    step_rows = math.gcd(vocab_block, 512)
    vocab_start = tensor_rank * vocab_block

    def embed_block(block_index):
        ids_here = vocab_start + block_index * step_rows + lax.iota(jnp.int32, step_rows)
        onehot = (ids_here[:, None] == ids_all[None, :]).astype(jnp.bfloat16)
        summed = jnp.dot(onehot, embed_all, preferred_element_type=jnp.float32)
        tallies = jnp.sum(onehot, axis=1, dtype=jnp.float32)
        return (summed, tallies)

    block_sums, block_counts = lax.map(
        embed_block, jnp.arange(vocab_block // step_rows, dtype=jnp.int32)
    )
    embed_sum = block_sums.reshape(vocab_block, col_block)
    counts = block_counts.reshape(vocab_block)
    divisor = factor_decay * old_embed_diag + (1.0 - factor_decay) * (counts / tokens_all) + damping
    precond_embed = learning_rate * embed_sum / divisor[:, None]
    return (precond_attn, precond_router, precond_norms, precond_embed)


def split_three(values):
    high = lax.reduce_precision(values, 8, 7)
    rest = values - high
    middle = lax.reduce_precision(rest, 8, 7)
    return jnp.stack([high, middle, rest - middle], axis=-2).astype(jnp.bfloat16)


def swap(value, axis, size, step):
    return lax.ppermute(value, axis, [(i, i ^ step) for i in range(size)])


def local_diagonals(blocks):
    width = blocks.shape[1]
    pieces = []
    for start in range(0, width, 128):
        size = min(128, width - start)
        tile = blocks[:, start : start + size, start : start + size]
        pieces.append(jnp.sum(tile * jnp.eye(size, dtype=tile.dtype), axis=1))
    return jnp.concatenate(pieces, axis=1)


def rounded(values):
    return values.astype(jnp.bfloat16).astype(jnp.float32)


def params():
    return pltpu.CompilerParams(vmem_limit_bytes=40 * 1024 * 1024)


def layout_kernel(place_ref, *refs, weight):
    gathered, (features, rows, low_diag, trace, old) = refs[:4], refs[4:]
    own_place, layer, core, here = (place_ref[index] for index in range(4))
    steps, _, tokens = gathered[0].shape
    sections = len(gathered)
    groups, depth, _ = features.shape
    part = depth // (sections * steps)
    width = depth // steps
    for away in range(sections):
        section = here ^ away
        codes = jnp.zeros((16, tokens), jnp.float32)
        for step in range(steps):
            start = pl.multiple_of((step * sections + section) * part, 16)
            for group in range(groups):
                features[group, pl.ds(start, part)] = gathered[away][
                    step, group * part : (group + 1) * part
                ]
            codes += gathered[away][step, groups * part :].astype(jnp.float32)
        codes = codes[0:3] + codes[3:6] + codes[6:9]
        pieces = [codes[0:1], codes[1:2], codes[2:3, : width - 2 * tokens]]
        old[section ^ layer] = jnp.concatenate(pieces, axis=1)
    ones = jnp.ones((8, tokens), jnp.bfloat16)
    total = jnp.float32(0.0)
    for step in range(steps):
        squares = jnp.zeros((8, width), jnp.float32)
        for group in range(groups):
            values = features[group, step * width : (step + 1) * width].astype(jnp.float32)
            values = values * values
            high = values.astype(jnp.bfloat16)
            low = (values - high.astype(jnp.float32)).astype(jnp.bfloat16)
            for piece in (high, low):
                squares += lax.dot_general(
                    ones, piece, (((1,), (1,)), ((), ())), preferred_element_type=jnp.float32
                )
        diag = factor_decay * old[step] + weight * squares[0:1] + damping
        total += jnp.sum(diag)
        low_diag[step] = rounded(diag)
        start = pl.multiple_of((own_place ^ step) * width, width)
        mine = features[core, pl.ds(start, width)]
        rows[:, step * width : (step + 1) * width] = mine.T
    trace[0] = total


def lay_out(places, gathered, weight):
    steps, height, tokens = gathered[0].shape
    sections = len(gathered)
    part = (height - 16) // 2
    depth = sections * steps * part
    width = depth // steps
    vmem = pl.BlockSpec(memory_space=pltpu.VMEM)
    smem = pl.BlockSpec(memory_space=pltpu.SMEM)
    return pl.pallas_call(
        functools.partial(layout_kernel, weight=weight),
        in_specs=[smem] + [vmem] * sections,
        out_specs=[vmem, vmem, vmem, smem],
        out_shape=[
            jax.ShapeDtypeStruct((2, depth, tokens), jnp.bfloat16),
            jax.ShapeDtypeStruct((tokens, depth), jnp.bfloat16),
            jax.ShapeDtypeStruct((steps, 1, width), jnp.float32),
            jax.ShapeDtypeStruct((1,), jnp.float32),
        ],
        scratch_shapes=[pltpu.VMEM((steps, 1, width), jnp.float32)],
        compiler_params=params(),
        cost_estimate=pl.CostEstimate(
            flops=64 * depth * tokens, bytes_accessed=14 * depth * tokens, transcendentals=0
        ),
    )(places, *gathered)


def factor_kernel(place_ref, part, own, diag, *refs, step, weight):
    portions, out = refs[:-1], refs[-1]
    start = 0
    for old in portions:
        stop = start + old.shape[0]
        shape = (old.shape[0], out.shape[1])
        fresh = jnp.zeros(shape, jnp.float32)
        for index in range(part.shape[0]):
            fresh += lax.dot_general(
                part[index, start:stop],
                own[index],
                (((1,), (1,)), ((), ())),
                preferred_element_type=jnp.float32,
            )
        block = factor_decay * old[...].astype(jnp.float32) + weight * fresh
        on_diag = lax.broadcasted_iota(jnp.int32, shape, 0) + start == lax.broadcasted_iota(
            jnp.int32, shape, 1
        )
        block = jnp.where(on_diag & (place_ref[0] == step), diag[0], block)
        out[start:stop] = block.astype(jnp.bfloat16)
        start = stop


def factor_block(place, features, portions, diag, step, weight):
    groups, _, tokens = features.shape
    rows, cols = sum(old.shape[0] for old in portions), portions[0].shape[1]
    return pl.pallas_call(
        functools.partial(factor_kernel, step=step, weight=weight),
        grid_spec=pltpu.PrefetchScalarGridSpec(
            num_scalar_prefetch=1,
            grid=(1,),
            in_specs=[
                pl.BlockSpec((groups, rows, tokens), lambda i, place: (0, step, 0)),
                pl.BlockSpec((groups, cols, tokens), lambda i, place: (0, place[0], 0)),
                pl.BlockSpec((1, 1, cols), lambda i, place: (place[0], 0, 0)),
            ]
            + [pl.BlockSpec(old.shape, lambda i, place: (0, 0)) for old in portions],
            out_specs=pl.BlockSpec((rows, cols), lambda i, place: (0, 0)),
        ),
        out_shape=jax.ShapeDtypeStruct((rows, cols), jnp.bfloat16),
        compiler_params=params(),
        cost_estimate=pl.CostEstimate(
            flops=2 * groups * rows * cols * tokens,
            bytes_accessed=4 * rows * cols + 4 * groups * rows * tokens,
            transcendentals=0,
        ),
    )(place, features, features, diag, *portions)


def block_products(place_ref, halves, blocks, pieces):
    width = pieces.shape[2]
    for index, half in enumerate(halves):
        pieces[2 * index] = half[:, :width]
        pieces[2 * index + 1] = half[:, width:]
    products = [None, None]
    for step in range(4):
        piece = pieces[place_ref[0] ^ step]
        for index in range(2):
            term = jnp.dot(piece, blocks[4 * index + step][...], preferred_element_type=jnp.float32)
            products[index] = term if products[index] is None else products[index] + term
    return products


def first_parts(place_ref, scale, rows, diag, product, index):
    width = product.shape[1]
    square = scale * scale
    values = rows[:, index * width : (index + 1) * width].astype(jnp.float32)
    low_diag = diag[place_ref[0] ^ index]
    first_diag = rounded(2.0 * scale - square * low_diag)
    by_first = 2.0 * scale * values - square * product
    step_one = first_diag * values - square * (product - low_diag * values)
    return by_first, step_one, low_diag, first_diag


def first_kernel(place_ref, scale_ref, rows, diag, *refs):
    blocks, (kept, message, pieces) = refs[:8], refs[8:]
    half = rows.shape[1] // 2
    halves = [rows[:, :half], rows[:, half:]]
    products = block_products(place_ref, halves, blocks, pieces)
    lows = []
    for index in range(2):
        kept[index] = products[index]
        parts = first_parts(place_ref, scale_ref[0], rows, diag, products[index], index)
        lows.append(parts[1].astype(jnp.bfloat16))
    message[...] = jnp.concatenate(lows, axis=1)


def second_kernel(place_ref, scale_ref, mine, theirs, rows, diag, before, *refs):
    blocks, (kept, message, pieces) = refs[:8], refs[8:]
    products = block_products(place_ref, [mine[...], theirs[...]], blocks, pieces)
    square = scale_ref[0] * scale_ref[0]
    lows = []
    for index in range(2):
        by_first, one, low_diag, first_diag = first_parts(
            place_ref, scale_ref[0], rows, diag, before[index], index
        )
        two = products[index] + low_diag * (one - rounded(one))
        low = two.astype(jnp.bfloat16)
        kept[index] = (
            2.0 * by_first - first_diag * two - square * low_diag * low.astype(jnp.float32)
        )
        lows.append(low)
    message[...] = jnp.concatenate(lows, axis=1)


def third_kernel(place_ref, scale_ref, mine, theirs, before, *refs):
    blocks, (keep, give, pieces) = refs[:8], refs[8:]
    products = block_products(place_ref, [mine[...], theirs[...]], blocks, pieces)
    square = scale_ref[0] * scale_ref[0]
    for index, out in ((0, keep), (1, give)):
        out[...] = (before[index] + square * products[index]).T.astype(jnp.bfloat16)


def chain_call(kernel, scalars, arrays, blocks, out_shape):
    tokens = arrays[0].shape[0]
    depth, width = blocks[0].shape
    vmem = pl.BlockSpec(memory_space=pltpu.VMEM)
    return pl.pallas_call(
        kernel,
        in_specs=[pl.BlockSpec(memory_space=pltpu.SMEM)] * len(scalars)
        + [vmem] * (len(arrays) + len(blocks)),
        out_specs=[vmem] * len(out_shape),
        out_shape=out_shape,
        scratch_shapes=[pltpu.VMEM((4, tokens, depth), jnp.bfloat16)],
        compiler_params=params(),
        cost_estimate=pl.CostEstimate(
            flops=2 * len(blocks) * tokens * depth * width,
            bytes_accessed=2 * len(blocks) * depth * width,
            transcendentals=0,
        ),
    )(*scalars, *arrays, *blocks)


def output_kernel(where_ref, scale, matches, *refs):
    lefts, mine, others = (refs[:4], refs[4:8]), refs[8:12], refs[12:16]
    attn, embed = refs[16:18]
    left_held, held, found, attn_made, embed_made, sems, out_sems = refs[18:]
    shard, layer, turn = where_ref[0], where_ref[1], where_ref[2]
    first = shard == 0
    rows, tokens_all = held.shape[1:]

    found_copy = pltpu.make_async_copy(matches, found, sems.at[7])
    for slot in range(2):
        for group in range(2):
            for place in range(4):

                @pl.when((turn == place) & (((shard ^ slot) == group)))
                def _():
                    source = lefts[group][place].at[pl.ds(0, rows)]
                    pltpu.make_async_copy(source, left_held.at[slot], sems.at[5 + slot]).start()

        if slot == 0:
            for index, source in enumerate((0, 1, 3, 0, 3)):
                from_mine = first if index < 3 else jnp.logical_not(first)
                for place in range(4):
                    for group, wanted in ((mine, from_mine), (others, jnp.logical_not(from_mine))):

                        @pl.when(wanted & ((layer ^ source) == place))
                        def _():
                            pltpu.make_async_copy(
                                group[place], held.at[index], sems.at[index]
                            ).start()

            found_copy.start()

    def arrived(slot):
        target = held.at[slot] if slot < 5 else left_held.at[slot - 5]
        pltpu.make_async_copy(mine[0], target, sems.at[slot]).wait()

    results = []
    arrived(5)
    for slot in range(4):
        if slot == 3:
            arrived(6)
        arrived(slot)
        attn_made[slot] = learning_rate * lax.dot_general(
            left_held[slot // 3],
            held[slot],
            (((1,), (1,)), ((), ())),
            preferred_element_type=jnp.float32,
        )
        results.append(
            pltpu.make_async_copy(attn_made.at[slot], attn.at[slot], out_sems.at[slot])
        )
        results[-1].start()
    arrived(4)
    found_copy.wait()
    part = found.shape[1] // 4
    for index in range(4):
        cols = pl.ds(index * part, part)
        product = jnp.dot(held[4], found[:, cols], preferred_element_type=jnp.float32)
        embed_made[:, cols] = product * scale[:, cols]
        results.append(
            pltpu.make_async_copy(
                embed_made.at[:, cols], embed.at[:, cols], out_sems.at[4 + index]
            )
        )
        results[-1].start()
    for result in results:
        result.wait()


def output_products(where, scale, matches, lefts, mine, others):
    cols, tokens_all = mine[0].shape
    vocab_block = scale.shape[1]
    anywhere = pl.BlockSpec(memory_space=pl.ANY)
    return pl.pallas_call(
        output_kernel,
        in_specs=[
            pl.BlockSpec(memory_space=pltpu.SMEM),
            pl.BlockSpec(memory_space=pltpu.VMEM),
        ]
        + [anywhere] * 17,
        out_specs=(anywhere, anywhere),
        out_shape=(
            jax.ShapeDtypeStruct((4, cols, cols), jnp.float32),
            jax.ShapeDtypeStruct((cols, vocab_block), jnp.float32),
        ),
        scratch_shapes=[
            pltpu.VMEM((2, cols, tokens_all), jnp.bfloat16),
            pltpu.VMEM((5, cols, tokens_all), jnp.bfloat16),
            pltpu.VMEM((tokens_all, vocab_block), jnp.bfloat16),
            pltpu.VMEM((4, cols, cols), jnp.float32),
            pltpu.VMEM((cols, vocab_block), jnp.float32),
            pltpu.SemaphoreType.DMA((8,)),
            pltpu.SemaphoreType.DMA((8,)),
        ],
        compiler_params=pltpu.CompilerParams(vmem_limit_bytes=60 * 1024 * 1024),
        cost_estimate=pl.CostEstimate(
            flops=2 * cols * tokens_all * (4 * cols + vocab_block),
            bytes_accessed=4 * cols * (4 * cols + vocab_block) + 14 * cols * tokens_all,
            transcendentals=0,
        ),
    )(where, scale, matches, *lefts[0], *lefts[1], *mine, *others)


def layer_plan(
    activations,
    router_grad,
    token_ids,
    norm_terms,
    old_factors,
    old_router_factor,
    old_norm_diag,
    old_embed_diag,
):
    n_tensor = lax.axis_size("tensor")
    n_section = lax.axis_size("section")
    n_shard = lax.axis_size("shard")
    shard = lax.axis_index("shard")
    layer = lax.axis_index("tensor")
    section = lax.axis_index("section")
    core = section % 2
    owned, row_block, col_block = old_factors.shape
    tokens = activations.shape[1]
    features_dev = activations.shape[2]
    tokens_all = tokens * n_shard
    weight = (1.0 - factor_decay) / tokens_all
    own_place = section ^ layer
    place = own_place.reshape(1)
    axes = ("shard", "tensor")

    def by_index(array, index, axis=0):
        return lax.dynamic_index_in_dim(array, index, axis, False)

    def held_by(layer_index):
        return jnp.where(layer_index == 3, 3, lax.rem(layer_index + 1, 3))

    by_feature = jnp.swapaxes(activations, 1, 2)
    diagonals = local_diagonals(old_factors) * (layer == section).astype(jnp.float32)
    extra = jnp.pad(split_three(diagonals), ((0, 0), (0, 0), (0, 3 * tokens - col_block)))
    extra = jnp.pad(extra.reshape(owned, 9, tokens), ((0, 0), (0, 7), (0, 0)))
    collected = []
    for step in range(n_tensor):
        factor = held_by(layer ^ step)
        message = jnp.concatenate(
            [
                by_index(by_feature, shard * owned + factor),
                by_index(by_feature, (1 - shard) * owned + factor),
                by_index(extra, factor),
            ],
            axis=0,
        )
        collected.append(swap(message, "tensor", n_tensor, step) if step else message)
    collected = jnp.stack(collected)
    lows = [
        by_index(old_factors, held_by(layer ^ step)).astype(jnp.bfloat16)
        for step in range(n_tensor)
    ]

    def both_shards(value, axis):
        other = swap(value, "shard", n_shard, 1)
        return jnp.where(
            shard == 0,
            jnp.concatenate([value, other], axis=axis),
            jnp.concatenate([other, value], axis=axis),
        )

    grad_all = both_shards(router_grad, 1)
    ids_all = both_shards(token_ids, 0)
    norm_values = norm_terms.astype(jnp.float32)
    norm_sums = jnp.stack([jnp.sum(norm_values, axis=1), jnp.sum(norm_values * norm_values, axis=1)])
    norm_sums = norm_sums + swap(norm_sums, "shard", n_shard, 1)
    vocab_block = old_embed_diag.shape[0]
    ids_here = layer * vocab_block + lax.iota(jnp.int32, vocab_block)
    matches = (ids_all[:, None] == ids_here[None, :]).astype(jnp.bfloat16)
    counts = jnp.sum(matches, axis=0, dtype=jnp.float32)
    divisor = factor_decay * old_embed_diag + (1.0 - factor_decay) * (counts / tokens_all) + damping
    embed_scale = (learning_rate / divisor)[None, :]
    router_matrix = (
        factor_decay * old_router_factor
        + weight * jnp.einsum("en,fn->ef", grad_all, grad_all, preferred_element_type=jnp.float32)
        + damping * jnp.eye(EXPERTS, dtype=jnp.float32)
    )
    router_inverse = local_inverse(router_matrix)
    router_right = jnp.einsum(
        "en,ef->fn", grad_all, router_inverse, preferred_element_type=jnp.float32
    ).astype(jnp.bfloat16)

    collected, lows, small = lax.optimization_barrier(
        (collected, lows, (router_right, matches, embed_scale, norm_sums))
    )
    router_right, matches, embed_scale, norm_sums = small
    other_tokens = swap(collected[:, features_dev : 2 * features_dev], "shard", n_shard, 1)
    quarter = row_block // 4

    def portion(step, start, stop):
        return swap(lows[step][start:stop], "tensor", n_tensor, step)

    near_rows = portion(2, 0, quarter)
    other_tokens, near_rows = lax.optimization_barrier((other_tokens, near_rows))
    collected = jnp.concatenate(
        [collected[:, :features_dev], other_tokens, collected[:, 2 * features_dev :]], axis=1
    )
    by_side = swap(collected, "section", n_section, 2)
    by_core = swap(collected, "section", n_section, 1)
    middle_rows = portion(2, quarter, 3 * quarter)
    by_side, middle_rows = lax.optimization_barrier((by_side, middle_rows))
    by_both = swap(by_side, "section", n_section, 1)
    far_block = portion(3, 0, row_block)
    last_rows = portion(2, 3 * quarter, row_block)
    blocks = [
        (lows[0],),
        (portion(1, 0, row_block),),
        (near_rows, middle_rows, last_rows),
        (far_block,),
    ]

    features, rows, low_diag, trace = lay_out(
        jnp.stack([own_place, layer, core, section]),
        (collected, by_core, by_side, by_both),
        weight,
    )
    scale = D / (3.0 * trace)
    own_cols = [
        factor_block(place, features, blocks[step], low_diag, step, weight)
        for step in range(n_tensor)
    ]
    other_cols = [swap(block, "section", n_section, 1) for block in own_cols]
    cols = own_cols + other_cols

    wide = jax.ShapeDtypeStruct((2, tokens, col_block), jnp.float32)
    sent = jax.ShapeDtypeStruct((tokens, 2 * col_block), jnp.bfloat16)
    part = jax.ShapeDtypeStruct((col_block, tokens), jnp.bfloat16)
    scalars = (place, scale)
    kept, message = chain_call(first_kernel, scalars, (rows, low_diag), cols, (wide, sent))
    theirs = swap(message, "section", n_section, 2)
    kept, message = chain_call(
        second_kernel, scalars, (message, theirs, rows, low_diag, kept), cols, (wide, sent)
    )
    theirs = swap(message, "section", n_section, 2)
    keep, give = chain_call(third_kernel, scalars, (message, theirs, kept), cols, (part, part))
    got = swap(give, "section", n_section, 1)
    own = jnp.where(
        core == shard, jnp.concatenate([keep, got], axis=1), jnp.concatenate([got, keep], axis=1)
    )

    planes = range(n_shard)
    layers = range(n_tensor)

    def useful(x, z):
        return z != 2 and (x, z) != (1, 1)

    def send(value, step, held):
        moves = [
            (x * n_tensor + z, x * n_tensor + (z ^ step))
            for x in planes
            for z in layers
            if useful(x, z ^ held)
        ]
        return lax.ppermute(value, axes, moves)

    def across(value, held):
        moves = [
            (x * n_tensor + z, (1 - x) * n_tensor + z)
            for x in planes
            for z in layers
            if useful(x, z ^ held)
        ]
        return lax.ppermute(value, axes, moves)

    everywhere = ("shard", "tensor", "section")

    def spot(x, z, s):
        return (x * n_tensor + z) * n_section + s

    def scatter(value, source):
        moved_here = lax.ppermute(
            value,
            everywhere,
            [(spot(x, source, s), spot(x, s, s)) for x in planes for s in layers if s != source],
        )
        return jnp.where(layer == source, value, moved_here)

    def hand_round(value, *ahead):
        sides = lax.ppermute(
            value, everywhere, [(spot(x, t, t), spot(x, t, t ^ 2)) for x in planes for t in layers]
        )
        sides, *ahead = lax.optimization_barrier((sides, *ahead))
        near = lax.ppermute(
            value, everywhere, [(spot(x, t, t), spot(x, t, t ^ 1)) for x in planes for t in layers]
        )
        far = lax.ppermute(
            sides,
            everywhere,
            [(spot(x, t, t ^ 2), spot(x, t, t ^ 3)) for x in planes for t in layers],
        )
        return (value, near, sides, far), *ahead

    near_1 = send(own, 1, 0)
    near_2 = send(own, 2, 0)
    over_0 = across(own, 0)
    left_here = scatter(own, 2)
    near_1, own = lax.optimization_barrier((near_1, own))
    over_1 = across(near_1, 1)
    left_there = lax.ppermute(
        left_here, everywhere, [(spot(x, t, t), spot(1 - x, t, t)) for x in planes for t in layers]
    )
    router_cols = learning_rate * jnp.einsum(
        "fn,cn->fc", router_right, own, preferred_element_type=jnp.float32
    )
    router_cols = jnp.where((shard == 1) & (layer == 1), router_cols, 0.0)
    router_all = lax.all_gather(lax.psum(router_cols, axes), "section", axis=0)
    precond_router = by_index(router_all, layer)
    (lefts_here,) = hand_round(left_here)
    near_2, over_0, over_1, left_there, precond_router = lax.optimization_barrier(
        (near_2, over_0, over_1, left_there, precond_router)
    )
    near_3 = send(near_2, 1, 2)
    over_2 = across(near_2, 2)
    near_3, over_2 = lax.optimization_barrier((near_3, over_2))
    over_3 = across(near_3, 3)
    lefts_there, over_3 = hand_round(left_there, over_3)
    turn = section ^ layer

    precond_attn, embed_columns = output_products(
        jnp.stack([shard, layer, turn]),
        embed_scale,
        matches,
        (lefts_here, lefts_there),
        (own, near_1, near_2, near_3),
        (over_0, over_1, over_2, over_3),
    )
    precond_embed = embed_columns.T

    precond_norms = (
        learning_rate
        * norm_sums[0]
        / (
            factor_decay * old_norm_diag
            + (1.0 - factor_decay) * (norm_sums[1] / tokens_all)
            + damping
        )
    )
    return (precond_attn, precond_router, precond_norms, precond_embed)


def per_device(*arguments):
    one_each = arguments[4].shape[0] == lax.axis_size("tensor") == lax.axis_size("section")
    if one_each and lax.axis_size("section") == 4 and lax.axis_size("shard") == 2:
        return layer_plan(*arguments)
    return general_plan(*arguments)


def solution(mesh):
    return jax.shard_map(
        per_device,
        mesh=mesh,
        in_specs=(
            P(None, "shard", ("tensor", "section")),
            P(None, "shard"),
            P("shard"),
            P(None, "shard", ("tensor", "section")),
            P("shard", "tensor", "section"),
            P(),
            P(None, ("tensor", "section")),
            P("tensor"),
        ),
        out_specs=(
            P(None, "tensor", "section"),
            P(None, "tensor"),
            P(None, ("tensor", "section")),
            P("tensor", "section"),
        ),
        check_vma=False,
    )
```

```python
import functools
import math

import jax
import jax.numpy as jnp
from jax import lax
from jax.experimental import pallas as pl
from jax.experimental.pallas import tpu as pltpu
from jax.sharding import PartitionSpec as P

D = 2304
EXPERTS = 8
VOCAB = 8192


factor_decay = 0.5
damping = 0.01
learning_rate = 0.05


def local_inverse(matrix):
    width = matrix.shape[0]
    trace = jnp.sum(jnp.diagonal(matrix))
    factor_scale = width / (3.0 * trace)
    identity = jnp.eye(width, dtype=jnp.float32)
    matrix_low = lax.optimization_barrier(matrix.astype(jnp.bfloat16))
    first = 2.0 * factor_scale * identity - factor_scale * factor_scale * matrix_low.astype(
        jnp.float32
    )
    first_low = first.astype(jnp.bfloat16)
    image = jnp.dot(matrix_low, first_low, preferred_element_type=jnp.float32).astype(jnp.bfloat16)
    product = jnp.dot(first_low, image, preferred_element_type=jnp.float32)
    return (2.0 * first - product).astype(jnp.bfloat16)


def fold_with(columns, piece):
    return jnp.einsum("kij,kjl->kil", piece, columns, preferred_element_type=jnp.float32)


def general_plan(
    activations,
    router_grad,
    token_ids,
    norm_terms,
    old_factors,
    old_router_factor,
    old_norm_diag,
    old_embed_diag,
):
    n_tensor = lax.axis_size("tensor")
    n_section = lax.axis_size("section")
    n_shard = lax.axis_size("shard")
    tensor_rank = lax.axis_index("tensor")
    section_rank = lax.axis_index("section")
    row_block = D // n_tensor
    col_block = D // n_section
    tokens_all = activations.shape[1] * n_shard
    row_start = tensor_rank * row_block
    col_start = section_rank * col_block

    def collect(carry, piece):
        whole = lax.all_gather(piece, ("tensor", "section"), axis=1, tiled=True)
        rows_part = lax.dynamic_slice_in_dim(whole, row_start, row_block, 1)
        cols_part = lax.dynamic_slice_in_dim(whole, col_start, col_block, 1)
        return (carry, (rows_part, cols_part))

    unused_carry, (row_parts, col_parts) = lax.scan(collect, jnp.int32(0), activations)
    partial_value = jnp.einsum(
        "mnr,mnc->mrc", row_parts, col_parts, preferred_element_type=jnp.float32
    )
    fresh = lax.psum_scatter(partial_value, "shard", scatter_dimension=0, tiled=True) / tokens_all
    row_index = lax.broadcasted_iota(jnp.int32, (row_block, col_block), 0) + row_start
    col_index = lax.broadcasted_iota(jnp.int32, (row_block, col_block), 1) + col_start
    eye_block = (row_index == col_index).astype(jnp.float32)
    matrix = factor_decay * old_factors + (1.0 - factor_decay) * fresh + damping * eye_block
    diag_part = jnp.sum(matrix * eye_block, axis=(1, 2))
    trace = lax.psum(diag_part, ("tensor", "section"))
    factor_scale = (D / (3.0 * trace))[:, None, None]
    matrix_low = lax.optimization_barrier(matrix.astype(jnp.bfloat16))
    first = 2.0 * factor_scale * eye_block - factor_scale * factor_scale * matrix_low.astype(
        jnp.float32
    )
    first_low = first.astype(jnp.bfloat16)
    first_cols = lax.all_gather(first_low, "tensor", axis=1, tiled=True)
    image = fold_with(first_cols, lax.all_gather(matrix_low, "section", axis=2, tiled=True))
    image_cols = lax.all_gather(image.astype(jnp.bfloat16), "tensor", axis=1, tiled=True)
    product = fold_with(image_cols, lax.all_gather(first_low, "section", axis=2, tiled=True))
    inverse_low = (2.0 * first - product).astype(jnp.bfloat16)
    inverses = lax.all_gather(inverse_low, "shard", axis=0, tiled=True)
    left_terms = jnp.stack(
        [
            jnp.einsum("nc,rc->nr", col_parts[m], inverses[m], preferred_element_type=jnp.float32)
            for m in (0, 4, 6)
        ]
    )
    left = lax.psum(left_terms, "section").astype(jnp.bfloat16)
    right_terms = jnp.stack(
        [
            jnp.einsum("nr,rc->nc", row_parts[m], inverses[m], preferred_element_type=jnp.float32)
            for m in (1, 2, 3, 5, 7)
        ]
    )
    right = lax.psum(right_terms, "tensor").astype(jnp.bfloat16)
    norm_values = norm_terms.astype(jnp.float32)
    router_part = jnp.einsum(
        "en,fn->ef", router_grad, router_grad, preferred_element_type=jnp.float32
    )
    router_sum, norm_total, norm_squares = lax.psum(
        (router_part, jnp.sum(norm_values, axis=1), jnp.sum(norm_values * norm_values, axis=1)),
        "shard",
    )
    router_matrix = (
        factor_decay * old_router_factor
        + (1.0 - factor_decay) * (router_sum / tokens_all)
        + damping * jnp.eye(EXPERTS, dtype=jnp.float32)
    )
    router_inverse = local_inverse(router_matrix)
    router_right = jnp.einsum(
        "en,ef->nf", router_grad, router_inverse, preferred_element_type=jnp.float32
    ).astype(jnp.bfloat16)
    precond_norms = (
        learning_rate
        * norm_total
        / (
            factor_decay * old_norm_diag
            + (1.0 - factor_decay) * (norm_squares / tokens_all)
            + damping
        )
    )
    ids_all = lax.all_gather(token_ids, "shard", axis=0, tiled=True)
    embed_all = lax.all_gather(right[4], "shard", axis=0, tiled=True)
    paired_left = jnp.stack([left[0], left[0], left[0], left[1]])
    attn_terms = jnp.einsum(
        "wnr,wnc->wrc", paired_left, right[:4], preferred_element_type=jnp.float32
    )
    router_term = jnp.einsum("nf,nr->fr", router_right, left[2], preferred_element_type=jnp.float32)
    attn_sum, router_total = lax.psum((attn_terms, router_term), "shard")
    precond_attn = learning_rate * attn_sum
    precond_router = learning_rate * router_total
    vocab_block = VOCAB // n_tensor
    step_rows = math.gcd(vocab_block, 512)
    vocab_start = tensor_rank * vocab_block

    def embed_block(block_index):
        ids_here = vocab_start + block_index * step_rows + lax.iota(jnp.int32, step_rows)
        onehot = (ids_here[:, None] == ids_all[None, :]).astype(jnp.bfloat16)
        summed = jnp.dot(onehot, embed_all, preferred_element_type=jnp.float32)
        tallies = jnp.sum(onehot, axis=1, dtype=jnp.float32)
        return (summed, tallies)

    block_sums, block_counts = lax.map(
        embed_block, jnp.arange(vocab_block // step_rows, dtype=jnp.int32)
    )
    embed_sum = block_sums.reshape(vocab_block, col_block)
    counts = block_counts.reshape(vocab_block)
    divisor = factor_decay * old_embed_diag + (1.0 - factor_decay) * (counts / tokens_all) + damping
    precond_embed = learning_rate * embed_sum / divisor[:, None]
    return (precond_attn, precond_router, precond_norms, precond_embed)


def split_three(values):
    high = lax.reduce_precision(values, 8, 7)
    rest = values - high
    middle = lax.reduce_precision(rest, 8, 7)
    return jnp.stack([high, middle, rest - middle], axis=-2).astype(jnp.bfloat16)


def swap(value, axis, size, step):
    return lax.ppermute(value, axis, [(i, i ^ step) for i in range(size)])


def local_diagonals(blocks):
    width = blocks.shape[1]
    pieces = []
    for start in range(0, width, 128):
        size = min(128, width - start)
        tile = blocks[:, start : start + size, start : start + size]
        pieces.append(jnp.sum(tile * jnp.eye(size, dtype=tile.dtype), axis=1))
    return jnp.concatenate(pieces, axis=1)


def rounded(values):
    return values.astype(jnp.bfloat16).astype(jnp.float32)


def params():
    return pltpu.CompilerParams(vmem_limit_bytes=40 * 1024 * 1024)


def layout_kernel(place_ref, *refs, weight):
    gathered, (features, rows, low_diag, trace, old) = refs[:4], refs[4:]
    own_place, layer, core, here = (place_ref[index] for index in range(4))
    steps, _, tokens = gathered[0].shape
    sections = len(gathered)
    groups, depth, _ = features.shape
    part = depth // (sections * steps)
    width = depth // steps
    for away in range(sections):
        section = here ^ away
        codes = jnp.zeros((16, tokens), jnp.float32)
        for step in range(steps):
            start = pl.multiple_of((step * sections + section) * part, 16)
            for group in range(groups):
                features[group, pl.ds(start, part)] = gathered[away][
                    step, group * part : (group + 1) * part
                ]
            codes += gathered[away][step, groups * part :].astype(jnp.float32)
        codes = codes[0:3] + codes[3:6] + codes[6:9]
        pieces = [codes[0:1], codes[1:2], codes[2:3, : width - 2 * tokens]]
        old[section ^ layer] = jnp.concatenate(pieces, axis=1)
    ones = jnp.ones((8, tokens), jnp.bfloat16)
    total = jnp.float32(0.0)
    for step in range(steps):
        squares = jnp.zeros((8, width), jnp.float32)
        for group in range(groups):
            values = features[group, step * width : (step + 1) * width].astype(jnp.float32)
            values = values * values
            high = values.astype(jnp.bfloat16)
            low = (values - high.astype(jnp.float32)).astype(jnp.bfloat16)
            for piece in (high, low):
                squares += lax.dot_general(
                    ones, piece, (((1,), (1,)), ((), ())), preferred_element_type=jnp.float32
                )
        diag = factor_decay * old[step] + weight * squares[0:1] + damping
        total += jnp.sum(diag)
        low_diag[step] = rounded(diag)
        start = pl.multiple_of((own_place ^ step) * width, width)
        mine = features[core, pl.ds(start, width)]
        rows[:, step * width : (step + 1) * width] = mine.T
    trace[0] = total


def lay_out(places, gathered, weight):
    steps, height, tokens = gathered[0].shape
    sections = len(gathered)
    part = (height - 16) // 2
    depth = sections * steps * part
    width = depth // steps
    vmem = pl.BlockSpec(memory_space=pltpu.VMEM)
    smem = pl.BlockSpec(memory_space=pltpu.SMEM)
    return pl.pallas_call(
        functools.partial(layout_kernel, weight=weight),
        in_specs=[smem] + [vmem] * sections,
        out_specs=[vmem, vmem, vmem, smem],
        out_shape=[
            jax.ShapeDtypeStruct((2, depth, tokens), jnp.bfloat16),
            jax.ShapeDtypeStruct((tokens, depth), jnp.bfloat16),
            jax.ShapeDtypeStruct((steps, 1, width), jnp.float32),
            jax.ShapeDtypeStruct((1,), jnp.float32),
        ],
        scratch_shapes=[pltpu.VMEM((steps, 1, width), jnp.float32)],
        compiler_params=params(),
        cost_estimate=pl.CostEstimate(
            flops=64 * depth * tokens, bytes_accessed=14 * depth * tokens, transcendentals=0
        ),
    )(places, *gathered)


def factor_kernel(place_ref, part, own, diag, *refs, step, weight):
    portions, out = refs[:-1], refs[-1]
    start = 0
    for old in portions:
        stop = start + old.shape[0]
        shape = (old.shape[0], out.shape[1])
        fresh = jnp.zeros(shape, jnp.float32)
        for index in range(part.shape[0]):
            fresh += lax.dot_general(
                part[index, start:stop],
                own[index],
                (((1,), (1,)), ((), ())),
                preferred_element_type=jnp.float32,
            )
        block = factor_decay * old[...].astype(jnp.float32) + weight * fresh
        on_diag = lax.broadcasted_iota(jnp.int32, shape, 0) + start == lax.broadcasted_iota(
            jnp.int32, shape, 1
        )
        block = jnp.where(on_diag & (place_ref[0] == step), diag[0], block)
        out[start:stop] = block.astype(jnp.bfloat16)
        start = stop


def factor_block(place, features, portions, diag, step, weight):
    groups, _, tokens = features.shape
    rows, cols = sum(old.shape[0] for old in portions), portions[0].shape[1]
    return pl.pallas_call(
        functools.partial(factor_kernel, step=step, weight=weight),
        grid_spec=pltpu.PrefetchScalarGridSpec(
            num_scalar_prefetch=1,
            grid=(1,),
            in_specs=[
                pl.BlockSpec((groups, rows, tokens), lambda i, place: (0, step, 0)),
                pl.BlockSpec((groups, cols, tokens), lambda i, place: (0, place[0], 0)),
                pl.BlockSpec((1, 1, cols), lambda i, place: (place[0], 0, 0)),
            ]
            + [pl.BlockSpec(old.shape, lambda i, place: (0, 0)) for old in portions],
            out_specs=pl.BlockSpec((rows, cols), lambda i, place: (0, 0)),
        ),
        out_shape=jax.ShapeDtypeStruct((rows, cols), jnp.bfloat16),
        compiler_params=params(),
        cost_estimate=pl.CostEstimate(
            flops=2 * groups * rows * cols * tokens,
            bytes_accessed=4 * rows * cols + 4 * groups * rows * tokens,
            transcendentals=0,
        ),
    )(place, features, features, diag, *portions)


def block_products(place_ref, halves, blocks, pieces):
    width = pieces.shape[2]
    for index, half in enumerate(halves):
        pieces[2 * index] = half[:, :width]
        pieces[2 * index + 1] = half[:, width:]
    products = [None, None]
    for step in range(4):
        piece = pieces[place_ref[0] ^ step]
        for index in range(2):
            term = jnp.dot(piece, blocks[4 * index + step][...], preferred_element_type=jnp.float32)
            products[index] = term if products[index] is None else products[index] + term
    return products


def first_parts(place_ref, scale, rows, diag, product, index):
    width = product.shape[1]
    square = scale * scale
    values = rows[:, index * width : (index + 1) * width].astype(jnp.float32)
    low_diag = diag[place_ref[0] ^ index]
    first_diag = rounded(2.0 * scale - square * low_diag)
    by_first = 2.0 * scale * values - square * product
    step_one = first_diag * values - square * (product - low_diag * values)
    return by_first, step_one, low_diag, first_diag


def first_kernel(place_ref, scale_ref, rows, diag, *refs):
    blocks, (kept, message, pieces) = refs[:8], refs[8:]
    half = rows.shape[1] // 2
    halves = [rows[:, :half], rows[:, half:]]
    products = block_products(place_ref, halves, blocks, pieces)
    lows = []
    for index in range(2):
        kept[index] = products[index]
        parts = first_parts(place_ref, scale_ref[0], rows, diag, products[index], index)
        lows.append(parts[1].astype(jnp.bfloat16))
    message[...] = jnp.concatenate(lows, axis=1)


def second_kernel(place_ref, scale_ref, mine, theirs, rows, diag, before, *refs):
    blocks, (kept, message, pieces) = refs[:8], refs[8:]
    products = block_products(place_ref, [mine[...], theirs[...]], blocks, pieces)
    square = scale_ref[0] * scale_ref[0]
    lows = []
    for index in range(2):
        by_first, one, low_diag, first_diag = first_parts(
            place_ref, scale_ref[0], rows, diag, before[index], index
        )
        two = products[index] + low_diag * (one - rounded(one))
        low = two.astype(jnp.bfloat16)
        kept[index] = (
            2.0 * by_first - first_diag * two - square * low_diag * low.astype(jnp.float32)
        )
        lows.append(low)
    message[...] = jnp.concatenate(lows, axis=1)


def third_kernel(place_ref, scale_ref, mine, theirs, before, *refs):
    blocks, (keep, give, pieces) = refs[:8], refs[8:]
    products = block_products(place_ref, [mine[...], theirs[...]], blocks, pieces)
    square = scale_ref[0] * scale_ref[0]
    for index, out in ((0, keep), (1, give)):
        out[...] = (before[index] + square * products[index]).T.astype(jnp.bfloat16)


def chain_call(kernel, scalars, arrays, blocks, out_shape):
    tokens = arrays[0].shape[0]
    depth, width = blocks[0].shape
    vmem = pl.BlockSpec(memory_space=pltpu.VMEM)
    return pl.pallas_call(
        kernel,
        in_specs=[pl.BlockSpec(memory_space=pltpu.SMEM)] * len(scalars)
        + [vmem] * (len(arrays) + len(blocks)),
        out_specs=[vmem] * len(out_shape),
        out_shape=out_shape,
        scratch_shapes=[pltpu.VMEM((4, tokens, depth), jnp.bfloat16)],
        compiler_params=params(),
        cost_estimate=pl.CostEstimate(
            flops=2 * len(blocks) * tokens * depth * width,
            bytes_accessed=2 * len(blocks) * depth * width,
            transcendentals=0,
        ),
    )(*scalars, *arrays, *blocks)


def output_kernel(where_ref, scale, matches, *refs):
    lefts, mine, others = (refs[:4], refs[4:8]), refs[8:12], refs[12:16]
    attn, embed = refs[16:18]
    left_held, held, found, attn_made, embed_made, sems, out_sems = refs[18:]
    shard, layer, turn = where_ref[0], where_ref[1], where_ref[2]
    first = shard == 0
    rows, tokens_all = held.shape[1:]

    found_copy = pltpu.make_async_copy(matches, found, sems.at[7])
    for slot in range(2):
        for group in range(2):
            for place in range(4):

                @pl.when((turn == place) & (((shard ^ slot) == group)))
                def _():
                    source = lefts[group][place].at[pl.ds(0, rows)]
                    pltpu.make_async_copy(source, left_held.at[slot], sems.at[5 + slot]).start()

        if slot == 0:
            for index, source in enumerate((0, 1, 3, 0, 3)):
                from_mine = first if index < 3 else jnp.logical_not(first)
                for place in range(4):
                    for group, wanted in ((mine, from_mine), (others, jnp.logical_not(from_mine))):

                        @pl.when(wanted & ((layer ^ source) == place))
                        def _():
                            pltpu.make_async_copy(
                                group[place], held.at[index], sems.at[index]
                            ).start()

            found_copy.start()

    def arrived(slot):
        target = held.at[slot] if slot < 5 else left_held.at[slot - 5]
        pltpu.make_async_copy(mine[0], target, sems.at[slot]).wait()

    results = []
    arrived(5)
    for slot in range(4):
        if slot == 3:
            arrived(6)
        arrived(slot)
        attn_made[slot] = learning_rate * lax.dot_general(
            left_held[slot // 3],
            held[slot],
            (((1,), (1,)), ((), ())),
            preferred_element_type=jnp.float32,
        )
        results.append(
            pltpu.make_async_copy(attn_made.at[slot], attn.at[slot], out_sems.at[slot])
        )
        results[-1].start()
    arrived(4)
    found_copy.wait()
    part = found.shape[1] // 4
    for index in range(4):
        cols = pl.ds(index * part, part)
        product = jnp.dot(held[4], found[:, cols], preferred_element_type=jnp.float32)
        embed_made[:, cols] = product * scale[:, cols]
        results.append(
            pltpu.make_async_copy(
                embed_made.at[:, cols], embed.at[:, cols], out_sems.at[4 + index]
            )
        )
        results[-1].start()
    for result in results:
        result.wait()


def output_products(where, scale, matches, lefts, mine, others):
    cols, tokens_all = mine[0].shape
    vocab_block = scale.shape[1]
    anywhere = pl.BlockSpec(memory_space=pl.ANY)
    return pl.pallas_call(
        output_kernel,
        in_specs=[
            pl.BlockSpec(memory_space=pltpu.SMEM),
            pl.BlockSpec(memory_space=pltpu.VMEM),
        ]
        + [anywhere] * 17,
        out_specs=(anywhere, anywhere),
        out_shape=(
            jax.ShapeDtypeStruct((4, cols, cols), jnp.float32),
            jax.ShapeDtypeStruct((cols, vocab_block), jnp.float32),
        ),
        scratch_shapes=[
            pltpu.VMEM((2, cols, tokens_all), jnp.bfloat16),
            pltpu.VMEM((5, cols, tokens_all), jnp.bfloat16),
            pltpu.VMEM((tokens_all, vocab_block), jnp.bfloat16),
            pltpu.VMEM((4, cols, cols), jnp.float32),
            pltpu.VMEM((cols, vocab_block), jnp.float32),
            pltpu.SemaphoreType.DMA((8,)),
            pltpu.SemaphoreType.DMA((8,)),
        ],
        compiler_params=pltpu.CompilerParams(vmem_limit_bytes=60 * 1024 * 1024),
        cost_estimate=pl.CostEstimate(
            flops=2 * cols * tokens_all * (4 * cols + vocab_block),
            bytes_accessed=4 * cols * (4 * cols + vocab_block) + 14 * cols * tokens_all,
            transcendentals=0,
        ),
    )(where, scale, matches, *lefts[0], *lefts[1], *mine, *others)


def layer_plan(
    activations,
    router_grad,
    token_ids,
    norm_terms,
    old_factors,
    old_router_factor,
    old_norm_diag,
    old_embed_diag,
):
    n_tensor = lax.axis_size("tensor")
    n_section = lax.axis_size("section")
    n_shard = lax.axis_size("shard")
    shard = lax.axis_index("shard")
    layer = lax.axis_index("tensor")
    section = lax.axis_index("section")
    core = section % 2
    owned, row_block, col_block = old_factors.shape
    tokens = activations.shape[1]
    features_dev = activations.shape[2]
    tokens_all = tokens * n_shard
    weight = (1.0 - factor_decay) / tokens_all
    own_place = section ^ layer
    place = own_place.reshape(1)
    axes = ("shard", "tensor")

    def by_index(array, index, axis=0):
        return lax.dynamic_index_in_dim(array, index, axis, False)

    def held_by(layer_index):
        return jnp.where(layer_index == 3, 3, lax.rem(layer_index + 1, 3))

    by_feature = jnp.swapaxes(activations, 1, 2)
    diagonals = local_diagonals(old_factors) * (layer == section).astype(jnp.float32)
    extra = jnp.pad(split_three(diagonals), ((0, 0), (0, 0), (0, 3 * tokens - col_block)))
    extra = jnp.pad(extra.reshape(owned, 9, tokens), ((0, 0), (0, 7), (0, 0)))
    collected = []
    for step in range(n_tensor):
        factor = held_by(layer ^ step)
        message = jnp.concatenate(
            [
                by_index(by_feature, shard * owned + factor),
                by_index(by_feature, (1 - shard) * owned + factor),
                by_index(extra, factor),
            ],
            axis=0,
        )
        collected.append(swap(message, "tensor", n_tensor, step) if step else message)
    collected = jnp.stack(collected)
    lows = [
        by_index(old_factors, held_by(layer ^ step)).astype(jnp.bfloat16)
        for step in range(n_tensor)
    ]

    def both_shards(value, axis):
        other = swap(value, "shard", n_shard, 1)
        return jnp.where(
            shard == 0,
            jnp.concatenate([value, other], axis=axis),
            jnp.concatenate([other, value], axis=axis),
        )

    grad_all = both_shards(router_grad, 1)
    ids_all = both_shards(token_ids, 0)
    norm_values = norm_terms.astype(jnp.float32)
    norm_sums = jnp.stack([jnp.sum(norm_values, axis=1), jnp.sum(norm_values * norm_values, axis=1)])
    norm_sums = norm_sums + swap(norm_sums, "shard", n_shard, 1)
    vocab_block = old_embed_diag.shape[0]
    ids_here = layer * vocab_block + lax.iota(jnp.int32, vocab_block)
    matches = (ids_all[:, None] == ids_here[None, :]).astype(jnp.bfloat16)
    counts = jnp.sum(matches, axis=0, dtype=jnp.float32)
    divisor = factor_decay * old_embed_diag + (1.0 - factor_decay) * (counts / tokens_all) + damping
    embed_scale = (learning_rate / divisor)[None, :]
    router_matrix = (
        factor_decay * old_router_factor
        + weight * jnp.einsum("en,fn->ef", grad_all, grad_all, preferred_element_type=jnp.float32)
        + damping * jnp.eye(EXPERTS, dtype=jnp.float32)
    )
    router_inverse = local_inverse(router_matrix)
    router_right = jnp.einsum(
        "en,ef->fn", grad_all, router_inverse, preferred_element_type=jnp.float32
    ).astype(jnp.bfloat16)

    collected, lows, small = lax.optimization_barrier(
        (collected, lows, (router_right, matches, embed_scale, norm_sums))
    )
    router_right, matches, embed_scale, norm_sums = small
    other_tokens = swap(collected[:, features_dev : 2 * features_dev], "shard", n_shard, 1)
    quarter = row_block // 4

    def portion(step, start, stop):
        return swap(lows[step][start:stop], "tensor", n_tensor, step)

    near_rows = portion(2, 0, quarter)
    other_tokens, near_rows = lax.optimization_barrier((other_tokens, near_rows))
    collected = jnp.concatenate(
        [collected[:, :features_dev], other_tokens, collected[:, 2 * features_dev :]], axis=1
    )
    by_side = swap(collected, "section", n_section, 2)
    by_core = swap(collected, "section", n_section, 1)
    middle_rows = portion(2, quarter, 3 * quarter)
    by_side, middle_rows = lax.optimization_barrier((by_side, middle_rows))
    by_both = swap(by_side, "section", n_section, 1)
    far_block = portion(3, 0, row_block)
    last_rows = portion(2, 3 * quarter, row_block)
    blocks = [
        (lows[0],),
        (portion(1, 0, row_block),),
        (near_rows, middle_rows, last_rows),
        (far_block,),
    ]

    features, rows, low_diag, trace = lay_out(
        jnp.stack([own_place, layer, core, section]),
        (collected, by_core, by_side, by_both),
        weight,
    )
    scale = D / (3.0 * trace)
    own_cols = [
        factor_block(place, features, blocks[step], low_diag, step, weight)
        for step in range(n_tensor)
    ]
    other_cols = [swap(block, "section", n_section, 1) for block in own_cols]
    cols = own_cols + other_cols

    wide = jax.ShapeDtypeStruct((2, tokens, col_block), jnp.float32)
    sent = jax.ShapeDtypeStruct((tokens, 2 * col_block), jnp.bfloat16)
    part = jax.ShapeDtypeStruct((col_block, tokens), jnp.bfloat16)
    scalars = (place, scale)
    kept, message = chain_call(first_kernel, scalars, (rows, low_diag), cols, (wide, sent))
    theirs = swap(message, "section", n_section, 2)
    kept, message = chain_call(
        second_kernel, scalars, (message, theirs, rows, low_diag, kept), cols, (wide, sent)
    )
    theirs = swap(message, "section", n_section, 2)
    keep, give = chain_call(third_kernel, scalars, (message, theirs, kept), cols, (part, part))
    got = swap(give, "section", n_section, 1)
    own = jnp.where(
        core == shard, jnp.concatenate([keep, got], axis=1), jnp.concatenate([got, keep], axis=1)
    )

    planes = range(n_shard)
    layers = range(n_tensor)

    def useful(x, z):
        return z != 2 and (x, z) != (1, 1)

    def send(value, step, held):
        moves = [
            (x * n_tensor + z, x * n_tensor + (z ^ step))
            for x in planes
            for z in layers
            if useful(x, z ^ held)
        ]
        return lax.ppermute(value, axes, moves)

    def across(value, held):
        moves = [
            (x * n_tensor + z, (1 - x) * n_tensor + z)
            for x in planes
            for z in layers
            if useful(x, z ^ held)
        ]
        return lax.ppermute(value, axes, moves)

    everywhere = ("shard", "tensor", "section")

    def spot(x, z, s):
        return (x * n_tensor + z) * n_section + s

    def scatter(value, source):
        moved_here = lax.ppermute(
            value,
            everywhere,
            [(spot(x, source, s), spot(x, s, s)) for x in planes for s in layers if s != source],
        )
        return jnp.where(layer == source, value, moved_here)

    def to_side(value):
        return lax.ppermute(
            value, everywhere, [(spot(x, t, t), spot(x, t, t ^ 2)) for x in planes for t in layers]
        )

    def to_core(value):
        return lax.ppermute(
            value, everywhere, [(spot(x, t, t), spot(x, t, t ^ 1)) for x in planes for t in layers]
        )

    def to_far(value):
        return lax.ppermute(
            value,
            everywhere,
            [(spot(x, t, t ^ 2), spot(x, t, t ^ 3)) for x in planes for t in layers],
        )

    near_1 = send(own, 1, 0)
    near_2 = send(own, 2, 0)
    over_0 = across(own, 0)
    left_here = scatter(own, 2)
    near_1, own = lax.optimization_barrier((near_1, own))
    over_1 = across(near_1, 1)
    left_there = lax.ppermute(
        left_here, everywhere, [(spot(x, t, t), spot(1 - x, t, t)) for x in planes for t in layers]
    )
    router_cols = learning_rate * jnp.einsum(
        "fn,cn->fc", router_right, own, preferred_element_type=jnp.float32
    )
    router_moved = lax.ppermute(
        router_cols, everywhere, [(spot(1, 1, s), spot(1, s, s)) for s in layers if s != 1]
    )
    router_cols = jnp.where(layer == 1, router_cols, router_moved)
    side_here = to_side(left_here)
    lefts_here = (left_here, to_core(left_here), side_here, to_far(side_here))
    near_2, over_0, over_1, left_there, router_cols = lax.optimization_barrier(
        (near_2, over_0, over_1, left_there, router_cols)
    )
    near_3 = send(near_2, 1, 2)
    over_2 = across(near_2, 2)
    router_there = lax.ppermute(
        router_cols, everywhere, [(spot(1, t, t), spot(0, t, t)) for t in layers]
    )
    near_3, over_2, router_there = lax.optimization_barrier((near_3, over_2, router_there))
    over_3 = across(near_3, 3)
    router_cols = jnp.where(shard == 1, router_cols, router_there)
    router_side, router_core = to_side(router_cols), to_core(router_cols)
    side_there, over_3, router_side, router_core = lax.optimization_barrier(
        (to_side(left_there), over_3, router_side, router_core)
    )
    lefts_there = (left_there, to_core(left_there), side_there, to_far(side_there))
    routers = (router_cols, router_core, router_side, to_far(router_side))
    turn = section ^ layer
    precond_router = routers[3]
    for index in (2, 1, 0):
        precond_router = jnp.where(turn == index, routers[index], precond_router)

    precond_attn, embed_columns = output_products(
        jnp.stack([shard, layer, turn]),
        embed_scale,
        matches,
        (lefts_here, lefts_there),
        (own, near_1, near_2, near_3),
        (over_0, over_1, over_2, over_3),
    )
    precond_embed = embed_columns.T

    precond_norms = (
        learning_rate
        * norm_sums[0]
        / (
            factor_decay * old_norm_diag
            + (1.0 - factor_decay) * (norm_sums[1] / tokens_all)
            + damping
        )
    )
    return (precond_attn, precond_router, precond_norms, precond_embed)


def per_device(*arguments):
    one_each = arguments[4].shape[0] == lax.axis_size("tensor") == lax.axis_size("section")
    if one_each and lax.axis_size("section") == 4 and lax.axis_size("shard") == 2:
        return layer_plan(*arguments)
    return general_plan(*arguments)


def solution(mesh):
    return jax.shard_map(
        per_device,
        mesh=mesh,
        in_specs=(
            P(None, "shard", ("tensor", "section")),
            P(None, "shard"),
            P("shard"),
            P(None, "shard", ("tensor", "section")),
            P("shard", "tensor", "section"),
            P(),
            P(None, ("tensor", "section")),
            P("tensor"),
        ),
        out_specs=(
            P(None, "tensor", "section"),
            P(None, "tensor"),
            P(None, ("tensor", "section")),
            P("tensor", "section"),
        ),
        check_vma=False,
    )
```

```python
import functools
import math

import jax
import jax.numpy as jnp
from jax import lax
from jax.experimental import pallas as pl
from jax.experimental.pallas import tpu as pltpu
from jax.sharding import PartitionSpec as P

D = 2304
EXPERTS = 8
VOCAB = 8192


factor_decay = 0.5
damping = 0.01
learning_rate = 0.05


def local_inverse(matrix):
    width = matrix.shape[0]
    trace = jnp.sum(jnp.diagonal(matrix))
    factor_scale = width / (3.0 * trace)
    identity = jnp.eye(width, dtype=jnp.float32)
    matrix_low = lax.optimization_barrier(matrix.astype(jnp.bfloat16))
    first = 2.0 * factor_scale * identity - factor_scale * factor_scale * matrix_low.astype(
        jnp.float32
    )
    first_low = first.astype(jnp.bfloat16)
    image = jnp.dot(matrix_low, first_low, preferred_element_type=jnp.float32).astype(jnp.bfloat16)
    product = jnp.dot(first_low, image, preferred_element_type=jnp.float32)
    return (2.0 * first - product).astype(jnp.bfloat16)


def fold_with(columns, piece):
    return jnp.einsum("kij,kjl->kil", piece, columns, preferred_element_type=jnp.float32)


def general_plan(
    activations,
    router_grad,
    token_ids,
    norm_terms,
    old_factors,
    old_router_factor,
    old_norm_diag,
    old_embed_diag,
):
    n_tensor = lax.axis_size("tensor")
    n_section = lax.axis_size("section")
    n_shard = lax.axis_size("shard")
    tensor_rank = lax.axis_index("tensor")
    section_rank = lax.axis_index("section")
    row_block = D // n_tensor
    col_block = D // n_section
    tokens_all = activations.shape[1] * n_shard
    row_start = tensor_rank * row_block
    col_start = section_rank * col_block

    def collect(carry, piece):
        whole = lax.all_gather(piece, ("tensor", "section"), axis=1, tiled=True)
        rows_part = lax.dynamic_slice_in_dim(whole, row_start, row_block, 1)
        cols_part = lax.dynamic_slice_in_dim(whole, col_start, col_block, 1)
        return (carry, (rows_part, cols_part))

    unused_carry, (row_parts, col_parts) = lax.scan(collect, jnp.int32(0), activations)
    partial_value = jnp.einsum(
        "mnr,mnc->mrc", row_parts, col_parts, preferred_element_type=jnp.float32
    )
    fresh = lax.psum_scatter(partial_value, "shard", scatter_dimension=0, tiled=True) / tokens_all
    row_index = lax.broadcasted_iota(jnp.int32, (row_block, col_block), 0) + row_start
    col_index = lax.broadcasted_iota(jnp.int32, (row_block, col_block), 1) + col_start
    eye_block = (row_index == col_index).astype(jnp.float32)
    matrix = factor_decay * old_factors + (1.0 - factor_decay) * fresh + damping * eye_block
    diag_part = jnp.sum(matrix * eye_block, axis=(1, 2))
    trace = lax.psum(diag_part, ("tensor", "section"))
    factor_scale = (D / (3.0 * trace))[:, None, None]
    matrix_low = lax.optimization_barrier(matrix.astype(jnp.bfloat16))
    first = 2.0 * factor_scale * eye_block - factor_scale * factor_scale * matrix_low.astype(
        jnp.float32
    )
    first_low = first.astype(jnp.bfloat16)
    first_cols = lax.all_gather(first_low, "tensor", axis=1, tiled=True)
    image = fold_with(first_cols, lax.all_gather(matrix_low, "section", axis=2, tiled=True))
    image_cols = lax.all_gather(image.astype(jnp.bfloat16), "tensor", axis=1, tiled=True)
    product = fold_with(image_cols, lax.all_gather(first_low, "section", axis=2, tiled=True))
    inverse_low = (2.0 * first - product).astype(jnp.bfloat16)
    inverses = lax.all_gather(inverse_low, "shard", axis=0, tiled=True)
    left_terms = jnp.stack(
        [
            jnp.einsum("nc,rc->nr", col_parts[m], inverses[m], preferred_element_type=jnp.float32)
            for m in (0, 4, 6)
        ]
    )
    left = lax.psum(left_terms, "section").astype(jnp.bfloat16)
    right_terms = jnp.stack(
        [
            jnp.einsum("nr,rc->nc", row_parts[m], inverses[m], preferred_element_type=jnp.float32)
            for m in (1, 2, 3, 5, 7)
        ]
    )
    right = lax.psum(right_terms, "tensor").astype(jnp.bfloat16)
    norm_values = norm_terms.astype(jnp.float32)
    router_part = jnp.einsum(
        "en,fn->ef", router_grad, router_grad, preferred_element_type=jnp.float32
    )
    router_sum, norm_total, norm_squares = lax.psum(
        (router_part, jnp.sum(norm_values, axis=1), jnp.sum(norm_values * norm_values, axis=1)),
        "shard",
    )
    router_matrix = (
        factor_decay * old_router_factor
        + (1.0 - factor_decay) * (router_sum / tokens_all)
        + damping * jnp.eye(EXPERTS, dtype=jnp.float32)
    )
    router_inverse = local_inverse(router_matrix)
    router_right = jnp.einsum(
        "en,ef->nf", router_grad, router_inverse, preferred_element_type=jnp.float32
    ).astype(jnp.bfloat16)
    precond_norms = (
        learning_rate
        * norm_total
        / (
            factor_decay * old_norm_diag
            + (1.0 - factor_decay) * (norm_squares / tokens_all)
            + damping
        )
    )
    ids_all = lax.all_gather(token_ids, "shard", axis=0, tiled=True)
    embed_all = lax.all_gather(right[4], "shard", axis=0, tiled=True)
    paired_left = jnp.stack([left[0], left[0], left[0], left[1]])
    attn_terms = jnp.einsum(
        "wnr,wnc->wrc", paired_left, right[:4], preferred_element_type=jnp.float32
    )
    router_term = jnp.einsum("nf,nr->fr", router_right, left[2], preferred_element_type=jnp.float32)
    attn_sum, router_total = lax.psum((attn_terms, router_term), "shard")
    precond_attn = learning_rate * attn_sum
    precond_router = learning_rate * router_total
    vocab_block = VOCAB // n_tensor
    step_rows = math.gcd(vocab_block, 512)
    vocab_start = tensor_rank * vocab_block

    def embed_block(block_index):
        ids_here = vocab_start + block_index * step_rows + lax.iota(jnp.int32, step_rows)
        onehot = (ids_here[:, None] == ids_all[None, :]).astype(jnp.bfloat16)
        summed = jnp.dot(onehot, embed_all, preferred_element_type=jnp.float32)
        tallies = jnp.sum(onehot, axis=1, dtype=jnp.float32)
        return (summed, tallies)

    block_sums, block_counts = lax.map(
        embed_block, jnp.arange(vocab_block // step_rows, dtype=jnp.int32)
    )
    embed_sum = block_sums.reshape(vocab_block, col_block)
    counts = block_counts.reshape(vocab_block)
    divisor = factor_decay * old_embed_diag + (1.0 - factor_decay) * (counts / tokens_all) + damping
    precond_embed = learning_rate * embed_sum / divisor[:, None]
    return (precond_attn, precond_router, precond_norms, precond_embed)


def split_three(values):
    high = lax.reduce_precision(values, 8, 7)
    rest = values - high
    middle = lax.reduce_precision(rest, 8, 7)
    return jnp.stack([high, middle, rest - middle], axis=-2).astype(jnp.bfloat16)


def swap(value, axis, size, step):
    return lax.ppermute(value, axis, [(i, i ^ step) for i in range(size)])


def local_diagonals(blocks):
    width = blocks.shape[1]
    pieces = []
    for start in range(0, width, 128):
        size = min(128, width - start)
        tile = blocks[:, start : start + size, start : start + size]
        pieces.append(jnp.sum(tile * jnp.eye(size, dtype=tile.dtype), axis=1))
    return jnp.concatenate(pieces, axis=1)


def rounded(values):
    return values.astype(jnp.bfloat16).astype(jnp.float32)


def params():
    return pltpu.CompilerParams(vmem_limit_bytes=40 * 1024 * 1024)


def layout_kernel(place_ref, *refs, weight):
    gathered, (features, rows, low_diag, trace, old) = refs[:4], refs[4:]
    own_place, layer, core, here = (place_ref[index] for index in range(4))
    steps, _, tokens = gathered[0].shape
    sections = len(gathered)
    groups, depth, _ = features.shape
    part = depth // (sections * steps)
    width = depth // steps
    for away in range(sections):
        section = here ^ away
        codes = jnp.zeros((16, tokens), jnp.float32)
        for step in range(steps):
            start = pl.multiple_of((step * sections + section) * part, 16)
            for group in range(groups):
                features[group, pl.ds(start, part)] = gathered[away][
                    step, group * part : (group + 1) * part
                ]
            codes += gathered[away][step, groups * part :].astype(jnp.float32)
        codes = codes[0:3] + codes[3:6] + codes[6:9]
        pieces = [codes[0:1], codes[1:2], codes[2:3, : width - 2 * tokens]]
        old[section ^ layer] = jnp.concatenate(pieces, axis=1)
    ones = jnp.ones((8, tokens), jnp.bfloat16)
    total = jnp.float32(0.0)
    for step in range(steps):
        squares = jnp.zeros((8, width), jnp.float32)
        for group in range(groups):
            values = features[group, step * width : (step + 1) * width].astype(jnp.float32)
            values = values * values
            high = values.astype(jnp.bfloat16)
            low = (values - high.astype(jnp.float32)).astype(jnp.bfloat16)
            for piece in (high, low):
                squares += lax.dot_general(
                    ones, piece, (((1,), (1,)), ((), ())), preferred_element_type=jnp.float32
                )
        diag = factor_decay * old[step] + weight * squares[0:1] + damping
        total += jnp.sum(diag)
        low_diag[step] = rounded(diag)
        start = pl.multiple_of((own_place ^ step) * width, width)
        mine = features[core, pl.ds(start, width)]
        rows[:, step * width : (step + 1) * width] = mine.T
    trace[0] = total


def lay_out(places, gathered, weight):
    steps, height, tokens = gathered[0].shape
    sections = len(gathered)
    part = (height - 16) // 2
    depth = sections * steps * part
    width = depth // steps
    vmem = pl.BlockSpec(memory_space=pltpu.VMEM)
    smem = pl.BlockSpec(memory_space=pltpu.SMEM)
    return pl.pallas_call(
        functools.partial(layout_kernel, weight=weight),
        in_specs=[smem] + [vmem] * sections,
        out_specs=[vmem, vmem, vmem, smem],
        out_shape=[
            jax.ShapeDtypeStruct((2, depth, tokens), jnp.bfloat16),
            jax.ShapeDtypeStruct((tokens, depth), jnp.bfloat16),
            jax.ShapeDtypeStruct((steps, 1, width), jnp.float32),
            jax.ShapeDtypeStruct((1,), jnp.float32),
        ],
        scratch_shapes=[pltpu.VMEM((steps, 1, width), jnp.float32)],
        compiler_params=params(),
        cost_estimate=pl.CostEstimate(
            flops=64 * depth * tokens, bytes_accessed=14 * depth * tokens, transcendentals=0
        ),
    )(places, *gathered)


def factor_kernel(place_ref, part, own, diag, *refs, step, weight):
    portions, out = refs[:-1], refs[-1]
    start = 0
    for old in portions:
        stop = start + old.shape[0]
        shape = (old.shape[0], out.shape[1])
        fresh = jnp.zeros(shape, jnp.float32)
        for index in range(part.shape[0]):
            fresh += lax.dot_general(
                part[index, start:stop],
                own[index],
                (((1,), (1,)), ((), ())),
                preferred_element_type=jnp.float32,
            )
        block = factor_decay * old[...].astype(jnp.float32) + weight * fresh
        on_diag = lax.broadcasted_iota(jnp.int32, shape, 0) + start == lax.broadcasted_iota(
            jnp.int32, shape, 1
        )
        block = jnp.where(on_diag & (place_ref[0] == step), diag[0], block)
        out[start:stop] = block.astype(jnp.bfloat16)
        start = stop


def factor_block(place, features, portions, diag, step, weight):
    groups, _, tokens = features.shape
    rows, cols = sum(old.shape[0] for old in portions), portions[0].shape[1]
    return pl.pallas_call(
        functools.partial(factor_kernel, step=step, weight=weight),
        grid_spec=pltpu.PrefetchScalarGridSpec(
            num_scalar_prefetch=1,
            grid=(1,),
            in_specs=[
                pl.BlockSpec((groups, rows, tokens), lambda i, place: (0, step, 0)),
                pl.BlockSpec((groups, cols, tokens), lambda i, place: (0, place[0], 0)),
                pl.BlockSpec((1, 1, cols), lambda i, place: (place[0], 0, 0)),
            ]
            + [pl.BlockSpec(old.shape, lambda i, place: (0, 0)) for old in portions],
            out_specs=pl.BlockSpec((rows, cols), lambda i, place: (0, 0)),
        ),
        out_shape=jax.ShapeDtypeStruct((rows, cols), jnp.bfloat16),
        compiler_params=params(),
        cost_estimate=pl.CostEstimate(
            flops=2 * groups * rows * cols * tokens,
            bytes_accessed=4 * rows * cols + 4 * groups * rows * tokens,
            transcendentals=0,
        ),
    )(place, features, features, diag, *portions)


def block_products(place_ref, halves, blocks, pieces):
    width = pieces.shape[2]
    for index, half in enumerate(halves):
        pieces[2 * index] = half[:, :width]
        pieces[2 * index + 1] = half[:, width:]
    products = [None, None]
    for step in range(4):
        piece = pieces[place_ref[0] ^ step]
        for index in range(2):
            term = jnp.dot(piece, blocks[4 * index + step][...], preferred_element_type=jnp.float32)
            products[index] = term if products[index] is None else products[index] + term
    return products


def first_parts(place_ref, scale, rows, diag, product, index):
    width = product.shape[1]
    square = scale * scale
    values = rows[:, index * width : (index + 1) * width].astype(jnp.float32)
    low_diag = diag[place_ref[0] ^ index]
    first_diag = rounded(2.0 * scale - square * low_diag)
    by_first = 2.0 * scale * values - square * product
    step_one = first_diag * values - square * (product - low_diag * values)
    return by_first, step_one, low_diag, first_diag


def first_kernel(place_ref, scale_ref, rows, diag, *refs):
    blocks, (kept, message, pieces) = refs[:8], refs[8:]
    half = rows.shape[1] // 2
    halves = [rows[:, :half], rows[:, half:]]
    products = block_products(place_ref, halves, blocks, pieces)
    lows = []
    for index in range(2):
        kept[index] = products[index]
        parts = first_parts(place_ref, scale_ref[0], rows, diag, products[index], index)
        lows.append(parts[1].astype(jnp.bfloat16))
    message[...] = jnp.concatenate(lows, axis=1)


def second_kernel(place_ref, scale_ref, mine, theirs, rows, diag, before, *refs):
    blocks, (kept, message, pieces) = refs[:8], refs[8:]
    products = block_products(place_ref, [mine[...], theirs[...]], blocks, pieces)
    square = scale_ref[0] * scale_ref[0]
    lows = []
    for index in range(2):
        by_first, one, low_diag, first_diag = first_parts(
            place_ref, scale_ref[0], rows, diag, before[index], index
        )
        two = products[index] + low_diag * (one - rounded(one))
        low = two.astype(jnp.bfloat16)
        kept[index] = (
            2.0 * by_first - first_diag * two - square * low_diag * low.astype(jnp.float32)
        )
        lows.append(low)
    message[...] = jnp.concatenate(lows, axis=1)


def third_kernel(place_ref, scale_ref, mine, theirs, before, *refs):
    blocks, (keep, give, pieces) = refs[:8], refs[8:]
    products = block_products(place_ref, [mine[...], theirs[...]], blocks, pieces)
    square = scale_ref[0] * scale_ref[0]
    for index, out in ((0, keep), (1, give)):
        out[...] = (before[index] + square * products[index]).T.astype(jnp.bfloat16)


def chain_call(kernel, scalars, arrays, blocks, out_shape):
    tokens = arrays[0].shape[0]
    depth, width = blocks[0].shape
    vmem = pl.BlockSpec(memory_space=pltpu.VMEM)
    return pl.pallas_call(
        kernel,
        in_specs=[pl.BlockSpec(memory_space=pltpu.SMEM)] * len(scalars)
        + [vmem] * (len(arrays) + len(blocks)),
        out_specs=[vmem] * len(out_shape),
        out_shape=out_shape,
        scratch_shapes=[pltpu.VMEM((4, tokens, depth), jnp.bfloat16)],
        compiler_params=params(),
        cost_estimate=pl.CostEstimate(
            flops=2 * len(blocks) * tokens * depth * width,
            bytes_accessed=2 * len(blocks) * depth * width,
            transcendentals=0,
        ),
    )(*scalars, *arrays, *blocks)


def output_kernel(where_ref, scale, matches, *refs):
    lefts, rights, refs = refs[:4], refs[4:8], refs[-9:]
    attn, embed, left_held, held, found, attn_made, embed_made, sems, out_sems = refs
    owner, layer, turn = where_ref[0], where_ref[1], where_ref[2]
    rows = held.shape[1]

    for place in range(4):

        @pl.when(turn == place)
        def _():
            pltpu.make_async_copy(lefts[place].at[pl.ds(0, rows)], left_held, sems.at[4]).start()

    def fetch(sources):
        for slot, source in enumerate(sources):
            for place in range(4):

                @pl.when((layer ^ source) == place)
                def _():
                    pltpu.make_async_copy(rights[place], held.at[slot], sems.at[slot]).start()

    def left_arrived():
        pltpu.make_async_copy(left_held, left_held, sems.at[4]).wait()

    def arrived(slot):
        pltpu.make_async_copy(held.at[slot], held.at[slot], sems.at[slot]).wait()
        return held[slot]

    def send_product(slot, target):
        attn_made[slot] = learning_rate * lax.dot_general(
            left_held[...],
            arrived(slot),
            (((1,), (1,)), ((), ())),
            preferred_element_type=jnp.float32,
        )
        copy = pltpu.make_async_copy(attn_made.at[slot], attn.at[target], out_sems.at[slot])
        copy.start()
        return copy

    @pl.when(owner == 0)
    def _():
        fetch((0, 1, 3))
        left_arrived()
        for copy in [send_product(slot, slot) for slot in range(3)]:
            copy.wait()

    @pl.when(owner == 1)
    def _():
        fetch((0, 3))
        found_copy = pltpu.make_async_copy(matches, found, sems.at[5])
        found_copy.start()
        left_arrived()
        results = [send_product(0, 3)]
        right = arrived(1)
        found_copy.wait()
        part = found.shape[1] // 4
        for index in range(4):
            cols = pl.ds(index * part, part)
            product = jnp.dot(right, found[:, cols], preferred_element_type=jnp.float32)
            embed_made[:, cols] = product * scale[:, cols]
            results.append(
                pltpu.make_async_copy(
                    embed_made.at[:, cols], embed.at[:, cols], out_sems.at[3 + index]
                )
            )
            results[-1].start()
        for copy in results:
            copy.wait()


def output_products(where, scale, matches, lefts, rights, made):
    cols, tokens_all = rights[0].shape
    vocab_block = scale.shape[1]
    anywhere = pl.BlockSpec(memory_space=pl.ANY)
    return pl.pallas_call(
        output_kernel,
        in_specs=[
            pl.BlockSpec(memory_space=pltpu.SMEM),
            pl.BlockSpec(memory_space=pltpu.VMEM),
        ]
        + [anywhere] * (9 + len(made)),
        out_specs=(anywhere, anywhere),
        out_shape=(
            jax.ShapeDtypeStruct((4, cols, cols), jnp.float32),
            jax.ShapeDtypeStruct((cols, vocab_block), jnp.float32),
        ),
        input_output_aliases={11: 0, 12: 1} if made else {},
        scratch_shapes=[
            pltpu.VMEM((cols, tokens_all), jnp.bfloat16),
            pltpu.VMEM((3, cols, tokens_all), jnp.bfloat16),
            pltpu.VMEM((tokens_all, vocab_block), jnp.bfloat16),
            pltpu.VMEM((3, cols, cols), jnp.float32),
            pltpu.VMEM((cols, vocab_block), jnp.float32),
            pltpu.SemaphoreType.DMA((6,)),
            pltpu.SemaphoreType.DMA((7,)),
        ],
        compiler_params=pltpu.CompilerParams(vmem_limit_bytes=60 * 1024 * 1024),
        cost_estimate=pl.CostEstimate(
            flops=6 * cols * cols * tokens_all,
            bytes_accessed=12 * cols * cols + 8 * cols * tokens_all,
            transcendentals=0,
        ),
    )(where, scale, matches, *lefts, *rights, *made)


def layer_plan(
    activations,
    router_grad,
    token_ids,
    norm_terms,
    old_factors,
    old_router_factor,
    old_norm_diag,
    old_embed_diag,
):
    n_tensor = lax.axis_size("tensor")
    n_section = lax.axis_size("section")
    n_shard = lax.axis_size("shard")
    shard = lax.axis_index("shard")
    layer = lax.axis_index("tensor")
    section = lax.axis_index("section")
    core = section % 2
    owned, row_block, col_block = old_factors.shape
    tokens = activations.shape[1]
    features_dev = activations.shape[2]
    tokens_all = tokens * n_shard
    weight = (1.0 - factor_decay) / tokens_all
    own_place = section ^ layer
    place = own_place.reshape(1)
    axes = ("shard", "tensor")

    def by_index(array, index, axis=0):
        return lax.dynamic_index_in_dim(array, index, axis, False)

    def held_by(layer_index):
        return jnp.where(layer_index == 3, 3, lax.rem(layer_index + 1, 3))

    by_feature = jnp.swapaxes(activations, 1, 2)
    diagonals = local_diagonals(old_factors) * (layer == section).astype(jnp.float32)
    extra = jnp.pad(split_three(diagonals), ((0, 0), (0, 0), (0, 3 * tokens - col_block)))
    extra = jnp.pad(extra.reshape(owned, 9, tokens), ((0, 0), (0, 7), (0, 0)))
    collected = []
    for step in range(n_tensor):
        factor = held_by(layer ^ step)
        message = jnp.concatenate(
            [
                by_index(by_feature, shard * owned + factor),
                by_index(by_feature, (1 - shard) * owned + factor),
                by_index(extra, factor),
            ],
            axis=0,
        )
        collected.append(swap(message, "tensor", n_tensor, step) if step else message)
    collected = jnp.stack(collected)

    def old_block(factors, step):
        return by_index(factors, held_by(layer ^ step)).astype(jnp.bfloat16)

    far_block = swap(old_block(old_factors, 2), "tensor", n_tensor, 2)
    later_factors = lax.optimization_barrier(old_factors)
    near_block = swap(old_block(later_factors, 1), "tensor", n_tensor, 1)
    here_block, farthest = old_block(later_factors, 0), old_block(later_factors, 3)

    def both_shards(value, axis):
        other = swap(value, "shard", n_shard, 1)
        return jnp.where(
            shard == 0,
            jnp.concatenate([value, other], axis=axis),
            jnp.concatenate([other, value], axis=axis),
        )

    grad_all = both_shards(router_grad, 1)
    ids_all = both_shards(token_ids, 0)
    norm_values = norm_terms.astype(jnp.float32)
    norm_sums = jnp.stack([jnp.sum(norm_values, axis=1), jnp.sum(norm_values * norm_values, axis=1)])
    norm_sums = norm_sums + swap(norm_sums, "shard", n_shard, 1)
    vocab_block = old_embed_diag.shape[0]
    ids_here = layer * vocab_block + lax.iota(jnp.int32, vocab_block)
    matches = (ids_all[:, None] == ids_here[None, :]).astype(jnp.bfloat16)
    counts = jnp.sum(matches, axis=0, dtype=jnp.float32)
    divisor = factor_decay * old_embed_diag + (1.0 - factor_decay) * (counts / tokens_all) + damping
    embed_scale = (learning_rate / divisor)[None, :]
    router_matrix = (
        factor_decay * old_router_factor
        + weight * jnp.einsum("en,fn->ef", grad_all, grad_all, preferred_element_type=jnp.float32)
        + damping * jnp.eye(EXPERTS, dtype=jnp.float32)
    )
    router_inverse = local_inverse(router_matrix)
    router_right = jnp.einsum(
        "en,ef->fn", grad_all, router_inverse, preferred_element_type=jnp.float32
    ).astype(jnp.bfloat16)

    other_tokens = swap(collected[:, features_dev : 2 * features_dev], "shard", n_shard, 1)
    small = (router_right, matches, embed_scale, norm_sums)
    other_tokens, collected, far_block, near_block, here_block, farthest, small = (
        lax.optimization_barrier(
            (other_tokens, collected, far_block, near_block, here_block, farthest, small)
        )
    )
    router_right, matches, embed_scale, norm_sums = small
    collected = jnp.concatenate(
        [collected[:, :features_dev], other_tokens, collected[:, 2 * features_dev :]], axis=1
    )
    by_side = swap(collected, "section", n_section, 2)
    by_core = swap(collected, "section", n_section, 1)
    part_rows = row_block // 2
    farthest_1 = swap(farthest[:part_rows], "tensor", n_tensor, 3)
    by_side, farthest_1 = lax.optimization_barrier((by_side, farthest_1))
    by_both = swap(by_side, "section", n_section, 1)
    farthest_2 = swap(farthest[part_rows:], "tensor", n_tensor, 3)
    blocks = [(here_block,), (near_block,), (far_block,), (farthest_1, farthest_2)]

    features, rows, low_diag, trace = lay_out(
        jnp.stack([own_place, layer, core, section]),
        (collected, by_core, by_side, by_both),
        weight,
    )
    scale = D / (3.0 * trace)
    own_cols = [
        factor_block(place, features, blocks[step], low_diag, step, weight)
        for step in range(n_tensor)
    ]
    other_cols = [swap(block, "section", n_section, 1) for block in own_cols]
    cols = own_cols + other_cols

    wide = jax.ShapeDtypeStruct((2, tokens, col_block), jnp.float32)
    sent = jax.ShapeDtypeStruct((tokens, 2 * col_block), jnp.bfloat16)
    part = jax.ShapeDtypeStruct((col_block, tokens), jnp.bfloat16)
    scalars = (place, scale)
    kept, message = chain_call(first_kernel, scalars, (rows, low_diag), cols, (wide, sent))
    theirs = swap(message, "section", n_section, 2)
    kept, message = chain_call(
        second_kernel, scalars, (message, theirs, rows, low_diag, kept), cols, (wide, sent)
    )
    theirs = swap(message, "section", n_section, 2)
    keep, give = chain_call(third_kernel, scalars, (message, theirs, kept), cols, (part, part))
    got = swap(give, "section", n_section, 1)
    own = jnp.where(
        core == shard, jnp.concatenate([keep, got], axis=1), jnp.concatenate([got, keep], axis=1)
    )

    planes = range(n_shard)
    layers = range(n_tensor)

    def useful(x, z):
        return z != 2 and (x, z) != (1, 1)

    def send(value, step, held):
        moves = [
            (x * n_tensor + z, x * n_tensor + (z ^ step))
            for x in planes
            for z in layers
            if useful(x, z ^ held)
        ]
        return lax.ppermute(value, axes, moves)

    def across(value, held):
        moves = [
            (x * n_tensor + z, (1 - x) * n_tensor + z)
            for x in planes
            for z in layers
            if useful(x, z ^ held)
        ]
        return lax.ppermute(value, axes, moves)

    everywhere = ("shard", "tensor", "section")

    def spot(x, z, s):
        return (x * n_tensor + z) * n_section + s

    def scatter(value, source):
        moved_here = lax.ppermute(
            value,
            everywhere,
            [(spot(x, source, s), spot(x, s, s)) for x in planes for s in layers if s != source],
        )
        return jnp.where(layer == source, value, moved_here)

    def to_side(value):
        return lax.ppermute(
            value, everywhere, [(spot(x, t, t), spot(x, t, t ^ 2)) for x in planes for t in layers]
        )

    def to_core(value):
        return lax.ppermute(
            value, everywhere, [(spot(x, t, t), spot(x, t, t ^ 1)) for x in planes for t in layers]
        )

    def to_far(value):
        return lax.ppermute(
            value,
            everywhere,
            [(spot(x, t, t ^ 2), spot(x, t, t ^ 3)) for x in planes for t in layers],
        )

    near_1 = send(own, 1, 0)
    near_2 = send(own, 2, 0)
    over_0 = across(own, 0)
    left_here = scatter(own, 2)
    near_1, own = lax.optimization_barrier((near_1, own))
    over_1 = across(near_1, 1)
    left_there = lax.ppermute(
        left_here, everywhere, [(spot(x, t, t), spot(1 - x, t, t)) for x in planes for t in layers]
    )
    router_cols = learning_rate * jnp.einsum(
        "fn,cn->fc", router_right, own, preferred_element_type=jnp.float32
    )
    router_moved = lax.ppermute(
        router_cols, everywhere, [(spot(1, 1, s), spot(1, s, s)) for s in layers if s != 1]
    )
    router_cols = jnp.where(layer == 1, router_cols, router_moved)
    side_here = to_side(left_here)
    lefts_here = (left_here, to_core(left_here), side_here, to_far(side_here))
    near_2, over_0, over_1, left_there, router_cols = lax.optimization_barrier(
        (near_2, over_0, over_1, left_there, router_cols)
    )
    near_3 = send(near_2, 1, 2)
    over_2 = across(near_2, 2)
    router_there = lax.ppermute(
        router_cols, everywhere, [(spot(1, t, t), spot(0, t, t)) for t in layers]
    )
    near_3, over_2, router_there = lax.optimization_barrier((near_3, over_2, router_there))
    over_3 = across(near_3, 3)
    router_cols = jnp.where(shard == 1, router_cols, router_there)
    router_side, router_core = to_side(router_cols), to_core(router_cols)
    turn = section ^ layer
    made = output_products(
        jnp.stack([shard, layer, turn]),
        embed_scale,
        matches,
        lefts_here,
        (own, near_1, near_2, near_3),
        (),
    )
    side_there, over_3, router_side, router_core, made = lax.optimization_barrier(
        (to_side(left_there), over_3, router_side, router_core, made)
    )
    lefts_there = (left_there, to_core(left_there), side_there, to_far(side_there))
    routers = (router_cols, router_core, router_side, to_far(router_side))
    precond_router = routers[3]
    for index in (2, 1, 0):
        precond_router = jnp.where(turn == index, routers[index], precond_router)

    precond_attn, embed_columns = output_products(
        jnp.stack([1 - shard, layer, turn]),
        embed_scale,
        matches,
        lefts_there,
        (over_0, over_1, over_2, over_3),
        made,
    )
    precond_embed = embed_columns.T

    precond_norms = (
        learning_rate
        * norm_sums[0]
        / (
            factor_decay * old_norm_diag
            + (1.0 - factor_decay) * (norm_sums[1] / tokens_all)
            + damping
        )
    )
    return (precond_attn, precond_router, precond_norms, precond_embed)


def per_device(*arguments):
    one_each = arguments[4].shape[0] == lax.axis_size("tensor") == lax.axis_size("section")
    if one_each and lax.axis_size("section") == 4 and lax.axis_size("shard") == 2:
        return layer_plan(*arguments)
    return general_plan(*arguments)


def solution(mesh):
    return jax.shard_map(
        per_device,
        mesh=mesh,
        in_specs=(
            P(None, "shard", ("tensor", "section")),
            P(None, "shard"),
            P("shard"),
            P(None, "shard", ("tensor", "section")),
            P("shard", "tensor", "section"),
            P(),
            P(None, ("tensor", "section")),
            P("tensor"),
        ),
        out_specs=(
            P(None, "tensor", "section"),
            P(None, "tensor"),
            P(None, ("tensor", "section")),
            P("tensor", "section"),
        ),
        check_vma=False,
    )
```

```python
import functools
import math

import jax
import jax.numpy as jnp
from jax import lax
from jax.experimental import pallas as pl
from jax.experimental.pallas import tpu as pltpu
from jax.sharding import PartitionSpec as P

D = 2304
EXPERTS = 8
VOCAB = 8192


factor_decay = 0.5
damping = 0.01
learning_rate = 0.05


def local_inverse(matrix):
    width = matrix.shape[0]
    trace = jnp.sum(jnp.diagonal(matrix))
    factor_scale = width / (3.0 * trace)
    identity = jnp.eye(width, dtype=jnp.float32)
    matrix_low = lax.optimization_barrier(matrix.astype(jnp.bfloat16))
    first = 2.0 * factor_scale * identity - factor_scale * factor_scale * matrix_low.astype(
        jnp.float32
    )
    first_low = first.astype(jnp.bfloat16)
    image = jnp.dot(matrix_low, first_low, preferred_element_type=jnp.float32).astype(jnp.bfloat16)
    product = jnp.dot(first_low, image, preferred_element_type=jnp.float32)
    return (2.0 * first - product).astype(jnp.bfloat16)


def fold_with(columns, piece):
    return jnp.einsum("kij,kjl->kil", piece, columns, preferred_element_type=jnp.float32)


def general_plan(
    activations,
    router_grad,
    token_ids,
    norm_terms,
    old_factors,
    old_router_factor,
    old_norm_diag,
    old_embed_diag,
):
    n_tensor = lax.axis_size("tensor")
    n_section = lax.axis_size("section")
    n_shard = lax.axis_size("shard")
    tensor_rank = lax.axis_index("tensor")
    section_rank = lax.axis_index("section")
    row_block = D // n_tensor
    col_block = D // n_section
    tokens_all = activations.shape[1] * n_shard
    row_start = tensor_rank * row_block
    col_start = section_rank * col_block

    def collect(carry, piece):
        whole = lax.all_gather(piece, ("tensor", "section"), axis=1, tiled=True)
        rows_part = lax.dynamic_slice_in_dim(whole, row_start, row_block, 1)
        cols_part = lax.dynamic_slice_in_dim(whole, col_start, col_block, 1)
        return (carry, (rows_part, cols_part))

    unused_carry, (row_parts, col_parts) = lax.scan(collect, jnp.int32(0), activations)
    partial_value = jnp.einsum(
        "mnr,mnc->mrc", row_parts, col_parts, preferred_element_type=jnp.float32
    )
    fresh = lax.psum_scatter(partial_value, "shard", scatter_dimension=0, tiled=True) / tokens_all
    row_index = lax.broadcasted_iota(jnp.int32, (row_block, col_block), 0) + row_start
    col_index = lax.broadcasted_iota(jnp.int32, (row_block, col_block), 1) + col_start
    eye_block = (row_index == col_index).astype(jnp.float32)
    matrix = factor_decay * old_factors + (1.0 - factor_decay) * fresh + damping * eye_block
    diag_part = jnp.sum(matrix * eye_block, axis=(1, 2))
    trace = lax.psum(diag_part, ("tensor", "section"))
    factor_scale = (D / (3.0 * trace))[:, None, None]
    matrix_low = lax.optimization_barrier(matrix.astype(jnp.bfloat16))
    first = 2.0 * factor_scale * eye_block - factor_scale * factor_scale * matrix_low.astype(
        jnp.float32
    )
    first_low = first.astype(jnp.bfloat16)
    first_cols = lax.all_gather(first_low, "tensor", axis=1, tiled=True)
    image = fold_with(first_cols, lax.all_gather(matrix_low, "section", axis=2, tiled=True))
    image_cols = lax.all_gather(image.astype(jnp.bfloat16), "tensor", axis=1, tiled=True)
    product = fold_with(image_cols, lax.all_gather(first_low, "section", axis=2, tiled=True))
    inverse_low = (2.0 * first - product).astype(jnp.bfloat16)
    inverses = lax.all_gather(inverse_low, "shard", axis=0, tiled=True)
    left_terms = jnp.stack(
        [
            jnp.einsum("nc,rc->nr", col_parts[m], inverses[m], preferred_element_type=jnp.float32)
            for m in (0, 4, 6)
        ]
    )
    left = lax.psum(left_terms, "section").astype(jnp.bfloat16)
    right_terms = jnp.stack(
        [
            jnp.einsum("nr,rc->nc", row_parts[m], inverses[m], preferred_element_type=jnp.float32)
            for m in (1, 2, 3, 5, 7)
        ]
    )
    right = lax.psum(right_terms, "tensor").astype(jnp.bfloat16)
    norm_values = norm_terms.astype(jnp.float32)
    router_part = jnp.einsum(
        "en,fn->ef", router_grad, router_grad, preferred_element_type=jnp.float32
    )
    router_sum, norm_total, norm_squares = lax.psum(
        (router_part, jnp.sum(norm_values, axis=1), jnp.sum(norm_values * norm_values, axis=1)),
        "shard",
    )
    router_matrix = (
        factor_decay * old_router_factor
        + (1.0 - factor_decay) * (router_sum / tokens_all)
        + damping * jnp.eye(EXPERTS, dtype=jnp.float32)
    )
    router_inverse = local_inverse(router_matrix)
    router_right = jnp.einsum(
        "en,ef->nf", router_grad, router_inverse, preferred_element_type=jnp.float32
    ).astype(jnp.bfloat16)
    precond_norms = (
        learning_rate
        * norm_total
        / (
            factor_decay * old_norm_diag
            + (1.0 - factor_decay) * (norm_squares / tokens_all)
            + damping
        )
    )
    ids_all = lax.all_gather(token_ids, "shard", axis=0, tiled=True)
    embed_all = lax.all_gather(right[4], "shard", axis=0, tiled=True)
    paired_left = jnp.stack([left[0], left[0], left[0], left[1]])
    attn_terms = jnp.einsum(
        "wnr,wnc->wrc", paired_left, right[:4], preferred_element_type=jnp.float32
    )
    router_term = jnp.einsum("nf,nr->fr", router_right, left[2], preferred_element_type=jnp.float32)
    attn_sum, router_total = lax.psum((attn_terms, router_term), "shard")
    precond_attn = learning_rate * attn_sum
    precond_router = learning_rate * router_total
    vocab_block = VOCAB // n_tensor
    step_rows = math.gcd(vocab_block, 512)
    vocab_start = tensor_rank * vocab_block

    def embed_block(block_index):
        ids_here = vocab_start + block_index * step_rows + lax.iota(jnp.int32, step_rows)
        onehot = (ids_here[:, None] == ids_all[None, :]).astype(jnp.bfloat16)
        summed = jnp.dot(onehot, embed_all, preferred_element_type=jnp.float32)
        tallies = jnp.sum(onehot, axis=1, dtype=jnp.float32)
        return (summed, tallies)

    block_sums, block_counts = lax.map(
        embed_block, jnp.arange(vocab_block // step_rows, dtype=jnp.int32)
    )
    embed_sum = block_sums.reshape(vocab_block, col_block)
    counts = block_counts.reshape(vocab_block)
    divisor = factor_decay * old_embed_diag + (1.0 - factor_decay) * (counts / tokens_all) + damping
    precond_embed = learning_rate * embed_sum / divisor[:, None]
    return (precond_attn, precond_router, precond_norms, precond_embed)


def split_three(values):
    high = lax.reduce_precision(values, 8, 7)
    rest = values - high
    middle = lax.reduce_precision(rest, 8, 7)
    return jnp.stack([high, middle, rest - middle], axis=-2).astype(jnp.bfloat16)


def swap(value, axis, size, step):
    return lax.ppermute(value, axis, [(i, i ^ step) for i in range(size)])


def local_diagonals(blocks):
    width = blocks.shape[1]
    pieces = []
    for start in range(0, width, 128):
        size = min(128, width - start)
        tile = blocks[:, start : start + size, start : start + size]
        pieces.append(jnp.sum(tile * jnp.eye(size, dtype=tile.dtype), axis=1))
    return jnp.concatenate(pieces, axis=1)


def rounded(values):
    return values.astype(jnp.bfloat16).astype(jnp.float32)


def params():
    return pltpu.CompilerParams(vmem_limit_bytes=40 * 1024 * 1024)


def layout_kernel(place_ref, *refs, weight):
    gathered, (features, rows, low_diag, trace, old) = refs[:4], refs[4:]
    own_place, layer, core, here = (place_ref[index] for index in range(4))
    steps, _, tokens = gathered[0].shape
    sections = len(gathered)
    groups, depth, _ = features.shape
    part = depth // (sections * steps)
    width = depth // steps
    for away in range(sections):
        section = here ^ away
        codes = jnp.zeros((16, tokens), jnp.float32)
        for step in range(steps):
            start = pl.multiple_of((step * sections + section) * part, 16)
            for group in range(groups):
                features[group, pl.ds(start, part)] = gathered[away][
                    step, group * part : (group + 1) * part
                ]
            codes += gathered[away][step, groups * part :].astype(jnp.float32)
        codes = codes[0:3] + codes[3:6] + codes[6:9]
        pieces = [codes[0:1], codes[1:2], codes[2:3, : width - 2 * tokens]]
        old[section ^ layer] = jnp.concatenate(pieces, axis=1)
    ones = jnp.ones((8, tokens), jnp.bfloat16)
    total = jnp.float32(0.0)
    for step in range(steps):
        squares = jnp.zeros((8, width), jnp.float32)
        for group in range(groups):
            values = features[group, step * width : (step + 1) * width].astype(jnp.float32)
            values = values * values
            high = values.astype(jnp.bfloat16)
            low = (values - high.astype(jnp.float32)).astype(jnp.bfloat16)
            for piece in (high, low):
                squares += lax.dot_general(
                    ones, piece, (((1,), (1,)), ((), ())), preferred_element_type=jnp.float32
                )
        diag = factor_decay * old[step] + weight * squares[0:1] + damping
        total += jnp.sum(diag)
        low_diag[step] = rounded(diag)
        start = pl.multiple_of((own_place ^ step) * width, width)
        mine = features[core, pl.ds(start, width)]
        rows[:, step * width : (step + 1) * width] = mine.T
    trace[0] = total


def lay_out(places, gathered, weight):
    steps, height, tokens = gathered[0].shape
    sections = len(gathered)
    part = (height - 16) // 2
    depth = sections * steps * part
    width = depth // steps
    vmem = pl.BlockSpec(memory_space=pltpu.VMEM)
    smem = pl.BlockSpec(memory_space=pltpu.SMEM)
    return pl.pallas_call(
        functools.partial(layout_kernel, weight=weight),
        in_specs=[smem] + [vmem] * sections,
        out_specs=[vmem, vmem, vmem, smem],
        out_shape=[
            jax.ShapeDtypeStruct((2, depth, tokens), jnp.bfloat16),
            jax.ShapeDtypeStruct((tokens, depth), jnp.bfloat16),
            jax.ShapeDtypeStruct((steps, 1, width), jnp.float32),
            jax.ShapeDtypeStruct((1,), jnp.float32),
        ],
        scratch_shapes=[pltpu.VMEM((steps, 1, width), jnp.float32)],
        compiler_params=params(),
        cost_estimate=pl.CostEstimate(
            flops=64 * depth * tokens, bytes_accessed=14 * depth * tokens, transcendentals=0
        ),
    )(places, *gathered)


def factor_kernel(place_ref, part, own, diag, *refs, step, weight):
    portions, out = refs[:-1], refs[-1]
    start = 0
    for old in portions:
        stop = start + old.shape[0]
        shape = (old.shape[0], out.shape[1])
        fresh = jnp.zeros(shape, jnp.float32)
        for index in range(part.shape[0]):
            fresh += lax.dot_general(
                part[index, start:stop],
                own[index],
                (((1,), (1,)), ((), ())),
                preferred_element_type=jnp.float32,
            )
        block = factor_decay * old[...].astype(jnp.float32) + weight * fresh
        on_diag = lax.broadcasted_iota(jnp.int32, shape, 0) + start == lax.broadcasted_iota(
            jnp.int32, shape, 1
        )
        block = jnp.where(on_diag & (place_ref[0] == step), diag[0], block)
        out[start:stop] = block.astype(jnp.bfloat16)
        start = stop


def factor_block(place, features, portions, diag, step, weight):
    groups, _, tokens = features.shape
    rows, cols = sum(old.shape[0] for old in portions), portions[0].shape[1]
    return pl.pallas_call(
        functools.partial(factor_kernel, step=step, weight=weight),
        grid_spec=pltpu.PrefetchScalarGridSpec(
            num_scalar_prefetch=1,
            grid=(1,),
            in_specs=[
                pl.BlockSpec((groups, rows, tokens), lambda i, place: (0, step, 0)),
                pl.BlockSpec((groups, cols, tokens), lambda i, place: (0, place[0], 0)),
                pl.BlockSpec((1, 1, cols), lambda i, place: (place[0], 0, 0)),
            ]
            + [pl.BlockSpec(old.shape, lambda i, place: (0, 0)) for old in portions],
            out_specs=pl.BlockSpec((rows, cols), lambda i, place: (0, 0)),
        ),
        out_shape=jax.ShapeDtypeStruct((rows, cols), jnp.bfloat16),
        compiler_params=params(),
        cost_estimate=pl.CostEstimate(
            flops=2 * groups * rows * cols * tokens,
            bytes_accessed=4 * rows * cols + 4 * groups * rows * tokens,
            transcendentals=0,
        ),
    )(place, features, features, diag, *portions)


def block_products(place_ref, halves, blocks, pieces):
    width = pieces.shape[2]
    for index, half in enumerate(halves):
        pieces[2 * index] = half[:, :width]
        pieces[2 * index + 1] = half[:, width:]
    products = [None, None]
    for step in range(4):
        piece = pieces[place_ref[0] ^ step]
        for index in range(2):
            term = jnp.dot(piece, blocks[4 * index + step][...], preferred_element_type=jnp.float32)
            products[index] = term if products[index] is None else products[index] + term
    return products


def first_parts(place_ref, scale, rows, diag, product, index):
    width = product.shape[1]
    square = scale * scale
    values = rows[:, index * width : (index + 1) * width].astype(jnp.float32)
    low_diag = diag[place_ref[0] ^ index]
    first_diag = rounded(2.0 * scale - square * low_diag)
    by_first = 2.0 * scale * values - square * product
    step_one = first_diag * values - square * (product - low_diag * values)
    return by_first, step_one, low_diag, first_diag


def first_kernel(place_ref, scale_ref, rows, diag, *refs):
    blocks, (kept, message, pieces) = refs[:8], refs[8:]
    half = rows.shape[1] // 2
    halves = [rows[:, :half], rows[:, half:]]
    products = block_products(place_ref, halves, blocks, pieces)
    lows = []
    for index in range(2):
        kept[index] = products[index]
        parts = first_parts(place_ref, scale_ref[0], rows, diag, products[index], index)
        lows.append(parts[1].astype(jnp.bfloat16))
    message[...] = jnp.concatenate(lows, axis=1)


def second_kernel(place_ref, scale_ref, mine, theirs, rows, diag, before, *refs):
    blocks, (kept, message, pieces) = refs[:8], refs[8:]
    products = block_products(place_ref, [mine[...], theirs[...]], blocks, pieces)
    square = scale_ref[0] * scale_ref[0]
    lows = []
    for index in range(2):
        by_first, one, low_diag, first_diag = first_parts(
            place_ref, scale_ref[0], rows, diag, before[index], index
        )
        two = products[index] + low_diag * (one - rounded(one))
        low = two.astype(jnp.bfloat16)
        kept[index] = (
            2.0 * by_first - first_diag * two - square * low_diag * low.astype(jnp.float32)
        )
        lows.append(low)
    message[...] = jnp.concatenate(lows, axis=1)


def third_kernel(place_ref, scale_ref, mine, theirs, before, *refs):
    blocks, (keep, give, pieces) = refs[:8], refs[8:]
    products = block_products(place_ref, [mine[...], theirs[...]], blocks, pieces)
    square = scale_ref[0] * scale_ref[0]
    for index, out in ((0, keep), (1, give)):
        out[...] = (before[index] + square * products[index]).T.astype(jnp.bfloat16)


def chain_call(kernel, scalars, arrays, blocks, out_shape):
    tokens = arrays[0].shape[0]
    depth, width = blocks[0].shape
    vmem = pl.BlockSpec(memory_space=pltpu.VMEM)
    return pl.pallas_call(
        kernel,
        in_specs=[pl.BlockSpec(memory_space=pltpu.SMEM)] * len(scalars)
        + [vmem] * (len(arrays) + len(blocks)),
        out_specs=[vmem] * len(out_shape),
        out_shape=out_shape,
        scratch_shapes=[pltpu.VMEM((4, tokens, depth), jnp.bfloat16)],
        compiler_params=params(),
        cost_estimate=pl.CostEstimate(
            flops=2 * len(blocks) * tokens * depth * width,
            bytes_accessed=2 * len(blocks) * depth * width,
            transcendentals=0,
        ),
    )(*scalars, *arrays, *blocks)


def output_kernel(where_ref, scale, matches, *refs):
    lefts, rights, refs = refs[:4], refs[4:10], refs[-9:]
    rights = ((rights[0],), (rights[1],), rights[2:4], rights[4:6])
    attn, embed, left_held, held, found, attn_made, embed_made, sems, out_sems = refs
    owner, layer, turn = where_ref[0], where_ref[1], where_ref[2]
    rows = held.shape[1]

    for place in range(4):

        @pl.when(turn == place)
        def _():
            pltpu.make_async_copy(lefts[place].at[pl.ds(0, rows)], left_held, sems.at[4]).start()

    def fetch(sources):
        for slot, source in enumerate(sources):
            for place in range(4):

                @pl.when((layer ^ source) == place)
                def _():
                    start = 0
                    for part in rights[place]:
                        target = held.at[slot, pl.ds(start, part.shape[0])]
                        pltpu.make_async_copy(part, target, sems.at[slot]).start()
                        start += part.shape[0]

    def left_arrived():
        pltpu.make_async_copy(left_held, left_held, sems.at[4]).wait()

    def arrived(slot):
        pltpu.make_async_copy(held.at[slot], held.at[slot], sems.at[slot]).wait()
        return held[slot]

    def send_product(slot, target):
        attn_made[slot] = learning_rate * lax.dot_general(
            left_held[...],
            arrived(slot),
            (((1,), (1,)), ((), ())),
            preferred_element_type=jnp.float32,
        )
        copy = pltpu.make_async_copy(attn_made.at[slot], attn.at[target], out_sems.at[slot])
        copy.start()
        return copy

    @pl.when(owner == 0)
    def _():
        fetch((0, 1, 3))
        left_arrived()
        for copy in [send_product(slot, slot) for slot in range(3)]:
            copy.wait()

    @pl.when(owner == 1)
    def _():
        fetch((0, 3))
        found_copy = pltpu.make_async_copy(matches, found, sems.at[5])
        found_copy.start()
        left_arrived()
        results = [send_product(0, 3)]
        right = arrived(1)
        found_copy.wait()
        part = found.shape[1] // 4
        for index in range(4):
            cols = pl.ds(index * part, part)
            product = jnp.dot(right, found[:, cols], preferred_element_type=jnp.float32)
            embed_made[:, cols] = product * scale[:, cols]
            results.append(
                pltpu.make_async_copy(
                    embed_made.at[:, cols], embed.at[:, cols], out_sems.at[3 + index]
                )
            )
            results[-1].start()
        for copy in results:
            copy.wait()


def output_products(where, scale, matches, lefts, rights, made):
    cols, tokens_all = rights[0].shape
    vocab_block = scale.shape[1]
    anywhere = pl.BlockSpec(memory_space=pl.ANY)
    return pl.pallas_call(
        output_kernel,
        in_specs=[
            pl.BlockSpec(memory_space=pltpu.SMEM),
            pl.BlockSpec(memory_space=pltpu.VMEM),
        ]
        + [anywhere] * (11 + len(made)),
        out_specs=(anywhere, anywhere),
        out_shape=(
            jax.ShapeDtypeStruct((4, cols, cols), jnp.float32),
            jax.ShapeDtypeStruct((cols, vocab_block), jnp.float32),
        ),
        input_output_aliases={13: 0, 14: 1} if made else {},
        scratch_shapes=[
            pltpu.VMEM((cols, tokens_all), jnp.bfloat16),
            pltpu.VMEM((3, cols, tokens_all), jnp.bfloat16),
            pltpu.VMEM((tokens_all, vocab_block), jnp.bfloat16),
            pltpu.VMEM((3, cols, cols), jnp.float32),
            pltpu.VMEM((cols, vocab_block), jnp.float32),
            pltpu.SemaphoreType.DMA((6,)),
            pltpu.SemaphoreType.DMA((7,)),
        ],
        compiler_params=pltpu.CompilerParams(vmem_limit_bytes=60 * 1024 * 1024),
        cost_estimate=pl.CostEstimate(
            flops=6 * cols * cols * tokens_all,
            bytes_accessed=12 * cols * cols + 8 * cols * tokens_all,
            transcendentals=0,
        ),
    )(where, scale, matches, *lefts, *rights, *made)


def layer_plan(
    activations,
    router_grad,
    token_ids,
    norm_terms,
    old_factors,
    old_router_factor,
    old_norm_diag,
    old_embed_diag,
):
    n_tensor = lax.axis_size("tensor")
    n_section = lax.axis_size("section")
    n_shard = lax.axis_size("shard")
    shard = lax.axis_index("shard")
    layer = lax.axis_index("tensor")
    section = lax.axis_index("section")
    core = section % 2
    owned, row_block, col_block = old_factors.shape
    tokens = activations.shape[1]
    features_dev = activations.shape[2]
    tokens_all = tokens * n_shard
    weight = (1.0 - factor_decay) / tokens_all
    own_place = section ^ layer
    place = own_place.reshape(1)
    axes = ("shard", "tensor")

    def by_index(array, index, axis=0):
        return lax.dynamic_index_in_dim(array, index, axis, False)

    def held_by(layer_index):
        return jnp.where(layer_index == 3, 3, lax.rem(layer_index + 1, 3))

    by_feature = jnp.swapaxes(activations, 1, 2)
    diagonals = local_diagonals(old_factors) * (layer == section).astype(jnp.float32)
    extra = jnp.pad(split_three(diagonals), ((0, 0), (0, 0), (0, 3 * tokens - col_block)))
    extra = jnp.pad(extra.reshape(owned, 9, tokens), ((0, 0), (0, 7), (0, 0)))
    collected = []
    for step in range(n_tensor):
        factor = held_by(layer ^ step)
        message = jnp.concatenate(
            [
                by_index(by_feature, shard * owned + factor),
                by_index(by_feature, (1 - shard) * owned + factor),
                by_index(extra, factor),
            ],
            axis=0,
        )
        collected.append(swap(message, "tensor", n_tensor, step) if step else message)
    collected = jnp.stack(collected)

    def old_block(factors, step):
        return by_index(factors, held_by(layer ^ step)).astype(jnp.bfloat16)

    far_block = swap(old_block(old_factors, 2), "tensor", n_tensor, 2)
    later_factors = lax.optimization_barrier(old_factors)
    near_block = swap(old_block(later_factors, 1), "tensor", n_tensor, 1)
    here_block, farthest = old_block(later_factors, 0), old_block(later_factors, 3)

    def both_shards(value, axis):
        other = swap(value, "shard", n_shard, 1)
        return jnp.where(
            shard == 0,
            jnp.concatenate([value, other], axis=axis),
            jnp.concatenate([other, value], axis=axis),
        )

    grad_all = both_shards(router_grad, 1)
    ids_all = both_shards(token_ids, 0)
    norm_values = norm_terms.astype(jnp.float32)
    norm_sums = jnp.stack([jnp.sum(norm_values, axis=1), jnp.sum(norm_values * norm_values, axis=1)])
    norm_sums = norm_sums + swap(norm_sums, "shard", n_shard, 1)
    vocab_block = old_embed_diag.shape[0]
    ids_here = layer * vocab_block + lax.iota(jnp.int32, vocab_block)
    matches = (ids_all[:, None] == ids_here[None, :]).astype(jnp.bfloat16)
    counts = jnp.sum(matches, axis=0, dtype=jnp.float32)
    divisor = factor_decay * old_embed_diag + (1.0 - factor_decay) * (counts / tokens_all) + damping
    embed_scale = (learning_rate / divisor)[None, :]
    router_matrix = (
        factor_decay * old_router_factor
        + weight * jnp.einsum("en,fn->ef", grad_all, grad_all, preferred_element_type=jnp.float32)
        + damping * jnp.eye(EXPERTS, dtype=jnp.float32)
    )
    router_inverse = local_inverse(router_matrix)
    router_right = jnp.einsum(
        "en,ef->fn", grad_all, router_inverse, preferred_element_type=jnp.float32
    ).astype(jnp.bfloat16)

    other_tokens = swap(collected[:, features_dev : 2 * features_dev], "shard", n_shard, 1)
    small = (router_right, matches, embed_scale, norm_sums)
    other_tokens, collected, far_block, near_block, here_block, farthest, small = (
        lax.optimization_barrier(
            (other_tokens, collected, far_block, near_block, here_block, farthest, small)
        )
    )
    router_right, matches, embed_scale, norm_sums = small
    collected = jnp.concatenate(
        [collected[:, :features_dev], other_tokens, collected[:, 2 * features_dev :]], axis=1
    )
    by_side = swap(collected, "section", n_section, 2)
    by_core = swap(collected, "section", n_section, 1)
    part_rows = row_block // 2
    farthest_1 = swap(farthest[:part_rows], "tensor", n_tensor, 3)
    by_side, farthest_1 = lax.optimization_barrier((by_side, farthest_1))
    by_both = swap(by_side, "section", n_section, 1)
    farthest_2 = swap(farthest[part_rows:], "tensor", n_tensor, 3)
    blocks = [(here_block,), (near_block,), (far_block,), (farthest_1, farthest_2)]

    features, rows, low_diag, trace = lay_out(
        jnp.stack([own_place, layer, core, section]),
        (collected, by_core, by_side, by_both),
        weight,
    )
    scale = D / (3.0 * trace)
    own_cols = [
        factor_block(place, features, blocks[step], low_diag, step, weight)
        for step in range(n_tensor)
    ]
    other_cols = [swap(block, "section", n_section, 1) for block in own_cols]
    cols = own_cols + other_cols

    wide = jax.ShapeDtypeStruct((2, tokens, col_block), jnp.float32)
    sent = jax.ShapeDtypeStruct((tokens, 2 * col_block), jnp.bfloat16)
    part = jax.ShapeDtypeStruct((col_block, tokens), jnp.bfloat16)
    scalars = (place, scale)
    kept, message = chain_call(first_kernel, scalars, (rows, low_diag), cols, (wide, sent))
    theirs = swap(message, "section", n_section, 2)
    kept, message = chain_call(
        second_kernel, scalars, (message, theirs, rows, low_diag, kept), cols, (wide, sent)
    )
    theirs = swap(message, "section", n_section, 2)
    keep, give = chain_call(third_kernel, scalars, (message, theirs, kept), cols, (part, part))
    got = swap(give, "section", n_section, 1)
    own = jnp.where(
        core == shard, jnp.concatenate([keep, got], axis=1), jnp.concatenate([got, keep], axis=1)
    )

    planes = range(n_shard)
    layers = range(n_tensor)

    def useful(x, z):
        return z != 2 and (x, z) != (1, 1)

    def send(value, step, held):
        moves = [
            (x * n_tensor + z, x * n_tensor + (z ^ step))
            for x in planes
            for z in layers
            if useful(x, z ^ held)
        ]
        return lax.ppermute(value, axes, moves)

    def across(value, held):
        moves = [
            (x * n_tensor + z, (1 - x) * n_tensor + z)
            for x in planes
            for z in layers
            if useful(x, z ^ held)
        ]
        return lax.ppermute(value, axes, moves)

    everywhere = ("shard", "tensor", "section")

    def spot(x, z, s):
        return (x * n_tensor + z) * n_section + s

    def scatter(value, source):
        moved_here = lax.ppermute(
            value,
            everywhere,
            [(spot(x, source, s), spot(x, s, s)) for x in planes for s in layers if s != source],
        )
        return jnp.where(layer == source, value, moved_here)

    def to_side(value):
        return lax.ppermute(
            value, everywhere, [(spot(x, t, t), spot(x, t, t ^ 2)) for x in planes for t in layers]
        )

    def to_core(value):
        return lax.ppermute(
            value, everywhere, [(spot(x, t, t), spot(x, t, t ^ 1)) for x in planes for t in layers]
        )

    def to_far(value):
        return lax.ppermute(
            value,
            everywhere,
            [(spot(x, t, t ^ 2), spot(x, t, t ^ 3)) for x in planes for t in layers],
        )

    near_1 = send(own, 1, 0)
    cut = col_block // 2
    near_2 = [send(own[:cut], 2, 0), send(own[cut:], 2, 0)]
    over_0 = across(own, 0)
    left_here = scatter(own, 2)
    near_1, near_2[0], own = lax.optimization_barrier((near_1, near_2[0], own))
    over_1 = across(near_1, 1)
    left_there = lax.ppermute(
        left_here, everywhere, [(spot(x, t, t), spot(1 - x, t, t)) for x in planes for t in layers]
    )
    router_cols = learning_rate * jnp.einsum(
        "fn,cn->fc", router_right, own, preferred_element_type=jnp.float32
    )
    router_moved = lax.ppermute(
        router_cols, everywhere, [(spot(1, 1, s), spot(1, s, s)) for s in layers if s != 1]
    )
    router_cols = jnp.where(layer == 1, router_cols, router_moved)
    side_here = to_side(left_here)
    lefts_here = (left_here, to_core(left_here), side_here, to_far(side_here))
    near_3, over_2 = [send(near_2[0], 1, 2)], [across(near_2[0], 2)]
    near_2[1], near_3[0], over_0, over_1, left_there, router_cols = lax.optimization_barrier(
        (near_2[1], near_3[0], over_0, over_1, left_there, router_cols)
    )
    near_3.append(send(near_2[1], 1, 2))
    over_2.append(across(near_2[1], 2))
    router_there = lax.ppermute(
        router_cols, everywhere, [(spot(1, t, t), spot(0, t, t)) for t in layers]
    )
    near_3, over_2, router_there = lax.optimization_barrier((near_3, over_2, router_there))
    over_3 = [across(part, 3) for part in near_3]
    router_cols = jnp.where(shard == 1, router_cols, router_there)
    router_side, router_core = to_side(router_cols), to_core(router_cols)
    turn = section ^ layer
    made = output_products(
        jnp.stack([shard, layer, turn]),
        embed_scale,
        matches,
        lefts_here,
        (own, near_1, *near_2, *near_3),
        (),
    )
    side_there, over_3, router_side, router_core, made = lax.optimization_barrier(
        (to_side(left_there), over_3, router_side, router_core, made)
    )
    lefts_there = (left_there, to_core(left_there), side_there, to_far(side_there))
    routers = (router_cols, router_core, router_side, to_far(router_side))
    precond_router = routers[3]
    for index in (2, 1, 0):
        precond_router = jnp.where(turn == index, routers[index], precond_router)

    precond_attn, embed_columns = output_products(
        jnp.stack([1 - shard, layer, turn]),
        embed_scale,
        matches,
        lefts_there,
        (over_0, over_1, *over_2, *over_3),
        made,
    )
    precond_embed = embed_columns.T

    precond_norms = (
        learning_rate
        * norm_sums[0]
        / (
            factor_decay * old_norm_diag
            + (1.0 - factor_decay) * (norm_sums[1] / tokens_all)
            + damping
        )
    )
    return (precond_attn, precond_router, precond_norms, precond_embed)


def per_device(*arguments):
    one_each = arguments[4].shape[0] == lax.axis_size("tensor") == lax.axis_size("section")
    if one_each and lax.axis_size("section") == 4 and lax.axis_size("shard") == 2:
        return layer_plan(*arguments)
    return general_plan(*arguments)


def solution(mesh):
    return jax.shard_map(
        per_device,
        mesh=mesh,
        in_specs=(
            P(None, "shard", ("tensor", "section")),
            P(None, "shard"),
            P("shard"),
            P(None, "shard", ("tensor", "section")),
            P("shard", "tensor", "section"),
            P(),
            P(None, ("tensor", "section")),
            P("tensor"),
        ),
        out_specs=(
            P(None, "tensor", "section"),
            P(None, "tensor"),
            P(None, ("tensor", "section")),
            P("tensor", "section"),
        ),
        check_vma=False,
    )
```

```python
import functools
import math

import jax
import jax.numpy as jnp
from jax import lax
from jax.experimental import pallas as pl
from jax.experimental.pallas import tpu as pltpu
from jax.sharding import PartitionSpec as P

D = 2304
EXPERTS = 8
VOCAB = 8192


factor_decay = 0.5
damping = 0.01
learning_rate = 0.05


def local_inverse(matrix):
    width = matrix.shape[0]
    trace = jnp.sum(jnp.diagonal(matrix))
    factor_scale = width / (3.0 * trace)
    identity = jnp.eye(width, dtype=jnp.float32)
    matrix_low = lax.optimization_barrier(matrix.astype(jnp.bfloat16))
    first = 2.0 * factor_scale * identity - factor_scale * factor_scale * matrix_low.astype(
        jnp.float32
    )
    first_low = first.astype(jnp.bfloat16)
    image = jnp.dot(matrix_low, first_low, preferred_element_type=jnp.float32).astype(jnp.bfloat16)
    product = jnp.dot(first_low, image, preferred_element_type=jnp.float32)
    return (2.0 * first - product).astype(jnp.bfloat16)


def fold_with(columns, piece):
    return jnp.einsum("kij,kjl->kil", piece, columns, preferred_element_type=jnp.float32)


def general_plan(
    activations,
    router_grad,
    token_ids,
    norm_terms,
    old_factors,
    old_router_factor,
    old_norm_diag,
    old_embed_diag,
):
    n_tensor = lax.axis_size("tensor")
    n_section = lax.axis_size("section")
    n_shard = lax.axis_size("shard")
    tensor_rank = lax.axis_index("tensor")
    section_rank = lax.axis_index("section")
    row_block = D // n_tensor
    col_block = D // n_section
    tokens_all = activations.shape[1] * n_shard
    row_start = tensor_rank * row_block
    col_start = section_rank * col_block

    def collect(carry, piece):
        whole = lax.all_gather(piece, ("tensor", "section"), axis=1, tiled=True)
        rows_part = lax.dynamic_slice_in_dim(whole, row_start, row_block, 1)
        cols_part = lax.dynamic_slice_in_dim(whole, col_start, col_block, 1)
        return (carry, (rows_part, cols_part))

    unused_carry, (row_parts, col_parts) = lax.scan(collect, jnp.int32(0), activations)
    partial_value = jnp.einsum(
        "mnr,mnc->mrc", row_parts, col_parts, preferred_element_type=jnp.float32
    )
    fresh = lax.psum_scatter(partial_value, "shard", scatter_dimension=0, tiled=True) / tokens_all
    row_index = lax.broadcasted_iota(jnp.int32, (row_block, col_block), 0) + row_start
    col_index = lax.broadcasted_iota(jnp.int32, (row_block, col_block), 1) + col_start
    eye_block = (row_index == col_index).astype(jnp.float32)
    matrix = factor_decay * old_factors + (1.0 - factor_decay) * fresh + damping * eye_block
    diag_part = jnp.sum(matrix * eye_block, axis=(1, 2))
    trace = lax.psum(diag_part, ("tensor", "section"))
    factor_scale = (D / (3.0 * trace))[:, None, None]
    matrix_low = lax.optimization_barrier(matrix.astype(jnp.bfloat16))
    first = 2.0 * factor_scale * eye_block - factor_scale * factor_scale * matrix_low.astype(
        jnp.float32
    )
    first_low = first.astype(jnp.bfloat16)
    first_cols = lax.all_gather(first_low, "tensor", axis=1, tiled=True)
    image = fold_with(first_cols, lax.all_gather(matrix_low, "section", axis=2, tiled=True))
    image_cols = lax.all_gather(image.astype(jnp.bfloat16), "tensor", axis=1, tiled=True)
    product = fold_with(image_cols, lax.all_gather(first_low, "section", axis=2, tiled=True))
    inverse_low = (2.0 * first - product).astype(jnp.bfloat16)
    inverses = lax.all_gather(inverse_low, "shard", axis=0, tiled=True)
    left_terms = jnp.stack(
        [
            jnp.einsum("nc,rc->nr", col_parts[m], inverses[m], preferred_element_type=jnp.float32)
            for m in (0, 4, 6)
        ]
    )
    left = lax.psum(left_terms, "section").astype(jnp.bfloat16)
    right_terms = jnp.stack(
        [
            jnp.einsum("nr,rc->nc", row_parts[m], inverses[m], preferred_element_type=jnp.float32)
            for m in (1, 2, 3, 5, 7)
        ]
    )
    right = lax.psum(right_terms, "tensor").astype(jnp.bfloat16)
    norm_values = norm_terms.astype(jnp.float32)
    router_part = jnp.einsum(
        "en,fn->ef", router_grad, router_grad, preferred_element_type=jnp.float32
    )
    router_sum, norm_total, norm_squares = lax.psum(
        (router_part, jnp.sum(norm_values, axis=1), jnp.sum(norm_values * norm_values, axis=1)),
        "shard",
    )
    router_matrix = (
        factor_decay * old_router_factor
        + (1.0 - factor_decay) * (router_sum / tokens_all)
        + damping * jnp.eye(EXPERTS, dtype=jnp.float32)
    )
    router_inverse = local_inverse(router_matrix)
    router_right = jnp.einsum(
        "en,ef->nf", router_grad, router_inverse, preferred_element_type=jnp.float32
    ).astype(jnp.bfloat16)
    precond_norms = (
        learning_rate
        * norm_total
        / (
            factor_decay * old_norm_diag
            + (1.0 - factor_decay) * (norm_squares / tokens_all)
            + damping
        )
    )
    ids_all = lax.all_gather(token_ids, "shard", axis=0, tiled=True)
    embed_all = lax.all_gather(right[4], "shard", axis=0, tiled=True)
    paired_left = jnp.stack([left[0], left[0], left[0], left[1]])
    attn_terms = jnp.einsum(
        "wnr,wnc->wrc", paired_left, right[:4], preferred_element_type=jnp.float32
    )
    router_term = jnp.einsum("nf,nr->fr", router_right, left[2], preferred_element_type=jnp.float32)
    attn_sum, router_total = lax.psum((attn_terms, router_term), "shard")
    precond_attn = learning_rate * attn_sum
    precond_router = learning_rate * router_total
    vocab_block = VOCAB // n_tensor
    step_rows = math.gcd(vocab_block, 512)
    vocab_start = tensor_rank * vocab_block

    def embed_block(block_index):
        ids_here = vocab_start + block_index * step_rows + lax.iota(jnp.int32, step_rows)
        onehot = (ids_here[:, None] == ids_all[None, :]).astype(jnp.bfloat16)
        summed = jnp.dot(onehot, embed_all, preferred_element_type=jnp.float32)
        tallies = jnp.sum(onehot, axis=1, dtype=jnp.float32)
        return (summed, tallies)

    block_sums, block_counts = lax.map(
        embed_block, jnp.arange(vocab_block // step_rows, dtype=jnp.int32)
    )
    embed_sum = block_sums.reshape(vocab_block, col_block)
    counts = block_counts.reshape(vocab_block)
    divisor = factor_decay * old_embed_diag + (1.0 - factor_decay) * (counts / tokens_all) + damping
    precond_embed = learning_rate * embed_sum / divisor[:, None]
    return (precond_attn, precond_router, precond_norms, precond_embed)


def split_three(values):
    high = lax.reduce_precision(values, 8, 7)
    rest = values - high
    middle = lax.reduce_precision(rest, 8, 7)
    return jnp.stack([high, middle, rest - middle], axis=-2).astype(jnp.bfloat16)


def swap(value, axis, size, step):
    return lax.ppermute(value, axis, [(i, i ^ step) for i in range(size)])


def local_diagonals(blocks):
    width = blocks.shape[1]
    pieces = []
    for start in range(0, width, 128):
        size = min(128, width - start)
        tile = blocks[:, start : start + size, start : start + size]
        pieces.append(jnp.sum(tile * jnp.eye(size, dtype=tile.dtype), axis=1))
    return jnp.concatenate(pieces, axis=1)


def rounded(values):
    return values.astype(jnp.bfloat16).astype(jnp.float32)


def params():
    return pltpu.CompilerParams(vmem_limit_bytes=40 * 1024 * 1024)


def layout_kernel(place_ref, *refs, weight):
    gathered, (features, rows, low_diag, trace, old) = refs[:4], refs[4:]
    own_place, layer, core, here = (place_ref[index] for index in range(4))
    steps, _, tokens = gathered[0].shape
    sections = len(gathered)
    groups, depth, _ = features.shape
    part = depth // (sections * steps)
    width = depth // steps
    for away in range(sections):
        section = here ^ away
        codes = jnp.zeros((16, tokens), jnp.float32)
        for step in range(steps):
            start = pl.multiple_of((step * sections + section) * part, 16)
            for group in range(groups):
                features[group, pl.ds(start, part)] = gathered[away][
                    step, group * part : (group + 1) * part
                ]
            codes += gathered[away][step, groups * part :].astype(jnp.float32)
        codes = codes[0:3] + codes[3:6] + codes[6:9]
        pieces = [codes[0:1], codes[1:2], codes[2:3, : width - 2 * tokens]]
        old[section ^ layer] = jnp.concatenate(pieces, axis=1)
    ones = jnp.ones((8, tokens), jnp.bfloat16)
    total = jnp.float32(0.0)
    for step in range(steps):
        squares = jnp.zeros((8, width), jnp.float32)
        for group in range(groups):
            values = features[group, step * width : (step + 1) * width].astype(jnp.float32)
            values = values * values
            high = values.astype(jnp.bfloat16)
            low = (values - high.astype(jnp.float32)).astype(jnp.bfloat16)
            for piece in (high, low):
                squares += lax.dot_general(
                    ones, piece, (((1,), (1,)), ((), ())), preferred_element_type=jnp.float32
                )
        diag = factor_decay * old[step] + weight * squares[0:1] + damping
        total += jnp.sum(diag)
        low_diag[step] = rounded(diag)
        start = pl.multiple_of((own_place ^ step) * width, width)
        mine = features[core, pl.ds(start, width)]
        rows[:, step * width : (step + 1) * width] = mine.T
    trace[0] = total


def lay_out(places, gathered, weight):
    steps, height, tokens = gathered[0].shape
    sections = len(gathered)
    part = (height - 16) // 2
    depth = sections * steps * part
    width = depth // steps
    vmem = pl.BlockSpec(memory_space=pltpu.VMEM)
    smem = pl.BlockSpec(memory_space=pltpu.SMEM)
    return pl.pallas_call(
        functools.partial(layout_kernel, weight=weight),
        in_specs=[smem] + [vmem] * sections,
        out_specs=[vmem, vmem, vmem, smem],
        out_shape=[
            jax.ShapeDtypeStruct((2, depth, tokens), jnp.bfloat16),
            jax.ShapeDtypeStruct((tokens, depth), jnp.bfloat16),
            jax.ShapeDtypeStruct((steps, 1, width), jnp.float32),
            jax.ShapeDtypeStruct((1,), jnp.float32),
        ],
        scratch_shapes=[pltpu.VMEM((steps, 1, width), jnp.float32)],
        compiler_params=params(),
        cost_estimate=pl.CostEstimate(
            flops=64 * depth * tokens, bytes_accessed=14 * depth * tokens, transcendentals=0
        ),
    )(places, *gathered)


def factor_kernel(place_ref, part, own, diag, *refs, step, weight):
    portions, out = refs[:-1], refs[-1]
    start = 0
    for old in portions:
        stop = start + old.shape[0]
        shape = (old.shape[0], out.shape[1])
        fresh = jnp.zeros(shape, jnp.float32)
        for index in range(part.shape[0]):
            fresh += lax.dot_general(
                part[index, start:stop],
                own[index],
                (((1,), (1,)), ((), ())),
                preferred_element_type=jnp.float32,
            )
        block = factor_decay * old[...].astype(jnp.float32) + weight * fresh
        on_diag = lax.broadcasted_iota(jnp.int32, shape, 0) + start == lax.broadcasted_iota(
            jnp.int32, shape, 1
        )
        block = jnp.where(on_diag & (place_ref[0] == step), diag[0], block)
        out[start:stop] = block.astype(jnp.bfloat16)
        start = stop


def factor_block(place, features, portions, diag, step, weight):
    groups, _, tokens = features.shape
    rows, cols = sum(old.shape[0] for old in portions), portions[0].shape[1]
    return pl.pallas_call(
        functools.partial(factor_kernel, step=step, weight=weight),
        grid_spec=pltpu.PrefetchScalarGridSpec(
            num_scalar_prefetch=1,
            grid=(1,),
            in_specs=[
                pl.BlockSpec((groups, rows, tokens), lambda i, place: (0, step, 0)),
                pl.BlockSpec((groups, cols, tokens), lambda i, place: (0, place[0], 0)),
                pl.BlockSpec((1, 1, cols), lambda i, place: (place[0], 0, 0)),
            ]
            + [pl.BlockSpec(old.shape, lambda i, place: (0, 0)) for old in portions],
            out_specs=pl.BlockSpec((rows, cols), lambda i, place: (0, 0)),
        ),
        out_shape=jax.ShapeDtypeStruct((rows, cols), jnp.bfloat16),
        compiler_params=params(),
        cost_estimate=pl.CostEstimate(
            flops=2 * groups * rows * cols * tokens,
            bytes_accessed=4 * rows * cols + 4 * groups * rows * tokens,
            transcendentals=0,
        ),
    )(place, features, features, diag, *portions)


def block_products(place_ref, halves, blocks, pieces):
    width = pieces.shape[2]
    for index, half in enumerate(halves):
        pieces[2 * index] = half[:, :width]
        pieces[2 * index + 1] = half[:, width:]
    products = [None, None]
    for step in range(4):
        piece = pieces[place_ref[0] ^ step]
        for index in range(2):
            term = jnp.dot(piece, blocks[4 * index + step][...], preferred_element_type=jnp.float32)
            products[index] = term if products[index] is None else products[index] + term
    return products


def first_parts(place_ref, scale, rows, diag, product, index):
    width = product.shape[1]
    square = scale * scale
    values = rows[:, index * width : (index + 1) * width].astype(jnp.float32)
    low_diag = diag[place_ref[0] ^ index]
    first_diag = rounded(2.0 * scale - square * low_diag)
    by_first = 2.0 * scale * values - square * product
    step_one = first_diag * values - square * (product - low_diag * values)
    return by_first, step_one, low_diag, first_diag


def first_kernel(place_ref, scale_ref, rows, diag, *refs):
    blocks, (kept, message, pieces) = refs[:8], refs[8:]
    half = rows.shape[1] // 2
    halves = [rows[:, :half], rows[:, half:]]
    products = block_products(place_ref, halves, blocks, pieces)
    lows = []
    for index in range(2):
        kept[index] = products[index]
        parts = first_parts(place_ref, scale_ref[0], rows, diag, products[index], index)
        lows.append(parts[1].astype(jnp.bfloat16))
    message[...] = jnp.concatenate(lows, axis=1)


def second_kernel(place_ref, scale_ref, mine, theirs, rows, diag, before, *refs):
    blocks, (kept, message, pieces) = refs[:8], refs[8:]
    products = block_products(place_ref, [mine[...], theirs[...]], blocks, pieces)
    square = scale_ref[0] * scale_ref[0]
    lows = []
    for index in range(2):
        by_first, one, low_diag, first_diag = first_parts(
            place_ref, scale_ref[0], rows, diag, before[index], index
        )
        two = products[index] + low_diag * (one - rounded(one))
        low = two.astype(jnp.bfloat16)
        kept[index] = (
            2.0 * by_first - first_diag * two - square * low_diag * low.astype(jnp.float32)
        )
        lows.append(low)
    message[...] = jnp.concatenate(lows, axis=1)


def third_kernel(place_ref, scale_ref, mine, theirs, before, *refs):
    blocks, (keep, give, pieces) = refs[:8], refs[8:]
    products = block_products(place_ref, [mine[...], theirs[...]], blocks, pieces)
    square = scale_ref[0] * scale_ref[0]
    for index, out in ((0, keep), (1, give)):
        out[...] = (before[index] + square * products[index]).T.astype(jnp.bfloat16)


def chain_call(kernel, scalars, arrays, blocks, out_shape):
    tokens = arrays[0].shape[0]
    depth, width = blocks[0].shape
    vmem = pl.BlockSpec(memory_space=pltpu.VMEM)
    return pl.pallas_call(
        kernel,
        in_specs=[pl.BlockSpec(memory_space=pltpu.SMEM)] * len(scalars)
        + [vmem] * (len(arrays) + len(blocks)),
        out_specs=[vmem] * len(out_shape),
        out_shape=out_shape,
        scratch_shapes=[pltpu.VMEM((4, tokens, depth), jnp.bfloat16)],
        compiler_params=params(),
        cost_estimate=pl.CostEstimate(
            flops=2 * len(blocks) * tokens * depth * width,
            bytes_accessed=2 * len(blocks) * depth * width,
            transcendentals=0,
        ),
    )(*scalars, *arrays, *blocks)


def output_kernel(where_ref, scale, matches, *refs):
    lefts, rights, refs = refs[:4], refs[4:8], refs[-9:]
    attn, embed, left_held, held, found, attn_made, embed_made, sems, out_sems = refs
    owner, layer, turn = where_ref[0], where_ref[1], where_ref[2]
    rows = held.shape[1]

    for place in range(4):

        @pl.when(turn == place)
        def _():
            pltpu.make_async_copy(lefts[place].at[pl.ds(0, rows)], left_held, sems.at[4]).start()

    def fetch(sources):
        for slot, source in enumerate(sources):
            for place in range(4):

                @pl.when((layer ^ source) == place)
                def _():
                    pltpu.make_async_copy(rights[place], held.at[slot], sems.at[slot]).start()

    def left_arrived():
        pltpu.make_async_copy(left_held, left_held, sems.at[4]).wait()

    def arrived(slot):
        pltpu.make_async_copy(held.at[slot], held.at[slot], sems.at[slot]).wait()
        return held[slot]

    def send_product(slot, target):
        attn_made[slot] = learning_rate * lax.dot_general(
            left_held[...],
            arrived(slot),
            (((1,), (1,)), ((), ())),
            preferred_element_type=jnp.float32,
        )
        copy = pltpu.make_async_copy(attn_made.at[slot], attn.at[target], out_sems.at[slot])
        copy.start()
        return copy

    @pl.when(owner == 0)
    def _():
        fetch((0, 1, 3))
        left_arrived()
        for copy in [send_product(slot, slot) for slot in range(3)]:
            copy.wait()

    @pl.when(owner == 1)
    def _():
        fetch((0, 3))
        found_copy = pltpu.make_async_copy(matches, found, sems.at[5])
        found_copy.start()
        left_arrived()
        results = [send_product(0, 3)]
        right = arrived(1)
        found_copy.wait()
        part = found.shape[1] // 4
        for index in range(4):
            cols = pl.ds(index * part, part)
            product = jnp.dot(right, found[:, cols], preferred_element_type=jnp.float32)
            embed_made[:, cols] = product * scale[:, cols]
            results.append(
                pltpu.make_async_copy(
                    embed_made.at[:, cols], embed.at[:, cols], out_sems.at[3 + index]
                )
            )
            results[-1].start()
        for copy in results:
            copy.wait()


def output_products(where, scale, matches, lefts, rights, made):
    cols, tokens_all = rights[0].shape
    vocab_block = scale.shape[1]
    anywhere = pl.BlockSpec(memory_space=pl.ANY)
    return pl.pallas_call(
        output_kernel,
        in_specs=[
            pl.BlockSpec(memory_space=pltpu.SMEM),
            pl.BlockSpec(memory_space=pltpu.VMEM),
        ]
        + [anywhere] * (9 + len(made)),
        out_specs=(anywhere, anywhere),
        out_shape=(
            jax.ShapeDtypeStruct((4, cols, cols), jnp.float32),
            jax.ShapeDtypeStruct((cols, vocab_block), jnp.float32),
        ),
        input_output_aliases={11: 0, 12: 1} if made else {},
        scratch_shapes=[
            pltpu.VMEM((cols, tokens_all), jnp.bfloat16),
            pltpu.VMEM((3, cols, tokens_all), jnp.bfloat16),
            pltpu.VMEM((tokens_all, vocab_block), jnp.bfloat16),
            pltpu.VMEM((3, cols, cols), jnp.float32),
            pltpu.VMEM((cols, vocab_block), jnp.float32),
            pltpu.SemaphoreType.DMA((6,)),
            pltpu.SemaphoreType.DMA((7,)),
        ],
        compiler_params=pltpu.CompilerParams(vmem_limit_bytes=60 * 1024 * 1024),
        cost_estimate=pl.CostEstimate(
            flops=6 * cols * cols * tokens_all,
            bytes_accessed=12 * cols * cols + 8 * cols * tokens_all,
            transcendentals=0,
        ),
    )(where, scale, matches, *lefts, *rights, *made)


def layer_plan(
    activations,
    router_grad,
    token_ids,
    norm_terms,
    old_factors,
    old_router_factor,
    old_norm_diag,
    old_embed_diag,
):
    n_tensor = lax.axis_size("tensor")
    n_section = lax.axis_size("section")
    n_shard = lax.axis_size("shard")
    shard = lax.axis_index("shard")
    layer = lax.axis_index("tensor")
    section = lax.axis_index("section")
    core = section % 2
    owned, row_block, col_block = old_factors.shape
    tokens = activations.shape[1]
    features_dev = activations.shape[2]
    tokens_all = tokens * n_shard
    weight = (1.0 - factor_decay) / tokens_all
    own_place = section ^ layer
    place = own_place.reshape(1)
    axes = ("shard", "tensor")

    def by_index(array, index, axis=0):
        return lax.dynamic_index_in_dim(array, index, axis, False)

    def held_by(layer_index):
        return jnp.where(layer_index == 3, 3, lax.rem(layer_index + 1, 3))

    by_feature = jnp.swapaxes(activations, 1, 2)
    diagonals = local_diagonals(old_factors) * (layer == section).astype(jnp.float32)
    extra = jnp.pad(split_three(diagonals), ((0, 0), (0, 0), (0, 3 * tokens - col_block)))
    extra = jnp.pad(extra.reshape(owned, 9, tokens), ((0, 0), (0, 7), (0, 0)))
    collected = []
    for step in range(n_tensor):
        factor = held_by(layer ^ step)
        message = jnp.concatenate(
            [
                by_index(by_feature, shard * owned + factor),
                by_index(by_feature, (1 - shard) * owned + factor),
                by_index(extra, factor),
            ],
            axis=0,
        )
        collected.append(swap(message, "tensor", n_tensor, step) if step else message)
    collected = jnp.stack(collected)

    def old_block(factors, step):
        return by_index(factors, held_by(layer ^ step)).astype(jnp.bfloat16)

    part_rows = row_block // 2
    away_block = old_block(old_factors, 2)
    far_1 = swap(away_block[:part_rows], "tensor", n_tensor, 2)

    def both_shards(value, axis):
        other = swap(value, "shard", n_shard, 1)
        return jnp.where(
            shard == 0,
            jnp.concatenate([value, other], axis=axis),
            jnp.concatenate([other, value], axis=axis),
        )

    grad_all = both_shards(router_grad, 1)
    ids_all = both_shards(token_ids, 0)
    norm_values = norm_terms.astype(jnp.float32)
    norm_sums = jnp.stack([jnp.sum(norm_values, axis=1), jnp.sum(norm_values * norm_values, axis=1)])
    norm_sums = norm_sums + swap(norm_sums, "shard", n_shard, 1)
    vocab_block = old_embed_diag.shape[0]
    ids_here = layer * vocab_block + lax.iota(jnp.int32, vocab_block)
    matches = (ids_all[:, None] == ids_here[None, :]).astype(jnp.bfloat16)
    counts = jnp.sum(matches, axis=0, dtype=jnp.float32)
    divisor = factor_decay * old_embed_diag + (1.0 - factor_decay) * (counts / tokens_all) + damping
    embed_scale = (learning_rate / divisor)[None, :]
    router_matrix = (
        factor_decay * old_router_factor
        + weight * jnp.einsum("en,fn->ef", grad_all, grad_all, preferred_element_type=jnp.float32)
        + damping * jnp.eye(EXPERTS, dtype=jnp.float32)
    )
    router_inverse = local_inverse(router_matrix)
    router_right = jnp.einsum(
        "en,ef->fn", grad_all, router_inverse, preferred_element_type=jnp.float32
    ).astype(jnp.bfloat16)

    later_factors, router_right = lax.optimization_barrier((old_factors, router_right))
    near_away = old_block(later_factors, 1)
    here_block, farthest = old_block(later_factors, 0), old_block(later_factors, 3)
    collected, far_1, near_away = lax.optimization_barrier((collected, far_1, near_away))
    other_tokens = swap(collected[:, features_dev : 2 * features_dev], "shard", n_shard, 1)
    far_2 = swap(away_block[part_rows:], "tensor", n_tensor, 2)
    near_block = swap(near_away, "tensor", n_tensor, 1)
    small = (router_right, matches, embed_scale, norm_sums)
    other_tokens, collected, far_2, near_block, here_block, farthest, small = (
        lax.optimization_barrier(
            (other_tokens, collected, far_2, near_block, here_block, farthest, small)
        )
    )
    router_right, matches, embed_scale, norm_sums = small
    collected = jnp.concatenate(
        [collected[:, :features_dev], other_tokens, collected[:, 2 * features_dev :]], axis=1
    )
    by_side = swap(collected, "section", n_section, 2)
    by_core = swap(collected, "section", n_section, 1)
    farthest_1 = swap(farthest[:part_rows], "tensor", n_tensor, 3)
    by_side, farthest_1 = lax.optimization_barrier((by_side, farthest_1))
    by_both = swap(by_side, "section", n_section, 1)
    farthest_2 = swap(farthest[part_rows:], "tensor", n_tensor, 3)
    blocks = [(here_block,), (near_block,), (far_1, far_2), (farthest_1, farthest_2)]

    features, rows, low_diag, trace = lay_out(
        jnp.stack([own_place, layer, core, section]),
        (collected, by_core, by_side, by_both),
        weight,
    )
    scale = D / (3.0 * trace)
    own_cols = [
        factor_block(place, features, blocks[step], low_diag, step, weight)
        for step in range(n_tensor)
    ]
    other_cols = [swap(block, "section", n_section, 1) for block in own_cols]
    cols = own_cols + other_cols

    wide = jax.ShapeDtypeStruct((2, tokens, col_block), jnp.float32)
    sent = jax.ShapeDtypeStruct((tokens, 2 * col_block), jnp.bfloat16)
    part = jax.ShapeDtypeStruct((col_block, tokens), jnp.bfloat16)
    scalars = (place, scale)
    kept, message = chain_call(first_kernel, scalars, (rows, low_diag), cols, (wide, sent))
    theirs = swap(message, "section", n_section, 2)
    kept, message = chain_call(
        second_kernel, scalars, (message, theirs, rows, low_diag, kept), cols, (wide, sent)
    )
    theirs = swap(message, "section", n_section, 2)
    keep, give = chain_call(third_kernel, scalars, (message, theirs, kept), cols, (part, part))
    got = swap(give, "section", n_section, 1)
    own = jnp.where(
        core == shard, jnp.concatenate([keep, got], axis=1), jnp.concatenate([got, keep], axis=1)
    )

    planes = range(n_shard)
    layers = range(n_tensor)

    def useful(x, z):
        return z != 2 and (x, z) != (1, 1)

    def send(value, step, held):
        moves = [
            (x * n_tensor + z, x * n_tensor + (z ^ step))
            for x in planes
            for z in layers
            if useful(x, z ^ held)
        ]
        return lax.ppermute(value, axes, moves)

    def across(value, held):
        moves = [
            (x * n_tensor + z, (1 - x) * n_tensor + z)
            for x in planes
            for z in layers
            if useful(x, z ^ held)
        ]
        return lax.ppermute(value, axes, moves)

    everywhere = ("shard", "tensor", "section")

    def spot(x, z, s):
        return (x * n_tensor + z) * n_section + s

    def scatter(value, source):
        moved_here = lax.ppermute(
            value,
            everywhere,
            [(spot(x, source, s), spot(x, s, s)) for x in planes for s in layers if s != source],
        )
        return jnp.where(layer == source, value, moved_here)

    def to_side(value):
        return lax.ppermute(
            value, everywhere, [(spot(x, t, t), spot(x, t, t ^ 2)) for x in planes for t in layers]
        )

    def to_core(value):
        return lax.ppermute(
            value, everywhere, [(spot(x, t, t), spot(x, t, t ^ 1)) for x in planes for t in layers]
        )

    def to_far(value):
        return lax.ppermute(
            value,
            everywhere,
            [(spot(x, t, t ^ 2), spot(x, t, t ^ 3)) for x in planes for t in layers],
        )

    near_1 = send(own, 1, 0)
    near_2 = send(own, 2, 0)
    over_0 = across(own, 0)
    left_here = scatter(own, 2)
    near_1, own = lax.optimization_barrier((near_1, own))
    over_1 = across(near_1, 1)
    left_there = lax.ppermute(
        left_here, everywhere, [(spot(x, t, t), spot(1 - x, t, t)) for x in planes for t in layers]
    )
    router_cols = learning_rate * jnp.einsum(
        "fn,cn->fc", router_right, own, preferred_element_type=jnp.float32
    )
    router_moved = lax.ppermute(
        router_cols, everywhere, [(spot(1, 1, s), spot(1, s, s)) for s in layers if s != 1]
    )
    router_cols = jnp.where(layer == 1, router_cols, router_moved)
    side_here = to_side(left_here)
    lefts_here = (left_here, to_core(left_here), side_here, to_far(side_here))
    near_2, over_0, over_1, left_there, router_cols = lax.optimization_barrier(
        (near_2, over_0, over_1, left_there, router_cols)
    )
    near_3 = send(near_2, 1, 2)
    over_2 = across(near_2, 2)
    router_there = lax.ppermute(
        router_cols, everywhere, [(spot(1, t, t), spot(0, t, t)) for t in layers]
    )
    near_3, over_2, router_there = lax.optimization_barrier((near_3, over_2, router_there))
    over_3 = across(near_3, 3)
    router_cols = jnp.where(shard == 1, router_cols, router_there)
    router_side, router_core = to_side(router_cols), to_core(router_cols)
    turn = section ^ layer
    made = output_products(
        jnp.stack([shard, layer, turn]),
        embed_scale,
        matches,
        lefts_here,
        (own, near_1, near_2, near_3),
        (),
    )
    side_there = to_side(left_there)
    lefts_there = (left_there, to_core(left_there), side_there, to_far(side_there))
    routers = (router_cols, router_core, router_side, to_far(router_side))
    lefts_there, over_3, routers, made = lax.optimization_barrier(
        (lefts_there, over_3, routers, made)
    )
    precond_router = routers[3]
    for index in (2, 1, 0):
        precond_router = jnp.where(turn == index, routers[index], precond_router)

    precond_attn, embed_columns = output_products(
        jnp.stack([1 - shard, layer, turn]),
        embed_scale,
        matches,
        lefts_there,
        (over_0, over_1, over_2, over_3),
        made,
    )
    precond_embed = embed_columns.T

    precond_norms = (
        learning_rate
        * norm_sums[0]
        / (
            factor_decay * old_norm_diag
            + (1.0 - factor_decay) * (norm_sums[1] / tokens_all)
            + damping
        )
    )
    return (precond_attn, precond_router, precond_norms, precond_embed)


def per_device(*arguments):
    one_each = arguments[4].shape[0] == lax.axis_size("tensor") == lax.axis_size("section")
    if one_each and lax.axis_size("section") == 4 and lax.axis_size("shard") == 2:
        return layer_plan(*arguments)
    return general_plan(*arguments)


def solution(mesh):
    return jax.shard_map(
        per_device,
        mesh=mesh,
        in_specs=(
            P(None, "shard", ("tensor", "section")),
            P(None, "shard"),
            P("shard"),
            P(None, "shard", ("tensor", "section")),
            P("shard", "tensor", "section"),
            P(),
            P(None, ("tensor", "section")),
            P("tensor"),
        ),
        out_specs=(
            P(None, "tensor", "section"),
            P(None, "tensor"),
            P(None, ("tensor", "section")),
            P("tensor", "section"),
        ),
        check_vma=False,
    )
```

```python
import functools
import math

import jax
import jax.numpy as jnp
from jax import lax
from jax.experimental import pallas as pl
from jax.experimental.pallas import tpu as pltpu
from jax.sharding import PartitionSpec as P

D = 2304
EXPERTS = 8
VOCAB = 8192


factor_decay = 0.5
damping = 0.01
learning_rate = 0.05


def local_inverse(matrix):
    width = matrix.shape[0]
    trace = jnp.sum(jnp.diagonal(matrix))
    factor_scale = width / (3.0 * trace)
    identity = jnp.eye(width, dtype=jnp.float32)
    matrix_low = lax.optimization_barrier(matrix.astype(jnp.bfloat16))
    first = 2.0 * factor_scale * identity - factor_scale * factor_scale * matrix_low.astype(
        jnp.float32
    )
    first_low = first.astype(jnp.bfloat16)
    image = jnp.dot(matrix_low, first_low, preferred_element_type=jnp.float32).astype(jnp.bfloat16)
    product = jnp.dot(first_low, image, preferred_element_type=jnp.float32)
    return (2.0 * first - product).astype(jnp.bfloat16)


def fold_with(columns, piece):
    return jnp.einsum("kij,kjl->kil", piece, columns, preferred_element_type=jnp.float32)


def general_plan(
    activations,
    router_grad,
    token_ids,
    norm_terms,
    old_factors,
    old_router_factor,
    old_norm_diag,
    old_embed_diag,
):
    n_tensor = lax.axis_size("tensor")
    n_section = lax.axis_size("section")
    n_shard = lax.axis_size("shard")
    tensor_rank = lax.axis_index("tensor")
    section_rank = lax.axis_index("section")
    row_block = D // n_tensor
    col_block = D // n_section
    tokens_all = activations.shape[1] * n_shard
    row_start = tensor_rank * row_block
    col_start = section_rank * col_block

    def collect(carry, piece):
        whole = lax.all_gather(piece, ("tensor", "section"), axis=1, tiled=True)
        rows_part = lax.dynamic_slice_in_dim(whole, row_start, row_block, 1)
        cols_part = lax.dynamic_slice_in_dim(whole, col_start, col_block, 1)
        return (carry, (rows_part, cols_part))

    unused_carry, (row_parts, col_parts) = lax.scan(collect, jnp.int32(0), activations)
    partial_value = jnp.einsum(
        "mnr,mnc->mrc", row_parts, col_parts, preferred_element_type=jnp.float32
    )
    fresh = lax.psum_scatter(partial_value, "shard", scatter_dimension=0, tiled=True) / tokens_all
    row_index = lax.broadcasted_iota(jnp.int32, (row_block, col_block), 0) + row_start
    col_index = lax.broadcasted_iota(jnp.int32, (row_block, col_block), 1) + col_start
    eye_block = (row_index == col_index).astype(jnp.float32)
    matrix = factor_decay * old_factors + (1.0 - factor_decay) * fresh + damping * eye_block
    diag_part = jnp.sum(matrix * eye_block, axis=(1, 2))
    trace = lax.psum(diag_part, ("tensor", "section"))
    factor_scale = (D / (3.0 * trace))[:, None, None]
    matrix_low = lax.optimization_barrier(matrix.astype(jnp.bfloat16))
    first = 2.0 * factor_scale * eye_block - factor_scale * factor_scale * matrix_low.astype(
        jnp.float32
    )
    first_low = first.astype(jnp.bfloat16)
    first_cols = lax.all_gather(first_low, "tensor", axis=1, tiled=True)
    image = fold_with(first_cols, lax.all_gather(matrix_low, "section", axis=2, tiled=True))
    image_cols = lax.all_gather(image.astype(jnp.bfloat16), "tensor", axis=1, tiled=True)
    product = fold_with(image_cols, lax.all_gather(first_low, "section", axis=2, tiled=True))
    inverse_low = (2.0 * first - product).astype(jnp.bfloat16)
    inverses = lax.all_gather(inverse_low, "shard", axis=0, tiled=True)
    left_terms = jnp.stack(
        [
            jnp.einsum("nc,rc->nr", col_parts[m], inverses[m], preferred_element_type=jnp.float32)
            for m in (0, 4, 6)
        ]
    )
    left = lax.psum(left_terms, "section").astype(jnp.bfloat16)
    right_terms = jnp.stack(
        [
            jnp.einsum("nr,rc->nc", row_parts[m], inverses[m], preferred_element_type=jnp.float32)
            for m in (1, 2, 3, 5, 7)
        ]
    )
    right = lax.psum(right_terms, "tensor").astype(jnp.bfloat16)
    norm_values = norm_terms.astype(jnp.float32)
    router_part = jnp.einsum(
        "en,fn->ef", router_grad, router_grad, preferred_element_type=jnp.float32
    )
    router_sum, norm_total, norm_squares = lax.psum(
        (router_part, jnp.sum(norm_values, axis=1), jnp.sum(norm_values * norm_values, axis=1)),
        "shard",
    )
    router_matrix = (
        factor_decay * old_router_factor
        + (1.0 - factor_decay) * (router_sum / tokens_all)
        + damping * jnp.eye(EXPERTS, dtype=jnp.float32)
    )
    router_inverse = local_inverse(router_matrix)
    router_right = jnp.einsum(
        "en,ef->nf", router_grad, router_inverse, preferred_element_type=jnp.float32
    ).astype(jnp.bfloat16)
    precond_norms = (
        learning_rate
        * norm_total
        / (
            factor_decay * old_norm_diag
            + (1.0 - factor_decay) * (norm_squares / tokens_all)
            + damping
        )
    )
    ids_all = lax.all_gather(token_ids, "shard", axis=0, tiled=True)
    embed_all = lax.all_gather(right[4], "shard", axis=0, tiled=True)
    paired_left = jnp.stack([left[0], left[0], left[0], left[1]])
    attn_terms = jnp.einsum(
        "wnr,wnc->wrc", paired_left, right[:4], preferred_element_type=jnp.float32
    )
    router_term = jnp.einsum("nf,nr->fr", router_right, left[2], preferred_element_type=jnp.float32)
    attn_sum, router_total = lax.psum((attn_terms, router_term), "shard")
    precond_attn = learning_rate * attn_sum
    precond_router = learning_rate * router_total
    vocab_block = VOCAB // n_tensor
    step_rows = math.gcd(vocab_block, 512)
    vocab_start = tensor_rank * vocab_block

    def embed_block(block_index):
        ids_here = vocab_start + block_index * step_rows + lax.iota(jnp.int32, step_rows)
        onehot = (ids_here[:, None] == ids_all[None, :]).astype(jnp.bfloat16)
        summed = jnp.dot(onehot, embed_all, preferred_element_type=jnp.float32)
        tallies = jnp.sum(onehot, axis=1, dtype=jnp.float32)
        return (summed, tallies)

    block_sums, block_counts = lax.map(
        embed_block, jnp.arange(vocab_block // step_rows, dtype=jnp.int32)
    )
    embed_sum = block_sums.reshape(vocab_block, col_block)
    counts = block_counts.reshape(vocab_block)
    divisor = factor_decay * old_embed_diag + (1.0 - factor_decay) * (counts / tokens_all) + damping
    precond_embed = learning_rate * embed_sum / divisor[:, None]
    return (precond_attn, precond_router, precond_norms, precond_embed)


def split_three(values):
    high = lax.reduce_precision(values, 8, 7)
    rest = values - high
    middle = lax.reduce_precision(rest, 8, 7)
    return jnp.stack([high, middle, rest - middle], axis=-2).astype(jnp.bfloat16)


def swap(value, axis, size, step):
    return lax.ppermute(value, axis, [(i, i ^ step) for i in range(size)])


def local_diagonals(blocks):
    width = blocks.shape[1]
    pieces = []
    for start in range(0, width, 128):
        size = min(128, width - start)
        tile = blocks[:, start : start + size, start : start + size]
        pieces.append(jnp.sum(tile * jnp.eye(size, dtype=tile.dtype), axis=1))
    return jnp.concatenate(pieces, axis=1)


def rounded(values):
    return values.astype(jnp.bfloat16).astype(jnp.float32)


def params():
    return pltpu.CompilerParams(vmem_limit_bytes=40 * 1024 * 1024)


def layout_kernel(place_ref, *refs, weight):
    gathered, (features, rows, low_diag, trace, old) = refs[:4], refs[4:]
    own_place, layer, core, here = (place_ref[index] for index in range(4))
    steps, _, tokens = gathered[0].shape
    sections = len(gathered)
    groups, depth, _ = features.shape
    part = depth // (sections * steps)
    width = depth // steps
    for away in range(sections):
        section = here ^ away
        codes = jnp.zeros((16, tokens), jnp.float32)
        for step in range(steps):
            start = pl.multiple_of((step * sections + section) * part, 16)
            for group in range(groups):
                features[group, pl.ds(start, part)] = gathered[away][
                    step, group * part : (group + 1) * part
                ]
            codes += gathered[away][step, groups * part :].astype(jnp.float32)
        codes = codes[0:3] + codes[3:6] + codes[6:9]
        pieces = [codes[0:1], codes[1:2], codes[2:3, : width - 2 * tokens]]
        old[section ^ layer] = jnp.concatenate(pieces, axis=1)
    ones = jnp.ones((8, tokens), jnp.bfloat16)
    total = jnp.float32(0.0)
    for step in range(steps):
        squares = jnp.zeros((8, width), jnp.float32)
        for group in range(groups):
            values = features[group, step * width : (step + 1) * width].astype(jnp.float32)
            values = values * values
            high = values.astype(jnp.bfloat16)
            low = (values - high.astype(jnp.float32)).astype(jnp.bfloat16)
            for piece in (high, low):
                squares += lax.dot_general(
                    ones, piece, (((1,), (1,)), ((), ())), preferred_element_type=jnp.float32
                )
        diag = factor_decay * old[step] + weight * squares[0:1] + damping
        total += jnp.sum(diag)
        low_diag[step] = rounded(diag)
        start = pl.multiple_of((own_place ^ step) * width, width)
        mine = features[core, pl.ds(start, width)]
        rows[:, step * width : (step + 1) * width] = mine.T
    trace[0] = total


def lay_out(places, gathered, weight):
    steps, height, tokens = gathered[0].shape
    sections = len(gathered)
    part = (height - 16) // 2
    depth = sections * steps * part
    width = depth // steps
    vmem = pl.BlockSpec(memory_space=pltpu.VMEM)
    smem = pl.BlockSpec(memory_space=pltpu.SMEM)
    return pl.pallas_call(
        functools.partial(layout_kernel, weight=weight),
        in_specs=[smem] + [vmem] * sections,
        out_specs=[vmem, vmem, vmem, smem],
        out_shape=[
            jax.ShapeDtypeStruct((2, depth, tokens), jnp.bfloat16),
            jax.ShapeDtypeStruct((tokens, depth), jnp.bfloat16),
            jax.ShapeDtypeStruct((steps, 1, width), jnp.float32),
            jax.ShapeDtypeStruct((1,), jnp.float32),
        ],
        scratch_shapes=[pltpu.VMEM((steps, 1, width), jnp.float32)],
        compiler_params=params(),
        cost_estimate=pl.CostEstimate(
            flops=64 * depth * tokens, bytes_accessed=14 * depth * tokens, transcendentals=0
        ),
    )(places, *gathered)


def factor_kernel(place_ref, part, own, diag, *refs, step, weight):
    portions, out = refs[:-1], refs[-1]
    start = 0
    for old in portions:
        stop = start + old.shape[0]
        shape = (old.shape[0], out.shape[1])
        fresh = jnp.zeros(shape, jnp.float32)
        for index in range(part.shape[0]):
            fresh += lax.dot_general(
                part[index, start:stop],
                own[index],
                (((1,), (1,)), ((), ())),
                preferred_element_type=jnp.float32,
            )
        block = factor_decay * old[...].astype(jnp.float32) + weight * fresh
        on_diag = lax.broadcasted_iota(jnp.int32, shape, 0) + start == lax.broadcasted_iota(
            jnp.int32, shape, 1
        )
        block = jnp.where(on_diag & (place_ref[0] == step), diag[0], block)
        out[start:stop] = block.astype(jnp.bfloat16)
        start = stop


def factor_block(place, features, portions, diag, step, weight):
    groups, _, tokens = features.shape
    rows, cols = sum(old.shape[0] for old in portions), portions[0].shape[1]
    return pl.pallas_call(
        functools.partial(factor_kernel, step=step, weight=weight),
        grid_spec=pltpu.PrefetchScalarGridSpec(
            num_scalar_prefetch=1,
            grid=(1,),
            in_specs=[
                pl.BlockSpec((groups, rows, tokens), lambda i, place: (0, step, 0)),
                pl.BlockSpec((groups, cols, tokens), lambda i, place: (0, place[0], 0)),
                pl.BlockSpec((1, 1, cols), lambda i, place: (place[0], 0, 0)),
            ]
            + [pl.BlockSpec(old.shape, lambda i, place: (0, 0)) for old in portions],
            out_specs=pl.BlockSpec((rows, cols), lambda i, place: (0, 0)),
        ),
        out_shape=jax.ShapeDtypeStruct((rows, cols), jnp.bfloat16),
        compiler_params=params(),
        cost_estimate=pl.CostEstimate(
            flops=2 * groups * rows * cols * tokens,
            bytes_accessed=4 * rows * cols + 4 * groups * rows * tokens,
            transcendentals=0,
        ),
    )(place, features, features, diag, *portions)


def block_products(place_ref, halves, blocks, pieces):
    width = pieces.shape[2]
    for index, half in enumerate(halves):
        pieces[2 * index] = half[:, :width]
        pieces[2 * index + 1] = half[:, width:]
    products = [None, None]
    for step in range(4):
        piece = pieces[place_ref[0] ^ step]
        for index in range(2):
            term = jnp.dot(piece, blocks[4 * index + step][...], preferred_element_type=jnp.float32)
            products[index] = term if products[index] is None else products[index] + term
    return products


def first_parts(place_ref, scale, rows, diag, product, index):
    width = product.shape[1]
    square = scale * scale
    values = rows[:, index * width : (index + 1) * width].astype(jnp.float32)
    low_diag = diag[place_ref[0] ^ index]
    first_diag = rounded(2.0 * scale - square * low_diag)
    by_first = 2.0 * scale * values - square * product
    step_one = first_diag * values - square * (product - low_diag * values)
    return by_first, step_one, low_diag, first_diag


def first_kernel(place_ref, scale_ref, rows, diag, *refs):
    blocks, (kept, message, pieces) = refs[:8], refs[8:]
    half = rows.shape[1] // 2
    halves = [rows[:, :half], rows[:, half:]]
    products = block_products(place_ref, halves, blocks, pieces)
    lows = []
    for index in range(2):
        kept[index] = products[index]
        parts = first_parts(place_ref, scale_ref[0], rows, diag, products[index], index)
        lows.append(parts[1].astype(jnp.bfloat16))
    message[...] = jnp.concatenate(lows, axis=1)


def second_kernel(place_ref, scale_ref, mine, theirs, rows, diag, before, *refs):
    blocks, (kept, message, pieces) = refs[:8], refs[8:]
    products = block_products(place_ref, [mine[...], theirs[...]], blocks, pieces)
    square = scale_ref[0] * scale_ref[0]
    lows = []
    for index in range(2):
        by_first, one, low_diag, first_diag = first_parts(
            place_ref, scale_ref[0], rows, diag, before[index], index
        )
        two = products[index] + low_diag * (one - rounded(one))
        low = two.astype(jnp.bfloat16)
        kept[index] = (
            2.0 * by_first - first_diag * two - square * low_diag * low.astype(jnp.float32)
        )
        lows.append(low)
    message[...] = jnp.concatenate(lows, axis=1)


def third_kernel(place_ref, scale_ref, mine, theirs, before, *refs):
    blocks, (keep, give, pieces) = refs[:8], refs[8:]
    products = block_products(place_ref, [mine[...], theirs[...]], blocks, pieces)
    square = scale_ref[0] * scale_ref[0]
    for index, out in ((0, keep), (1, give)):
        out[...] = (before[index] + square * products[index]).T.astype(jnp.bfloat16)


def chain_call(kernel, scalars, arrays, blocks, out_shape):
    tokens = arrays[0].shape[0]
    depth, width = blocks[0].shape
    vmem = pl.BlockSpec(memory_space=pltpu.VMEM)
    return pl.pallas_call(
        kernel,
        in_specs=[pl.BlockSpec(memory_space=pltpu.SMEM)] * len(scalars)
        + [vmem] * (len(arrays) + len(blocks)),
        out_specs=[vmem] * len(out_shape),
        out_shape=out_shape,
        scratch_shapes=[pltpu.VMEM((4, tokens, depth), jnp.bfloat16)],
        compiler_params=params(),
        cost_estimate=pl.CostEstimate(
            flops=2 * len(blocks) * tokens * depth * width,
            bytes_accessed=2 * len(blocks) * depth * width,
            transcendentals=0,
        ),
    )(*scalars, *arrays, *blocks)


def output_kernel(where_ref, scale, matches, *refs):
    lefts, rights, refs = refs[:4], refs[4:8], refs[-9:]
    attn, embed, left_held, held, found, attn_made, embed_made, sems, out_sems = refs
    owner, layer, turn = where_ref[0], where_ref[1], where_ref[2]
    rows = held.shape[1]

    for place in range(4):

        @pl.when(turn == place)
        def _():
            pltpu.make_async_copy(lefts[place].at[pl.ds(0, rows)], left_held, sems.at[4]).start()

    def fetch(sources):
        for slot, source in enumerate(sources):
            for place in range(4):

                @pl.when((layer ^ source) == place)
                def _():
                    pltpu.make_async_copy(rights[place], held.at[slot], sems.at[slot]).start()

    def left_arrived():
        pltpu.make_async_copy(left_held, left_held, sems.at[4]).wait()

    def arrived(slot):
        pltpu.make_async_copy(held.at[slot], held.at[slot], sems.at[slot]).wait()
        return held[slot]

    def send_product(slot, target):
        attn_made[slot] = learning_rate * lax.dot_general(
            left_held[...],
            arrived(slot),
            (((1,), (1,)), ((), ())),
            preferred_element_type=jnp.float32,
        )
        copy = pltpu.make_async_copy(attn_made.at[slot], attn.at[target], out_sems.at[slot])
        copy.start()
        return copy

    @pl.when(owner == 0)
    def _():
        fetch((0, 1, 3))
        left_arrived()
        for copy in [send_product(slot, slot) for slot in range(3)]:
            copy.wait()

    @pl.when(owner == 1)
    def _():
        fetch((0, 3))
        found_copy = pltpu.make_async_copy(matches, found, sems.at[5])
        found_copy.start()
        left_arrived()
        results = [send_product(0, 3)]
        right = arrived(1)
        found_copy.wait()
        part = found.shape[1] // 4
        for index in range(4):
            cols = pl.ds(index * part, part)
            product = jnp.dot(right, found[:, cols], preferred_element_type=jnp.float32)
            embed_made[:, cols] = product * scale[:, cols]
            results.append(
                pltpu.make_async_copy(
                    embed_made.at[:, cols], embed.at[:, cols], out_sems.at[3 + index]
                )
            )
            results[-1].start()
        for copy in results:
            copy.wait()


def output_products(where, scale, matches, lefts, rights, made):
    cols, tokens_all = rights[0].shape
    vocab_block = scale.shape[1]
    anywhere = pl.BlockSpec(memory_space=pl.ANY)
    return pl.pallas_call(
        output_kernel,
        in_specs=[
            pl.BlockSpec(memory_space=pltpu.SMEM),
            pl.BlockSpec(memory_space=pltpu.VMEM),
        ]
        + [anywhere] * (9 + len(made)),
        out_specs=(anywhere, anywhere),
        out_shape=(
            jax.ShapeDtypeStruct((4, cols, cols), jnp.float32),
            jax.ShapeDtypeStruct((cols, vocab_block), jnp.float32),
        ),
        input_output_aliases={11: 0, 12: 1} if made else {},
        scratch_shapes=[
            pltpu.VMEM((cols, tokens_all), jnp.bfloat16),
            pltpu.VMEM((3, cols, tokens_all), jnp.bfloat16),
            pltpu.VMEM((tokens_all, vocab_block), jnp.bfloat16),
            pltpu.VMEM((3, cols, cols), jnp.float32),
            pltpu.VMEM((cols, vocab_block), jnp.float32),
            pltpu.SemaphoreType.DMA((6,)),
            pltpu.SemaphoreType.DMA((7,)),
        ],
        compiler_params=pltpu.CompilerParams(vmem_limit_bytes=60 * 1024 * 1024),
        cost_estimate=pl.CostEstimate(
            flops=6 * cols * cols * tokens_all,
            bytes_accessed=12 * cols * cols + 8 * cols * tokens_all,
            transcendentals=0,
        ),
    )(where, scale, matches, *lefts, *rights, *made)


def layer_plan(
    activations,
    router_grad,
    token_ids,
    norm_terms,
    old_factors,
    old_router_factor,
    old_norm_diag,
    old_embed_diag,
):
    n_tensor = lax.axis_size("tensor")
    n_section = lax.axis_size("section")
    n_shard = lax.axis_size("shard")
    shard = lax.axis_index("shard")
    layer = lax.axis_index("tensor")
    section = lax.axis_index("section")
    core = section % 2
    owned, row_block, col_block = old_factors.shape
    tokens = activations.shape[1]
    features_dev = activations.shape[2]
    tokens_all = tokens * n_shard
    weight = (1.0 - factor_decay) / tokens_all
    own_place = section ^ layer
    place = own_place.reshape(1)
    axes = ("shard", "tensor")

    def by_index(array, index, axis=0):
        return lax.dynamic_index_in_dim(array, index, axis, False)

    def held_by(layer_index):
        return jnp.where(layer_index == 3, 3, lax.rem(layer_index + 1, 3))

    by_feature = jnp.swapaxes(activations, 1, 2)
    diagonals = local_diagonals(old_factors) * (layer == section).astype(jnp.float32)
    extra = jnp.pad(split_three(diagonals), ((0, 0), (0, 0), (0, 3 * tokens - col_block)))
    extra = jnp.pad(extra.reshape(owned, 9, tokens), ((0, 0), (0, 7), (0, 0)))
    collected = []
    for step in range(n_tensor):
        factor = held_by(layer ^ step)
        message = jnp.concatenate(
            [
                by_index(by_feature, shard * owned + factor),
                by_index(by_feature, (1 - shard) * owned + factor),
                by_index(extra, factor),
            ],
            axis=0,
        )
        collected.append(swap(message, "tensor", n_tensor, step) if step else message)
    collected = jnp.stack(collected)

    def old_block(factors, step):
        return by_index(factors, held_by(layer ^ step)).astype(jnp.bfloat16)

    far_block = swap(old_block(old_factors, 2), "tensor", n_tensor, 2)

    def both_shards(value, axis):
        other = swap(value, "shard", n_shard, 1)
        return jnp.where(
            shard == 0,
            jnp.concatenate([value, other], axis=axis),
            jnp.concatenate([other, value], axis=axis),
        )

    grad_all = both_shards(router_grad, 1)
    ids_all = both_shards(token_ids, 0)
    norm_values = norm_terms.astype(jnp.float32)
    norm_sums = jnp.stack([jnp.sum(norm_values, axis=1), jnp.sum(norm_values * norm_values, axis=1)])
    norm_sums = norm_sums + swap(norm_sums, "shard", n_shard, 1)
    vocab_block = old_embed_diag.shape[0]
    ids_here = layer * vocab_block + lax.iota(jnp.int32, vocab_block)
    matches = (ids_all[:, None] == ids_here[None, :]).astype(jnp.bfloat16)
    counts = jnp.sum(matches, axis=0, dtype=jnp.float32)
    divisor = factor_decay * old_embed_diag + (1.0 - factor_decay) * (counts / tokens_all) + damping
    embed_scale = (learning_rate / divisor)[None, :]
    router_matrix = (
        factor_decay * old_router_factor
        + weight * jnp.einsum("en,fn->ef", grad_all, grad_all, preferred_element_type=jnp.float32)
        + damping * jnp.eye(EXPERTS, dtype=jnp.float32)
    )
    router_inverse = local_inverse(router_matrix)
    router_right = jnp.einsum(
        "en,ef->fn", grad_all, router_inverse, preferred_element_type=jnp.float32
    ).astype(jnp.bfloat16)

    later_factors, router_right = lax.optimization_barrier((old_factors, router_right))
    near_block = swap(old_block(later_factors, 1), "tensor", n_tensor, 1)
    here_block, farthest = old_block(later_factors, 0), old_block(later_factors, 3)
    other_tokens = swap(collected[:, features_dev : 2 * features_dev], "shard", n_shard, 1)
    small = (router_right, matches, embed_scale, norm_sums)
    other_tokens, collected, far_block, near_block, here_block, farthest, small = (
        lax.optimization_barrier(
            (other_tokens, collected, far_block, near_block, here_block, farthest, small)
        )
    )
    router_right, matches, embed_scale, norm_sums = small
    collected = jnp.concatenate(
        [collected[:, :features_dev], other_tokens, collected[:, 2 * features_dev :]], axis=1
    )
    by_side = swap(collected, "section", n_section, 2)
    by_core = swap(collected, "section", n_section, 1)
    part_rows = row_block // 2
    farthest_1 = swap(farthest[:part_rows], "tensor", n_tensor, 3)
    by_side, farthest_1 = lax.optimization_barrier((by_side, farthest_1))
    by_both = swap(by_side, "section", n_section, 1)
    farthest_2 = swap(farthest[part_rows:], "tensor", n_tensor, 3)
    blocks = [(here_block,), (near_block,), (far_block,), (farthest_1, farthest_2)]

    features, rows, low_diag, trace = lay_out(
        jnp.stack([own_place, layer, core, section]),
        (collected, by_core, by_side, by_both),
        weight,
    )
    scale = D / (3.0 * trace)
    own_cols = [
        factor_block(place, features, blocks[step], low_diag, step, weight)
        for step in range(n_tensor)
    ]
    other_cols = [swap(block, "section", n_section, 1) for block in own_cols]
    cols = own_cols + other_cols

    wide = jax.ShapeDtypeStruct((2, tokens, col_block), jnp.float32)
    sent = jax.ShapeDtypeStruct((tokens, 2 * col_block), jnp.bfloat16)
    part = jax.ShapeDtypeStruct((col_block, tokens), jnp.bfloat16)
    scalars = (place, scale)
    kept, message = chain_call(first_kernel, scalars, (rows, low_diag), cols, (wide, sent))
    theirs = swap(message, "section", n_section, 2)
    kept, message = chain_call(
        second_kernel, scalars, (message, theirs, rows, low_diag, kept), cols, (wide, sent)
    )
    theirs = swap(message, "section", n_section, 2)
    keep, give = chain_call(third_kernel, scalars, (message, theirs, kept), cols, (part, part))
    got = swap(give, "section", n_section, 1)
    own = jnp.where(
        core == shard, jnp.concatenate([keep, got], axis=1), jnp.concatenate([got, keep], axis=1)
    )

    planes = range(n_shard)
    layers = range(n_tensor)

    def useful(x, z):
        return z != 2 and (x, z) != (1, 1)

    def send(value, step, held):
        moves = [
            (x * n_tensor + z, x * n_tensor + (z ^ step))
            for x in planes
            for z in layers
            if useful(x, z ^ held)
        ]
        return lax.ppermute(value, axes, moves)

    def across(value, held):
        moves = [
            (x * n_tensor + z, (1 - x) * n_tensor + z)
            for x in planes
            for z in layers
            if useful(x, z ^ held)
        ]
        return lax.ppermute(value, axes, moves)

    everywhere = ("shard", "tensor", "section")

    def spot(x, z, s):
        return (x * n_tensor + z) * n_section + s

    def scatter(value, source):
        moved_here = lax.ppermute(
            value,
            everywhere,
            [(spot(x, source, s), spot(x, s, s)) for x in planes for s in layers if s != source],
        )
        return jnp.where(layer == source, value, moved_here)

    def to_side(value):
        return lax.ppermute(
            value, everywhere, [(spot(x, t, t), spot(x, t, t ^ 2)) for x in planes for t in layers]
        )

    def to_core(value):
        return lax.ppermute(
            value, everywhere, [(spot(x, t, t), spot(x, t, t ^ 1)) for x in planes for t in layers]
        )

    def to_far(value):
        return lax.ppermute(
            value,
            everywhere,
            [(spot(x, t, t ^ 2), spot(x, t, t ^ 3)) for x in planes for t in layers],
        )

    near_1 = send(own, 1, 0)
    near_2 = send(own, 2, 0)
    over_0 = across(own, 0)
    left_here = scatter(own, 2)
    near_1, own = lax.optimization_barrier((near_1, own))
    over_1 = across(near_1, 1)
    left_there = lax.ppermute(
        left_here, everywhere, [(spot(x, t, t), spot(1 - x, t, t)) for x in planes for t in layers]
    )
    router_cols = learning_rate * jnp.einsum(
        "fn,cn->fc", router_right, own, preferred_element_type=jnp.float32
    )
    router_moved = lax.ppermute(
        router_cols, everywhere, [(spot(1, 1, s), spot(1, s, s)) for s in layers if s != 1]
    )
    router_cols = jnp.where(layer == 1, router_cols, router_moved)
    side_here = to_side(left_here)
    lefts_here = (left_here, to_core(left_here), side_here, to_far(side_here))
    near_2, over_0, over_1, left_there, router_cols = lax.optimization_barrier(
        (near_2, over_0, over_1, left_there, router_cols)
    )
    near_3 = send(near_2, 1, 2)
    over_2 = across(near_2, 2)
    router_there = lax.ppermute(
        router_cols, everywhere, [(spot(1, t, t), spot(0, t, t)) for t in layers]
    )
    near_3, over_2, router_there = lax.optimization_barrier((near_3, over_2, router_there))
    over_3 = across(near_3, 3)
    router_cols = jnp.where(shard == 1, router_cols, router_there)
    router_side, router_core = to_side(router_cols), to_core(router_cols)
    turn = section ^ layer
    made = output_products(
        jnp.stack([shard, layer, turn]),
        embed_scale,
        matches,
        lefts_here,
        (own, near_1, near_2, near_3),
        (),
    )
    side_there, over_3, router_side, router_core, made = lax.optimization_barrier(
        (to_side(left_there), over_3, router_side, router_core, made)
    )
    lefts_there = (left_there, to_core(left_there), side_there, to_far(side_there))
    routers = (router_cols, router_core, router_side, to_far(router_side))
    precond_router = routers[3]
    for index in (2, 1, 0):
        precond_router = jnp.where(turn == index, routers[index], precond_router)

    precond_attn, embed_columns = output_products(
        jnp.stack([1 - shard, layer, turn]),
        embed_scale,
        matches,
        lefts_there,
        (over_0, over_1, over_2, over_3),
        made,
    )
    precond_embed = embed_columns.T

    precond_norms = (
        learning_rate
        * norm_sums[0]
        / (
            factor_decay * old_norm_diag
            + (1.0 - factor_decay) * (norm_sums[1] / tokens_all)
            + damping
        )
    )
    return (precond_attn, precond_router, precond_norms, precond_embed)


def per_device(*arguments):
    one_each = arguments[4].shape[0] == lax.axis_size("tensor") == lax.axis_size("section")
    if one_each and lax.axis_size("section") == 4 and lax.axis_size("shard") == 2:
        return layer_plan(*arguments)
    return general_plan(*arguments)


def solution(mesh):
    return jax.shard_map(
        per_device,
        mesh=mesh,
        in_specs=(
            P(None, "shard", ("tensor", "section")),
            P(None, "shard"),
            P("shard"),
            P(None, "shard", ("tensor", "section")),
            P("shard", "tensor", "section"),
            P(),
            P(None, ("tensor", "section")),
            P("tensor"),
        ),
        out_specs=(
            P(None, "tensor", "section"),
            P(None, "tensor"),
            P(None, ("tensor", "section")),
            P("tensor", "section"),
        ),
        check_vma=False,
    )
```

```python
import functools
import math

import jax
import jax.numpy as jnp
from jax import lax
from jax.experimental import pallas as pl
from jax.experimental.pallas import tpu as pltpu
from jax.sharding import PartitionSpec as P

D = 2304
EXPERTS = 8
VOCAB = 8192


factor_decay = 0.5
damping = 0.01
learning_rate = 0.05


def local_inverse(matrix):
    width = matrix.shape[0]
    trace = jnp.sum(jnp.diagonal(matrix))
    factor_scale = width / (3.0 * trace)
    identity = jnp.eye(width, dtype=jnp.float32)
    matrix_low = lax.optimization_barrier(matrix.astype(jnp.bfloat16))
    first = 2.0 * factor_scale * identity - factor_scale * factor_scale * matrix_low.astype(
        jnp.float32
    )
    first_low = first.astype(jnp.bfloat16)
    image = jnp.dot(matrix_low, first_low, preferred_element_type=jnp.float32).astype(jnp.bfloat16)
    product = jnp.dot(first_low, image, preferred_element_type=jnp.float32)
    return (2.0 * first - product).astype(jnp.bfloat16)


def fold_with(columns, piece):
    return jnp.einsum("kij,kjl->kil", piece, columns, preferred_element_type=jnp.float32)


def general_plan(
    activations,
    router_grad,
    token_ids,
    norm_terms,
    old_factors,
    old_router_factor,
    old_norm_diag,
    old_embed_diag,
):
    n_tensor = lax.axis_size("tensor")
    n_section = lax.axis_size("section")
    n_shard = lax.axis_size("shard")
    tensor_rank = lax.axis_index("tensor")
    section_rank = lax.axis_index("section")
    row_block = D // n_tensor
    col_block = D // n_section
    tokens_all = activations.shape[1] * n_shard
    row_start = tensor_rank * row_block
    col_start = section_rank * col_block

    def collect(carry, piece):
        whole = lax.all_gather(piece, ("tensor", "section"), axis=1, tiled=True)
        rows_part = lax.dynamic_slice_in_dim(whole, row_start, row_block, 1)
        cols_part = lax.dynamic_slice_in_dim(whole, col_start, col_block, 1)
        return (carry, (rows_part, cols_part))

    unused_carry, (row_parts, col_parts) = lax.scan(collect, jnp.int32(0), activations)
    partial_value = jnp.einsum(
        "mnr,mnc->mrc", row_parts, col_parts, preferred_element_type=jnp.float32
    )
    fresh = lax.psum_scatter(partial_value, "shard", scatter_dimension=0, tiled=True) / tokens_all
    row_index = lax.broadcasted_iota(jnp.int32, (row_block, col_block), 0) + row_start
    col_index = lax.broadcasted_iota(jnp.int32, (row_block, col_block), 1) + col_start
    eye_block = (row_index == col_index).astype(jnp.float32)
    matrix = factor_decay * old_factors + (1.0 - factor_decay) * fresh + damping * eye_block
    diag_part = jnp.sum(matrix * eye_block, axis=(1, 2))
    trace = lax.psum(diag_part, ("tensor", "section"))
    factor_scale = (D / (3.0 * trace))[:, None, None]
    matrix_low = lax.optimization_barrier(matrix.astype(jnp.bfloat16))
    first = 2.0 * factor_scale * eye_block - factor_scale * factor_scale * matrix_low.astype(
        jnp.float32
    )
    first_low = first.astype(jnp.bfloat16)
    first_cols = lax.all_gather(first_low, "tensor", axis=1, tiled=True)
    image = fold_with(first_cols, lax.all_gather(matrix_low, "section", axis=2, tiled=True))
    image_cols = lax.all_gather(image.astype(jnp.bfloat16), "tensor", axis=1, tiled=True)
    product = fold_with(image_cols, lax.all_gather(first_low, "section", axis=2, tiled=True))
    inverse_low = (2.0 * first - product).astype(jnp.bfloat16)
    inverses = lax.all_gather(inverse_low, "shard", axis=0, tiled=True)
    left_terms = jnp.stack(
        [
            jnp.einsum("nc,rc->nr", col_parts[m], inverses[m], preferred_element_type=jnp.float32)
            for m in (0, 4, 6)
        ]
    )
    left = lax.psum(left_terms, "section").astype(jnp.bfloat16)
    right_terms = jnp.stack(
        [
            jnp.einsum("nr,rc->nc", row_parts[m], inverses[m], preferred_element_type=jnp.float32)
            for m in (1, 2, 3, 5, 7)
        ]
    )
    right = lax.psum(right_terms, "tensor").astype(jnp.bfloat16)
    norm_values = norm_terms.astype(jnp.float32)
    router_part = jnp.einsum(
        "en,fn->ef", router_grad, router_grad, preferred_element_type=jnp.float32
    )
    router_sum, norm_total, norm_squares = lax.psum(
        (router_part, jnp.sum(norm_values, axis=1), jnp.sum(norm_values * norm_values, axis=1)),
        "shard",
    )
    router_matrix = (
        factor_decay * old_router_factor
        + (1.0 - factor_decay) * (router_sum / tokens_all)
        + damping * jnp.eye(EXPERTS, dtype=jnp.float32)
    )
    router_inverse = local_inverse(router_matrix)
    router_right = jnp.einsum(
        "en,ef->nf", router_grad, router_inverse, preferred_element_type=jnp.float32
    ).astype(jnp.bfloat16)
    precond_norms = (
        learning_rate
        * norm_total
        / (
            factor_decay * old_norm_diag
            + (1.0 - factor_decay) * (norm_squares / tokens_all)
            + damping
        )
    )
    ids_all = lax.all_gather(token_ids, "shard", axis=0, tiled=True)
    embed_all = lax.all_gather(right[4], "shard", axis=0, tiled=True)
    paired_left = jnp.stack([left[0], left[0], left[0], left[1]])
    attn_terms = jnp.einsum(
        "wnr,wnc->wrc", paired_left, right[:4], preferred_element_type=jnp.float32
    )
    router_term = jnp.einsum("nf,nr->fr", router_right, left[2], preferred_element_type=jnp.float32)
    attn_sum, router_total = lax.psum((attn_terms, router_term), "shard")
    precond_attn = learning_rate * attn_sum
    precond_router = learning_rate * router_total
    vocab_block = VOCAB // n_tensor
    step_rows = math.gcd(vocab_block, 512)
    vocab_start = tensor_rank * vocab_block

    def embed_block(block_index):
        ids_here = vocab_start + block_index * step_rows + lax.iota(jnp.int32, step_rows)
        onehot = (ids_here[:, None] == ids_all[None, :]).astype(jnp.bfloat16)
        summed = jnp.dot(onehot, embed_all, preferred_element_type=jnp.float32)
        tallies = jnp.sum(onehot, axis=1, dtype=jnp.float32)
        return (summed, tallies)

    block_sums, block_counts = lax.map(
        embed_block, jnp.arange(vocab_block // step_rows, dtype=jnp.int32)
    )
    embed_sum = block_sums.reshape(vocab_block, col_block)
    counts = block_counts.reshape(vocab_block)
    divisor = factor_decay * old_embed_diag + (1.0 - factor_decay) * (counts / tokens_all) + damping
    precond_embed = learning_rate * embed_sum / divisor[:, None]
    return (precond_attn, precond_router, precond_norms, precond_embed)


def split_three(values):
    high = lax.reduce_precision(values, 8, 7)
    rest = values - high
    middle = lax.reduce_precision(rest, 8, 7)
    return jnp.stack([high, middle, rest - middle], axis=-2).astype(jnp.bfloat16)


def swap(value, axis, size, step):
    return lax.ppermute(value, axis, [(i, i ^ step) for i in range(size)])


def local_diagonals(blocks):
    width = blocks.shape[1]
    pieces = []
    for start in range(0, width, 128):
        size = min(128, width - start)
        tile = blocks[:, start : start + size, start : start + size]
        pieces.append(jnp.sum(tile * jnp.eye(size, dtype=tile.dtype), axis=1))
    return jnp.concatenate(pieces, axis=1)


def rounded(values):
    return values.astype(jnp.bfloat16).astype(jnp.float32)


def params():
    return pltpu.CompilerParams(vmem_limit_bytes=40 * 1024 * 1024)


def layout_kernel(place_ref, *refs, weight):
    gathered, (features, rows, low_diag, trace, old) = refs[:4], refs[4:]
    own_place, layer, core, here = (place_ref[index] for index in range(4))
    steps, _, tokens = gathered[0].shape
    sections = len(gathered)
    groups, depth, _ = features.shape
    part = depth // (sections * steps)
    width = depth // steps
    for away in range(sections):
        section = here ^ away
        codes = jnp.zeros((16, tokens), jnp.float32)
        for step in range(steps):
            start = pl.multiple_of((step * sections + section) * part, 16)
            for group in range(groups):
                features[group, pl.ds(start, part)] = gathered[away][
                    step, group * part : (group + 1) * part
                ]
            codes += gathered[away][step, groups * part :].astype(jnp.float32)
        codes = codes[0:3] + codes[3:6] + codes[6:9]
        pieces = [codes[0:1], codes[1:2], codes[2:3, : width - 2 * tokens]]
        old[section ^ layer] = jnp.concatenate(pieces, axis=1)
    ones = jnp.ones((8, tokens), jnp.bfloat16)
    total = jnp.float32(0.0)
    for step in range(steps):
        squares = jnp.zeros((8, width), jnp.float32)
        for group in range(groups):
            values = features[group, step * width : (step + 1) * width].astype(jnp.float32)
            values = values * values
            high = values.astype(jnp.bfloat16)
            low = (values - high.astype(jnp.float32)).astype(jnp.bfloat16)
            for piece in (high, low):
                squares += lax.dot_general(
                    ones, piece, (((1,), (1,)), ((), ())), preferred_element_type=jnp.float32
                )
        diag = factor_decay * old[step] + weight * squares[0:1] + damping
        total += jnp.sum(diag)
        low_diag[step] = rounded(diag)
        start = pl.multiple_of((own_place ^ step) * width, width)
        mine = features[core, pl.ds(start, width)]
        rows[:, step * width : (step + 1) * width] = mine.T
    trace[0] = total


def lay_out(places, gathered, weight):
    steps, height, tokens = gathered[0].shape
    sections = len(gathered)
    part = (height - 16) // 2
    depth = sections * steps * part
    width = depth // steps
    vmem = pl.BlockSpec(memory_space=pltpu.VMEM)
    smem = pl.BlockSpec(memory_space=pltpu.SMEM)
    return pl.pallas_call(
        functools.partial(layout_kernel, weight=weight),
        in_specs=[smem] + [vmem] * sections,
        out_specs=[vmem, vmem, vmem, smem],
        out_shape=[
            jax.ShapeDtypeStruct((2, depth, tokens), jnp.bfloat16),
            jax.ShapeDtypeStruct((tokens, depth), jnp.bfloat16),
            jax.ShapeDtypeStruct((steps, 1, width), jnp.float32),
            jax.ShapeDtypeStruct((1,), jnp.float32),
        ],
        scratch_shapes=[pltpu.VMEM((steps, 1, width), jnp.float32)],
        compiler_params=params(),
        cost_estimate=pl.CostEstimate(
            flops=64 * depth * tokens, bytes_accessed=14 * depth * tokens, transcendentals=0
        ),
    )(places, *gathered)


def factor_kernel(place_ref, part, own, diag, *refs, step, weight):
    portions, out = refs[:-1], refs[-1]
    start = 0
    for old in portions:
        stop = start + old.shape[0]
        shape = (old.shape[0], out.shape[1])
        fresh = jnp.zeros(shape, jnp.float32)
        for index in range(part.shape[0]):
            fresh += lax.dot_general(
                part[index, start:stop],
                own[index],
                (((1,), (1,)), ((), ())),
                preferred_element_type=jnp.float32,
            )
        block = factor_decay * old[...].astype(jnp.float32) + weight * fresh
        on_diag = lax.broadcasted_iota(jnp.int32, shape, 0) + start == lax.broadcasted_iota(
            jnp.int32, shape, 1
        )
        block = jnp.where(on_diag & (place_ref[0] == step), diag[0], block)
        out[start:stop] = block.astype(jnp.bfloat16)
        start = stop


def factor_block(place, features, portions, diag, step, weight):
    groups, _, tokens = features.shape
    rows, cols = sum(old.shape[0] for old in portions), portions[0].shape[1]
    return pl.pallas_call(
        functools.partial(factor_kernel, step=step, weight=weight),
        grid_spec=pltpu.PrefetchScalarGridSpec(
            num_scalar_prefetch=1,
            grid=(1,),
            in_specs=[
                pl.BlockSpec((groups, rows, tokens), lambda i, place: (0, step, 0)),
                pl.BlockSpec((groups, cols, tokens), lambda i, place: (0, place[0], 0)),
                pl.BlockSpec((1, 1, cols), lambda i, place: (place[0], 0, 0)),
            ]
            + [pl.BlockSpec(old.shape, lambda i, place: (0, 0)) for old in portions],
            out_specs=pl.BlockSpec((rows, cols), lambda i, place: (0, 0)),
        ),
        out_shape=jax.ShapeDtypeStruct((rows, cols), jnp.bfloat16),
        compiler_params=params(),
        cost_estimate=pl.CostEstimate(
            flops=2 * groups * rows * cols * tokens,
            bytes_accessed=4 * rows * cols + 4 * groups * rows * tokens,
            transcendentals=0,
        ),
    )(place, features, features, diag, *portions)


def block_products(place_ref, halves, blocks, pieces):
    width = pieces.shape[2]
    for index, half in enumerate(halves):
        pieces[2 * index] = half[:, :width]
        pieces[2 * index + 1] = half[:, width:]
    products = [None, None]
    for step in range(4):
        piece = pieces[place_ref[0] ^ step]
        for index in range(2):
            term = jnp.dot(piece, blocks[4 * index + step][...], preferred_element_type=jnp.float32)
            products[index] = term if products[index] is None else products[index] + term
    return products


def first_parts(place_ref, scale, rows, diag, product, index):
    width = product.shape[1]
    square = scale * scale
    values = rows[:, index * width : (index + 1) * width].astype(jnp.float32)
    low_diag = diag[place_ref[0] ^ index]
    first_diag = rounded(2.0 * scale - square * low_diag)
    by_first = 2.0 * scale * values - square * product
    step_one = first_diag * values - square * (product - low_diag * values)
    return by_first, step_one, low_diag, first_diag


def first_kernel(place_ref, scale_ref, rows, diag, *refs):
    blocks, (kept, message, pieces) = refs[:8], refs[8:]
    half = rows.shape[1] // 2
    halves = [rows[:, :half], rows[:, half:]]
    products = block_products(place_ref, halves, blocks, pieces)
    lows = []
    for index in range(2):
        kept[index] = products[index]
        parts = first_parts(place_ref, scale_ref[0], rows, diag, products[index], index)
        lows.append(parts[1].astype(jnp.bfloat16))
    message[...] = jnp.concatenate(lows, axis=1)


def second_kernel(place_ref, scale_ref, mine, theirs, rows, diag, before, *refs):
    blocks, (kept, message, pieces) = refs[:8], refs[8:]
    products = block_products(place_ref, [mine[...], theirs[...]], blocks, pieces)
    square = scale_ref[0] * scale_ref[0]
    lows = []
    for index in range(2):
        by_first, one, low_diag, first_diag = first_parts(
            place_ref, scale_ref[0], rows, diag, before[index], index
        )
        two = products[index] + low_diag * (one - rounded(one))
        low = two.astype(jnp.bfloat16)
        kept[index] = (
            2.0 * by_first - first_diag * two - square * low_diag * low.astype(jnp.float32)
        )
        lows.append(low)
    message[...] = jnp.concatenate(lows, axis=1)


def third_kernel(place_ref, scale_ref, mine, theirs, before, *refs):
    blocks, (keep, give, pieces) = refs[:8], refs[8:]
    products = block_products(place_ref, [mine[...], theirs[...]], blocks, pieces)
    square = scale_ref[0] * scale_ref[0]
    for index, out in ((0, keep), (1, give)):
        out[...] = (before[index] + square * products[index]).T.astype(jnp.bfloat16)


def chain_call(kernel, scalars, arrays, blocks, out_shape):
    tokens = arrays[0].shape[0]
    depth, width = blocks[0].shape
    vmem = pl.BlockSpec(memory_space=pltpu.VMEM)
    return pl.pallas_call(
        kernel,
        in_specs=[pl.BlockSpec(memory_space=pltpu.SMEM)] * len(scalars)
        + [vmem] * (len(arrays) + len(blocks)),
        out_specs=[vmem] * len(out_shape),
        out_shape=out_shape,
        scratch_shapes=[pltpu.VMEM((4, tokens, depth), jnp.bfloat16)],
        compiler_params=params(),
        cost_estimate=pl.CostEstimate(
            flops=2 * len(blocks) * tokens * depth * width,
            bytes_accessed=2 * len(blocks) * depth * width,
            transcendentals=0,
        ),
    )(*scalars, *arrays, *blocks)


def output_kernel(where_ref, scale, matches, *refs):
    lefts, rights, refs = refs[:4], refs[4:8], refs[-9:]
    attn, embed, left_held, held, found, attn_made, embed_made, sems, out_sems = refs
    owner, layer, turn = where_ref[0], where_ref[1], where_ref[2]
    rows = held.shape[1]

    for place in range(4):

        @pl.when(turn == place)
        def _():
            pltpu.make_async_copy(lefts[place].at[pl.ds(0, rows)], left_held, sems.at[4]).start()

    def fetch(sources):
        for slot, source in enumerate(sources):
            for place in range(4):

                @pl.when((layer ^ source) == place)
                def _():
                    pltpu.make_async_copy(rights[place], held.at[slot], sems.at[slot]).start()

    def left_arrived():
        pltpu.make_async_copy(left_held, left_held, sems.at[4]).wait()

    def arrived(slot):
        pltpu.make_async_copy(held.at[slot], held.at[slot], sems.at[slot]).wait()
        return held[slot]

    def send_product(slot, target):
        attn_made[slot] = learning_rate * lax.dot_general(
            left_held[...],
            arrived(slot),
            (((1,), (1,)), ((), ())),
            preferred_element_type=jnp.float32,
        )
        copy = pltpu.make_async_copy(attn_made.at[slot], attn.at[target], out_sems.at[slot])
        copy.start()
        return copy

    @pl.when(owner == 0)
    def _():
        fetch((0, 1, 3))
        left_arrived()
        for copy in [send_product(slot, slot) for slot in range(3)]:
            copy.wait()

    @pl.when(owner == 1)
    def _():
        fetch((0, 3))
        found_copy = pltpu.make_async_copy(matches, found, sems.at[5])
        found_copy.start()
        left_arrived()
        results = [send_product(0, 3)]
        right = arrived(1)
        found_copy.wait()
        part = found.shape[1] // 4
        for index in range(4):
            cols = pl.ds(index * part, part)
            product = jnp.dot(right, found[:, cols], preferred_element_type=jnp.float32)
            embed_made[:, cols] = product * scale[:, cols]
            results.append(
                pltpu.make_async_copy(
                    embed_made.at[:, cols], embed.at[:, cols], out_sems.at[3 + index]
                )
            )
            results[-1].start()
        for copy in results:
            copy.wait()


def output_products(where, scale, matches, lefts, rights, made):
    cols, tokens_all = rights[0].shape
    vocab_block = scale.shape[1]
    anywhere = pl.BlockSpec(memory_space=pl.ANY)
    return pl.pallas_call(
        output_kernel,
        in_specs=[
            pl.BlockSpec(memory_space=pltpu.SMEM),
            pl.BlockSpec(memory_space=pltpu.VMEM),
        ]
        + [anywhere] * (9 + len(made)),
        out_specs=(anywhere, anywhere),
        out_shape=(
            jax.ShapeDtypeStruct((4, cols, cols), jnp.float32),
            jax.ShapeDtypeStruct((cols, vocab_block), jnp.float32),
        ),
        input_output_aliases={11: 0, 12: 1} if made else {},
        scratch_shapes=[
            pltpu.VMEM((cols, tokens_all), jnp.bfloat16),
            pltpu.VMEM((3, cols, tokens_all), jnp.bfloat16),
            pltpu.VMEM((tokens_all, vocab_block), jnp.bfloat16),
            pltpu.VMEM((3, cols, cols), jnp.float32),
            pltpu.VMEM((cols, vocab_block), jnp.float32),
            pltpu.SemaphoreType.DMA((6,)),
            pltpu.SemaphoreType.DMA((7,)),
        ],
        compiler_params=pltpu.CompilerParams(vmem_limit_bytes=60 * 1024 * 1024),
        cost_estimate=pl.CostEstimate(
            flops=6 * cols * cols * tokens_all,
            bytes_accessed=12 * cols * cols + 8 * cols * tokens_all,
            transcendentals=0,
        ),
    )(where, scale, matches, *lefts, *rights, *made)


def layer_plan(
    activations,
    router_grad,
    token_ids,
    norm_terms,
    old_factors,
    old_router_factor,
    old_norm_diag,
    old_embed_diag,
):
    n_tensor = lax.axis_size("tensor")
    n_section = lax.axis_size("section")
    n_shard = lax.axis_size("shard")
    shard = lax.axis_index("shard")
    layer = lax.axis_index("tensor")
    section = lax.axis_index("section")
    core = section % 2
    owned, row_block, col_block = old_factors.shape
    tokens = activations.shape[1]
    features_dev = activations.shape[2]
    tokens_all = tokens * n_shard
    weight = (1.0 - factor_decay) / tokens_all
    own_place = section ^ layer
    place = own_place.reshape(1)
    axes = ("shard", "tensor")

    def by_index(array, index, axis=0):
        return lax.dynamic_index_in_dim(array, index, axis, False)

    def held_by(layer_index):
        return jnp.where(layer_index == 3, 3, lax.rem(layer_index + 1, 3))

    by_feature = jnp.swapaxes(activations, 1, 2)
    diagonals = local_diagonals(old_factors) * (layer == section).astype(jnp.float32)
    extra = jnp.pad(split_three(diagonals), ((0, 0), (0, 0), (0, 3 * tokens - col_block)))
    extra = jnp.pad(extra.reshape(owned, 9, tokens), ((0, 0), (0, 7), (0, 0)))
    collected = []
    for step in range(n_tensor):
        factor = held_by(layer ^ step)
        message = jnp.concatenate(
            [
                by_index(by_feature, shard * owned + factor),
                by_index(by_feature, (1 - shard) * owned + factor),
                by_index(extra, factor),
            ],
            axis=0,
        )
        collected.append(swap(message, "tensor", n_tensor, step) if step else message)
    collected = jnp.stack(collected)

    def old_block(factors, step):
        return by_index(factors, held_by(layer ^ step)).astype(jnp.bfloat16)

    far_block = swap(old_block(old_factors, 2), "tensor", n_tensor, 2)

    def both_shards(value, axis):
        other = swap(value, "shard", n_shard, 1)
        return jnp.where(
            shard == 0,
            jnp.concatenate([value, other], axis=axis),
            jnp.concatenate([other, value], axis=axis),
        )

    grad_all = both_shards(router_grad, 1)
    ids_all = both_shards(token_ids, 0)
    norm_values = norm_terms.astype(jnp.float32)
    norm_sums = jnp.stack([jnp.sum(norm_values, axis=1), jnp.sum(norm_values * norm_values, axis=1)])
    norm_sums = norm_sums + swap(norm_sums, "shard", n_shard, 1)
    vocab_block = old_embed_diag.shape[0]
    ids_here = layer * vocab_block + lax.iota(jnp.int32, vocab_block)
    matches = (ids_all[:, None] == ids_here[None, :]).astype(jnp.bfloat16)
    counts = jnp.sum(matches, axis=0, dtype=jnp.float32)
    divisor = factor_decay * old_embed_diag + (1.0 - factor_decay) * (counts / tokens_all) + damping
    embed_scale = (learning_rate / divisor)[None, :]
    router_matrix = (
        factor_decay * old_router_factor
        + weight * jnp.einsum("en,fn->ef", grad_all, grad_all, preferred_element_type=jnp.float32)
        + damping * jnp.eye(EXPERTS, dtype=jnp.float32)
    )
    router_inverse = local_inverse(router_matrix)
    router_right = jnp.einsum(
        "en,ef->fn", grad_all, router_inverse, preferred_element_type=jnp.float32
    ).astype(jnp.bfloat16)

    later_factors, router_right = lax.optimization_barrier((old_factors, router_right))
    near_block = swap(old_block(later_factors, 1), "tensor", n_tensor, 1)
    here_block, farthest = old_block(later_factors, 0), old_block(later_factors, 3)
    other_tokens = swap(collected[:, features_dev : 2 * features_dev], "shard", n_shard, 1)
    small = (router_right, matches, embed_scale, norm_sums)
    other_tokens, collected, far_block, near_block, here_block, farthest, small = (
        lax.optimization_barrier(
            (other_tokens, collected, far_block, near_block, here_block, farthest, small)
        )
    )
    router_right, matches, embed_scale, norm_sums = small
    collected = jnp.concatenate(
        [collected[:, :features_dev], other_tokens, collected[:, 2 * features_dev :]], axis=1
    )
    by_side = swap(collected, "section", n_section, 2)
    by_core = swap(collected, "section", n_section, 1)
    part_rows = row_block // 2
    farthest_1 = swap(farthest[:part_rows], "tensor", n_tensor, 3)
    by_side, farthest_1 = lax.optimization_barrier((by_side, farthest_1))
    by_both = swap(by_side, "section", n_section, 1)
    farthest_2 = swap(farthest[part_rows:], "tensor", n_tensor, 3)
    blocks = [(here_block,), (near_block,), (far_block,), (farthest_1, farthest_2)]

    features, rows, low_diag, trace = lay_out(
        jnp.stack([own_place, layer, core, section]),
        (collected, by_core, by_side, by_both),
        weight,
    )
    scale = D / (3.0 * trace)
    own_cols = [
        factor_block(place, features, blocks[step], low_diag, step, weight)
        for step in range(n_tensor)
    ]
    other_cols = [swap(block, "section", n_section, 1) for block in own_cols]
    cols = own_cols + other_cols

    wide = jax.ShapeDtypeStruct((2, tokens, col_block), jnp.float32)
    sent = jax.ShapeDtypeStruct((tokens, 2 * col_block), jnp.bfloat16)
    part = jax.ShapeDtypeStruct((col_block, tokens), jnp.bfloat16)
    scalars = (place, scale)
    kept, message = chain_call(first_kernel, scalars, (rows, low_diag), cols, (wide, sent))
    theirs = swap(message, "section", n_section, 2)
    kept, message = chain_call(
        second_kernel, scalars, (message, theirs, rows, low_diag, kept), cols, (wide, sent)
    )
    theirs = swap(message, "section", n_section, 2)
    keep, give = chain_call(third_kernel, scalars, (message, theirs, kept), cols, (part, part))
    got = swap(give, "section", n_section, 1)
    own = jnp.where(
        core == shard, jnp.concatenate([keep, got], axis=1), jnp.concatenate([got, keep], axis=1)
    )

    planes = range(n_shard)
    layers = range(n_tensor)

    def useful(x, z):
        return z != 2 and (x, z) != (1, 1)

    def send(value, step, held):
        moves = [
            (x * n_tensor + z, x * n_tensor + (z ^ step))
            for x in planes
            for z in layers
            if useful(x, z ^ held)
        ]
        return lax.ppermute(value, axes, moves)

    def across(value, held):
        moves = [
            (x * n_tensor + z, (1 - x) * n_tensor + z)
            for x in planes
            for z in layers
            if useful(x, z ^ held)
        ]
        return lax.ppermute(value, axes, moves)

    everywhere = ("shard", "tensor", "section")

    def spot(x, z, s):
        return (x * n_tensor + z) * n_section + s

    def scatter(value, source):
        moved_here = lax.ppermute(
            value,
            everywhere,
            [(spot(x, source, s), spot(x, s, s)) for x in planes for s in layers if s != source],
        )
        return jnp.where(layer == source, value, moved_here)

    def to_side(value):
        return lax.ppermute(
            value, everywhere, [(spot(x, t, t), spot(x, t, t ^ 2)) for x in planes for t in layers]
        )

    def to_core(value):
        return lax.ppermute(
            value, everywhere, [(spot(x, t, t), spot(x, t, t ^ 1)) for x in planes for t in layers]
        )

    def to_far(value):
        return lax.ppermute(
            value,
            everywhere,
            [(spot(x, t, t ^ 2), spot(x, t, t ^ 3)) for x in planes for t in layers],
        )

    near_1 = send(own, 1, 0)
    near_2 = send(own, 2, 0)
    over_0 = across(own, 0)
    left_here = scatter(own, 2)
    near_1, own = lax.optimization_barrier((near_1, own))
    over_1 = across(near_1, 1)
    left_there = lax.ppermute(
        left_here, everywhere, [(spot(x, t, t), spot(1 - x, t, t)) for x in planes for t in layers]
    )
    router_cols = learning_rate * jnp.einsum(
        "fn,cn->fc", router_right, own, preferred_element_type=jnp.float32
    )
    router_moved = lax.ppermute(
        router_cols, everywhere, [(spot(1, 1, s), spot(1, s, s)) for s in layers if s != 1]
    )
    router_cols = jnp.where(layer == 1, router_cols, router_moved)
    side_here = to_side(left_here)
    lefts_here = (left_here, to_core(left_here), side_here, to_far(side_here))
    near_2, over_0, over_1, router_cols = lax.optimization_barrier(
        (near_2, over_0, over_1, router_cols)
    )
    near_3 = send(near_2, 1, 2)
    over_2 = across(near_2, 2)
    router_there = lax.ppermute(
        router_cols, everywhere, [(spot(1, t, t), spot(0, t, t)) for t in layers]
    )
    near_3, over_2, router_there, left_there = lax.optimization_barrier(
        (near_3, over_2, router_there, left_there)
    )
    over_3 = across(near_3, 3)
    router_cols = jnp.where(shard == 1, router_cols, router_there)
    router_side, router_core = to_side(router_cols), to_core(router_cols)
    turn = section ^ layer
    made = output_products(
        jnp.stack([shard, layer, turn]),
        embed_scale,
        matches,
        lefts_here,
        (own, near_1, near_2, near_3),
        (),
    )
    side_there, over_3, router_side, router_core, made = lax.optimization_barrier(
        (to_side(left_there), over_3, router_side, router_core, made)
    )
    lefts_there = (left_there, to_core(left_there), side_there, to_far(side_there))
    routers = (router_cols, router_core, router_side, to_far(router_side))
    precond_router = routers[3]
    for index in (2, 1, 0):
        precond_router = jnp.where(turn == index, routers[index], precond_router)

    precond_attn, embed_columns = output_products(
        jnp.stack([1 - shard, layer, turn]),
        embed_scale,
        matches,
        lefts_there,
        (over_0, over_1, over_2, over_3),
        made,
    )
    precond_embed = embed_columns.T

    precond_norms = (
        learning_rate
        * norm_sums[0]
        / (
            factor_decay * old_norm_diag
            + (1.0 - factor_decay) * (norm_sums[1] / tokens_all)
            + damping
        )
    )
    return (precond_attn, precond_router, precond_norms, precond_embed)


def per_device(*arguments):
    one_each = arguments[4].shape[0] == lax.axis_size("tensor") == lax.axis_size("section")
    if one_each and lax.axis_size("section") == 4 and lax.axis_size("shard") == 2:
        return layer_plan(*arguments)
    return general_plan(*arguments)


def solution(mesh):
    return jax.shard_map(
        per_device,
        mesh=mesh,
        in_specs=(
            P(None, "shard", ("tensor", "section")),
            P(None, "shard"),
            P("shard"),
            P(None, "shard", ("tensor", "section")),
            P("shard", "tensor", "section"),
            P(),
            P(None, ("tensor", "section")),
            P("tensor"),
        ),
        out_specs=(
            P(None, "tensor", "section"),
            P(None, "tensor"),
            P(None, ("tensor", "section")),
            P("tensor", "section"),
        ),
        check_vma=False,
    )
```

```python
import functools
import math

import jax
import jax.numpy as jnp
from jax import lax
from jax.experimental import pallas as pl
from jax.experimental.pallas import tpu as pltpu
from jax.sharding import PartitionSpec as P

D = 2304
EXPERTS = 8
VOCAB = 8192


factor_decay = 0.5
damping = 0.01
learning_rate = 0.05


def local_inverse(matrix):
    width = matrix.shape[0]
    trace = jnp.sum(jnp.diagonal(matrix))
    factor_scale = width / (3.0 * trace)
    identity = jnp.eye(width, dtype=jnp.float32)
    matrix_low = lax.optimization_barrier(matrix.astype(jnp.bfloat16))
    first = 2.0 * factor_scale * identity - factor_scale * factor_scale * matrix_low.astype(
        jnp.float32
    )
    first_low = first.astype(jnp.bfloat16)
    image = jnp.dot(matrix_low, first_low, preferred_element_type=jnp.float32).astype(jnp.bfloat16)
    product = jnp.dot(first_low, image, preferred_element_type=jnp.float32)
    return (2.0 * first - product).astype(jnp.bfloat16)


def fold_with(columns, piece):
    return jnp.einsum("kij,kjl->kil", piece, columns, preferred_element_type=jnp.float32)


def general_plan(
    activations,
    router_grad,
    token_ids,
    norm_terms,
    old_factors,
    old_router_factor,
    old_norm_diag,
    old_embed_diag,
):
    n_tensor = lax.axis_size("tensor")
    n_section = lax.axis_size("section")
    n_shard = lax.axis_size("shard")
    tensor_rank = lax.axis_index("tensor")
    section_rank = lax.axis_index("section")
    row_block = D // n_tensor
    col_block = D // n_section
    tokens_all = activations.shape[1] * n_shard
    row_start = tensor_rank * row_block
    col_start = section_rank * col_block

    def collect(carry, piece):
        whole = lax.all_gather(piece, ("tensor", "section"), axis=1, tiled=True)
        rows_part = lax.dynamic_slice_in_dim(whole, row_start, row_block, 1)
        cols_part = lax.dynamic_slice_in_dim(whole, col_start, col_block, 1)
        return (carry, (rows_part, cols_part))

    unused_carry, (row_parts, col_parts) = lax.scan(collect, jnp.int32(0), activations)
    partial_value = jnp.einsum(
        "mnr,mnc->mrc", row_parts, col_parts, preferred_element_type=jnp.float32
    )
    fresh = lax.psum_scatter(partial_value, "shard", scatter_dimension=0, tiled=True) / tokens_all
    row_index = lax.broadcasted_iota(jnp.int32, (row_block, col_block), 0) + row_start
    col_index = lax.broadcasted_iota(jnp.int32, (row_block, col_block), 1) + col_start
    eye_block = (row_index == col_index).astype(jnp.float32)
    matrix = factor_decay * old_factors + (1.0 - factor_decay) * fresh + damping * eye_block
    diag_part = jnp.sum(matrix * eye_block, axis=(1, 2))
    trace = lax.psum(diag_part, ("tensor", "section"))
    factor_scale = (D / (3.0 * trace))[:, None, None]
    matrix_low = lax.optimization_barrier(matrix.astype(jnp.bfloat16))
    first = 2.0 * factor_scale * eye_block - factor_scale * factor_scale * matrix_low.astype(
        jnp.float32
    )
    first_low = first.astype(jnp.bfloat16)
    first_cols = lax.all_gather(first_low, "tensor", axis=1, tiled=True)
    image = fold_with(first_cols, lax.all_gather(matrix_low, "section", axis=2, tiled=True))
    image_cols = lax.all_gather(image.astype(jnp.bfloat16), "tensor", axis=1, tiled=True)
    product = fold_with(image_cols, lax.all_gather(first_low, "section", axis=2, tiled=True))
    inverse_low = (2.0 * first - product).astype(jnp.bfloat16)
    inverses = lax.all_gather(inverse_low, "shard", axis=0, tiled=True)
    left_terms = jnp.stack(
        [
            jnp.einsum("nc,rc->nr", col_parts[m], inverses[m], preferred_element_type=jnp.float32)
            for m in (0, 4, 6)
        ]
    )
    left = lax.psum(left_terms, "section").astype(jnp.bfloat16)
    right_terms = jnp.stack(
        [
            jnp.einsum("nr,rc->nc", row_parts[m], inverses[m], preferred_element_type=jnp.float32)
            for m in (1, 2, 3, 5, 7)
        ]
    )
    right = lax.psum(right_terms, "tensor").astype(jnp.bfloat16)
    norm_values = norm_terms.astype(jnp.float32)
    router_part = jnp.einsum(
        "en,fn->ef", router_grad, router_grad, preferred_element_type=jnp.float32
    )
    router_sum, norm_total, norm_squares = lax.psum(
        (router_part, jnp.sum(norm_values, axis=1), jnp.sum(norm_values * norm_values, axis=1)),
        "shard",
    )
    router_matrix = (
        factor_decay * old_router_factor
        + (1.0 - factor_decay) * (router_sum / tokens_all)
        + damping * jnp.eye(EXPERTS, dtype=jnp.float32)
    )
    router_inverse = local_inverse(router_matrix)
    router_right = jnp.einsum(
        "en,ef->nf", router_grad, router_inverse, preferred_element_type=jnp.float32
    ).astype(jnp.bfloat16)
    precond_norms = (
        learning_rate
        * norm_total
        / (
            factor_decay * old_norm_diag
            + (1.0 - factor_decay) * (norm_squares / tokens_all)
            + damping
        )
    )
    ids_all = lax.all_gather(token_ids, "shard", axis=0, tiled=True)
    embed_all = lax.all_gather(right[4], "shard", axis=0, tiled=True)
    paired_left = jnp.stack([left[0], left[0], left[0], left[1]])
    attn_terms = jnp.einsum(
        "wnr,wnc->wrc", paired_left, right[:4], preferred_element_type=jnp.float32
    )
    router_term = jnp.einsum("nf,nr->fr", router_right, left[2], preferred_element_type=jnp.float32)
    attn_sum, router_total = lax.psum((attn_terms, router_term), "shard")
    precond_attn = learning_rate * attn_sum
    precond_router = learning_rate * router_total
    vocab_block = VOCAB // n_tensor
    step_rows = math.gcd(vocab_block, 512)
    vocab_start = tensor_rank * vocab_block

    def embed_block(block_index):
        ids_here = vocab_start + block_index * step_rows + lax.iota(jnp.int32, step_rows)
        onehot = (ids_here[:, None] == ids_all[None, :]).astype(jnp.bfloat16)
        summed = jnp.dot(onehot, embed_all, preferred_element_type=jnp.float32)
        tallies = jnp.sum(onehot, axis=1, dtype=jnp.float32)
        return (summed, tallies)

    block_sums, block_counts = lax.map(
        embed_block, jnp.arange(vocab_block // step_rows, dtype=jnp.int32)
    )
    embed_sum = block_sums.reshape(vocab_block, col_block)
    counts = block_counts.reshape(vocab_block)
    divisor = factor_decay * old_embed_diag + (1.0 - factor_decay) * (counts / tokens_all) + damping
    precond_embed = learning_rate * embed_sum / divisor[:, None]
    return (precond_attn, precond_router, precond_norms, precond_embed)


def split_three(values):
    high = lax.reduce_precision(values, 8, 7)
    rest = values - high
    middle = lax.reduce_precision(rest, 8, 7)
    return jnp.stack([high, middle, rest - middle], axis=-2).astype(jnp.bfloat16)


def swap(value, axis, size, step):
    return lax.ppermute(value, axis, [(i, i ^ step) for i in range(size)])


def local_diagonals(blocks):
    width = blocks.shape[1]
    pieces = []
    for start in range(0, width, 128):
        size = min(128, width - start)
        tile = blocks[:, start : start + size, start : start + size]
        pieces.append(jnp.sum(tile * jnp.eye(size, dtype=tile.dtype), axis=1))
    return jnp.concatenate(pieces, axis=1)


def rounded(values):
    return values.astype(jnp.bfloat16).astype(jnp.float32)


def params():
    return pltpu.CompilerParams(vmem_limit_bytes=40 * 1024 * 1024)


def layout_kernel(place_ref, *refs, weight):
    gathered, (features, rows, low_diag, trace, old) = refs[:4], refs[4:]
    own_place, layer, core, here = (place_ref[index] for index in range(4))
    steps, _, tokens = gathered[0].shape
    sections = len(gathered)
    groups, depth, _ = features.shape
    part = depth // (sections * steps)
    width = depth // steps
    for away in range(sections):
        section = here ^ away
        codes = jnp.zeros((16, tokens), jnp.float32)
        for step in range(steps):
            start = pl.multiple_of((step * sections + section) * part, 16)
            for group in range(groups):
                features[group, pl.ds(start, part)] = gathered[away][
                    step, group * part : (group + 1) * part
                ]
            codes += gathered[away][step, groups * part :].astype(jnp.float32)
        codes = codes[0:3] + codes[3:6] + codes[6:9]
        pieces = [codes[0:1], codes[1:2], codes[2:3, : width - 2 * tokens]]
        old[section ^ layer] = jnp.concatenate(pieces, axis=1)
    ones = jnp.ones((8, tokens), jnp.bfloat16)
    total = jnp.float32(0.0)
    for step in range(steps):
        squares = jnp.zeros((8, width), jnp.float32)
        for group in range(groups):
            values = features[group, step * width : (step + 1) * width].astype(jnp.float32)
            values = values * values
            high = values.astype(jnp.bfloat16)
            low = (values - high.astype(jnp.float32)).astype(jnp.bfloat16)
            for piece in (high, low):
                squares += lax.dot_general(
                    ones, piece, (((1,), (1,)), ((), ())), preferred_element_type=jnp.float32
                )
        diag = factor_decay * old[step] + weight * squares[0:1] + damping
        total += jnp.sum(diag)
        low_diag[step] = rounded(diag)
        start = pl.multiple_of((own_place ^ step) * width, width)
        mine = features[core, pl.ds(start, width)]
        rows[:, step * width : (step + 1) * width] = mine.T
    trace[0] = total


def lay_out(places, gathered, weight):
    steps, height, tokens = gathered[0].shape
    sections = len(gathered)
    part = (height - 16) // 2
    depth = sections * steps * part
    width = depth // steps
    vmem = pl.BlockSpec(memory_space=pltpu.VMEM)
    smem = pl.BlockSpec(memory_space=pltpu.SMEM)
    return pl.pallas_call(
        functools.partial(layout_kernel, weight=weight),
        in_specs=[smem] + [vmem] * sections,
        out_specs=[vmem, vmem, vmem, smem],
        out_shape=[
            jax.ShapeDtypeStruct((2, depth, tokens), jnp.bfloat16),
            jax.ShapeDtypeStruct((tokens, depth), jnp.bfloat16),
            jax.ShapeDtypeStruct((steps, 1, width), jnp.float32),
            jax.ShapeDtypeStruct((1,), jnp.float32),
        ],
        scratch_shapes=[pltpu.VMEM((steps, 1, width), jnp.float32)],
        compiler_params=params(),
        cost_estimate=pl.CostEstimate(
            flops=64 * depth * tokens, bytes_accessed=14 * depth * tokens, transcendentals=0
        ),
    )(places, *gathered)


def factor_kernel(place_ref, part, own, diag, *refs, step, weight):
    portions, out = refs[:-1], refs[-1]
    start = 0
    for old in portions:
        stop = start + old.shape[0]
        shape = (old.shape[0], out.shape[1])
        fresh = jnp.zeros(shape, jnp.float32)
        for index in range(part.shape[0]):
            fresh += lax.dot_general(
                part[index, start:stop],
                own[index],
                (((1,), (1,)), ((), ())),
                preferred_element_type=jnp.float32,
            )
        block = factor_decay * old[...].astype(jnp.float32) + weight * fresh
        on_diag = lax.broadcasted_iota(jnp.int32, shape, 0) + start == lax.broadcasted_iota(
            jnp.int32, shape, 1
        )
        block = jnp.where(on_diag & (place_ref[0] == step), diag[0], block)
        out[start:stop] = block.astype(jnp.bfloat16)
        start = stop


def factor_block(place, features, portions, diag, step, weight):
    groups, _, tokens = features.shape
    rows, cols = sum(old.shape[0] for old in portions), portions[0].shape[1]
    return pl.pallas_call(
        functools.partial(factor_kernel, step=step, weight=weight),
        grid_spec=pltpu.PrefetchScalarGridSpec(
            num_scalar_prefetch=1,
            grid=(1,),
            in_specs=[
                pl.BlockSpec((groups, rows, tokens), lambda i, place: (0, step, 0)),
                pl.BlockSpec((groups, cols, tokens), lambda i, place: (0, place[0], 0)),
                pl.BlockSpec((1, 1, cols), lambda i, place: (place[0], 0, 0)),
            ]
            + [pl.BlockSpec(old.shape, lambda i, place: (0, 0)) for old in portions],
            out_specs=pl.BlockSpec((rows, cols), lambda i, place: (0, 0)),
        ),
        out_shape=jax.ShapeDtypeStruct((rows, cols), jnp.bfloat16),
        compiler_params=params(),
        cost_estimate=pl.CostEstimate(
            flops=2 * groups * rows * cols * tokens,
            bytes_accessed=4 * rows * cols + 4 * groups * rows * tokens,
            transcendentals=0,
        ),
    )(place, features, features, diag, *portions)


def block_products(place_ref, halves, blocks, pieces):
    width = pieces.shape[2]
    for index, half in enumerate(halves):
        pieces[2 * index] = half[:, :width]
        pieces[2 * index + 1] = half[:, width:]
    products = [None, None]
    for step in range(4):
        piece = pieces[place_ref[0] ^ step]
        for index in range(2):
            term = jnp.dot(piece, blocks[4 * index + step][...], preferred_element_type=jnp.float32)
            products[index] = term if products[index] is None else products[index] + term
    return products


def first_parts(place_ref, scale, rows, diag, product, index):
    width = product.shape[1]
    square = scale * scale
    values = rows[:, index * width : (index + 1) * width].astype(jnp.float32)
    low_diag = diag[place_ref[0] ^ index]
    first_diag = rounded(2.0 * scale - square * low_diag)
    by_first = 2.0 * scale * values - square * product
    step_one = first_diag * values - square * (product - low_diag * values)
    return by_first, step_one, low_diag, first_diag


def first_kernel(place_ref, scale_ref, rows, diag, *refs):
    blocks, (kept, message, pieces) = refs[:8], refs[8:]
    half = rows.shape[1] // 2
    halves = [rows[:, :half], rows[:, half:]]
    products = block_products(place_ref, halves, blocks, pieces)
    lows = []
    for index in range(2):
        kept[index] = products[index]
        parts = first_parts(place_ref, scale_ref[0], rows, diag, products[index], index)
        lows.append(parts[1].astype(jnp.bfloat16))
    message[...] = jnp.concatenate(lows, axis=1)


def second_kernel(place_ref, scale_ref, mine, theirs, rows, diag, before, *refs):
    blocks, (kept, message, pieces) = refs[:8], refs[8:]
    products = block_products(place_ref, [mine[...], theirs[...]], blocks, pieces)
    square = scale_ref[0] * scale_ref[0]
    lows = []
    for index in range(2):
        by_first, one, low_diag, first_diag = first_parts(
            place_ref, scale_ref[0], rows, diag, before[index], index
        )
        two = products[index] + low_diag * (one - rounded(one))
        low = two.astype(jnp.bfloat16)
        kept[index] = (
            2.0 * by_first - first_diag * two - square * low_diag * low.astype(jnp.float32)
        )
        lows.append(low)
    message[...] = jnp.concatenate(lows, axis=1)


def third_kernel(place_ref, scale_ref, mine, theirs, before, *refs):
    blocks, (keep, give, pieces) = refs[:8], refs[8:]
    products = block_products(place_ref, [mine[...], theirs[...]], blocks, pieces)
    square = scale_ref[0] * scale_ref[0]
    for index, out in ((0, keep), (1, give)):
        out[...] = (before[index] + square * products[index]).T.astype(jnp.bfloat16)


def chain_call(kernel, scalars, arrays, blocks, out_shape):
    tokens = arrays[0].shape[0]
    depth, width = blocks[0].shape
    vmem = pl.BlockSpec(memory_space=pltpu.VMEM)
    return pl.pallas_call(
        kernel,
        in_specs=[pl.BlockSpec(memory_space=pltpu.SMEM)] * len(scalars)
        + [vmem] * (len(arrays) + len(blocks)),
        out_specs=[vmem] * len(out_shape),
        out_shape=out_shape,
        scratch_shapes=[pltpu.VMEM((4, tokens, depth), jnp.bfloat16)],
        compiler_params=params(),
        cost_estimate=pl.CostEstimate(
            flops=2 * len(blocks) * tokens * depth * width,
            bytes_accessed=2 * len(blocks) * depth * width,
            transcendentals=0,
        ),
    )(*scalars, *arrays, *blocks)


def output_kernel(where_ref, scale, matches, *refs):
    lefts, rights, refs = refs[:4], refs[4:8], refs[-9:]
    attn, embed, left_held, held, found, attn_made, embed_made, sems, out_sems = refs
    owner, layer, turn = where_ref[0], where_ref[1], where_ref[2]
    rows = held.shape[1]

    for place in range(4):

        @pl.when(turn == place)
        def _():
            pltpu.make_async_copy(lefts[place].at[pl.ds(0, rows)], left_held, sems.at[4]).start()

    def fetch(sources):
        for slot, source in enumerate(sources):
            for place in range(4):

                @pl.when((layer ^ source) == place)
                def _():
                    pltpu.make_async_copy(rights[place], held.at[slot], sems.at[slot]).start()

    def left_arrived():
        pltpu.make_async_copy(left_held, left_held, sems.at[4]).wait()

    def arrived(slot):
        pltpu.make_async_copy(held.at[slot], held.at[slot], sems.at[slot]).wait()
        return held[slot]

    def send_product(slot, target):
        attn_made[slot] = learning_rate * lax.dot_general(
            left_held[...],
            arrived(slot),
            (((1,), (1,)), ((), ())),
            preferred_element_type=jnp.float32,
        )
        copy = pltpu.make_async_copy(attn_made.at[slot], attn.at[target], out_sems.at[slot])
        copy.start()
        return copy

    @pl.when(owner == 0)
    def _():
        fetch((0, 1, 3))
        left_arrived()
        for copy in [send_product(slot, slot) for slot in range(3)]:
            copy.wait()

    @pl.when(owner == 1)
    def _():
        fetch((0, 3))
        found_copy = pltpu.make_async_copy(matches, found, sems.at[5])
        found_copy.start()
        left_arrived()
        results = [send_product(0, 3)]
        right = arrived(1)
        found_copy.wait()
        part = found.shape[1] // 4
        for index in range(4):
            cols = pl.ds(index * part, part)
            product = jnp.dot(right, found[:, cols], preferred_element_type=jnp.float32)
            embed_made[:, cols] = product * scale[:, cols]
            results.append(
                pltpu.make_async_copy(
                    embed_made.at[:, cols], embed.at[:, cols], out_sems.at[3 + index]
                )
            )
            results[-1].start()
        for copy in results:
            copy.wait()


def output_products(where, scale, matches, lefts, rights, made):
    cols, tokens_all = rights[0].shape
    vocab_block = scale.shape[1]
    anywhere = pl.BlockSpec(memory_space=pl.ANY)
    return pl.pallas_call(
        output_kernel,
        in_specs=[
            pl.BlockSpec(memory_space=pltpu.SMEM),
            pl.BlockSpec(memory_space=pltpu.VMEM),
        ]
        + [anywhere] * (9 + len(made)),
        out_specs=(anywhere, anywhere),
        out_shape=(
            jax.ShapeDtypeStruct((4, cols, cols), jnp.float32),
            jax.ShapeDtypeStruct((cols, vocab_block), jnp.float32),
        ),
        input_output_aliases={11: 0, 12: 1} if made else {},
        scratch_shapes=[
            pltpu.VMEM((cols, tokens_all), jnp.bfloat16),
            pltpu.VMEM((3, cols, tokens_all), jnp.bfloat16),
            pltpu.VMEM((tokens_all, vocab_block), jnp.bfloat16),
            pltpu.VMEM((3, cols, cols), jnp.float32),
            pltpu.VMEM((cols, vocab_block), jnp.float32),
            pltpu.SemaphoreType.DMA((6,)),
            pltpu.SemaphoreType.DMA((7,)),
        ],
        compiler_params=pltpu.CompilerParams(vmem_limit_bytes=60 * 1024 * 1024),
        cost_estimate=pl.CostEstimate(
            flops=6 * cols * cols * tokens_all,
            bytes_accessed=12 * cols * cols + 8 * cols * tokens_all,
            transcendentals=0,
        ),
    )(where, scale, matches, *lefts, *rights, *made)


def layer_plan(
    activations,
    router_grad,
    token_ids,
    norm_terms,
    old_factors,
    old_router_factor,
    old_norm_diag,
    old_embed_diag,
):
    n_tensor = lax.axis_size("tensor")
    n_section = lax.axis_size("section")
    n_shard = lax.axis_size("shard")
    shard = lax.axis_index("shard")
    layer = lax.axis_index("tensor")
    section = lax.axis_index("section")
    core = section % 2
    owned, row_block, col_block = old_factors.shape
    tokens = activations.shape[1]
    features_dev = activations.shape[2]
    tokens_all = tokens * n_shard
    weight = (1.0 - factor_decay) / tokens_all
    own_place = section ^ layer
    place = own_place.reshape(1)
    axes = ("shard", "tensor")

    def by_index(array, index, axis=0):
        return lax.dynamic_index_in_dim(array, index, axis, False)

    def held_by(layer_index):
        return jnp.where(layer_index == 3, 3, lax.rem(layer_index + 1, 3))

    by_feature = jnp.swapaxes(activations, 1, 2)
    diagonals = local_diagonals(old_factors) * (layer == section).astype(jnp.float32)
    extra = jnp.pad(split_three(diagonals), ((0, 0), (0, 0), (0, 3 * tokens - col_block)))
    extra = jnp.pad(extra.reshape(owned, 9, tokens), ((0, 0), (0, 7), (0, 0)))
    collected = []
    for step in range(n_tensor):
        factor = held_by(layer ^ step)
        message = jnp.concatenate(
            [
                by_index(by_feature, shard * owned + factor),
                by_index(by_feature, (1 - shard) * owned + factor),
                by_index(extra, factor),
            ],
            axis=0,
        )
        collected.append(swap(message, "tensor", n_tensor, step) if step else message)
    collected = jnp.stack(collected)

    def old_block(factors, step):
        return by_index(factors, held_by(layer ^ step)).astype(jnp.bfloat16)

    far_block = swap(old_block(old_factors, 2), "tensor", n_tensor, 2)

    def both_shards(value, axis):
        other = swap(value, "shard", n_shard, 1)
        return jnp.where(
            shard == 0,
            jnp.concatenate([value, other], axis=axis),
            jnp.concatenate([other, value], axis=axis),
        )

    grad_all = both_shards(router_grad, 1)
    ids_all = both_shards(token_ids, 0)
    norm_values = norm_terms.astype(jnp.float32)
    norm_sums = jnp.stack([jnp.sum(norm_values, axis=1), jnp.sum(norm_values * norm_values, axis=1)])
    norm_sums = norm_sums + swap(norm_sums, "shard", n_shard, 1)
    vocab_block = old_embed_diag.shape[0]
    ids_here = layer * vocab_block + lax.iota(jnp.int32, vocab_block)
    matches = (ids_all[:, None] == ids_here[None, :]).astype(jnp.bfloat16)
    counts = jnp.sum(matches, axis=0, dtype=jnp.float32)
    divisor = factor_decay * old_embed_diag + (1.0 - factor_decay) * (counts / tokens_all) + damping
    embed_scale = (learning_rate / divisor)[None, :]
    router_matrix = (
        factor_decay * old_router_factor
        + weight * jnp.einsum("en,fn->ef", grad_all, grad_all, preferred_element_type=jnp.float32)
        + damping * jnp.eye(EXPERTS, dtype=jnp.float32)
    )
    router_inverse = local_inverse(router_matrix)
    router_right = jnp.einsum(
        "en,ef->fn", grad_all, router_inverse, preferred_element_type=jnp.float32
    ).astype(jnp.bfloat16)

    later_factors, router_right = lax.optimization_barrier((old_factors, router_right))
    near_block = swap(old_block(later_factors, 1), "tensor", n_tensor, 1)
    here_block, farthest = old_block(later_factors, 0), old_block(later_factors, 3)
    other_tokens = swap(collected[:, features_dev : 2 * features_dev], "shard", n_shard, 1)
    small = (router_right, matches, embed_scale, norm_sums)
    other_tokens, collected, far_block, near_block, here_block, farthest, small = (
        lax.optimization_barrier(
            (other_tokens, collected, far_block, near_block, here_block, farthest, small)
        )
    )
    router_right, matches, embed_scale, norm_sums = small
    collected = jnp.concatenate(
        [collected[:, :features_dev], other_tokens, collected[:, 2 * features_dev :]], axis=1
    )
    by_side = swap(collected, "section", n_section, 2)
    by_core = swap(collected, "section", n_section, 1)
    part_rows = row_block // 2
    farthest_1 = swap(farthest[:part_rows], "tensor", n_tensor, 3)
    by_side, farthest_1 = lax.optimization_barrier((by_side, farthest_1))
    by_both = swap(by_side, "section", n_section, 1)
    farthest_2 = swap(farthest[part_rows:], "tensor", n_tensor, 3)
    blocks = [(here_block,), (near_block,), (far_block,), (farthest_1, farthest_2)]

    features, rows, low_diag, trace = lay_out(
        jnp.stack([own_place, layer, core, section]),
        (collected, by_core, by_side, by_both),
        weight,
    )
    scale = D / (3.0 * trace)
    own_cols = [
        factor_block(place, features, blocks[step], low_diag, step, weight)
        for step in range(n_tensor)
    ]
    other_cols = [swap(block, "section", n_section, 1) for block in own_cols]
    cols = own_cols + other_cols

    wide = jax.ShapeDtypeStruct((2, tokens, col_block), jnp.float32)
    sent = jax.ShapeDtypeStruct((tokens, 2 * col_block), jnp.bfloat16)
    part = jax.ShapeDtypeStruct((col_block, tokens), jnp.bfloat16)
    scalars = (place, scale)
    kept, message = chain_call(first_kernel, scalars, (rows, low_diag), cols, (wide, sent))
    theirs = swap(message, "section", n_section, 2)
    kept, message = chain_call(
        second_kernel, scalars, (message, theirs, rows, low_diag, kept), cols, (wide, sent)
    )
    theirs = swap(message, "section", n_section, 2)
    keep, give = chain_call(third_kernel, scalars, (message, theirs, kept), cols, (part, part))
    got = swap(give, "section", n_section, 1)
    own = jnp.where(
        core == shard, jnp.concatenate([keep, got], axis=1), jnp.concatenate([got, keep], axis=1)
    )

    planes = range(n_shard)
    layers = range(n_tensor)

    def useful(x, z):
        return z != 2 and (x, z) != (1, 1)

    def send(value, step, held):
        moves = [
            (x * n_tensor + z, x * n_tensor + (z ^ step))
            for x in planes
            for z in layers
            if useful(x, z ^ held)
        ]
        return lax.ppermute(value, axes, moves)

    def across(value, held):
        moves = [
            (x * n_tensor + z, (1 - x) * n_tensor + z)
            for x in planes
            for z in layers
            if useful(x, z ^ held)
        ]
        return lax.ppermute(value, axes, moves)

    everywhere = ("shard", "tensor", "section")

    def spot(x, z, s):
        return (x * n_tensor + z) * n_section + s

    def scatter(value, source):
        moved_here = lax.ppermute(
            value,
            everywhere,
            [(spot(x, source, s), spot(x, s, s)) for x in planes for s in layers if s != source],
        )
        return jnp.where(layer == source, value, moved_here)

    def to_side(value):
        return lax.ppermute(
            value, everywhere, [(spot(x, t, t), spot(x, t, t ^ 2)) for x in planes for t in layers]
        )

    def to_core(value):
        return lax.ppermute(
            value, everywhere, [(spot(x, t, t), spot(x, t, t ^ 1)) for x in planes for t in layers]
        )

    def straight_far(value):
        return lax.ppermute(
            value, everywhere, [(spot(x, t, t), spot(x, t, t ^ 3)) for x in planes for t in layers]
        )

    def to_far(value):
        return lax.ppermute(
            value,
            everywhere,
            [(spot(x, t, t ^ 2), spot(x, t, t ^ 3)) for x in planes for t in layers],
        )

    near_1 = send(own, 1, 0)
    near_2 = send(own, 2, 0)
    over_0 = across(own, 0)
    left_here = scatter(own, 2)
    near_1, own = lax.optimization_barrier((near_1, own))
    over_1 = across(near_1, 1)
    left_there = lax.ppermute(
        left_here, everywhere, [(spot(x, t, t), spot(1 - x, t, t)) for x in planes for t in layers]
    )
    router_cols = learning_rate * jnp.einsum(
        "fn,cn->fc", router_right, own, preferred_element_type=jnp.float32
    )
    router_moved = lax.ppermute(
        router_cols, everywhere, [(spot(1, 1, s), spot(1, s, s)) for s in layers if s != 1]
    )
    router_cols = jnp.where(layer == 1, router_cols, router_moved)
    side_here = to_side(left_here)
    lefts_here = (left_here, to_core(left_here), side_here, to_far(side_here))
    near_2, over_0, over_1, router_cols = lax.optimization_barrier(
        (near_2, over_0, over_1, router_cols)
    )
    near_3 = send(near_2, 1, 2)
    over_2 = across(near_2, 2)
    router_there = lax.ppermute(
        router_cols, everywhere, [(spot(1, t, t), spot(0, t, t)) for t in layers]
    )
    near_3, over_2, router_there, left_there = lax.optimization_barrier(
        (near_3, over_2, router_there, left_there)
    )
    over_3 = across(near_3, 3)
    router_cols = jnp.where(shard == 1, router_cols, router_there)
    router_side, router_core = to_side(router_cols), to_core(router_cols)
    turn = section ^ layer
    made = output_products(
        jnp.stack([shard, layer, turn]),
        embed_scale,
        matches,
        lefts_here,
        (own, near_1, near_2, near_3),
        (),
    )
    side_there, far_there, over_3, router_side, router_core, made = lax.optimization_barrier(
        (to_side(left_there), straight_far(left_there), over_3, router_side, router_core, made)
    )
    lefts_there = (left_there, to_core(left_there), side_there, far_there)
    routers = (router_cols, router_core, router_side, to_far(router_side))
    precond_router = routers[3]
    for index in (2, 1, 0):
        precond_router = jnp.where(turn == index, routers[index], precond_router)

    precond_attn, embed_columns = output_products(
        jnp.stack([1 - shard, layer, turn]),
        embed_scale,
        matches,
        lefts_there,
        (over_0, over_1, over_2, over_3),
        made,
    )
    precond_embed = embed_columns.T

    precond_norms = (
        learning_rate
        * norm_sums[0]
        / (
            factor_decay * old_norm_diag
            + (1.0 - factor_decay) * (norm_sums[1] / tokens_all)
            + damping
        )
    )
    return (precond_attn, precond_router, precond_norms, precond_embed)


def per_device(*arguments):
    one_each = arguments[4].shape[0] == lax.axis_size("tensor") == lax.axis_size("section")
    if one_each and lax.axis_size("section") == 4 and lax.axis_size("shard") == 2:
        return layer_plan(*arguments)
    return general_plan(*arguments)


def solution(mesh):
    return jax.shard_map(
        per_device,
        mesh=mesh,
        in_specs=(
            P(None, "shard", ("tensor", "section")),
            P(None, "shard"),
            P("shard"),
            P(None, "shard", ("tensor", "section")),
            P("shard", "tensor", "section"),
            P(),
            P(None, ("tensor", "section")),
            P("tensor"),
        ),
        out_specs=(
            P(None, "tensor", "section"),
            P(None, "tensor"),
            P(None, ("tensor", "section")),
            P("tensor", "section"),
        ),
        check_vma=False,
    )
```
